32 devices in a mesh: fsdp: 8 (over y, x, core), seq: 4 (over z).
Axes of the slice: x: 2, y: 2, z: 4, core: 2. Of those that a mesh axis runs over, the one named last changes fastest.
Arguments:
- tokens: bfloat16 [2, 8, 1536, 512], P(None, 'fsdp', 'seq'), may hold values from -6 to 6
- encoded: bfloat16 [2, 8, 256, 512], P(None, 'fsdp', 'seq'), may hold values from -6 to 6
- segment_ids: int32 [2, 8, 1536], P(None, 'fsdp'), may hold values from 0 to 4, as said below
- prefix_len: int32 [2, 8, 4], P(None, 'fsdp'), may hold values from 128 to 512, as said below
- cotangent: bfloat16 [2, 8, 1536, 512], P(None, 'fsdp', 'seq'), may hold values from -6 to 6
- w_query: bfloat16 [512, 512], P('fsdp'), may hold values from -0.25 to 0.25
- w_key: bfloat16 [512, 512], P('fsdp'), may hold values from -0.25 to 0.25
- w_value: bfloat16 [512, 512], P('fsdp'), may hold values from -0.25 to 0.25
- w_out: bfloat16 [512, 512], P('fsdp'), may hold values from -1 to 1
- c_query: bfloat16 [512, 512], P('fsdp'), may hold values from -0.25 to 0.25
- c_key: bfloat16 [512, 512], P('fsdp'), may hold values from -0.25 to 0.25
- c_value: bfloat16 [512, 512], P('fsdp'), may hold values from -0.25 to 0.25
- c_out: bfloat16 [512, 512], P('fsdp'), may hold values from -1 to 1
- w_up: bfloat16 [512, 2048], P('fsdp'), may hold values from -0.25 to 0.25
- b_up: bfloat16 [2048], P('fsdp'), may hold values from -3 to 3
- w_down: bfloat16 [2048, 512], P('fsdp'), may hold values from -0.125 to 0.125
- b_down: bfloat16 [512], P('fsdp'), may hold values from -3 to 3
- gain_one: bfloat16 [512], P('fsdp'), may hold values from 0.099609375 to 1.8984375
- shift_one: bfloat16 [512], P('fsdp'), may hold values from -3 to 3
- gain_two: bfloat16 [512], P('fsdp'), may hold values from 0.099609375 to 1.8984375
- shift_two: bfloat16 [512], P('fsdp'), may hold values from -3 to 3
- gain_three: bfloat16 [512], P('fsdp'), may hold values from 0.099609375 to 1.8984375
- shift_three: bfloat16 [512], P('fsdp'), may hold values from -3 to 3
- w_slot: bfloat16 [1024, 512], P('fsdp'), may hold values from -0.1875 to 0.1875
Outputs:
- slot_out: bfloat16 [2, 8, 1536, 512], P(None, 'fsdp', 'seq')
- grad_tokens: float32 [2, 8, 1536, 512], P(None, 'fsdp', 'seq')
- grad_encoded: float32 [2, 8, 256, 512], P(None, 'fsdp', 'seq')
- grad_w_query: float32 [512, 512], P('fsdp')
- grad_w_key: float32 [512, 512], P('fsdp')
- grad_w_value: float32 [512, 512], P('fsdp')
- grad_w_out: float32 [512, 512], P('fsdp')
- grad_c_query: float32 [512, 512], P('fsdp')
- grad_c_key: float32 [512, 512], P('fsdp')
- grad_c_value: float32 [512, 512], P('fsdp')
- grad_c_out: float32 [512, 512], P('fsdp')
- grad_w_up: float32 [512, 2048], P('fsdp')
- grad_b_up: float32 [2048], P('fsdp')
- grad_w_down: float32 [2048, 512], P('fsdp')
- grad_b_down: float32 [512], P('fsdp')
- grad_gain_one: float32 [512], P('fsdp')
- grad_shift_one: float32 [512], P('fsdp')
- grad_gain_two: float32 [512], P('fsdp')
- grad_shift_two: float32 [512], P('fsdp')
- grad_gain_three: float32 [512], P('fsdp')
- grad_shift_three: float32 [512], P('fsdp')
- grad_w_slot: float32 [1024, 512], P('fsdp')
The draws below stay inside these ranges and needn't reach their ends.
Inputs may be any that keep to these rules, and one draw needn't show every extreme that they name: `segment_ids`: in every group, positions 0 to 511 hold 0; the later positions hold continuation numbers 1 to 4, never falling, each number present on 128 or more positions. prefix_len[m, g, c] is the number of leading prompt positions that continuation c + 1 sees; continuation 1 of every group sees the whole prompt.
All inputs are finite; a program needn't handle non-finite values.
Results may differ from the reference program's by a relative error of at most 0.024.
Values may be sent and summed in bfloat16 or wider, within the bound.
A program may use at most 128 MiB of HBM per device.

```python
import math
import jax
import jax.numpy as jnp
from jax import lax

D = 512
HEADS = 8
HD = 64
FF = 2048
CONTS = 4
MICRO = 2
GROUPS = 8
PROMPT = 512
CONT = 256
GLEN = 1536
ENC = 256
QB = 512


def draw_segment_ids(key, part):
    shifts = jax.random.randint(key, (MICRO, GROUPS, CONTS - 1), -(CONT // 4), CONT // 4 + 1)
    bounds = PROMPT + CONT * jnp.arange(1, CONTS, dtype=jnp.int32) + shifts
    places = jnp.arange(GLEN, dtype=jnp.int32)
    later = jnp.sum((places[None, None, :, None] >= bounds[:, :, None, :]).astype(jnp.int32), axis=3)
    return jnp.where(places[None, None, :] >= PROMPT, 1 + later, 0).astype(jnp.int32)


def draw_prefix_len(key, part):
    seen_rows = jax.random.randint(key, (MICRO, GROUPS, CONTS), PROMPT // 4, PROMPT + 1)
    return seen_rows.at[:, :, 0].set(PROMPT).astype(jnp.int32)


def block_scale(rng, dims, pieces, smallest, top_value):
    loudness = 1.0
    for position, parts in pieces:
        heights = jax.random.uniform(jax.random.fold_in(jax.random.fold_in(rng, 6), position), (parts,), jnp.float32, smallest / len(pieces), top_value / len(pieces))
        loudness = loudness * jnp.repeat(jnp.exp(heights), dims[position] // parts).reshape((-1,) + (1,) * (len(dims) - 1 - position))
    return loudness


def normal_values(own_key, extent, width, bound, pieces=(), held_as=jnp.bfloat16):
    values = jax.random.normal(own_key, extent, jnp.float32) * width
    if len(pieces) > 0:
        values = block_scale(own_key, extent, pieces, -0.22, 0.18) * values
    return jnp.clip(values, min=-bound, max=bound).astype(held_as)


def setup_inputs(seed: int = 0) -> dict:
    streams_of = jax.random.split(jax.random.key(seed), 25)
    tokens = normal_values(streams_of[0], (MICRO, GROUPS, GLEN, D), 1.0, 6.0, ((1, 8), (2, 4)))
    encoded = normal_values(streams_of[1], (MICRO, GROUPS, ENC, D), 1.0, 6.0, ((1, 8), (2, 4)))
    segment_ids = draw_segment_ids(jax.random.fold_in(streams_of[24], 71), 0)
    prefix_len = draw_prefix_len(jax.random.fold_in(streams_of[24], 71), 0)
    cotangent = normal_values(streams_of[4], (MICRO, GROUPS, GLEN, D), 1.0, 6.0, ((1, 8), (2, 4)))
    w_query = normal_values(streams_of[5], (D, D), D ** -0.5, 0.25, ((0, 8),))
    w_key = normal_values(streams_of[6], (D, D), D ** -0.5, 0.25, ((0, 8),))
    w_value = normal_values(streams_of[7], (D, D), D ** -0.5, 0.25, ((0, 8),))
    w_out = normal_values(streams_of[8], (D, D), (D // 16) ** -0.5, 1.0, ((0, 8),))
    c_query = normal_values(streams_of[9], (D, D), D ** -0.5, 0.25, ((0, 8),))
    c_key = normal_values(streams_of[10], (D, D), D ** -0.5, 0.25, ((0, 8),))
    c_value = normal_values(streams_of[11], (D, D), D ** -0.5, 0.25, ((0, 8),))
    c_out = normal_values(streams_of[12], (D, D), (D // 16) ** -0.5, 1.0, ((0, 8),))
    w_up = normal_values(streams_of[13], (D, FF), D ** -0.5, 0.25, ((0, 8),))
    b_up = normal_values(streams_of[14], (FF,), 0.5, 3.0, ((0, 8),))
    w_down = normal_values(streams_of[15], (FF, D), FF ** -0.5, 0.125, ((0, 8),))
    b_down = normal_values(streams_of[16], (D,), 0.5, 3.0, ((0, 8),))
    gain_one = jnp.clip(1.0 + 0.18 * jax.random.normal(streams_of[17], (D,), jnp.float32), 0.099609375, 1.8984375).astype(jnp.bfloat16)
    shift_one = normal_values(streams_of[18], (D,), 0.5, 3.0, ((0, 8),))
    gain_two = jnp.clip(1.0 + 0.18 * jax.random.normal(streams_of[19], (D,), jnp.float32), 0.099609375, 1.8984375).astype(jnp.bfloat16)
    shift_two = normal_values(streams_of[20], (D,), 0.5, 3.0, ((0, 8),))
    gain_three = jnp.clip(1.0 + 0.18 * jax.random.normal(streams_of[21], (D,), jnp.float32), 0.099609375, 1.8984375).astype(jnp.bfloat16)
    shift_three = normal_values(streams_of[22], (D,), 0.5, 3.0, ((0, 8),))
    w_slot = normal_values(streams_of[23], (2 * D, D), (2 * D) ** -0.5, 0.1875, ((0, 8),))
    return {"tokens": tokens, "encoded": encoded, "segment_ids": segment_ids, "prefix_len": prefix_len, "cotangent": cotangent, "w_query": w_query, "w_key": w_key, "w_value": w_value, "w_out": w_out, "c_query": c_query, "c_key": c_key, "c_value": c_value, "c_out": c_out, "w_up": w_up, "b_up": b_up, "w_down": w_down, "b_down": b_down, "gain_one": gain_one, "shift_one": shift_one, "gain_two": gain_two, "shift_two": shift_two, "gain_three": gain_three, "shift_three": shift_three, "w_slot": w_slot}


EPSILON = 1e-05
HIGHEST = lax.Precision.HIGHEST

@jax.custom_vjp
def low(v):
    return lax.optimization_barrier(v.astype(jnp.bfloat16)).astype(jnp.float32)

@jax.custom_vjp
def low_back(v):
    return v

def low_keep(v):
    return (low(v), None)

def low_pass(kept, grad):
    return (grad,)

def back_keep(v):
    return (v, None)

def back_low(kept, grad):
    return (low(grad),)
low.defvjp(low_keep, low_pass)
low_back.defvjp(back_keep, back_low)

def layer_norm(residual, gain, shift):
    average = lax.optimization_barrier(jnp.mean(residual, axis=-1, keepdims=True))
    centred = residual - average
    variance = lax.optimization_barrier(jnp.mean(centred * centred, axis=-1, keepdims=True))
    return centred * lax.rsqrt(variance + EPSILON) * gain + shift

def matmul(left_side, right_side):
    return jnp.dot(left_side, right_side, precision=HIGHEST)

def visible(segment, prefix, offset, length):
    own_segment = lax.dynamic_slice_in_dim(segment, offset, length)
    numbers = jnp.arange(1, prefix.shape[0] + 1, dtype=jnp.int32)
    own_prefix = lax.optimization_barrier(jnp.sum(jnp.where(own_segment[:, None] == numbers[None, :], prefix[None, :], 0), axis=1))
    places = jnp.arange(segment.shape[0], dtype=jnp.int32)
    same_part = own_segment[:, None] == segment[None, :]
    prompt_part = (segment[None, :] == 0) & (places[None, :] < own_prefix[:, None])
    return same_part | prompt_part

def attend(query, keys, values, segment, prefix):
    span = keys.shape[0]
    head_keys = keys.reshape(span, HEADS, HD)
    head_values = values.reshape(span, HEADS, HD)
    scale = 1.0 / math.sqrt(HD)

    def one_block(number):
        offset = number * QB
        queries = lax.dynamic_slice_in_dim(query, offset, QB, 0).reshape(QB, HEADS, HD)
        scores = low_back(jnp.einsum('qhd,khd->hqk', queries, head_keys, precision=HIGHEST) * scale)
        if segment is not None:
            scores = jnp.where(visible(segment, prefix, offset, QB)[None], scores, -1e+30)
        maximum = lax.optimization_barrier(jnp.max(scores, axis=-1, keepdims=True))
        raw_weight = jnp.exp(scores - maximum)
        attn_prob = raw_weight / lax.optimization_barrier(jnp.sum(raw_weight, axis=-1, keepdims=True))
        mixture = jnp.einsum('hqk,khd->qhd', low(attn_prob), head_values, precision=HIGHEST)
        return mixture.reshape(QB, HEADS * HD)
    blocks = lax.map(jax.checkpoint(one_block), jnp.arange(GLEN // QB, dtype=jnp.int32))
    return blocks.reshape(GLEN, HEADS * HD)

def forward(token_rows, encoded_rows, segment, prefix, weights):
    w_query, w_key, w_value, w_out, c_query, c_key, c_value, c_out, w_up, b_up, w_down, b_down, gain_one, shift_one, gain_two, shift_two, gain_three, shift_three, w_slot = weights
    query = low_back(low(matmul(token_rows, w_query)))
    keys = low_back(low(matmul(token_rows, w_key)))
    values = low_back(low(matmul(token_rows, w_value)))
    self_mix = low_back(low(attend(query, keys, values, segment, prefix)))
    attn_out = low_back(matmul(self_mix, w_out))
    normed_one = layer_norm(token_rows + attn_out, gain_one, shift_one)
    normed_one_low = low(normed_one)
    cross_query = low_back(low(matmul(normed_one_low, c_query)))
    cross_keys = low_back(low(matmul(encoded_rows, c_key)))
    cross_values = low_back(low(matmul(encoded_rows, c_value)))
    cross_mix = low_back(low(attend(cross_query, cross_keys, cross_values, None, None)))
    cross_out = low_back(matmul(cross_mix, c_out))
    normed_two = layer_norm(normed_one + cross_out, gain_two, shift_two)
    normed_two_low = low(normed_two)
    pre_act = low_back(matmul(normed_two_low, w_up) + b_up)
    activation = low(jax.nn.gelu(pre_act))
    ffn_out = low_back(matmul(activation, w_down) + b_down)
    normed_three = layer_norm(normed_two + ffn_out, gain_three, shift_three)
    normed_three_low = low(normed_three)
    follow_mask = jnp.concatenate([segment[1:] == segment[:-1], jnp.zeros((1,), dtype=bool)]).astype(jnp.float32)[:, None]
    shifted = jnp.concatenate([normed_three_low[1:], jnp.zeros((1, D), jnp.float32)], axis=0)
    follow = low_back(shifted) * follow_mask
    joined = jnp.concatenate([normed_three_low, follow], axis=1)
    return matmul(joined, w_slot)

def reference(tokens, encoded, segment_ids, prefix_len, cotangent, w_query, w_key, w_value, w_out, c_query, c_key, c_value, c_out, w_up, b_up, w_down, b_down, gain_one, shift_one, gain_two, shift_two, gain_three, shift_three, w_slot):
    weights = tuple((weight_arg.astype(jnp.float32) for weight_arg in (w_query, w_key, w_value, w_out, c_query, c_key, c_value, c_out, w_up, b_up, w_down, b_down, gain_one, shift_one, gain_two, shift_two, gain_three, shift_three, w_slot)))
    items = MICRO * GROUPS
    token_all = tokens.astype(jnp.float32).reshape(items, GLEN, D)
    encoded_all = encoded.astype(jnp.float32).reshape(items, ENC, D)
    segment_all = segment_ids.reshape(items, GLEN)
    prefix_all = prefix_len.reshape(items, CONTS)
    upstream_all = cotangent.astype(jnp.float32).reshape(items, GLEN, D)

    def one_group(totals, item):
        token_rows, encoded_rows, segment, prefix, upstream = item

        def apply_layer(token_arg, encoded_arg, weight_args):
            return forward(token_arg, encoded_arg, segment, prefix, weight_args)
        slot_rows, backward = jax.vjp(apply_layer, token_rows, encoded_rows, weights)
        grad_rows, grad_states, grad_weights = backward(upstream)
        totals = jax.tree.map(lambda total_arg, grad_arg: total_arg + grad_arg, totals, grad_weights)
        return (totals, (slot_rows.astype(jnp.bfloat16), grad_rows, grad_states))
    zero_grads = jax.tree.map(jnp.zeros_like, weights)
    totals, (slots, grad_rows, grad_states) = lax.scan(one_group, zero_grads, (token_all, encoded_all, segment_all, prefix_all, upstream_all))
    t_query, t_key, t_value, t_out, t_cquery, t_ckey, t_cvalue, t_cout, t_up, t_upbias, t_down, t_downbias, t_gain_one, t_shift_one, t_gain_two, t_shift_two, t_gain_three, t_shift_three, t_slot = totals
    return (slots.reshape(MICRO, GROUPS, GLEN, D), grad_rows.reshape(MICRO, GROUPS, GLEN, D), grad_states.reshape(MICRO, GROUPS, ENC, D), t_query, t_key, t_value, t_out, t_cquery, t_ckey, t_cvalue, t_cout, t_up, t_upbias, t_down, t_downbias, t_gain_one, t_shift_one, t_gain_two, t_shift_two, t_gain_three, t_shift_three, t_slot)
```

```python
import functools
import math

import jax
import jax.numpy as jnp
from jax import lax
from jax.experimental import pallas as pl
from jax.experimental.pallas import tpu as pltpu
from jax.sharding import PartitionSpec as P

D = 512
HD = 64
HEADS = 8
FF = 2048
MICRO = 2
HALO = 16
EPSILON = 1e-05
BF = jnp.bfloat16
F32 = jnp.float32
SCALE = 1.0 / math.sqrt(HD)
NEG = -1e30
MIB = 1024 * 1024
GELU_C = math.sqrt(2.0 / math.pi)

VM = pl.BlockSpec(memory_space=pltpu.VMEM)


def nn(a, b):
    return lax.dot_general(a, b, (((1,), (0,)), ((), ())), preferred_element_type=F32)


def nt(a, b):
    return lax.dot_general(a, b, (((1,), (1,)), ((), ())), preferred_element_type=F32)


def tn(a, b):
    return lax.dot_general(a, b, (((0,), (0,)), ((), ())), preferred_element_type=F32)


def lanes_of(pair):
    return pl.ds(pl.multiple_of(pair * 128, 128), 128)


def head_masked(value, head):
    lane = lax.broadcasted_iota(jnp.int32, value.shape, 1)
    return jnp.where((lane >= 64) == (head == 1), value, jnp.zeros_like(value))


def softmax_parts(scores):
    top = jnp.max(scores, axis=-1, keepdims=True)
    raw = jnp.exp(scores - top)
    total = jnp.sum(raw, axis=-1, keepdims=True)
    return raw, top, total


def attend_pair(query_pair, key_pair, value_pair, bias, pair, lse_ref):
    mixed = []
    for head in range(2):
        scores = nt(head_masked(query_pair, head), key_pair)
        if bias is not None:
            scores = scores + bias
        raw, top, total = softmax_parts(scores)
        mixed.append(nn(raw.astype(BF), value_pair) / total)
        lane = lax.broadcasted_iota(jnp.int32, lse_ref.shape, 1)
        lse_ref[...] = jnp.where(lane == pair * 2 + head, top + jnp.log(total), lse_ref[...])
    lane = lax.broadcasted_iota(jnp.int32, mixed[0].shape, 1)
    return jnp.where(lane < 64, mixed[0], mixed[1])


def self_forward_kernel(
    glen, rows, x_ref, wq_ref, wk_ref, wv_ref, col_ref, row_ref,
    q_ref, k_ref, v_ref, mix_ref, lse_out, bias, lse_sc,
):
    prompt = glen // 3
    rank = lax.axis_index("seq")
    off = pl.multiple_of(rank * rows, 128)
    edge = pl.multiple_of(jnp.minimum(rank * rows + rows, glen - HALO), HALO)
    wk = wk_ref[...].reshape(D, D)
    wv = wv_ref[...].reshape(D, D)
    wq = wq_ref[...].reshape(D, D)

    def project(tile, _):
        at = pl.ds(pl.multiple_of(tile * 256, 256), 256)
        part = x_ref[0, at, :]
        k_ref[0, at, :] = nn(part, wk).astype(BF)
        v_ref[0, at, :] = nn(part, wv).astype(BF)
        return 0

    lax.fori_loop(0, glen // 256, project, 0)
    q_ref[0, 0:rows, :] = (nn(x_ref[0, pl.ds(off, rows), :], wq).astype(BF) * SCALE).astype(BF)
    q_ref[0, rows : rows + HALO, :] = (
        nn(x_ref[0, pl.ds(edge, HALO), :], wq).astype(BF) * SCALE
    ).astype(BF)
    seg_row = row_ref[0, 0:1, :]
    place = lax.broadcasted_iota(jnp.int32, (1, glen), 1)
    for start, count, src in ((0, rows, off), (rows, HALO, edge)):
        info = col_ref[0, pl.ds(src, count), :]
        limit = info[:, 0:1]
        seg = info[:, 1:2]
        seen = jnp.where(place < prompt, (place < limit).astype(jnp.int32), (seg_row == seg).astype(jnp.int32))
        bias[start : start + count, :] = jnp.where(seen == 1, 0.0, NEG)

    def one_pair(pair, _):
        at = lanes_of(pair)
        mix = attend_pair(q_ref[0, :, at], k_ref[0, :, at], v_ref[0, :, at], bias[...], pair, lse_sc)
        mix_ref[0, :, at] = mix.astype(BF)
        return 0

    lax.fori_loop(0, HEADS // 2, one_pair, 0)
    lse_out[0] = lse_sc[0:rows, :].T[0:HEADS, :]


def self_forward(x_all, wq, wk, wv, col, row, rows):
    glen = x_all.shape[1]
    ext = rows + HALO
    n, piece = wq.shape[0], wq.shape[1]
    weight = pl.BlockSpec((n, piece, D), lambda m: (0, 0, 0))

    def micro(*shape):
        return pl.BlockSpec((1,) + shape, lambda m: (m, 0, 0))

    return pl.pallas_call(
        functools.partial(self_forward_kernel, glen, rows),
        grid=(MICRO,),
        in_specs=[micro(glen, D), weight, weight, weight, micro(glen, 2), micro(1, glen)],
        out_specs=[micro(ext, D), micro(glen, D), micro(glen, D), micro(ext, D), micro(HEADS, rows)],
        out_shape=[
            jax.ShapeDtypeStruct((MICRO, ext, D), BF),
            jax.ShapeDtypeStruct((MICRO, glen, D), BF),
            jax.ShapeDtypeStruct((MICRO, glen, D), BF),
            jax.ShapeDtypeStruct((MICRO, ext, D), BF),
            jax.ShapeDtypeStruct((MICRO, HEADS, rows), F32),
        ],
        scratch_shapes=[pltpu.VMEM((ext, glen), F32), pltpu.VMEM((ext, 128), F32)],
        compiler_params=pltpu.CompilerParams(vmem_limit_bytes=56 * MIB),
        name="self_forward",
    )(x_all, wq, wk, wv, col, row)


def norm_forward(residual, gain, shift):
    average = jnp.mean(residual, axis=-1, keepdims=True)
    centred = residual - average
    variance = jnp.mean(centred * centred, axis=-1, keepdims=True)
    rstd = lax.rsqrt(variance + EPSILON)
    hat = centred * rstd
    return hat * gain + shift, hat, rstd


def norm_backward(upstream, hat, rstd, gain):
    d_hat = upstream * gain
    mean_d = jnp.mean(d_hat, axis=-1, keepdims=True)
    mean_dh = jnp.mean(d_hat * hat, axis=-1, keepdims=True)
    d_gain = jnp.sum(upstream * hat, axis=0, keepdims=True)
    d_shift = jnp.sum(upstream, axis=0, keepdims=True)
    return rstd * (d_hat - mean_d - hat * mean_dh), d_gain, d_shift


def gelu_parts(value):
    square = value * value
    t = jnp.tanh(GELU_C * value * (1.0 + 0.044715 * square))
    half = 0.5 * (1.0 + t)
    slope = half + 0.5 * value * (1.0 - t * t) * (GELU_C * (1.0 + 3.0 * 0.044715 * square))
    return value * half, slope


def head_sums(product_rows):
    rows, cols = 16, product_rows.shape[1]
    head = lax.broadcasted_iota(jnp.int32, (rows, cols), 0)
    lane = lax.broadcasted_iota(jnp.int32, (rows, cols), 1)
    pick = ((lane // HD) == head).astype(F32)
    return lax.dot_general(
        pick, product_rows, (((1,), (1,)), ((), ())),
        preferred_element_type=F32, precision=lax.Precision.HIGHEST,
    )[0:HEADS, :]


def middle_kernel(
    rows, enc,
    mix_ref, x_ref, e_ref, cot_ref, shifted_ref, flag_ref,
    wout_ref, cq_ref, ck_ref, cv_ref, cout_ref, up_ref, down_ref, slot_ref,
    bup_ref, vec_ref,
    slot_out, dmix_out, dr1_out, genc_out,
    gout, gcq, gck, gcv, gcout, gup, gdown, gslot, gbup, gvec,
    lowx, lown, cqs, cks, cvs, lse_sc, lse_row, cmix, h1s, hats, rstds, slope,
    act, dpre, dffn, dcross, dcqs, dattn, dcks, dcvs, ckt, h3s, h2low,
):
    ext = rows + HALO
    n = wout_ref.shape[0]
    gbup[...] = jnp.zeros_like(gbup)
    gvec[...] = jnp.zeros_like(gvec)

    def vec(i):
        return vec_ref[i : i + 1, :]

    def one_micro(m, _):
        own = pl.ds(0, rows)
        attn = nn(mix_ref[m], wout_ref[...].reshape(D, D))
        h1, hat, rstd = norm_forward(x_ref[m].astype(F32) + attn, vec(1), vec(2))
        h1s[...] = h1
        dr1_out[m] = hat[0:rows]
        rstds[:, 0:1] = rstd[0:rows]
        h1_low = h1.astype(BF)
        lown[0, m] = h1_low[0:rows]
        cqs[...] = (nn(h1_low, cq_ref[...].reshape(D, D)).astype(BF) * SCALE).astype(BF)
        cks[...] = nn(e_ref[m], ck_ref[...].reshape(D, D)).astype(BF)
        cvs[...] = nn(e_ref[m], cv_ref[...].reshape(D, D)).astype(BF)

        def cross_pair(pair, _):
            at = lanes_of(pair)
            mix = attend_pair(cqs[:, at], cks[:, at], cvs[:, at], None, pair, lse_sc)
            cmix[:, at] = mix.astype(BF)
            return 0

        lax.fori_loop(0, HEADS // 2, cross_pair, 0)
        lse_row[0:HEADS, :] = lse_sc[0:rows, :].T[0:HEADS, :]
        lowx[m] = cmix[0:rows, :]
        h2, hat, rstd = norm_forward(
            h1s[...] + nn(cmix[...], cout_ref[...].reshape(D, D)), vec(3), vec(4)
        )
        h1s[...] = h2
        hats[...] = hat[0:rows]
        rstds[:, 1:2] = rstd[0:rows]
        h2low[...] = h2.astype(BF)
        lown[1, m] = h2low[0:rows, :]
        h3s[...] = jnp.zeros_like(h3s)

        for c in range(FF // D):
            at = slice(c * D, (c + 1) * D)
            pre = nn(h2low[...], up_ref[:, :, at].reshape(D, D)) + bup_ref[0:1, at]
            value, grad = gelu_parts(pre)
            value = value.astype(BF)
            act[m, :, at] = value[0:rows]
            slope[:, at] = grad[0:rows]
            down = down_ref[...].reshape(FF, D)[c * D : (c + 1) * D, :]
            h3s[...] += nn(value, down)
        h3, hat, rstd = norm_forward(h1s[...] + h3s[...] + vec(0), vec(5), vec(6))
        h3_low = h3.astype(BF)
        h3s[...] = h3_low.astype(F32)
        lown[2, m] = h3_low[0:rows]
        top = slot_ref[...].reshape(2 * D, D)[0:D, :]
        bottom = slot_ref[...].reshape(2 * D, D)[D : 2 * D, :]
        flags = flag_ref[m]
        follow = (h3s[pl.ds(1, rows), :] * flags[:, 0:1]).astype(BF)
        slot_out[m] = (nn(h3_low[0:rows], top) + nn(follow, bottom)).astype(BF)
        d_follow = nt(shifted_ref[m], bottom).astype(BF).astype(F32) * flags[:, 1:2]
        d_three = nt(cot_ref[m], top) + d_follow
        d_r3, d_gain, d_shift = norm_backward(d_three, hat[0:rows], rstd[0:rows], vec(5))
        gvec[5:6, :] += d_gain
        gvec[6:7, :] += d_shift
        d_ffn = d_r3.astype(BF)
        dffn[m] = d_ffn
        gvec[0:1, :] += jnp.sum(d_ffn.astype(F32), axis=0, keepdims=True)
        d_two = d_r3
        for c in range(FF // D):
            at = slice(c * D, (c + 1) * D)
            down = down_ref[...].reshape(FF, D)[c * D : (c + 1) * D, :]
            grad = (nt(d_ffn, down) * slope[:, at]).astype(BF)
            dpre[m, :, at] = grad
            gbup[0:1, at] += jnp.sum(grad.astype(F32), axis=0, keepdims=True)
            d_two = d_two + nt(grad, up_ref[:, :, at].reshape(D, D))
        d_r2, d_gain, d_shift = norm_backward(d_two, hats[...], rstds[:, 1:2], vec(3))
        gvec[3:4, :] += d_gain
        gvec[4:5, :] += d_shift
        d_cross = d_r2.astype(BF)
        dcross[m] = d_cross
        d_cmix = nt(d_cross, cout_ref[...].reshape(D, D)).astype(BF)
        dmix_out[m] = d_cmix
        delta = head_sums(d_cmix.astype(F32) * cmix[0:rows, :].astype(F32))
        lse_row[HEADS : 2 * HEADS, :] = delta
        ckt[...] = cks[...].T

        def cross_back(pair, _):
            at = lanes_of(pair)
            kp, vp = cks[:, at], cvs[:, at]
            qp, dp = cqs[0:rows, at], dmix_out[m, :, at]
            kt = ckt[at, :]
            d_k = d_v = None
            d_qt = []
            for head in range(2):
                qm, dm = head_masked(qp, head), head_masked(dp, head)
                row = pair * 2 + head
                prob = jnp.exp(nt(kp, qm) - lse_row[pl.ds(row, 1), :])
                d_score = (prob * (nt(vp, dm) - lse_row[pl.ds(HEADS + row, 1), :])).astype(BF)
                dk, dv = nn(d_score, qm), nn(prob.astype(BF), dm)
                d_k = dk if d_k is None else d_k + dk
                d_v = dv if d_v is None else d_v + dv
                d_qt.append(nn(kt, d_score))
            sub = lax.broadcasted_iota(jnp.int32, d_qt[0].shape, 0)
            d_q = jnp.where(sub < 64, d_qt[0], d_qt[1]) * SCALE
            dcqs[m, :, at] = d_q.T.astype(BF)
            dcks[m, :, at] = d_k.astype(BF)
            dcvs[m, :, at] = d_v.astype(BF)
            return 0

        lax.fori_loop(0, HEADS // 2, cross_back, 0)
        genc_out[m] = (
            nt(dcks[m], ck_ref[...].reshape(D, D)) + nt(dcvs[m], cv_ref[...].reshape(D, D))
        ).astype(BF)
        d_one = d_r2 + nt(dcqs[m], cq_ref[...].reshape(D, D))
        d_r1, d_gain, d_shift = norm_backward(d_one, dr1_out[m], rstds[:, 0:1], vec(1))
        gvec[1:2, :] += d_gain
        gvec[2:3, :] += d_shift
        dr1_out[m] = d_r1
        d_attn = d_r1.astype(BF)
        dattn[m] = d_attn
        dmix_out[m] = nt(d_attn, wout_ref[...].reshape(D, D)).astype(BF)
        return 0

    lax.fori_loop(0, MICRO, one_micro, 0)

    total = MICRO * rows

    def flat(ref, *lead):
        return ref[lead].reshape(total, D) if lead else ref[...].reshape(total, D)

    def grad_of(left, right):
        return tn(left, right).astype(BF)

    cot = cot_ref[...].reshape(total, D)
    flagged = jnp.concatenate(
        [(shifted_ref[m].astype(F32) * flag_ref[m][:, 1:2]).astype(BF) for m in range(MICRO)], axis=0
    )
    h3_all = lown[2].reshape(total, D)
    half = n // 2
    gslot[0:half] = grad_of(h3_all, cot).reshape(half, D // half, D)
    gslot[half:n] = grad_of(h3_all, flagged).reshape(half, D // half, D)
    many = n * D // FF
    dffn_all = dffn[...].reshape(total, D)
    for c in range(FF // D):
        at = slice(c * D, (c + 1) * D)
        gdown[c * many : (c + 1) * many] = grad_of(
            act[:, :, at].reshape(total, D), dffn_all
        ).reshape(many, D // many, D)
        gup[:, :, at] = grad_of(lown[1].reshape(total, D), dpre[:, :, at].reshape(total, D)).reshape(
            n, D // n, D
        )
    gcout[...] = grad_of(lowx[...].reshape(total, D), dcross[...].reshape(total, D)).reshape(gcout.shape)
    gcq[...] = grad_of(lown[0].reshape(total, D), dcqs[...].reshape(total, D)).reshape(gcq.shape)
    e_all = e_ref[...].reshape(MICRO * enc, D)
    gck[...] = grad_of(e_all, dcks[...].reshape(MICRO * enc, D)).reshape(gck.shape)
    gcv[...] = grad_of(e_all, dcvs[...].reshape(MICRO * enc, D)).reshape(gcv.shape)
    mix_all = jnp.concatenate([mix_ref[m, 0:rows, :] for m in range(MICRO)], axis=0)
    gout[...] = grad_of(mix_all, dattn[...].reshape(total, D)).reshape(gout.shape)


def middle(mix, x_ext, e_all, cot, shifted, flags, weights, bup, vecs, rows):
    enc = e_all.shape[1]
    ext = rows + HALO
    wout, cq, ck, cv, cout, up, down, slot = weights

    def like(a):
        return jax.ShapeDtypeStruct(a.shape, BF)

    out_shape = [
        jax.ShapeDtypeStruct((MICRO, rows, D), BF),
        jax.ShapeDtypeStruct((MICRO, rows, D), BF),
        jax.ShapeDtypeStruct((MICRO, rows, D), F32),
        jax.ShapeDtypeStruct((MICRO, enc, D), BF),
        like(wout), like(cq), like(ck), like(cv), like(cout), like(up), like(down), like(slot),
        jax.ShapeDtypeStruct((8, FF), F32),
        jax.ShapeDtypeStruct((8, D), F32),
    ]
    V = pltpu.VMEM
    scratch = [
        V((MICRO, rows, D), BF),
        V((3, MICRO, rows, D), BF),
        V((ext, D), BF), V((enc, D), BF), V((enc, D), BF),
        V((ext, 128), F32), V((2 * HEADS, rows), F32),
        V((ext, D), BF),
        V((ext, D), F32),
        V((rows, D), F32), V((rows, 128), F32),
        V((rows, FF), F32),
        V((MICRO, rows, FF), BF), V((MICRO, rows, FF), BF),
        V((MICRO, rows, D), BF), V((MICRO, rows, D), BF), V((MICRO, rows, D), BF),
        V((MICRO, rows, D), BF),
        V((MICRO, enc, D), BF), V((MICRO, enc, D), BF),
        V((D, enc), BF),
        V((ext, D), F32), V((ext, D), BF),
    ]
    return pl.pallas_call(
        functools.partial(middle_kernel, rows, enc),
        in_specs=[VM] * 16,
        out_specs=[VM] * len(out_shape),
        out_shape=out_shape,
        scratch_shapes=scratch,
        compiler_params=pltpu.CompilerParams(vmem_limit_bytes=60 * MIB),
        name="middle",
    )(mix, x_ext, e_all, cot, shifted, flags, wout, cq, ck, cv, cout, up, down, slot, bup, vecs)


def self_backward_kernel(
    glen, rows,
    x_ref, q_ref, k_ref, v_ref, mix_ref, dmix_ref, dr1_ref, lse_ref, row_ref,
    wq_ref, wk_ref, wv_ref,
    own_out, part_out, gq, gk, gv,
    bias, stats, dqt, dqs, dks, dvs,
):
    prompt = glen // 3
    tile = 256
    rank = lax.axis_index("seq")
    off = pl.multiple_of(rank * rows, 128)

    def one_micro(m, _):
        limit = row_ref[m, 0:1, pl.ds(off, rows)]
        seg = row_ref[m, 1:2, pl.ds(off, rows)]

        def masks(t, _):
            at = pl.ds(pl.multiple_of(t * tile, tile), tile)
            place = lax.broadcasted_iota(jnp.int32, (tile, 1), 0) + t * tile
            key_seg = jnp.broadcast_to(row_ref[m, 1:2, at], (8, tile)).T[:, 0:1]
            seen = jnp.where(
                place < prompt, (place < limit).astype(jnp.int32), (key_seg == seg).astype(jnp.int32)
            )
            bias[at, :] = jnp.where(seen == 1, 0.0, NEG)
            return 0

        lax.fori_loop(0, glen // tile, masks, 0)
        stats[0:HEADS, :] = lse_ref[m]
        stats[HEADS : 2 * HEADS, :] = head_sums(
            dmix_ref[m].astype(F32) * mix_ref[m, 0:rows, :].astype(F32)
        )

        def one_pair(pair, _):
            at = lanes_of(pair)
            qp, dp = q_ref[m, 0:rows, at], dmix_ref[m, :, at]
            qm = [head_masked(qp, h) for h in range(2)]
            dm = [head_masked(dp, h) for h in range(2)]
            dqt[...] = jnp.zeros_like(dqt)

            def one_tile(t, _):
                span = pl.ds(pl.multiple_of(t * tile, tile), tile)
                kp, vp = k_ref[m, span, at], v_ref[m, span, at]
                kt = kp.T
                seen = bias[span, :]
                d_k = d_v = None
                d_q = []
                for h in range(2):
                    row = pair * 2 + h
                    prob = jnp.exp(nt(kp, qm[h]) + seen - stats[pl.ds(row, 1), :])
                    d_score = (prob * (nt(vp, dm[h]) - stats[pl.ds(HEADS + row, 1), :])).astype(BF)
                    dk, dv = nn(d_score, qm[h]), nn(prob.astype(BF), dm[h])
                    d_k = dk if d_k is None else d_k + dk
                    d_v = dv if d_v is None else d_v + dv
                    d_q.append(nn(kt, d_score))
                sub = lax.broadcasted_iota(jnp.int32, d_q[0].shape, 0)
                dqt[...] += jnp.where(sub < 64, d_q[0], d_q[1])
                dks[m, span, at] = d_k.astype(BF)
                dvs[m, span, at] = d_v.astype(BF)
                return 0

            lax.fori_loop(0, glen // tile, one_tile, 0)
            dqs[m, :, at] = (dqt[...] * SCALE).T.astype(BF)
            return 0

        lax.fori_loop(0, HEADS // 2, one_pair, 0)
        own_out[m] = dr1_ref[m] + nt(dqs[m], wq_ref[...].reshape(D, D))

        def spread(t, _):
            span = pl.ds(pl.multiple_of(t * tile, tile), tile)
            part_out[m, span, :] = (
                nt(dks[m, span, :], wk_ref[...].reshape(D, D))
                + nt(dvs[m, span, :], wv_ref[...].reshape(D, D))
            ).astype(BF)
            return 0

        lax.fori_loop(0, glen // tile, spread, 0)
        return 0

    lax.fori_loop(0, MICRO, one_micro, 0)
    x_own = jnp.concatenate([x_ref[m, pl.ds(off, rows), :] for m in range(MICRO)], axis=0)
    gq[...] = tn(x_own, dqs[...].reshape(MICRO * rows, D)).astype(BF).reshape(gq.shape)
    x_all = x_ref[...].reshape(MICRO * glen, D)
    gk[...] = tn(x_all, dks[...].reshape(MICRO * glen, D)).astype(BF).reshape(gk.shape)
    gv[...] = tn(x_all, dvs[...].reshape(MICRO * glen, D)).astype(BF).reshape(gv.shape)


def self_backward(x_all, q, k, v, mix, dmix, dr1, lse, row, wq, wk, wv, rows):
    glen = x_all.shape[1]
    V = pltpu.VMEM

    def like(a):
        return jax.ShapeDtypeStruct(a.shape, BF)

    return pl.pallas_call(
        functools.partial(self_backward_kernel, glen, rows),
        in_specs=[VM] * 12,
        out_specs=[VM] * 5,
        out_shape=[
            jax.ShapeDtypeStruct((MICRO, rows, D), F32),
            jax.ShapeDtypeStruct((MICRO, glen, D), BF),
            like(wq), like(wk), like(wv),
        ],
        scratch_shapes=[
            V((glen, rows), F32), V((2 * HEADS, rows), F32), V((128, rows), F32),
            V((MICRO, rows, D), BF), V((MICRO, glen, D), BF), V((MICRO, glen, D), BF),
        ],
        compiler_params=pltpu.CompilerParams(vmem_limit_bytes=60 * MIB),
        name="self_backward",
    )(x_all, q, k, v, mix, dmix, dr1, lse, row, wq, wk, wv)


def passed_along(value, axis, steps):
    count = lax.axis_size(axis)
    first, last = (max(0, -steps), min(count, count - steps))
    return lax.ppermute(value, axis, [(source, source + steps) for source in range(first, last)])


MATRICES = ("wq", "wk", "wv", "wout", "cq", "ck", "cv", "cout", "up", "down", "slot")


def on_device(
    tokens, encoded, segment_ids, prefix_len, cotangent,
    w_query, w_key, w_value, w_out, c_query, c_key, c_value, c_out,
    w_up, b_up, w_down, b_down,
    gain_one, shift_one, gain_two, shift_two, gain_three, shift_three, w_slot,
):
    n = lax.axis_size("fsdp")
    rank = lax.axis_index("seq")
    tokens = tokens[:, 0]
    rows = tokens.shape[1]
    seg = segment_ids[:, 0]
    glen = seg.shape[1]
    prompt = glen // 3
    prefix = prefix_len[:, 0]
    cot = cotangent[:, 0]

    shards = (w_query, w_key, w_value, w_out, c_query, c_key, c_value, c_out, w_up, w_down, w_slot)
    full = [lax.all_gather(w, "fsdp", axis=0, tiled=False) for w in shards]
    wq, wk, wv, wout, cq, ck, cv, cout, up, down, slot = full
    small = jnp.concatenate(
        [b_up, b_down, gain_one, shift_one, gain_two, shift_two, gain_three, shift_three]
    )
    small_all = lax.all_gather(small, "fsdp", axis=0, tiled=False)
    edge = FF // n
    bup = small_all[:, :edge].reshape(1, FF).astype(F32)
    vecs = small_all[:, edge:].reshape(n, 7, D // n).transpose(1, 0, 2).reshape(7, D).astype(F32)
    vecs = jnp.concatenate([vecs, jnp.zeros((1, D), F32)], axis=0)

    x_all = lax.all_gather(tokens, "seq", axis=1, tiled=True)
    e_all = lax.all_gather(encoded[:, 0], "seq", axis=1, tiled=True)
    previous = passed_along(cot[:, rows - HALO :], "seq", 1)[:, HALO - 1 :]
    shifted = jnp.concatenate([previous, cot[:, : rows - 1]], axis=1)

    numbers = jnp.arange(1, prefix.shape[1] + 1, dtype=jnp.int32)
    limit = jnp.sum(
        jnp.where(seg[:, :, None] == numbers[None, None, :], prefix[:, None, :], 0), axis=2
    )
    limit = jnp.where(seg == 0, prompt, limit)
    col = jnp.stack([limit, seg], axis=2)
    row = jnp.stack([limit, seg], axis=1)
    same = jnp.concatenate(
        [jnp.zeros((MICRO, 1), F32), (seg[:, 1:] == seg[:, :-1]).astype(F32), jnp.zeros((MICRO, 1), F32)],
        axis=1,
    )
    offset = rank * rows
    flags = jnp.stack(
        [
            lax.dynamic_slice_in_dim(same, offset + 1, rows, 1),
            lax.dynamic_slice_in_dim(same, offset, rows, 1),
        ],
        axis=2,
    )
    start = jnp.minimum(offset + rows, glen - HALO)
    x_ext = jnp.concatenate([tokens, lax.dynamic_slice_in_dim(x_all, start, HALO, 1)], axis=1)

    q, k, v, mix, lse = self_forward(x_all, wq, wk, wv, col, row[:, 1:2], rows)
    (
        slot_out, dmix, dr1, genc,
        g_out, g_cq, g_ck, g_cv, g_cout, g_up, g_down, g_slot, g_bup, g_vec,
    ) = middle(mix, x_ext, e_all, cot, shifted, flags, (wout, cq, ck, cv, cout, up, down, slot), bup, vecs, rows)
    own, part, g_q, g_k, g_v = self_backward(
        x_all, q, k, v, mix, dmix, dr1, lse, row, wq, wk, wv, rows
    )

    grad_tokens = own + lax.psum_scatter(part, "seq", scatter_dimension=1, tiled=True).astype(F32)
    grad_encoded = lax.psum_scatter(genc, "seq", scatter_dimension=1, tiled=True).astype(F32)
    grads = (g_q, g_k, g_v, g_out, g_cq, g_ck, g_cv, g_cout, g_up, g_down, g_slot)

    def reduced(g):
        g = lax.psum_scatter(g, "fsdp", scatter_dimension=0, tiled=False)
        return lax.psum(g, "seq").astype(F32)

    (g_q, g_k, g_v, g_out, g_cq, g_ck, g_cv, g_cout, g_up, g_down, g_slot) = [reduced(g) for g in grads]
    packed = jnp.concatenate(
        [
            g_bup[0:1].reshape(n, FF // n),
            g_vec[:7].reshape(7, n, D // n).transpose(1, 0, 2).reshape(n, 7 * (D // n)),
        ],
        axis=1,
    )
    packed = lax.psum(packed, ("fsdp", "seq"))
    mine = lax.dynamic_slice_in_dim(packed, lax.axis_index("fsdp"), 1, 0)[0]
    b_up_g = mine[:edge]
    b_down_g, g1, s1, g2, s2, g3, s3 = [
        mine[edge + i * (D // n) : edge + (i + 1) * (D // n)] for i in range(7)
    ]
    return (
        slot_out[:, None], grad_tokens[:, None], grad_encoded[:, None],
        g_q, g_k, g_v, g_out, g_cq, g_ck, g_cv, g_cout,
        g_up, b_up_g, g_down, b_down_g, g1, s1, g2, s2, g3, s3, g_slot,
    )


def solution(mesh):
    act = P(None, "fsdp", "seq", None)
    ids = P(None, "fsdp", None)
    mat, one = P("fsdp", None), P("fsdp")
    in_specs = (
        (act, act, ids, ids, act) + (mat,) * 9 + (one, mat) + (one,) * 7 + (mat,)
    )
    out_specs = (act, act, act) + (mat,) * 9 + (one, mat) + (one,) * 7 + (mat,)
    return jax.shard_map(
        on_device, mesh=mesh, in_specs=in_specs, out_specs=out_specs, check_vma=False
    )
```

```python
import functools
import math

import jax
import jax.numpy as jnp
from jax import lax
from jax.experimental import pallas as pl
from jax.experimental.pallas import tpu as pltpu
from jax.sharding import PartitionSpec as P

D = 512
HD = 64
HEADS = 8
FF = 2048
MICRO = 2
HALO = 16
EPSILON = 1e-05
BF = jnp.bfloat16
F32 = jnp.float32
SCALE = 1.0 / math.sqrt(HD)
NEG = -1e30
MIB = 1024 * 1024
GELU_C = math.sqrt(2.0 / math.pi)

VM = pl.BlockSpec(memory_space=pltpu.VMEM)


def nn(a, b):
    return lax.dot_general(a, b, (((1,), (0,)), ((), ())), preferred_element_type=F32)


def nt(a, b):
    return lax.dot_general(a, b, (((1,), (1,)), ((), ())), preferred_element_type=F32)


def tn(a, b):
    return lax.dot_general(a, b, (((0,), (0,)), ((), ())), preferred_element_type=F32)


def lanes_of(pair):
    return pl.ds(pl.multiple_of(pair * 128, 128), 128)


def head_masked(value, head):
    lane = lax.broadcasted_iota(jnp.int32, value.shape, 1)
    return jnp.where((lane >= 64) == (head == 1), value, jnp.zeros_like(value))


def softmax_parts(scores):
    top = jnp.max(scores, axis=-1, keepdims=True)
    raw = jnp.exp(scores - top)
    total = jnp.sum(raw, axis=-1, keepdims=True)
    return raw, top, total


def attend_pair(query_pair, key_pair, value_pair, bias, pair, lse_ref):
    mixed = []
    for head in range(2):
        scores = nt(head_masked(query_pair, head), key_pair)
        if bias is not None:
            scores = scores + bias
        raw, top, total = softmax_parts(scores)
        mixed.append(nn(raw.astype(BF), value_pair) / total)
        lane = lax.broadcasted_iota(jnp.int32, lse_ref.shape, 1)
        lse_ref[...] = jnp.where(lane == pair * 2 + head, top + jnp.log(total), lse_ref[...])
    lane = lax.broadcasted_iota(jnp.int32, mixed[0].shape, 1)
    return jnp.where(lane < 64, mixed[0], mixed[1])


def bit_count(n):
    return n.bit_length() - 1


def qkv_rows(n):
    piece = D // n
    return {"wq": (0, piece), "wk": (piece, piece), "wv": (2 * piece, piece)}, 3 * piece


def rest_rows(n):
    piece = D // n
    table, start = {}, 0
    for name, times in (
        ("wout", 1), ("cq", 1), ("ck", 1), ("cv", 1), ("cout", 1), ("up", 4), ("down", 4), ("slot", 2)
    ):
        table[name] = (start, times * piece)
        start += times * piece
    return table, start


def square(ref, table, name):
    start, count = table[name]
    return ref[:, start : start + count, :].reshape(D, D)


def up_part(ref, table, c):
    start, count = table["up"]
    piece = count // 4
    return ref[:, start + c * piece : start + (c + 1) * piece, :].reshape(D, D)


def row_part(ref, table, name, c):
    start, count = table[name]
    many = D // count
    return ref[c * many : (c + 1) * many, start : start + count, :].reshape(D, D)


def store_square(ref, table, name, value):
    start, count = table[name]
    ref[:, start : start + count, :] = value.reshape(ref.shape[0], count, D)


def store_up(ref, table, c, value):
    start, count = table["up"]
    piece = count // 4
    ref[:, start + c * piece : start + (c + 1) * piece, :] = value.reshape(ref.shape[0], piece, D)


def store_part(ref, table, name, c, value):
    start, count = table[name]
    many = D // count
    ref[c * many : (c + 1) * many, start : start + count, :] = value.reshape(many, count, D)


def my_place(n):
    me = lax.axis_index("fsdp")
    bits = [(me // (1 << b)) % 2 for b in range(bit_count(n))]
    return me, bits


def partner_of(me, bits, b):
    return me + (1 - 2 * bits[b]) * (1 << b)


def orders(n):
    d = bit_count(n)
    far = list(range(1, d))
    return [far + [0], far[::-1] + [0]]


def at_bits(bits, free, fixed=None):
    fixed = fixed or {}
    return tuple(
        slice(None) if b in free else fixed.get(b, bits[b]) for b in range(len(bits) - 1, -1, -1)
    )


MESH_ID = pl.DeviceIdType.MESH


def self_forward_kernel(
    glen, rows, x_ref, w_ref, col_ref, row_ref,
    q_ref, k_ref, v_ref, mix_ref, lse_out, bias, lse_sc,
):
    prompt = glen // 3
    rank = lax.axis_index("seq")
    off = pl.multiple_of(rank * rows, 128)
    edge = pl.multiple_of(jnp.minimum(rank * rows + rows, glen - HALO), HALO)
    table, _ = qkv_rows(w_ref.shape[0])
    wq, wk, wv = [square(w_ref, table, name) for name in ("wq", "wk", "wv")]

    def project(tile, _):
        at = pl.ds(pl.multiple_of(tile * 256, 256), 256)
        part = x_ref[0, at, :]
        k_ref[0, at, :] = nn(part, wk).astype(BF)
        v_ref[0, at, :] = nn(part, wv).astype(BF)
        return 0

    lax.fori_loop(0, glen // 256, project, 0)
    q_ref[0, 0:rows, :] = (nn(x_ref[0, pl.ds(off, rows), :], wq).astype(BF) * SCALE).astype(BF)
    q_ref[0, rows : rows + HALO, :] = (
        nn(x_ref[0, pl.ds(edge, HALO), :], wq).astype(BF) * SCALE
    ).astype(BF)
    seg_row = row_ref[0, 0:1, :]
    place = lax.broadcasted_iota(jnp.int32, (1, glen), 1)
    for start, count, src in ((0, rows, off), (rows, HALO, edge)):
        info = col_ref[0, pl.ds(src, count), :]
        limit = info[:, 0:1]
        seg = info[:, 1:2]
        seen = jnp.where(place < prompt, (place < limit).astype(jnp.int32), (seg_row == seg).astype(jnp.int32))
        bias[start : start + count, :] = jnp.where(seen == 1, 0.0, NEG)

    def one_pair(pair, _):
        at = lanes_of(pair)
        mix = attend_pair(q_ref[0, :, at], k_ref[0, :, at], v_ref[0, :, at], bias[...], pair, lse_sc)
        mix_ref[0, :, at] = mix.astype(BF)
        return 0

    lax.fori_loop(0, HEADS // 2, one_pair, 0)
    lse_out[0] = lse_sc[0:rows, :].T[0:HEADS, :]


def self_forward(x_all, w, col, row, rows):
    glen = x_all.shape[1]
    ext = rows + HALO
    weight = pl.BlockSpec(w.shape, lambda m: (0, 0, 0))

    def micro(*shape):
        return pl.BlockSpec((1,) + shape, lambda m: (m, 0, 0))

    return pl.pallas_call(
        functools.partial(self_forward_kernel, glen, rows),
        grid=(MICRO,),
        in_specs=[micro(glen, D), weight, micro(glen, 2), micro(1, glen)],
        out_specs=[micro(ext, D), micro(glen, D), micro(glen, D), micro(ext, D), micro(HEADS, rows)],
        out_shape=[
            jax.ShapeDtypeStruct((MICRO, ext, D), BF),
            jax.ShapeDtypeStruct((MICRO, glen, D), BF),
            jax.ShapeDtypeStruct((MICRO, glen, D), BF),
            jax.ShapeDtypeStruct((MICRO, ext, D), BF),
            jax.ShapeDtypeStruct((MICRO, HEADS, rows), F32),
        ],
        scratch_shapes=[pltpu.VMEM((ext, glen), F32), pltpu.VMEM((ext, 128), F32)],
        compiler_params=pltpu.CompilerParams(vmem_limit_bytes=56 * MIB),
        name="self_forward",
    )(x_all, w, col, row)


def norm_forward(residual, gain, shift):
    average = jnp.mean(residual, axis=-1, keepdims=True)
    centred = residual - average
    variance = jnp.mean(centred * centred, axis=-1, keepdims=True)
    rstd = lax.rsqrt(variance + EPSILON)
    hat = centred * rstd
    return hat * gain + shift, hat, rstd


def norm_backward(upstream, hat, rstd, gain):
    d_hat = upstream * gain
    mean_d = jnp.mean(d_hat, axis=-1, keepdims=True)
    mean_dh = jnp.mean(d_hat * hat, axis=-1, keepdims=True)
    d_gain = jnp.sum(upstream * hat, axis=0, keepdims=True)
    d_shift = jnp.sum(upstream, axis=0, keepdims=True)
    return rstd * (d_hat - mean_d - hat * mean_dh), d_gain, d_shift


def gelu_parts(value):
    square = value * value
    t = jnp.tanh(GELU_C * value * (1.0 + 0.044715 * square))
    half = 0.5 * (1.0 + t)
    slope = half + 0.5 * value * (1.0 - t * t) * (GELU_C * (1.0 + 3.0 * 0.044715 * square))
    return value * half, slope


def head_sums(product_rows):
    rows, cols = 16, product_rows.shape[1]
    head = lax.broadcasted_iota(jnp.int32, (rows, cols), 0)
    lane = lax.broadcasted_iota(jnp.int32, (rows, cols), 1)
    pick = ((lane // HD) == head).astype(F32)
    return lax.dot_general(
        pick, product_rows, (((1,), (1,)), ((), ())),
        preferred_element_type=F32, precision=lax.Precision.HIGHEST,
    )[0:HEADS, :]


def middle_kernel(
    rows, enc,
    mix_ref, x_ref, e_ref, cot_ref, shifted_ref, flag_ref,
    w_ref, bup_ref, vec_ref,
    slot_out, dmix_out, dr1_out, genc_out, g_ref, gbup, gvec,
    lowx, lown, cqs, cks, cvs, lse_sc, lse_row, cmix, h1s, hats, rstds, slope,
    act, dpre, dffn, dcross, dcqs, dattn, dcks, dcvs, ckt, h3s, h2low,
):
    ext = rows + HALO
    table, _ = rest_rows(w_ref.shape[0])
    gbup[...] = jnp.zeros_like(gbup)
    gvec[...] = jnp.zeros_like(gvec)

    def vec(i):
        return vec_ref[i : i + 1, :]

    def one_micro(m, _):
        own = pl.ds(0, rows)
        attn = nn(mix_ref[m], square(w_ref, table, "wout"))
        h1, hat, rstd = norm_forward(x_ref[m].astype(F32) + attn, vec(1), vec(2))
        h1s[...] = h1
        dr1_out[m] = hat[0:rows]
        rstds[:, 0:1] = rstd[0:rows]
        h1_low = h1.astype(BF)
        lown[0, m] = h1_low[0:rows]
        cqs[...] = (nn(h1_low, square(w_ref, table, "cq")).astype(BF) * SCALE).astype(BF)
        cks[...] = nn(e_ref[m], square(w_ref, table, "ck")).astype(BF)
        cvs[...] = nn(e_ref[m], square(w_ref, table, "cv")).astype(BF)

        def cross_pair(pair, _):
            at = lanes_of(pair)
            mix = attend_pair(cqs[:, at], cks[:, at], cvs[:, at], None, pair, lse_sc)
            cmix[:, at] = mix.astype(BF)
            return 0

        lax.fori_loop(0, HEADS // 2, cross_pair, 0)
        lse_row[0:HEADS, :] = lse_sc[0:rows, :].T[0:HEADS, :]
        lowx[m] = cmix[0:rows, :]
        h2, hat, rstd = norm_forward(
            h1s[...] + nn(cmix[...], square(w_ref, table, "cout")), vec(3), vec(4)
        )
        h1s[...] = h2
        hats[...] = hat[0:rows]
        rstds[:, 1:2] = rstd[0:rows]
        h2low[...] = h2.astype(BF)
        lown[1, m] = h2low[0:rows, :]
        h3s[...] = jnp.zeros_like(h3s)

        for c in range(FF // D):
            at = slice(c * D, (c + 1) * D)
            pre = nn(h2low[...], up_part(w_ref, table, c)) + bup_ref[0:1, at]
            value, grad = gelu_parts(pre)
            value = value.astype(BF)
            act[m, :, at] = value[0:rows]
            slope[:, at] = grad[0:rows]
            down = row_part(w_ref, table, "down", c)
            h3s[...] += nn(value, down)
        h3, hat, rstd = norm_forward(h1s[...] + h3s[...] + vec(0), vec(5), vec(6))
        h3_low = h3.astype(BF)
        h3s[...] = h3_low.astype(F32)
        lown[2, m] = h3_low[0:rows]
        top = row_part(w_ref, table, "slot", 0)
        bottom = row_part(w_ref, table, "slot", 1)
        flags = flag_ref[m]
        follow = (h3s[pl.ds(1, rows), :] * flags[:, 0:1]).astype(BF)
        slot_out[m] = (nn(h3_low[0:rows], top) + nn(follow, bottom)).astype(BF)
        d_follow = nt(shifted_ref[m], bottom).astype(BF).astype(F32) * flags[:, 1:2]
        d_three = nt(cot_ref[m], top) + d_follow
        d_r3, d_gain, d_shift = norm_backward(d_three, hat[0:rows], rstd[0:rows], vec(5))
        gvec[5:6, :] += d_gain
        gvec[6:7, :] += d_shift
        d_ffn = d_r3.astype(BF)
        dffn[m] = d_ffn
        gvec[0:1, :] += jnp.sum(d_ffn.astype(F32), axis=0, keepdims=True)
        d_two = d_r3
        for c in range(FF // D):
            at = slice(c * D, (c + 1) * D)
            down = row_part(w_ref, table, "down", c)
            grad = (nt(d_ffn, down) * slope[:, at]).astype(BF)
            dpre[m, :, at] = grad
            gbup[0:1, at] += jnp.sum(grad.astype(F32), axis=0, keepdims=True)
            d_two = d_two + nt(grad, up_part(w_ref, table, c))
        d_r2, d_gain, d_shift = norm_backward(d_two, hats[...], rstds[:, 1:2], vec(3))
        gvec[3:4, :] += d_gain
        gvec[4:5, :] += d_shift
        d_cross = d_r2.astype(BF)
        dcross[m] = d_cross
        d_cmix = nt(d_cross, square(w_ref, table, "cout")).astype(BF)
        dmix_out[m] = d_cmix
        delta = head_sums(d_cmix.astype(F32) * cmix[0:rows, :].astype(F32))
        lse_row[HEADS : 2 * HEADS, :] = delta
        ckt[...] = cks[...].T

        def cross_back(pair, _):
            at = lanes_of(pair)
            kp, vp = cks[:, at], cvs[:, at]
            qp, dp = cqs[0:rows, at], dmix_out[m, :, at]
            kt = ckt[at, :]
            d_k = d_v = None
            d_qt = []
            for head in range(2):
                qm, dm = head_masked(qp, head), head_masked(dp, head)
                row = pair * 2 + head
                prob = jnp.exp(nt(kp, qm) - lse_row[pl.ds(row, 1), :])
                d_score = (prob * (nt(vp, dm) - lse_row[pl.ds(HEADS + row, 1), :])).astype(BF)
                dk, dv = nn(d_score, qm), nn(prob.astype(BF), dm)
                d_k = dk if d_k is None else d_k + dk
                d_v = dv if d_v is None else d_v + dv
                d_qt.append(nn(kt, d_score))
            sub = lax.broadcasted_iota(jnp.int32, d_qt[0].shape, 0)
            d_q = jnp.where(sub < 64, d_qt[0], d_qt[1]) * SCALE
            dcqs[m, :, at] = d_q.T.astype(BF)
            dcks[m, :, at] = d_k.astype(BF)
            dcvs[m, :, at] = d_v.astype(BF)
            return 0

        lax.fori_loop(0, HEADS // 2, cross_back, 0)
        genc_out[m] = (
            nt(dcks[m], square(w_ref, table, "ck")) + nt(dcvs[m], square(w_ref, table, "cv"))
        ).astype(BF)
        d_one = d_r2 + nt(dcqs[m], square(w_ref, table, "cq"))
        d_r1, d_gain, d_shift = norm_backward(d_one, dr1_out[m], rstds[:, 0:1], vec(1))
        gvec[1:2, :] += d_gain
        gvec[2:3, :] += d_shift
        dr1_out[m] = d_r1
        d_attn = d_r1.astype(BF)
        dattn[m] = d_attn
        dmix_out[m] = nt(d_attn, square(w_ref, table, "wout")).astype(BF)
        return 0

    lax.fori_loop(0, MICRO, one_micro, 0)

    total = MICRO * rows

    def flat(ref, *lead):
        return ref[lead].reshape(total, D) if lead else ref[...].reshape(total, D)

    def grad_of(left, right):
        return tn(left, right).astype(BF)

    cot = cot_ref[...].reshape(total, D)
    flagged = jnp.concatenate(
        [(shifted_ref[m].astype(F32) * flag_ref[m][:, 1:2]).astype(BF) for m in range(MICRO)], axis=0
    )
    h3_all = lown[2].reshape(total, D)
    store_part(g_ref, table, "slot", 0, grad_of(h3_all, cot))
    store_part(g_ref, table, "slot", 1, grad_of(h3_all, flagged))
    dffn_all = dffn[...].reshape(total, D)
    h2_all = lown[1].reshape(total, D)
    for c in range(FF // D):
        at = slice(c * D, (c + 1) * D)
        store_part(g_ref, table, "down", c, grad_of(act[:, :, at].reshape(total, D), dffn_all))
        store_up(g_ref, table, c, grad_of(h2_all, dpre[:, :, at].reshape(total, D)))
    store_square(g_ref, table, "cout", grad_of(lowx[...].reshape(total, D), dcross[...].reshape(total, D)))
    store_square(g_ref, table, "cq", grad_of(lown[0].reshape(total, D), dcqs[...].reshape(total, D)))
    e_all = e_ref[...].reshape(MICRO * enc, D)
    store_square(g_ref, table, "ck", grad_of(e_all, dcks[...].reshape(MICRO * enc, D)))
    store_square(g_ref, table, "cv", grad_of(e_all, dcvs[...].reshape(MICRO * enc, D)))
    mix_all = jnp.concatenate([mix_ref[m, 0:rows, :] for m in range(MICRO)], axis=0)
    store_square(g_ref, table, "wout", grad_of(mix_all, dattn[...].reshape(total, D)))


def middle(mix, x_ext, e_all, cot, shifted, flags, w, bup, vecs, rows):
    enc = e_all.shape[1]
    ext = rows + HALO
    out_shape = [
        jax.ShapeDtypeStruct((MICRO, rows, D), BF),
        jax.ShapeDtypeStruct((MICRO, rows, D), BF),
        jax.ShapeDtypeStruct((MICRO, rows, D), F32),
        jax.ShapeDtypeStruct((MICRO, enc, D), BF),
        jax.ShapeDtypeStruct(w.shape, BF),
        jax.ShapeDtypeStruct((8, FF), F32),
        jax.ShapeDtypeStruct((8, D), F32),
    ]
    V = pltpu.VMEM
    scratch = [
        V((MICRO, rows, D), BF),
        V((3, MICRO, rows, D), BF),
        V((ext, D), BF), V((enc, D), BF), V((enc, D), BF),
        V((ext, 128), F32), V((2 * HEADS, rows), F32),
        V((ext, D), BF),
        V((ext, D), F32),
        V((rows, D), F32), V((rows, 128), F32),
        V((rows, FF), F32),
        V((MICRO, rows, FF), BF), V((MICRO, rows, FF), BF),
        V((MICRO, rows, D), BF), V((MICRO, rows, D), BF), V((MICRO, rows, D), BF),
        V((MICRO, rows, D), BF),
        V((MICRO, enc, D), BF), V((MICRO, enc, D), BF),
        V((D, enc), BF),
        V((ext, D), F32), V((ext, D), BF),
    ]
    return pl.pallas_call(
        functools.partial(middle_kernel, rows, enc),
        in_specs=[VM] * 9,
        out_specs=[VM] * len(out_shape),
        out_shape=out_shape,
        scratch_shapes=scratch,
        compiler_params=pltpu.CompilerParams(vmem_limit_bytes=60 * MIB),
        name="middle",
    )(mix, x_ext, e_all, cot, shifted, flags, w, bup, vecs)


def self_backward_kernel(
    glen, rows,
    x_ref, q_ref, k_ref, v_ref, mix_ref, dmix_ref, dr1_ref, lse_ref, row_ref,
    w_ref, own_out, part_out, g_ref,
    bias, stats, dqt, dqs, dks, dvs,
):
    prompt = glen // 3
    tile = 256
    table, _ = qkv_rows(w_ref.shape[0])
    rank = lax.axis_index("seq")
    off = pl.multiple_of(rank * rows, 128)

    def one_micro(m, _):
        limit = row_ref[m, 0:1, pl.ds(off, rows)]
        seg = row_ref[m, 1:2, pl.ds(off, rows)]

        def masks(t, _):
            at = pl.ds(pl.multiple_of(t * tile, tile), tile)
            place = lax.broadcasted_iota(jnp.int32, (tile, 1), 0) + t * tile
            key_seg = jnp.broadcast_to(row_ref[m, 1:2, at], (8, tile)).T[:, 0:1]
            seen = jnp.where(
                place < prompt, (place < limit).astype(jnp.int32), (key_seg == seg).astype(jnp.int32)
            )
            bias[at, :] = jnp.where(seen == 1, 0.0, NEG)
            return 0

        lax.fori_loop(0, glen // tile, masks, 0)
        stats[0:HEADS, :] = lse_ref[m]
        stats[HEADS : 2 * HEADS, :] = head_sums(
            dmix_ref[m].astype(F32) * mix_ref[m, 0:rows, :].astype(F32)
        )

        def one_pair(pair, _):
            at = lanes_of(pair)
            qp, dp = q_ref[m, 0:rows, at], dmix_ref[m, :, at]
            qm = [head_masked(qp, h) for h in range(2)]
            dm = [head_masked(dp, h) for h in range(2)]
            dqt[...] = jnp.zeros_like(dqt)

            def one_tile(t, _):
                span = pl.ds(pl.multiple_of(t * tile, tile), tile)
                kp, vp = k_ref[m, span, at], v_ref[m, span, at]
                kt = kp.T
                seen = bias[span, :]
                d_k = d_v = None
                d_q = []
                for h in range(2):
                    row = pair * 2 + h
                    prob = jnp.exp(nt(kp, qm[h]) + seen - stats[pl.ds(row, 1), :])
                    d_score = (prob * (nt(vp, dm[h]) - stats[pl.ds(HEADS + row, 1), :])).astype(BF)
                    dk, dv = nn(d_score, qm[h]), nn(prob.astype(BF), dm[h])
                    d_k = dk if d_k is None else d_k + dk
                    d_v = dv if d_v is None else d_v + dv
                    d_q.append(nn(kt, d_score))
                sub = lax.broadcasted_iota(jnp.int32, d_q[0].shape, 0)
                dqt[...] += jnp.where(sub < 64, d_q[0], d_q[1])
                dks[m, span, at] = d_k.astype(BF)
                dvs[m, span, at] = d_v.astype(BF)
                return 0

            lax.fori_loop(0, glen // tile, one_tile, 0)
            dqs[m, :, at] = (dqt[...] * SCALE).T.astype(BF)
            return 0

        lax.fori_loop(0, HEADS // 2, one_pair, 0)
        own_out[m] = dr1_ref[m] + nt(dqs[m], square(w_ref, table, "wq"))

        def spread(t, _):
            span = pl.ds(pl.multiple_of(t * tile, tile), tile)
            part_out[m, span, :] = (
                nt(dks[m, span, :], square(w_ref, table, "wk"))
                + nt(dvs[m, span, :], square(w_ref, table, "wv"))
            ).astype(BF)
            return 0

        lax.fori_loop(0, glen // tile, spread, 0)
        return 0

    lax.fori_loop(0, MICRO, one_micro, 0)
    x_own = jnp.concatenate([x_ref[m, pl.ds(off, rows), :] for m in range(MICRO)], axis=0)
    store_square(g_ref, table, "wq", tn(x_own, dqs[...].reshape(MICRO * rows, D)).astype(BF))
    x_all = x_ref[...].reshape(MICRO * glen, D)
    store_square(g_ref, table, "wk", tn(x_all, dks[...].reshape(MICRO * glen, D)).astype(BF))
    store_square(g_ref, table, "wv", tn(x_all, dvs[...].reshape(MICRO * glen, D)).astype(BF))


def self_backward(x_all, q, k, v, mix, dmix, dr1, lse, row, w, rows):
    glen = x_all.shape[1]
    V = pltpu.VMEM
    return pl.pallas_call(
        functools.partial(self_backward_kernel, glen, rows),
        in_specs=[VM] * 10,
        out_specs=[VM] * 3,
        out_shape=[
            jax.ShapeDtypeStruct((MICRO, rows, D), F32),
            jax.ShapeDtypeStruct((MICRO, glen, D), BF),
            jax.ShapeDtypeStruct(w.shape, BF),
        ],
        scratch_shapes=[
            V((glen, rows), F32), V((2 * HEADS, rows), F32), V((128, rows), F32),
            V((MICRO, rows, D), BF), V((MICRO, glen, D), BF), V((MICRO, glen, D), BF),
        ],
        compiler_params=pltpu.CompilerParams(vmem_limit_bytes=60 * MIB),
        name="self_backward",
    )(x_all, q, k, v, mix, dmix, dr1, lse, row, w)


class Chain:
    def __init__(self, ref, rows, sems, lane, rank, count):
        self.ref, self.rows, self.lane = ref, rows, lane
        self.send, self.recv = sems
        self.rank, self.count = rank, count

    def copy(self, side, step, block, target):
        at = pl.ds(pl.multiple_of(block * self.rows, 16), self.rows)
        part = self.ref.at[:, at] if len(self.ref.shape) == 3 else self.ref.at[at]
        return pltpu.make_async_remote_copy(
            src_ref=part, dst_ref=part,
            send_sem=self.send.at[self.lane, side, step], recv_sem=self.recv.at[self.lane, side, step],
            device_id={"seq": target}, device_id_type=MESH_ID,
        )

    def start(self, step):
        r, last = self.rank, self.count - 1

        @pl.when((r < last) & (r - step >= 0))
        def _():
            self.copy(0, step, r - step, r + 1).start()

        @pl.when((r > 0) & (r + step <= last))
        def _():
            self.copy(1, step, r + step, r - 1).start()

    def arrived(self, step):
        r, last = self.rank, self.count - 1

        @pl.when(r - 1 - step >= 0)
        def _():
            self.copy(0, step, r - 1 - step, r - 1).wait_recv()

        @pl.when(r + 1 + step <= last)
        def _():
            self.copy(1, step, r + 1 + step, r + 1).wait_recv()

    def sent(self, step):
        r, last = self.rank, self.count - 1

        @pl.when((r < last) & (r - step >= 0))
        def _():
            self.copy(0, step, r - step, r + 1).wait_send()

        @pl.when((r > 0) & (r + step <= last))
        def _():
            self.copy(1, step, r + step, r - 1).wait_send()


def weight_units(n):
    piece = D // n
    units = []
    for array, start, count in (
        (0, 0, 3 * piece), (1, 0, 5 * piece), (1, 5 * piece, 4 * piece),
        (1, 9 * piece, 4 * piece), (1, 13 * piece, 2 * piece),
    ):
        for half in range(2):
            units.append((array, start, count, half * 256, 256, half))
    return units


def greet(peers):
    barrier = pltpu.get_barrier_semaphore()
    for axis, target, when in peers:
        if when is None:
            pl.semaphore_signal(barrier, inc=1, device_id={axis: target}, device_id_type=MESH_ID)
        else:

            @pl.when(when)
            def _():
                pl.semaphore_signal(barrier, inc=1, device_id={axis: target}, device_id_type=MESH_ID)

    always = sum(1 for peer in peers if peer[2] is None)
    amount = jnp.int32(always)
    for axis, target, when in peers:
        if when is not None:
            amount = amount + when.astype(jnp.int32)
    pl.semaphore_wait(barrier, amount if always < len(peers) else always)


def gather_kernel(n, count, rows, erows, *refs):
    shards = refs[0:11]
    small, tok, enc, cot = refs[11:15]
    wa, wb, small_all, x_all, e_all, prev = refs[15:21]
    local, fsend, frecv, zsend, zrecv, csend, crecv = refs[21:]
    me, bits = my_place(n)
    rank = lax.axis_index("seq")
    last = count - 1
    piece = D // n
    d = bit_count(n)

    here = at_bits(bits, ())
    table_a, _ = qkv_rows(n)
    table_b, _ = rest_rows(n)
    copies = []

    def keep(src, dst):
        copy = pltpu.make_async_copy(src, dst, local.at[len(copies)])
        copy.start()
        copies.append(copy)

    keep(tok, x_all.at[:, pl.ds(pl.multiple_of(rank * rows, 16), rows)])
    keep(enc, e_all.at[:, pl.ds(pl.multiple_of(rank * erows, 16), erows)])
    names = ("wq", "wk", "wv", "wout", "cq", "ck", "cv", "cout", "up", "down", "slot")
    for name, shard in zip(names, shards):
        table, target = (table_a, wa) if name in table_a else (table_b, wb)
        start, size = table[name]
        if name == "up":
            for c in range(4):
                keep(
                    shard.at[:, pl.ds(c * D, D)],
                    target.at[here + (pl.ds(start + c * piece, piece), slice(None))],
                )
        else:
            keep(shard, target.at[here + (pl.ds(start, size), slice(None))])
    keep(small, small_all.at[here])

    peers = [("fsdp", partner_of(me, bits, b), None) for b in range(d)]
    peers += [("seq", rank - 1, rank > 0), ("seq", rank + 1, rank < last)]
    greet(peers)

    arrays = (wa, wb, small_all)
    units = weight_units(n) + [(2, 0, 8, 0, 128, 0)]
    order_list = orders(n)

    def hop(u, phase):
        array, r0, nr, c0, nc, which = units[u]
        order = order_list[which]
        b = order[phase]
        part = arrays[array].at[at_bits(bits, order[:phase]) + (pl.ds(r0, nr), pl.ds(c0, nc))]
        return pltpu.make_async_remote_copy(
            src_ref=part, dst_ref=part, send_sem=fsend.at[u, phase], recv_sem=frecv.at[u, phase],
            device_id={"fsdp": partner_of(me, bits, b)}, device_id_type=MESH_ID,
        )

    def landed(u, phase):
        array, r0, nr, c0, nc, which = units[u]
        order = order_list[which]
        b = order[phase]
        part = arrays[array].at[
            at_bits(bits, order[:phase], {b: 1 - bits[b]}) + (pl.ds(r0, nr), pl.ds(c0, nc))
        ]
        pltpu.make_async_remote_copy(
            src_ref=part, dst_ref=part, send_sem=fsend.at[u, phase], recv_sem=frecv.at[u, phase],
            device_id={"fsdp": partner_of(me, bits, b)}, device_id_type=MESH_ID,
        ).wait_recv()

    copies[0].wait()
    copies[1].wait()
    chains = [
        Chain(x_all.at[0], rows, (zsend, zrecv), 0, rank, count),
        Chain(e_all, erows, (zsend, zrecv), 1, rank, count),
        Chain(x_all.at[1], rows, (zsend, zrecv), 2, rank, count),
    ]
    for chain in chains:
        chain.start(0)
    halo = pltpu.make_async_remote_copy(
        src_ref=cot.at[:, pl.ds(rows - HALO, HALO)], dst_ref=prev, send_sem=csend, recv_sem=crecv,
        device_id={"seq": rank + 1}, device_id_type=MESH_ID,
    )

    @pl.when(rank < last)
    def _():
        halo.start()

    for copy in copies[2:]:
        copy.wait()
    for u in range(len(units)):
        hop(u, 0).start()
    jobs = []
    for phase in range(1, d):
        for u in range(len(units)):
            jobs.append((u, phase))
    steps = [(s, c) for s in range(1, count) for c in chains]
    share = -(-len(jobs) // max(1, len(steps)))
    while jobs or steps:
        for u, phase in jobs[:share]:
            landed(u, phase - 1)
            hop(u, phase).start()
        jobs = jobs[share:]
        if steps:
            s, chain = steps.pop(0)
            chain.arrived(s - 1)
            if s < count - 1:
                chain.start(s)
    for u in range(len(units)):
        landed(u, d - 1)

    first = pltpu.make_async_copy(cot.at[:, pl.ds(rows - HALO, HALO)], prev, local.at[len(copies)])

    @pl.when(rank > 0)
    def _():
        halo.wait_recv()

    @pl.when(rank == 0)
    def _():
        first.start()
        first.wait()

    @pl.when(rank < last)
    def _():
        halo.wait_send()

    for u in range(len(units)):
        for phase in range(d):
            hop(u, phase).wait_send()
    for chain in chains:
        for s in range(count - 1):
            chain.sent(s)


def gather(n, count, shards, small, tok, enc, cot):
    rows, erows = tok.shape[1], enc.shape[1]
    lead = (2,) * bit_count(n)
    _, ra = qkv_rows(n)
    _, rb = rest_rows(n)
    units = len(weight_units(n)) + 1
    d = bit_count(n)
    hbm = pl.BlockSpec(memory_space=pl.ANY)
    dma = pltpu.SemaphoreType.DMA
    return pl.pallas_call(
        functools.partial(gather_kernel, n, count, rows, erows),
        in_specs=[hbm] * 15,
        out_specs=[hbm] * 6,
        out_shape=[
            jax.ShapeDtypeStruct(lead + (ra, D), BF),
            jax.ShapeDtypeStruct(lead + (rb, D), BF),
            jax.ShapeDtypeStruct(lead + (8, 128), F32),
            jax.ShapeDtypeStruct((MICRO, count * rows, D), BF),
            jax.ShapeDtypeStruct((MICRO, count * erows, D), BF),
            jax.ShapeDtypeStruct((MICRO, HALO, D), BF),
        ],
        scratch_shapes=[
            dma((18,)), dma((units, d)), dma((units, d)),
            dma((3, 2, count)), dma((3, 2, count)), dma(()), dma(()),
        ],
        compiler_params=pltpu.CompilerParams(
            collective_id=0, has_side_effects=True, vmem_limit_bytes=60 * MIB
        ),
        name="gather",
    )(*shards, small, tok, enc, cot)


def reduce_kernel(n, count, rows, erows, *refs):
    grads = refs[0:3]
    part, genc, own = refs[3:6]
    outs = refs[6:9]
    tok_out, enc_out = refs[9:11]
    rest = list(refs[11:])
    d = bit_count(n)

    def take(k):
        got = rest[:k]
        del rest[:k]
        return got

    accs, zls, zrs, zss, fins = take(3), take(3), take(3), take(3), take(3)
    recvs = [take(d) for _ in range(3)]
    tbuf, ebuf = take(2)
    fsend, frecv, zsend, zrecv, tsend, trecv, esend, erecv = rest
    me, bits = my_place(n)
    rank = lax.axis_index("seq")
    last = count - 1
    peers = [("fsdp", partner_of(me, bits, b), None) for b in range(d)]
    peers += [("seq", lax.rem(rank + k, count), None) for k in range(1, count)]
    greet(peers)

    moves = []
    for k in range(1, count):
        to = lax.rem(rank + k, count)
        for m in range(MICRO):
            moves.append(
                pltpu.make_async_remote_copy(
                    src_ref=part.at[m, pl.ds(pl.multiple_of(to * rows, 16), rows)],
                    dst_ref=tbuf.at[k - 1, m],
                    send_sem=tsend.at[k - 1, m], recv_sem=trecv.at[k - 1, m],
                    device_id={"seq": to}, device_id_type=MESH_ID,
                )
            )
        moves.append(
            pltpu.make_async_remote_copy(
                src_ref=genc.at[:, pl.ds(pl.multiple_of(to * erows, 16), erows)],
                dst_ref=ebuf.at[k - 1],
                send_sem=esend.at[k - 1], recv_sem=erecv.at[k - 1],
                device_id={"seq": to}, device_id_type=MESH_ID,
            )
        )

    units = weight_units(n)
    units = units[2:] + units[:2] + [(2, 0, 8, 0, 128, 0)]
    order_list = [o[::-1] for o in orders(n)]

    def hop(u, phase):
        array, r0, nr, c0, nc, which = units[u]
        order = order_list[which]
        b = order[phase]
        free = [x for x in range(d) if x not in order[: phase + 1]]
        cut = (pl.ds(r0, nr), pl.ds(c0, nc))
        index = at_bits(bits, free, {b: 1 - bits[b]})
        src = grads[array].at[index + cut] if phase == 0 else accs[array].at[index[:-1] + cut]
        dst = recvs[array][phase].at[(slice(None),) * len(free) + cut]
        return pltpu.make_async_remote_copy(
            src_ref=src, dst_ref=dst, send_sem=fsend.at[u, phase], recv_sem=frecv.at[u, phase],
            device_id={"fsdp": partner_of(me, bits, b)}, device_id_type=MESH_ID,
        )

    def add(u, phase):
        array, r0, nr, c0, nc, which = units[u]
        order = order_list[which]
        free = [x for x in range(d) if x not in order[: phase + 1]]
        cut = (slice(r0, r0 + nr), slice(c0, c0 + nc))
        index = at_bits(bits, free)
        base = grads[array][index + cut] if phase == 0 else accs[array][index[:-1] + cut]
        more = recvs[array][phase][(slice(None),) * len(free) + cut]
        accs[array][index[:-1] + cut] = (base.astype(F32) + more.astype(F32)).astype(base.dtype)

    here = at_bits(bits, ())[:-1]

    def root_of(which):
        return (count - 1) // 2 if which == 0 else count // 2

    def z_copy(u, kind, src, dst, target):
        return pltpu.make_async_remote_copy(
            src_ref=src, dst_ref=dst, send_sem=zsend.at[u, kind], recv_sem=zrecv.at[u, kind],
            device_id={"seq": target}, device_id_type=MESH_ID,
        )

    def z_refs(u):
        array, r0, nr, c0, nc, which = units[u]
        cut = (pl.ds(r0, nr), pl.ds(c0, nc))
        return [x[array].at[cut] for x in (zss, zls, zrs, fins)], root_of(which)

    def z_in(u):
        array, r0, nr, c0, nc, which = units[u]
        cut = (slice(r0, r0 + nr), slice(c0, c0 + nc))
        (zs, zl, zr, fin), root = z_refs(u)
        zss[array][cut] = accs[array][here + cut]

        @pl.when((rank > 0) & (rank <= root))
        def _():
            z_copy(u, 0, zs, zl, rank - 1).wait_recv()
            zss[array][cut] = (
                zss[array][cut].astype(F32) + zls[array][cut].astype(F32)
            ).astype(zss[array].dtype)

        @pl.when((rank < last) & (rank >= root))
        def _():
            z_copy(u, 1, zs, zr, rank + 1).wait_recv()
            zss[array][cut] = (
                zss[array][cut].astype(F32) + zrs[array][cut].astype(F32)
            ).astype(zss[array].dtype)

        @pl.when(rank < root)
        def _():
            z_copy(u, 0, zs, zl, rank + 1).start()

        @pl.when(rank > root)
        def _():
            z_copy(u, 1, zs, zr, rank - 1).start()

        @pl.when(rank == root)
        def _():
            fins[array][cut] = zss[array][cut]

        @pl.when((rank == root) & (rank > 0))
        def _():
            z_copy(u, 2, fin, fin, rank - 1).start()

        @pl.when((rank == root) & (rank < last))
        def _():
            z_copy(u, 3, fin, fin, rank + 1).start()

    def z_out(u):
        array, r0, nr, c0, nc, which = units[u]
        (zs, zl, zr, fin), root = z_refs(u)

        @pl.when(rank < root)
        def _():
            z_copy(u, 2, fin, fin, rank + 1).wait_recv()

        @pl.when((rank < root) & (rank > 0))
        def _():
            z_copy(u, 2, fin, fin, rank - 1).start()

        @pl.when(rank > root)
        def _():
            z_copy(u, 3, fin, fin, rank - 1).wait_recv()

        @pl.when((rank > root) & (rank < last))
        def _():
            z_copy(u, 3, fin, fin, rank + 1).start()

        cut = (slice(r0, r0 + nr), slice(c0, c0 + nc))
        outs[array][cut] = fins[array][cut].astype(F32)

    def z_sent(u):
        (zs, zl, zr, fin), root = z_refs(u)

        @pl.when(rank < root)
        def _():
            z_copy(u, 0, zs, zl, rank + 1).wait_send()

        @pl.when(rank > root)
        def _():
            z_copy(u, 1, zs, zr, rank - 1).wait_send()

        @pl.when((rank <= root) & (rank > 0))
        def _():
            z_copy(u, 2, fin, fin, rank - 1).wait_send()

        @pl.when((rank >= root) & (rank < last))
        def _():
            z_copy(u, 3, fin, fin, rank + 1).wait_send()

    for u in range(len(units)):
        hop(u, 0).start()
    for move in moves:
        move.start()
    lag = 4
    for t in range(len(units) + d + lag + 1):
        for stage in range(d + 2):
            u = t - stage - (lag if stage == d + 1 else 0)
            if not 0 <= u < len(units):
                continue
            if stage < d:
                hop(u, stage).wait_recv()
                add(u, stage)
                if stage + 1 < d:
                    hop(u, stage + 1).start()
            elif stage == d:
                z_in(u)
            else:
                z_out(u)
    for move in moves:
        move.wait_recv()
    mine = pl.ds(pl.multiple_of(rank * rows, 16), rows)
    emine = pl.ds(pl.multiple_of(rank * erows, 16), erows)
    for m in range(MICRO):
        total = own[m] + part[m, mine, :].astype(F32)
        states = genc[m, emine, :].astype(F32)
        for k in range(1, count):
            total = total + tbuf[k - 1, m].astype(F32)
            states = states + ebuf[k - 1, m].astype(F32)
        tok_out[m] = total
        enc_out[m] = states
    for move in moves:
        move.wait_send()
    for u in range(len(units)):
        for phase in range(d):
            hop(u, phase).wait_send()
        z_sent(u)


def reduce_out(n, count, ga, gb, gs, part, genc, own):
    rows = own.shape[1]
    erows = genc.shape[1] // count
    d = bit_count(n)
    units = len(weight_units(n)) + 1
    dma = pltpu.SemaphoreType.DMA
    V = pltpu.VMEM
    grads = (ga, gb, gs)
    flat = [(g.shape[-2], g.shape[-1]) for g in grads]
    types = [g.dtype for g in grads]
    scratch = [V((2,) * (d - 1) + f, t) for f, t in zip(flat, types)]
    for _ in range(4):
        scratch += [V(f, t) for f, t in zip(flat, types)]
    for f, t in zip(flat, types):
        scratch += [V((2,) * (d - 1 - p) + f, t) for p in range(d)]
    scratch += [V((count - 1, MICRO, rows, D), BF), V((count - 1, MICRO, erows, D), BF)]
    scratch += [
        dma((units, d)), dma((units, d)), dma((units, 4)), dma((units, 4)),
        dma((count - 1, MICRO)), dma((count - 1, MICRO)), dma((count - 1,)), dma((count - 1,)),
    ]
    return pl.pallas_call(
        functools.partial(reduce_kernel, n, count, rows, erows),
        in_specs=[VM] * 6,
        out_specs=[VM] * 5,
        out_shape=[jax.ShapeDtypeStruct(f, F32) for f in flat]
        + [jax.ShapeDtypeStruct((MICRO, rows, D), F32), jax.ShapeDtypeStruct((MICRO, erows, D), F32)],
        scratch_shapes=scratch,
        compiler_params=pltpu.CompilerParams(
            collective_id=1, has_side_effects=True, vmem_limit_bytes=60 * MIB
        ),
        name="reduce_out",
    )(ga, gb, gs, part, genc, own)


def on_device(
    tokens, encoded, segment_ids, prefix_len, cotangent,
    w_query, w_key, w_value, w_out, c_query, c_key, c_value, c_out,
    w_up, b_up, w_down, b_down,
    gain_one, shift_one, gain_two, shift_two, gain_three, shift_three, w_slot,
):
    n = lax.axis_size("fsdp")
    count = lax.axis_size("seq")
    rank = lax.axis_index("seq")
    tokens = tokens[:, 0]
    rows = tokens.shape[1]
    seg = segment_ids[:, 0]
    glen = seg.shape[1]
    prompt = glen // 3
    prefix = prefix_len[:, 0]
    cot = cotangent[:, 0]

    shards = (w_query, w_key, w_value, w_out, c_query, c_key, c_value, c_out, w_up, w_down, w_slot)
    edge, side = FF // n, D // n
    small = jnp.concatenate(
        [b_up, b_down, gain_one, shift_one, gain_two, shift_two, gain_three, shift_three]
    ).astype(F32)
    small = jnp.pad(small, (0, 1024 - small.shape[0])).reshape(8, 128)
    wa, wb, small_all, x_all, e_all, previous = gather(
        n, count, shards, small, tokens, encoded[:, 0], cot
    )
    wa = wa.reshape((n,) + wa.shape[-2:])
    wb = wb.reshape((n,) + wb.shape[-2:])
    small_all = small_all.reshape(n, 1024)
    bup = small_all[:, :edge].reshape(1, FF)
    vecs = small_all[:, edge : edge + 7 * side].reshape(n, 7, side).transpose(1, 0, 2).reshape(7, D)
    vecs = jnp.concatenate([vecs, jnp.zeros((1, D), F32)], axis=0)
    shifted = jnp.concatenate([previous[:, HALO - 1 :], cot[:, : rows - 1]], axis=1)

    numbers = jnp.arange(1, prefix.shape[1] + 1, dtype=jnp.int32)
    limit = jnp.sum(
        jnp.where(seg[:, :, None] == numbers[None, None, :], prefix[:, None, :], 0), axis=2
    )
    limit = jnp.where(seg == 0, prompt, limit)
    col = jnp.stack([limit, seg], axis=2)
    row = jnp.stack([limit, seg], axis=1)
    same = jnp.concatenate(
        [jnp.zeros((MICRO, 1), F32), (seg[:, 1:] == seg[:, :-1]).astype(F32), jnp.zeros((MICRO, 1), F32)],
        axis=1,
    )
    offset = rank * rows
    flags = jnp.stack(
        [
            lax.dynamic_slice_in_dim(same, offset + 1, rows, 1),
            lax.dynamic_slice_in_dim(same, offset, rows, 1),
        ],
        axis=2,
    )
    start = jnp.minimum(offset + rows, glen - HALO)
    x_ext = jnp.concatenate([tokens, lax.dynamic_slice_in_dim(x_all, start, HALO, 1)], axis=1)

    q, k, v, mix, lse = self_forward(x_all, wa, col, row[:, 1:2], rows)
    slot_out, dmix, dr1, genc, gb, g_bup, g_vec = middle(
        mix, x_ext, e_all, cot, shifted, flags, wb, bup, vecs, rows
    )
    own, part, ga = self_backward(x_all, q, k, v, mix, dmix, dr1, lse, row, wa, rows)

    gs = jnp.concatenate(
        [
            g_bup[0:1].reshape(n, edge),
            g_vec[:7].reshape(7, n, side).transpose(1, 0, 2).reshape(n, 7 * side),
            jnp.zeros((n, 1024 - edge - 7 * side), F32),
        ],
        axis=1,
    )
    lead = (2,) * bit_count(n)
    ga = ga.reshape(lead + ga.shape[1:])
    gb = gb.reshape(lead + gb.shape[1:])
    gs = gs.reshape(lead + (8, 128))
    oa, ob, os, grad_tokens, grad_encoded = reduce_out(n, count, ga, gb, gs, part, genc, own)
    table_a, _ = qkv_rows(n)
    table_b, _ = rest_rows(n)
    g = {name: oa[start : start + size] for name, (start, size) in table_a.items()}
    g.update({name: ob[start : start + size] for name, (start, size) in table_b.items()})
    g["up"] = g["up"].reshape(4, side, D).transpose(1, 0, 2).reshape(side, FF)
    line = os.reshape(1024)
    b_up_g = line[:edge]
    b_down_g, g1, s1, g2, s2, g3, s3 = [
        line[edge + i * side : edge + (i + 1) * side] for i in range(7)
    ]
    return (
        slot_out[:, None], grad_tokens[:, None], grad_encoded[:, None],
        g["wq"], g["wk"], g["wv"], g["wout"], g["cq"], g["ck"], g["cv"], g["cout"],
        g["up"], b_up_g, g["down"], b_down_g, g1, s1, g2, s2, g3, s3, g["slot"],
    )


def solution(mesh):
    act = P(None, "fsdp", "seq", None)
    ids = P(None, "fsdp", None)
    mat, one = P("fsdp", None), P("fsdp")
    in_specs = (
        (act, act, ids, ids, act) + (mat,) * 9 + (one, mat) + (one,) * 7 + (mat,)
    )
    out_specs = (act, act, act) + (mat,) * 9 + (one, mat) + (one,) * 7 + (mat,)
    return jax.shard_map(
        on_device, mesh=mesh, in_specs=in_specs, out_specs=out_specs, check_vma=False
    )
```

```python
import functools
import math

import jax
import jax.numpy as jnp
from jax import lax
from jax.experimental import pallas as pl
from jax.experimental.pallas import tpu as pltpu
from jax.sharding import PartitionSpec as P

D = 512
HD = 64
HEADS = 8
FF = 2048
MICRO = 2
HALO = 16
EPSILON = 1e-05
BF = jnp.bfloat16
F32 = jnp.float32
SCALE = 1.0 / math.sqrt(HD)
NEG = -1e30
MIB = 1024 * 1024
GELU_C = math.sqrt(2.0 / math.pi)

VM = pl.BlockSpec(memory_space=pltpu.VMEM)


def nn(a, b):
    return lax.dot_general(a, b, (((1,), (0,)), ((), ())), preferred_element_type=F32)


def nt(a, b):
    return lax.dot_general(a, b, (((1,), (1,)), ((), ())), preferred_element_type=F32)


def tn(a, b):
    return lax.dot_general(a, b, (((0,), (0,)), ((), ())), preferred_element_type=F32)


def lanes_of(pair):
    return pl.ds(pl.multiple_of(pair * 128, 128), 128)


def head_masked(value, head):
    lane = lax.broadcasted_iota(jnp.int32, value.shape, 1)
    return jnp.where((lane >= 64) == (head == 1), value, jnp.zeros_like(value))


def softmax_parts(scores):
    top = jnp.max(scores, axis=-1, keepdims=True)
    raw = jnp.exp(scores - top)
    total = jnp.sum(raw, axis=-1, keepdims=True)
    return raw, top, total


def attend_pair(query_pair, key_pair, value_pair, bias, pair, lse_ref):
    mixed = []
    for head in range(2):
        scores = nt(head_masked(query_pair, head), key_pair)
        if bias is not None:
            scores = scores + bias
        raw, top, total = softmax_parts(scores)
        mixed.append(nn(raw.astype(BF), value_pair) / total)
        lane = lax.broadcasted_iota(jnp.int32, lse_ref.shape, 1)
        lse_ref[...] = jnp.where(lane == pair * 2 + head, top + jnp.log(total), lse_ref[...])
    lane = lax.broadcasted_iota(jnp.int32, mixed[0].shape, 1)
    return jnp.where(lane < 64, mixed[0], mixed[1])


def bit_count(n):
    return n.bit_length() - 1


def qkv_rows(n):
    piece = D // n
    return {"wq": (0, piece), "wk": (piece, piece), "wv": (2 * piece, piece)}, 3 * piece


def rest_rows(n):
    piece = D // n
    table, start = {}, 0
    for name, times in (
        ("wout", 1), ("cq", 1), ("ck", 1), ("cv", 1), ("cout", 1), ("up", 4), ("down", 4), ("slot", 2)
    ):
        table[name] = (start, times * piece)
        start += times * piece
    return table, start


def square(ref, table, name):
    start, count = table[name]
    return ref[:, start : start + count, :].reshape(D, D)


def up_part(ref, table, c):
    start, count = table["up"]
    piece = count // 4
    return ref[:, start + c * piece : start + (c + 1) * piece, :].reshape(D, D)


def row_part(ref, table, name, c):
    start, count = table[name]
    many = D // count
    return ref[c * many : (c + 1) * many, start : start + count, :].reshape(D, D)


def store_square(ref, table, name, value):
    start, count = table[name]
    ref[:, start : start + count, :] = value.reshape(ref.shape[0], count, D)


def store_up(ref, table, c, value):
    start, count = table["up"]
    piece = count // 4
    ref[:, start + c * piece : start + (c + 1) * piece, :] = value.reshape(ref.shape[0], piece, D)


def store_part(ref, table, name, c, value):
    start, count = table[name]
    many = D // count
    ref[c * many : (c + 1) * many, start : start + count, :] = value.reshape(many, count, D)


def my_place(n):
    me = lax.axis_index("fsdp")
    bits = [(me // (1 << b)) % 2 for b in range(bit_count(n))]
    return me, bits


def partner_of(me, bits, b):
    return me + (1 - 2 * bits[b]) * (1 << b)


def orders(n):
    d = bit_count(n)
    far = list(range(1, d))
    return [far + [0], far[::-1] + [0]]


def at_bits(bits, free, fixed=None):
    fixed = fixed or {}
    return tuple(
        slice(None) if b in free else fixed.get(b, bits[b]) for b in range(len(bits) - 1, -1, -1)
    )


MESH_ID = pl.DeviceIdType.MESH

def place_info(info, seg_ref, prefix_ref, m):
    glen = info.shape[1]
    prompt = glen // 3
    seg = jnp.broadcast_to(seg_ref[m], (8, glen))
    limit = jnp.where(seg == 0, prompt, 0)
    for c in range(prefix_ref.shape[1]):
        limit = jnp.where(seg == c + 1, prefix_ref[m, c], limit)
    place = lax.broadcasted_iota(jnp.int32, (8, glen), 1)
    after = (seg == pltpu.roll(seg, glen - 1, 1)) & (place < glen - 1)
    before = (seg == pltpu.roll(seg, 1, 1)) & (place > 0)
    sub = lax.broadcasted_iota(jnp.int32, (8, glen), 0)
    mixed = jnp.where(sub == 0, limit, seg)
    mixed = jnp.where(sub == 2, after.astype(jnp.int32), mixed)
    mixed = jnp.where(sub == 3, before.astype(jnp.int32), mixed)
    info[...] = mixed.astype(F32)


SMEM = pl.BlockSpec(memory_space=pltpu.SMEM)


def norm_forward(residual, gain, shift):
    average = jnp.mean(residual, axis=-1, keepdims=True)
    centred = residual - average
    variance = jnp.mean(centred * centred, axis=-1, keepdims=True)
    rstd = lax.rsqrt(variance + EPSILON)
    hat = centred * rstd
    return hat * gain + shift, hat, rstd


def norm_backward(upstream, hat, rstd, gain):
    d_hat = upstream * gain
    mean_d = jnp.mean(d_hat, axis=-1, keepdims=True)
    mean_dh = jnp.mean(d_hat * hat, axis=-1, keepdims=True)
    d_gain = jnp.sum(upstream * hat, axis=0, keepdims=True)
    d_shift = jnp.sum(upstream, axis=0, keepdims=True)
    return rstd * (d_hat - mean_d - hat * mean_dh), d_gain, d_shift


def gelu_parts(value):
    square = value * value
    t = jnp.tanh(GELU_C * value * (1.0 + 0.044715 * square))
    half = 0.5 * (1.0 + t)
    slope = half + 0.5 * value * (1.0 - t * t) * (GELU_C * (1.0 + 3.0 * 0.044715 * square))
    return value * half, slope


def head_sums(product_rows):
    rows, cols = 16, product_rows.shape[1]
    head = lax.broadcasted_iota(jnp.int32, (rows, cols), 0)
    lane = lax.broadcasted_iota(jnp.int32, (rows, cols), 1)
    pick = ((lane // HD) == head).astype(F32)
    return lax.dot_general(
        pick, product_rows, (((1,), (1,)), ((), ())),
        preferred_element_type=F32, precision=lax.Precision.HIGHEST,
    )[0:HEADS, :]


def middle_kernel(
    rows, enc,
    mix_ref, x_ref, edge_ref, e_ref, cot_ref, prev_ref, seg_ref, prefix_ref,
    w_ref, bup_ref, vec_ref,
    slot_out, dmix_out, dr1_out, genc_out, g_ref, gbup, gvec,
    lowx, lown, cqs, cks, cvs, lse_sc, lse_row, cmix, h1s, hats, rstds, slope,
    act, dpre, dffn, dcross, dcqs, dattn, dcks, dcvs, ckt, h3s, h2low, info, shs,
):
    ext = rows + HALO
    table, _ = rest_rows(w_ref.shape[0])
    gbup[...] = jnp.zeros_like(gbup)
    gvec[...] = jnp.zeros_like(gvec)

    def vec(i):
        return vec_ref[i : i + 1, :]

    def one_micro(m, _):
        own = pl.ds(0, rows)
        attn = nn(mix_ref[m], square(w_ref, table, "wout"))
        x_rows = jnp.concatenate([x_ref[m], edge_ref[m]], axis=0).astype(F32)
        h1, hat, rstd = norm_forward(x_rows + attn, vec(1), vec(2))
        h1s[...] = h1
        dr1_out[m] = hat[0:rows]
        rstds[:, 0:1] = rstd[0:rows]
        h1_low = h1.astype(BF)
        lown[0, m] = h1_low[0:rows]
        cqs[...] = (nn(h1_low, square(w_ref, table, "cq")).astype(BF) * SCALE).astype(BF)
        cks[...] = nn(e_ref[m], square(w_ref, table, "ck")).astype(BF)
        cvs[...] = nn(e_ref[m], square(w_ref, table, "cv")).astype(BF)

        def cross_pair(pair, _):
            at = lanes_of(pair)
            mix = attend_pair(cqs[:, at], cks[:, at], cvs[:, at], None, pair, lse_sc)
            cmix[:, at] = mix.astype(BF)
            return 0

        lax.fori_loop(0, HEADS // 2, cross_pair, 0)
        lse_row[0:HEADS, :] = lse_sc[0:rows, :].T[0:HEADS, :]
        lowx[m] = cmix[0:rows, :]
        h2, hat, rstd = norm_forward(
            h1s[...] + nn(cmix[...], square(w_ref, table, "cout")), vec(3), vec(4)
        )
        h1s[...] = h2
        hats[...] = hat[0:rows]
        rstds[:, 1:2] = rstd[0:rows]
        h2low[...] = h2.astype(BF)
        lown[1, m] = h2low[0:rows, :]
        h3s[...] = jnp.zeros_like(h3s)

        for c in range(FF // D):
            at = slice(c * D, (c + 1) * D)
            pre = nn(h2low[...], up_part(w_ref, table, c)) + bup_ref[0:1, at]
            value, grad = gelu_parts(pre)
            value = value.astype(BF)
            act[m, :, at] = value[0:rows]
            slope[:, at] = grad[0:rows]
            down = row_part(w_ref, table, "down", c)
            h3s[...] += nn(value, down)
        h3, hat, rstd = norm_forward(h1s[...] + h3s[...] + vec(0), vec(5), vec(6))
        h3_low = h3.astype(BF)
        h3s[...] = h3_low.astype(F32)
        lown[2, m] = h3_low[0:rows]
        top = row_part(w_ref, table, "slot", 0)
        bottom = row_part(w_ref, table, "slot", 1)
        place_info(info, seg_ref, prefix_ref, m)
        flags = info[:, pl.ds(pl.multiple_of(lax.axis_index("seq") * rows, 128), rows)].T
        follow = (h3s[pl.ds(1, rows), :] * flags[:, 2:3]).astype(BF)
        slot_out[m] = (nn(h3_low[0:rows], top) + nn(follow, bottom)).astype(BF)
        h3s[0:8, :] = prev_ref[m].astype(F32)[HALO - 8 : HALO]
        h3s[8 : rows + 8, :] = cot_ref[m].astype(F32)
        shifted = h3s[pl.ds(7, rows), :]
        shs[m] = (shifted * flags[:, 3:4]).astype(BF)
        d_follow = nt(shifted.astype(BF), bottom).astype(BF).astype(F32) * flags[:, 3:4]
        d_three = nt(cot_ref[m], top) + d_follow
        d_r3, d_gain, d_shift = norm_backward(d_three, hat[0:rows], rstd[0:rows], vec(5))
        gvec[5:6, :] += d_gain
        gvec[6:7, :] += d_shift
        d_ffn = d_r3.astype(BF)
        dffn[m] = d_ffn
        gvec[0:1, :] += jnp.sum(d_ffn.astype(F32), axis=0, keepdims=True)
        d_two = d_r3
        for c in range(FF // D):
            at = slice(c * D, (c + 1) * D)
            down = row_part(w_ref, table, "down", c)
            grad = (nt(d_ffn, down) * slope[:, at]).astype(BF)
            dpre[m, :, at] = grad
            gbup[0:1, at] += jnp.sum(grad.astype(F32), axis=0, keepdims=True)
            d_two = d_two + nt(grad, up_part(w_ref, table, c))
        d_r2, d_gain, d_shift = norm_backward(d_two, hats[...], rstds[:, 1:2], vec(3))
        gvec[3:4, :] += d_gain
        gvec[4:5, :] += d_shift
        d_cross = d_r2.astype(BF)
        dcross[m] = d_cross
        d_cmix = nt(d_cross, square(w_ref, table, "cout")).astype(BF)
        dmix_out[m] = d_cmix
        delta = head_sums(d_cmix.astype(F32) * cmix[0:rows, :].astype(F32))
        lse_row[HEADS : 2 * HEADS, :] = delta
        ckt[...] = cks[...].T

        def cross_back(pair, _):
            at = lanes_of(pair)
            kp, vp = cks[:, at], cvs[:, at]
            qp, dp = cqs[0:rows, at], dmix_out[m, :, at]
            kt = ckt[at, :]
            d_k = d_v = None
            d_qt = []
            for head in range(2):
                qm, dm = head_masked(qp, head), head_masked(dp, head)
                row = pair * 2 + head
                prob = jnp.exp(nt(kp, qm) - lse_row[pl.ds(row, 1), :])
                d_score = (prob * (nt(vp, dm) - lse_row[pl.ds(HEADS + row, 1), :])).astype(BF)
                dk, dv = nn(d_score, qm), nn(prob.astype(BF), dm)
                d_k = dk if d_k is None else d_k + dk
                d_v = dv if d_v is None else d_v + dv
                d_qt.append(nn(kt, d_score))
            sub = lax.broadcasted_iota(jnp.int32, d_qt[0].shape, 0)
            d_q = jnp.where(sub < 64, d_qt[0], d_qt[1]) * SCALE
            dcqs[m, :, at] = d_q.T.astype(BF)
            dcks[m, :, at] = d_k.astype(BF)
            dcvs[m, :, at] = d_v.astype(BF)
            return 0

        lax.fori_loop(0, HEADS // 2, cross_back, 0)
        genc_out[m] = (
            nt(dcks[m], square(w_ref, table, "ck")) + nt(dcvs[m], square(w_ref, table, "cv"))
        ).astype(BF)
        d_one = d_r2 + nt(dcqs[m], square(w_ref, table, "cq"))
        d_r1, d_gain, d_shift = norm_backward(d_one, dr1_out[m], rstds[:, 0:1], vec(1))
        gvec[1:2, :] += d_gain
        gvec[2:3, :] += d_shift
        dr1_out[m] = d_r1
        d_attn = d_r1.astype(BF)
        dattn[m] = d_attn
        dmix_out[m] = nt(d_attn, square(w_ref, table, "wout")).astype(BF)
        return 0

    lax.fori_loop(0, MICRO, one_micro, 0)

    total = MICRO * rows

    def flat(ref, *lead):
        return ref[lead].reshape(total, D) if lead else ref[...].reshape(total, D)

    def grad_of(left, right):
        return tn(left, right).astype(BF)

    cot = cot_ref[...].reshape(total, D)
    flagged = shs[...].reshape(total, D)
    h3_all = lown[2].reshape(total, D)
    store_part(g_ref, table, "slot", 0, grad_of(h3_all, cot))
    store_part(g_ref, table, "slot", 1, grad_of(h3_all, flagged))
    dffn_all = dffn[...].reshape(total, D)
    h2_all = lown[1].reshape(total, D)
    for c in range(FF // D):
        at = slice(c * D, (c + 1) * D)
        store_part(g_ref, table, "down", c, grad_of(act[:, :, at].reshape(total, D), dffn_all))
        store_up(g_ref, table, c, grad_of(h2_all, dpre[:, :, at].reshape(total, D)))
    store_square(g_ref, table, "cout", grad_of(lowx[...].reshape(total, D), dcross[...].reshape(total, D)))
    store_square(g_ref, table, "cq", grad_of(lown[0].reshape(total, D), dcqs[...].reshape(total, D)))
    e_all = e_ref[...].reshape(MICRO * enc, D)
    store_square(g_ref, table, "ck", grad_of(e_all, dcks[...].reshape(MICRO * enc, D)))
    store_square(g_ref, table, "cv", grad_of(e_all, dcvs[...].reshape(MICRO * enc, D)))
    mix_all = jnp.concatenate([mix_ref[m, 0:rows, :] for m in range(MICRO)], axis=0)
    store_square(g_ref, table, "wout", grad_of(mix_all, dattn[...].reshape(total, D)))


def middle(mix, tokens, edges, e_all, cot, prev, seg, prefix, w, bup, vecs, rows):
    glen = seg.shape[2]
    enc = e_all.shape[1]
    ext = rows + HALO
    out_shape = [
        jax.ShapeDtypeStruct((MICRO, rows, D), BF),
        jax.ShapeDtypeStruct((MICRO, rows, D), BF),
        jax.ShapeDtypeStruct((MICRO, rows, D), F32),
        jax.ShapeDtypeStruct((MICRO, enc, D), BF),
        jax.ShapeDtypeStruct(w.shape, BF),
        jax.ShapeDtypeStruct((8, FF), F32),
        jax.ShapeDtypeStruct((8, D), F32),
    ]
    V = pltpu.VMEM
    scratch = [
        V((MICRO, rows, D), BF),
        V((3, MICRO, rows, D), BF),
        V((ext, D), BF), V((enc, D), BF), V((enc, D), BF),
        V((ext, 128), F32), V((2 * HEADS, rows), F32),
        V((ext, D), BF),
        V((ext, D), F32),
        V((rows, D), F32), V((rows, 128), F32),
        V((rows, FF), F32),
        V((MICRO, rows, FF), BF), V((MICRO, rows, FF), BF),
        V((MICRO, rows, D), BF), V((MICRO, rows, D), BF), V((MICRO, rows, D), BF),
        V((MICRO, rows, D), BF),
        V((MICRO, enc, D), BF), V((MICRO, enc, D), BF),
        V((D, enc), BF),
        V((ext, D), F32), V((ext, D), BF),
        V((8, glen), F32), V((MICRO, rows, D), BF),
    ]
    return pl.pallas_call(
        functools.partial(middle_kernel, rows, enc),
        in_specs=[VM] * 7 + [SMEM] + [VM] * 3,
        out_specs=[VM] * len(out_shape),
        out_shape=out_shape,
        scratch_shapes=scratch,
        compiler_params=pltpu.CompilerParams(vmem_limit_bytes=60 * MIB),
        name="middle",
    )(mix, tokens, edges, e_all, cot, prev, seg, prefix, w, bup, vecs)


def self_backward_kernel(
    glen, rows,
    x_ref, q_ref, k_ref, v_ref, mix_ref, dmix_ref, dr1_ref, lse_ref, seg_ref, prefix_ref,
    w_ref, own_out, part_out, g_ref,
    bias, stats, dqt, dqs, dks, dvs, info,
):
    prompt = glen // 3
    tile = 256
    table, _ = qkv_rows(w_ref.shape[0])
    rank = lax.axis_index("seq")
    off = pl.multiple_of(rank * rows, 128)

    def one_micro(m, _):
        place_info(info, seg_ref, prefix_ref, m)
        limit = info[0:1, pl.ds(off, rows)]
        seg = info[1:2, pl.ds(off, rows)]

        def masks(t, _):
            at = pl.ds(pl.multiple_of(t * tile, tile), tile)
            place = lax.broadcasted_iota(jnp.int32, (tile, 1), 0) + t * tile
            key_seg = info[:, at].T[:, 1:2]
            seen = jnp.where(
                place < prompt, (place.astype(F32) < limit).astype(jnp.int32), (key_seg == seg).astype(jnp.int32)
            )
            bias[at, :] = jnp.where(seen == 1, 0.0, NEG)
            return 0

        lax.fori_loop(0, glen // tile, masks, 0)
        stats[0:HEADS, :] = lse_ref[m]
        stats[HEADS : 2 * HEADS, :] = head_sums(
            dmix_ref[m].astype(F32) * mix_ref[m, 0:rows, :].astype(F32)
        )

        def one_pair(pair, _):
            at = lanes_of(pair)
            qp, dp = q_ref[m, 0:rows, at], dmix_ref[m, :, at]
            qm = [head_masked(qp, h) for h in range(2)]
            dm = [head_masked(dp, h) for h in range(2)]
            dqt[...] = jnp.zeros_like(dqt)

            def one_tile(t, _):
                span = pl.ds(pl.multiple_of(t * tile, tile), tile)
                kp, vp = k_ref[m, span, at], v_ref[m, span, at]
                kt = kp.T
                seen = bias[span, :]
                d_k = d_v = None
                d_q = []
                for h in range(2):
                    row = pair * 2 + h
                    prob = jnp.exp(nt(kp, qm[h]) + seen - stats[pl.ds(row, 1), :])
                    d_score = (prob * (nt(vp, dm[h]) - stats[pl.ds(HEADS + row, 1), :])).astype(BF)
                    dk, dv = nn(d_score, qm[h]), nn(prob.astype(BF), dm[h])
                    d_k = dk if d_k is None else d_k + dk
                    d_v = dv if d_v is None else d_v + dv
                    d_q.append(nn(kt, d_score))
                sub = lax.broadcasted_iota(jnp.int32, d_q[0].shape, 0)
                dqt[...] += jnp.where(sub < 64, d_q[0], d_q[1])
                dks[m, span, at] = d_k.astype(BF)
                dvs[m, span, at] = d_v.astype(BF)
                return 0

            lax.fori_loop(0, glen // tile, one_tile, 0)
            dqs[m, :, at] = (dqt[...] * SCALE).T.astype(BF)
            return 0

        lax.fori_loop(0, HEADS // 2, one_pair, 0)
        own_out[m] = dr1_ref[m] + nt(dqs[m], square(w_ref, table, "wq"))

        def spread(t, _):
            span = pl.ds(pl.multiple_of(t * tile, tile), tile)
            part_out[m, span, :] = (
                nt(dks[m, span, :], square(w_ref, table, "wk"))
                + nt(dvs[m, span, :], square(w_ref, table, "wv"))
            ).astype(BF)
            return 0

        lax.fori_loop(0, glen // tile, spread, 0)
        return 0

    lax.fori_loop(0, MICRO, one_micro, 0)
    x_own = jnp.concatenate([x_ref[m, pl.ds(off, rows), :] for m in range(MICRO)], axis=0)
    store_square(g_ref, table, "wq", tn(x_own, dqs[...].reshape(MICRO * rows, D)).astype(BF))
    x_all = x_ref[...].reshape(MICRO * glen, D)
    store_square(g_ref, table, "wk", tn(x_all, dks[...].reshape(MICRO * glen, D)).astype(BF))
    store_square(g_ref, table, "wv", tn(x_all, dvs[...].reshape(MICRO * glen, D)).astype(BF))


def self_backward(x_all, q, k, v, mix, dmix, dr1, lse, seg, prefix, w, rows):
    glen = x_all.shape[1]
    V = pltpu.VMEM
    return pl.pallas_call(
        functools.partial(self_backward_kernel, glen, rows),
        in_specs=[VM] * 9 + [SMEM, VM],
        out_specs=[VM] * 3,
        out_shape=[
            jax.ShapeDtypeStruct((MICRO, rows, D), F32),
            jax.ShapeDtypeStruct((MICRO, glen, D), BF),
            jax.ShapeDtypeStruct(w.shape, BF),
        ],
        scratch_shapes=[
            V((glen, rows), F32), V((2 * HEADS, rows), F32), V((128, rows), F32),
            V((MICRO, rows, D), BF), V((MICRO, glen, D), BF), V((MICRO, glen, D), BF),
            V((8, glen), F32),
        ],
        compiler_params=pltpu.CompilerParams(vmem_limit_bytes=60 * MIB),
        name="self_backward",
    )(x_all, q, k, v, mix, dmix, dr1, lse, seg, prefix, w)


def weight_units(n):
    piece = D // n
    units = []
    for array, start, count in (
        (0, 0, 3 * piece), (1, 0, 5 * piece), (1, 5 * piece, 4 * piece),
        (1, 9 * piece, 4 * piece), (1, 13 * piece, 2 * piece),
    ):
        for half in range(2):
            units.append((array, start, count, half * 256, 256, half))
    return units


def greet(peers):
    barrier = pltpu.get_barrier_semaphore()
    for axis, target, when in peers:
        if when is None:
            pl.semaphore_signal(barrier, inc=1, device_id={axis: target}, device_id_type=MESH_ID)
        else:

            @pl.when(when)
            def _():
                pl.semaphore_signal(barrier, inc=1, device_id={axis: target}, device_id_type=MESH_ID)

    always = sum(1 for peer in peers if peer[2] is None)
    amount = jnp.int32(always)
    for axis, target, when in peers:
        if when is not None:
            amount = amount + when.astype(jnp.int32)
    pl.semaphore_wait(barrier, amount if always < len(peers) else always)


STRIP = 128


def key_span(rank, rows, glen):
    prompt = glen // 3
    least = (glen - prompt) // 8
    most = (glen - prompt) - 3 * least
    first, stop = rank * rows, (rank + 1) * rows + 1
    low = jnp.maximum(first - most, jnp.where(first >= prompt + most, prompt + least, prompt))
    high = jnp.minimum(stop + most, jnp.where(stop <= glen - most, glen - least, glen))
    return low, jnp.where(stop > prompt, high, 0)


class Chain:
    def __init__(self, ref, rows, strips, sems, lane, rank, count, needed):
        self.ref, self.rows, self.lane, self.needed = ref, rows, lane, needed
        self.strips, self.height = strips, rows // strips
        self.send, self.recv = sems
        self.rank, self.count = rank, count

    def copy(self, side, step, j, block, target):
        at = pl.ds(pl.multiple_of(block * self.rows + j * self.height, 16), self.height)
        part = self.ref.at[:, at] if len(self.ref.shape) == 3 else self.ref.at[at]
        return pltpu.make_async_remote_copy(
            src_ref=part, dst_ref=part,
            send_sem=self.send.at[self.lane, side, step, j],
            recv_sem=self.recv.at[self.lane, side, step, j],
            device_id={"seq": target}, device_id_type=MESH_ID,
        )

    def goes(self, side, sender, block, j):
        last = self.count - 1
        if side == 0:
            there = (sender >= 0) & (sender < last) & (block >= 0)
            taker = sender + 1
        else:
            there = (sender <= last) & (sender > 0) & (block <= last)
            taker = sender - 1
        if self.needed is None:
            return there
        return there & self.needed(side, taker, block * self.rows + j * self.height, self.height)

    def outgoing(self, step, j, act):
        r = self.rank
        for side, block, target in ((0, r - step, r + 1), (1, r + step, r - 1)):

            @pl.when(self.goes(side, r, block, j))
            def _():
                act(self.copy(side, step, j, block, target))

    def start(self, step):
        for j in range(self.strips):
            self.outgoing(step, j, lambda c: c.start())

    def arrived(self, step, onward):
        r = self.rank
        for j in range(self.strips):
            for side, block, source in ((0, r - 1 - step, r - 1), (1, r + 1 + step, r + 1)):

                @pl.when(self.goes(side, source, block, j))
                def _():
                    self.copy(side, step, j, block, source).wait_recv()

            if onward:
                self.outgoing(step + 1, j, lambda c: c.start())

    def sent(self, step):
        for j in range(self.strips):
            self.outgoing(step, j, lambda c: c.wait_send())


def front_kernel(n, count, rows, erows, *refs):
    shards = refs[0:11]
    small, tok, enc, cot, seg_ref, prefix_ref = refs[11:17]
    wa, wb, small_all, x_all, e_all, prev, halo_out, q_ref, k_ref, v_ref, mix_ref, lse_out = refs[17:29]
    stage, bias, lse_sc, info, local, fsend, frecv, zsend, zrecv, csend, crecv = refs[29:]
    me, bits = my_place(n)
    rank = lax.axis_index("seq")
    last = count - 1
    glen = count * rows
    prompt = glen // 3
    piece = D // n
    d = bit_count(n)

    here = at_bits(bits, ())
    table_a, _ = qkv_rows(n)
    table_b, _ = rest_rows(n)
    copies = []

    def keep(src, dst):
        copy = pltpu.make_async_copy(src, dst, local.at[len(copies)])
        copy.start()
        copies.append(copy)

    keep(tok, x_all.at[:, pl.ds(pl.multiple_of(rank * rows, 16), rows)])
    keep(enc, e_all.at[:, pl.ds(pl.multiple_of(rank * erows, 16), erows)])
    names = ("wq", "wk", "wv", "wout", "cq", "ck", "cv", "cout", "up", "down", "slot")
    for name, shard in zip(names, shards):
        start, size = (table_a if name in table_a else table_b)[name]
        target = wa.at[here] if name in table_a else stage
        if name == "up":
            for c in range(4):
                keep(shard.at[:, pl.ds(c * D, D)], target.at[pl.ds(start + c * piece, piece)])
        else:
            keep(shard, target.at[pl.ds(start, size)])
    keep(small, small_all.at[here])

    peers = [("fsdp", partner_of(me, bits, b), None) for b in range(d)]
    peers += [("seq", rank - 1, rank > 0), ("seq", rank + 1, rank < last)]
    greet(peers)

    arrays = (wa, wb, small_all)
    units = weight_units(n) + [(2, 0, 8, 0, 128, 0)]
    order_list = orders(n)

    def hop(u, phase, theirs=False):
        array, r0, nr, c0, nc, which = units[u]
        order = order_list[which]
        b = order[phase]
        cut = (pl.ds(r0, nr), pl.ds(c0, nc))
        fixed = {b: 1 - bits[b]} if theirs else {}
        part = arrays[array].at[at_bits(bits, order[:phase], fixed) + cut]
        src = stage.at[cut] if array == 1 and phase == 0 and not theirs else part
        return pltpu.make_async_remote_copy(
            src_ref=src, dst_ref=part, send_sem=fsend.at[u, phase], recv_sem=frecv.at[u, phase],
            device_id={"fsdp": partner_of(me, bits, b)}, device_id_type=MESH_ID,
        )

    def landed(u, phase):
        hop(u, phase, True).wait_recv()

    def onward(some, phase):
        for u in some:
            landed(u, phase - 1)
            hop(u, phase).start()

    def needed(side, taker, start, height):
        low, high = key_span(taker, rows, glen)
        if side == 0:
            return (start < prompt) | (start + height > low)
        return (start < prompt) | (start < high)

    copies[0].wait()
    copies[1].wait()
    sems = (zsend, zrecv)
    strips = rows // STRIP
    toks = [Chain(x_all.at[m], rows, strips, sems, m, rank, count, needed) for m in range(MICRO)]
    encs = Chain(e_all, erows, 1, sems, MICRO, rank, count, None)
    toks[0].start(0)
    encs.start(0)
    halo = pltpu.make_async_remote_copy(
        src_ref=cot.at[:, pl.ds(rows - HALO, HALO)], dst_ref=prev, send_sem=csend, recv_sem=crecv,
        device_id={"seq": rank + 1}, device_id_type=MESH_ID,
    )

    @pl.when(rank < last)
    def _():
        halo.start()

    for strip in range(glen // STRIP):
        start, block = strip * STRIP, strip * STRIP // rows
        side0, side1 = needed(0, rank, start, STRIP), needed(1, rank, start, STRIP)
        unseen = ((block < rank) & jnp.logical_not(side0)) | ((block > rank) & jnp.logical_not(side1))

        @pl.when(unseen)
        def _():
            x_all[:, start : start + STRIP, :] = jnp.zeros((MICRO, STRIP, D), BF)

    for copy in copies[2:]:
        copy.wait()
    everything = list(range(len(units)))
    for u in everything:
        hop(u, 0).start()
    settle = pltpu.make_async_copy(stage, wb.at[here], local.at[len(copies)])
    settle.start()
    first = pltpu.make_async_copy(cot.at[:, pl.ds(rows - HALO, HALO)], prev, local.at[len(copies) + 1])

    @pl.when(rank == 0)
    def _():
        first.start()

    settle.wait()
    onward(everything[:6], 1)
    for s in range(1, count):
        toks[0].arrived(s - 1, s < count - 1)
        if s == 1:
            onward(everything[6:], 1)
            toks[1].start(0) if count == 2 else None
        if s == count - 2:
            toks[1].start(0)
        encs.arrived(s - 1, s < count - 1)
    if d > 2:
        for phase in range(2, d):
            onward(everything[:2], phase)
    landed(0, d - 1)
    landed(1, d - 1)

    off = pl.multiple_of(rank * rows, 128)
    edge = pl.multiple_of(jnp.minimum(rank * rows + rows, glen - 128), 128)
    n_lead = (n, 3 * piece, D)

    def weight(name):
        start, size = table_a[name]
        return wa[(slice(None),) * d + (slice(start, start + size),)].reshape(D, D)

    def project(m):
        def one_tile(tile, _):
            at = pl.ds(pl.multiple_of(tile * 256, 256), 256)
            part = x_all[m, at, :]
            k_ref[m, at, :] = nn(part, weight("wk")).astype(BF)
            v_ref[m, at, :] = nn(part, weight("wv")).astype(BF)
            return 0

        lax.fori_loop(0, glen // 256, one_tile, 0)
        edge_rows = x_all[m, pl.ds(edge, HALO), :]
        halo_out[m] = edge_rows
        q_ref[m, 0:rows, :] = (nn(x_all[m, pl.ds(off, rows), :], weight("wq")).astype(BF) * SCALE).astype(BF)
        q_ref[m, rows : rows + HALO, :] = (nn(edge_rows, weight("wq")).astype(BF) * SCALE).astype(BF)
        place_info(info, seg_ref, prefix_ref, m)
        seg_row = info[1:2, :]
        place = lax.broadcasted_iota(jnp.int32, (1, glen), 1)
        for start, size, span in ((0, rows, pl.ds(off, rows)), (rows, HALO, pl.ds(edge, 128))):
            column = info[:, span].T[0:size]
            limit, seg = column[:, 0:1], column[:, 1:2]
            seen = jnp.where(
                place < prompt, (place.astype(F32) < limit).astype(jnp.int32), (seg_row == seg).astype(jnp.int32)
            )
            bias[start : start + size, :] = jnp.where(seen == 1, 0.0, NEG)

    def pairs(m, low, high):
        def one_pair(pair, _):
            at = lanes_of(pair)
            mix = attend_pair(
                q_ref[m, :, at], k_ref[m, :, at], v_ref[m, :, at], bias[...], pair, lse_sc
            )
            mix_ref[m, :, at] = mix.astype(BF)
            return 0

        lax.fori_loop(low, high, one_pair, 0)
        if high == HEADS // 2:
            lse_out[m] = lse_sc[0:rows, :].T[0:HEADS, :]

    rest = everything[2:]
    project(0)
    pairs(0, 0, 2)
    toks[1].arrived(0, count > 2)
    for phase in range(2, d):
        onward(rest[: len(rest) // 2], phase)
    pairs(0, 2, 4)
    for s in range(2, count):
        toks[1].arrived(s - 1, s < count - 1)
    for phase in range(2, d):
        onward(rest[len(rest) // 2 :], phase)
    project(1)
    pairs(1, 0, 4)

    for u in rest:
        landed(u, d - 1)

    @pl.when(rank > 0)
    def _():
        halo.wait_recv()

    @pl.when(rank == 0)
    def _():
        first.wait()

    @pl.when(rank < last)
    def _():
        halo.wait_send()

    for u in everything:
        for phase in range(d):
            hop(u, phase).wait_send()
    for chain in toks + [encs]:
        for s in range(count - 1):
            chain.sent(s)


def front(n, count, shards, small, tok, enc, cot, seg, prefix):
    rows, erows = tok.shape[1], enc.shape[1]
    glen = count * rows
    ext = rows + HALO
    lead = (2,) * bit_count(n)
    _, ra = qkv_rows(n)
    _, rb = rest_rows(n)
    units = len(weight_units(n)) + 1
    d = bit_count(n)
    hbm = pl.BlockSpec(memory_space=pl.ANY)
    dma = pltpu.SemaphoreType.DMA
    strips = rows // STRIP
    return pl.pallas_call(
        functools.partial(front_kernel, n, count, rows, erows),
        in_specs=[hbm] * 15 + [VM, SMEM],
        out_specs=[VM, hbm] + [VM] * 10,
        out_shape=[
            jax.ShapeDtypeStruct(lead + (ra, D), BF),
            jax.ShapeDtypeStruct(lead + (rb, D), BF),
            jax.ShapeDtypeStruct(lead + (8, 128), F32),
            jax.ShapeDtypeStruct((MICRO, glen, D), BF),
            jax.ShapeDtypeStruct((MICRO, count * erows, D), BF),
            jax.ShapeDtypeStruct((MICRO, HALO, D), BF),
            jax.ShapeDtypeStruct((MICRO, HALO, D), BF),
            jax.ShapeDtypeStruct((MICRO, ext, D), BF),
            jax.ShapeDtypeStruct((MICRO, glen, D), BF),
            jax.ShapeDtypeStruct((MICRO, glen, D), BF),
            jax.ShapeDtypeStruct((MICRO, ext, D), BF),
            jax.ShapeDtypeStruct((MICRO, HEADS, rows), F32),
        ],
        scratch_shapes=[
            pltpu.VMEM((rb, D), BF), pltpu.VMEM((ext, glen), F32), pltpu.VMEM((ext, 128), F32),
            pltpu.VMEM((8, glen), F32),
            dma((20,)), dma((units, d)), dma((units, d)),
            dma((MICRO + 1, 2, count, strips)), dma((MICRO + 1, 2, count, strips)), dma(()), dma(()),
        ],
        compiler_params=pltpu.CompilerParams(
            collective_id=0, has_side_effects=True, vmem_limit_bytes=60 * MIB
        ),
        name="front",
    )(*shards, small, tok, enc, cot, seg, prefix)


def reduce_kernel(n, count, rows, erows, *refs):
    grads = refs[0:3]
    part, genc, own = refs[3:6]
    outs = refs[6:9]
    tok_out, enc_out = refs[9:11]
    rest = list(refs[11:])
    d = bit_count(n)

    def take(k):
        got = rest[:k]
        del rest[:k]
        return got

    accs, zls, zrs, zss, fins = take(3), take(3), take(3), take(3), take(3)
    recvs = [take(d) for _ in range(3)]
    tbuf, ebuf = take(2)
    fsend, frecv, zsend, zrecv, tsend, trecv, esend, erecv = rest
    me, bits = my_place(n)
    rank = lax.axis_index("seq")
    last = count - 1
    peers = [("fsdp", partner_of(me, bits, b), None) for b in range(d)]
    peers += [("seq", lax.rem(rank + k, count), None) for k in range(1, count)]
    greet(peers)

    moves = []
    for k in range(1, count):
        to = lax.rem(rank + k, count)
        for m in range(MICRO):
            moves.append(
                pltpu.make_async_remote_copy(
                    src_ref=part.at[m, pl.ds(pl.multiple_of(to * rows, 16), rows)],
                    dst_ref=tbuf.at[k - 1, m],
                    send_sem=tsend.at[k - 1, m], recv_sem=trecv.at[k - 1, m],
                    device_id={"seq": to}, device_id_type=MESH_ID,
                )
            )
        moves.append(
            pltpu.make_async_remote_copy(
                src_ref=genc.at[:, pl.ds(pl.multiple_of(to * erows, 16), erows)],
                dst_ref=ebuf.at[k - 1],
                send_sem=esend.at[k - 1], recv_sem=erecv.at[k - 1],
                device_id={"seq": to}, device_id_type=MESH_ID,
            )
        )

    units = weight_units(n)
    units = units[2:] + units[:2] + [(2, 0, 8, 0, 128, 0)]
    order_list = [o[::-1] for o in orders(n)]

    def hop(u, phase):
        array, r0, nr, c0, nc, which = units[u]
        order = order_list[which]
        b = order[phase]
        free = [x for x in range(d) if x not in order[: phase + 1]]
        cut = (pl.ds(r0, nr), pl.ds(c0, nc))
        index = at_bits(bits, free, {b: 1 - bits[b]})
        src = grads[array].at[index + cut] if phase == 0 else accs[array].at[index[:-1] + cut]
        dst = recvs[array][phase].at[(slice(None),) * len(free) + cut]
        return pltpu.make_async_remote_copy(
            src_ref=src, dst_ref=dst, send_sem=fsend.at[u, phase], recv_sem=frecv.at[u, phase],
            device_id={"fsdp": partner_of(me, bits, b)}, device_id_type=MESH_ID,
        )

    def add(u, phase):
        array, r0, nr, c0, nc, which = units[u]
        order = order_list[which]
        free = [x for x in range(d) if x not in order[: phase + 1]]
        cut = (slice(r0, r0 + nr), slice(c0, c0 + nc))
        index = at_bits(bits, free)
        base = grads[array][index + cut] if phase == 0 else accs[array][index[:-1] + cut]
        more = recvs[array][phase][(slice(None),) * len(free) + cut]
        accs[array][index[:-1] + cut] = (base.astype(F32) + more.astype(F32)).astype(base.dtype)

    here = at_bits(bits, ())[:-1]

    def root_of(which):
        return (count - 1) // 2 if which == 0 else count // 2

    def z_copy(u, kind, src, dst, target):
        return pltpu.make_async_remote_copy(
            src_ref=src, dst_ref=dst, send_sem=zsend.at[u, kind], recv_sem=zrecv.at[u, kind],
            device_id={"seq": target}, device_id_type=MESH_ID,
        )

    def z_refs(u):
        array, r0, nr, c0, nc, which = units[u]
        cut = (pl.ds(r0, nr), pl.ds(c0, nc))
        return [x[array].at[cut] for x in (zss, zls, zrs, fins)], root_of(which)

    def z_in(u):
        array, r0, nr, c0, nc, which = units[u]
        cut = (slice(r0, r0 + nr), slice(c0, c0 + nc))
        (zs, zl, zr, fin), root = z_refs(u)
        zss[array][cut] = accs[array][here + cut]

        @pl.when((rank > 0) & (rank <= root))
        def _():
            z_copy(u, 0, zs, zl, rank - 1).wait_recv()
            zss[array][cut] = (
                zss[array][cut].astype(F32) + zls[array][cut].astype(F32)
            ).astype(zss[array].dtype)

        @pl.when((rank < last) & (rank >= root))
        def _():
            z_copy(u, 1, zs, zr, rank + 1).wait_recv()
            zss[array][cut] = (
                zss[array][cut].astype(F32) + zrs[array][cut].astype(F32)
            ).astype(zss[array].dtype)

        @pl.when(rank < root)
        def _():
            z_copy(u, 0, zs, zl, rank + 1).start()

        @pl.when(rank > root)
        def _():
            z_copy(u, 1, zs, zr, rank - 1).start()

        @pl.when(rank == root)
        def _():
            fins[array][cut] = zss[array][cut]

        @pl.when((rank == root) & (rank > 0))
        def _():
            z_copy(u, 2, fin, fin, rank - 1).start()

        @pl.when((rank == root) & (rank < last))
        def _():
            z_copy(u, 3, fin, fin, rank + 1).start()

    def z_out(u):
        array, r0, nr, c0, nc, which = units[u]
        (zs, zl, zr, fin), root = z_refs(u)

        @pl.when(rank < root)
        def _():
            z_copy(u, 2, fin, fin, rank + 1).wait_recv()

        @pl.when((rank < root) & (rank > 0))
        def _():
            z_copy(u, 2, fin, fin, rank - 1).start()

        @pl.when(rank > root)
        def _():
            z_copy(u, 3, fin, fin, rank - 1).wait_recv()

        @pl.when((rank > root) & (rank < last))
        def _():
            z_copy(u, 3, fin, fin, rank + 1).start()

        cut = (slice(r0, r0 + nr), slice(c0, c0 + nc))
        outs[array][cut] = fins[array][cut].astype(F32)

    def z_sent(u):
        (zs, zl, zr, fin), root = z_refs(u)

        @pl.when(rank < root)
        def _():
            z_copy(u, 0, zs, zl, rank + 1).wait_send()

        @pl.when(rank > root)
        def _():
            z_copy(u, 1, zs, zr, rank - 1).wait_send()

        @pl.when((rank <= root) & (rank > 0))
        def _():
            z_copy(u, 2, fin, fin, rank - 1).wait_send()

        @pl.when((rank >= root) & (rank < last))
        def _():
            z_copy(u, 3, fin, fin, rank + 1).wait_send()

    for u in range(len(units)):
        hop(u, 0).start()
    for move in moves:
        move.start()
    lag = 4
    for t in range(len(units) + d + lag + 1):
        for stage in range(d + 2):
            u = t - stage - (lag if stage == d + 1 else 0)
            if not 0 <= u < len(units):
                continue
            if stage < d:
                hop(u, stage).wait_recv()
                add(u, stage)
                if stage + 1 < d:
                    hop(u, stage + 1).start()
            elif stage == d:
                z_in(u)
            else:
                z_out(u)
    for move in moves:
        move.wait_recv()
    mine = pl.ds(pl.multiple_of(rank * rows, 16), rows)
    emine = pl.ds(pl.multiple_of(rank * erows, 16), erows)
    for m in range(MICRO):
        total = own[m] + part[m, mine, :].astype(F32)
        states = genc[m, emine, :].astype(F32)
        for k in range(1, count):
            total = total + tbuf[k - 1, m].astype(F32)
            states = states + ebuf[k - 1, m].astype(F32)
        tok_out[m] = total
        enc_out[m] = states
    for move in moves:
        move.wait_send()
    for u in range(len(units)):
        for phase in range(d):
            hop(u, phase).wait_send()
        z_sent(u)


def reduce_out(n, count, ga, gb, gs, part, genc, own):
    rows = own.shape[1]
    erows = genc.shape[1] // count
    d = bit_count(n)
    units = len(weight_units(n)) + 1
    dma = pltpu.SemaphoreType.DMA
    V = pltpu.VMEM
    grads = (ga, gb, gs)
    flat = [(g.shape[-2], g.shape[-1]) for g in grads]
    types = [g.dtype for g in grads]
    scratch = [V((2,) * (d - 1) + f, t) for f, t in zip(flat, types)]
    for _ in range(4):
        scratch += [V(f, t) for f, t in zip(flat, types)]
    for f, t in zip(flat, types):
        scratch += [V((2,) * (d - 1 - p) + f, t) for p in range(d)]
    scratch += [V((count - 1, MICRO, rows, D), BF), V((count - 1, MICRO, erows, D), BF)]
    scratch += [
        dma((units, d)), dma((units, d)), dma((units, 4)), dma((units, 4)),
        dma((count - 1, MICRO)), dma((count - 1, MICRO)), dma((count - 1,)), dma((count - 1,)),
    ]
    return pl.pallas_call(
        functools.partial(reduce_kernel, n, count, rows, erows),
        in_specs=[VM] * 6,
        out_specs=[VM] * 5,
        out_shape=[jax.ShapeDtypeStruct(f, F32) for f in flat]
        + [jax.ShapeDtypeStruct((MICRO, rows, D), F32), jax.ShapeDtypeStruct((MICRO, erows, D), F32)],
        scratch_shapes=scratch,
        compiler_params=pltpu.CompilerParams(
            collective_id=1, has_side_effects=True, vmem_limit_bytes=60 * MIB
        ),
        name="reduce_out",
    )(ga, gb, gs, part, genc, own)


def on_device(
    tokens, encoded, segment_ids, prefix_len, cotangent,
    w_query, w_key, w_value, w_out, c_query, c_key, c_value, c_out,
    w_up, b_up, w_down, b_down,
    gain_one, shift_one, gain_two, shift_two, gain_three, shift_three, w_slot,
):
    n = lax.axis_size("fsdp")
    count = lax.axis_size("seq")
    tokens = tokens[:, 0]
    rows = tokens.shape[1]
    prefix = prefix_len[:, 0]
    cot = cotangent[:, 0]

    shards = (w_query, w_key, w_value, w_out, c_query, c_key, c_value, c_out, w_up, w_down, w_slot)
    edge, side = FF // n, D // n
    small = jnp.concatenate(
        [b_up, b_down, gain_one, shift_one, gain_two, shift_two, gain_three, shift_three]
    ).astype(F32)
    small = jnp.pad(small, (0, 1024 - small.shape[0])).reshape(8, 128)
    (
        wa, wb, small_all, x_all, e_all, previous, edges, q, k, v, mix, lse
    ) = front(n, count, shards, small, tokens, encoded[:, 0], cot, segment_ids, prefix)
    wa = wa.reshape((n,) + wa.shape[-2:])
    wb = wb.reshape((n,) + wb.shape[-2:])
    small_all = small_all.reshape(n, 1024)
    bup = small_all[:, :edge].reshape(1, FF)
    vecs = small_all[:, edge : edge + 7 * side].reshape(n, 7, side).transpose(1, 0, 2).reshape(7, D)
    vecs = jnp.concatenate([vecs, jnp.zeros((1, D), F32)], axis=0)

    slot_out, dmix, dr1, genc, gb, g_bup, g_vec = middle(
        mix, tokens, edges, e_all, cot, previous, segment_ids, prefix, wb, bup, vecs, rows
    )
    own, part, ga = self_backward(
        x_all, q, k, v, mix, dmix, dr1, lse, segment_ids, prefix, wa, rows
    )

    gs = jnp.concatenate(
        [
            g_bup[0:1].reshape(n, edge),
            g_vec[:7].reshape(7, n, side).transpose(1, 0, 2).reshape(n, 7 * side),
            jnp.zeros((n, 1024 - edge - 7 * side), F32),
        ],
        axis=1,
    )
    lead = (2,) * bit_count(n)
    ga = ga.reshape(lead + ga.shape[1:])
    gb = gb.reshape(lead + gb.shape[1:])
    gs = gs.reshape(lead + (8, 128))
    oa, ob, os, grad_tokens, grad_encoded = reduce_out(n, count, ga, gb, gs, part, genc, own)
    table_a, _ = qkv_rows(n)
    table_b, _ = rest_rows(n)
    g = {name: oa[start : start + size] for name, (start, size) in table_a.items()}
    g.update({name: ob[start : start + size] for name, (start, size) in table_b.items()})
    g["up"] = g["up"].reshape(4, side, D).transpose(1, 0, 2).reshape(side, FF)
    line = os.reshape(1024)
    b_up_g = line[:edge]
    b_down_g, g1, s1, g2, s2, g3, s3 = [
        line[edge + i * side : edge + (i + 1) * side] for i in range(7)
    ]
    return (
        slot_out[:, None], grad_tokens[:, None], grad_encoded[:, None],
        g["wq"], g["wk"], g["wv"], g["wout"], g["cq"], g["ck"], g["cv"], g["cout"],
        g["up"], b_up_g, g["down"], b_down_g, g1, s1, g2, s2, g3, s3, g["slot"],
    )


def solution(mesh):
    act = P(None, "fsdp", "seq", None)
    ids = P(None, "fsdp", None)
    mat, one = P("fsdp", None), P("fsdp")
    in_specs = (
        (act, act, ids, ids, act) + (mat,) * 9 + (one, mat) + (one,) * 7 + (mat,)
    )
    out_specs = (act, act, act) + (mat,) * 9 + (one, mat) + (one,) * 7 + (mat,)
    return jax.shard_map(
        on_device, mesh=mesh, in_specs=in_specs, out_specs=out_specs, check_vma=False
    )
```

```python
import functools
import math

import jax
import jax.numpy as jnp
from jax import lax
from jax.experimental import pallas as pl
from jax.experimental.pallas import tpu as pltpu
from jax.sharding import PartitionSpec as P

D = 512
HD = 64
HEADS = 8
FF = 2048
MICRO = 2
HALO = 16
EPSILON = 1e-05
BF = jnp.bfloat16
F32 = jnp.float32
SCALE = 1.0 / math.sqrt(HD)
NEG = -1e30
MIB = 1024 * 1024
GELU_C = math.sqrt(2.0 / math.pi)

VM = pl.BlockSpec(memory_space=pltpu.VMEM)


def nn(a, b):
    return lax.dot_general(a, b, (((1,), (0,)), ((), ())), preferred_element_type=F32)


def nt(a, b):
    return lax.dot_general(a, b, (((1,), (1,)), ((), ())), preferred_element_type=F32)


def tn(a, b):
    return lax.dot_general(a, b, (((0,), (0,)), ((), ())), preferred_element_type=F32)


def lanes_of(pair):
    return pl.ds(pl.multiple_of(pair * 128, 128), 128)


def head_masked(value, head):
    lane = lax.broadcasted_iota(jnp.int32, value.shape, 1)
    return jnp.where((lane >= 64) == (head == 1), value, jnp.zeros_like(value))


def softmax_parts(scores):
    top = jnp.max(scores, axis=-1, keepdims=True)
    raw = jnp.exp(scores - top)
    total = jnp.sum(raw, axis=-1, keepdims=True)
    return raw, top, total


def attend_pair(query_pair, key_pair, value_pair, bias, pair, lse_ref):
    mixed = []
    for head in range(2):
        scores = nt(head_masked(query_pair, head), key_pair)
        if bias is not None:
            scores = scores + bias
        raw, top, total = softmax_parts(scores)
        mixed.append(nn(raw.astype(BF), value_pair) / total)
        lane = lax.broadcasted_iota(jnp.int32, lse_ref.shape, 1)
        lse_ref[...] = jnp.where(lane == pair * 2 + head, top + jnp.log(total), lse_ref[...])
    lane = lax.broadcasted_iota(jnp.int32, mixed[0].shape, 1)
    return jnp.where(lane < 64, mixed[0], mixed[1])


def bit_count(n):
    return n.bit_length() - 1


def qkv_rows(n):
    piece = D // n
    return {"wq": (0, piece), "wk": (piece, piece), "wv": (2 * piece, piece)}, 3 * piece


def rest_rows(n):
    piece = D // n
    table, start = {}, 0
    for name, times in (
        ("wout", 1), ("cq", 1), ("ck", 1), ("cv", 1), ("cout", 1), ("up", 4), ("down", 4), ("slot", 2)
    ):
        table[name] = (start, times * piece)
        start += times * piece
    return table, start


def square(ref, table, name):
    start, count = table[name]
    return ref[:, start : start + count, :].reshape(D, D)


def up_part(ref, table, c):
    start, count = table["up"]
    piece = count // 4
    return ref[:, start + c * piece : start + (c + 1) * piece, :].reshape(D, D)


def row_part(ref, table, name, c):
    start, count = table[name]
    many = D // count
    return ref[c * many : (c + 1) * many, start : start + count, :].reshape(D, D)


def store_square(ref, table, name, value):
    start, count = table[name]
    ref[:, start : start + count, :] = value.reshape(ref.shape[0], count, D)


def store_up(ref, table, c, value):
    start, count = table["up"]
    piece = count // 4
    ref[:, start + c * piece : start + (c + 1) * piece, :] = value.reshape(ref.shape[0], piece, D)


def store_part(ref, table, name, c, value):
    start, count = table[name]
    many = D // count
    ref[c * many : (c + 1) * many, start : start + count, :] = value.reshape(many, count, D)


def my_place(n):
    me = lax.axis_index("fsdp")
    bits = [(me // (1 << b)) % 2 for b in range(bit_count(n))]
    return me, bits


def partner_of(me, bits, b):
    return me + (1 - 2 * bits[b]) * (1 << b)


def orders(n):
    d = bit_count(n)
    far = list(range(1, d))
    return [far + [0], far[::-1] + [0]]


def at_bits(bits, free, fixed=None):
    fixed = fixed or {}
    return tuple(
        slice(None) if b in free else fixed.get(b, bits[b]) for b in range(len(bits) - 1, -1, -1)
    )


MESH_ID = pl.DeviceIdType.MESH

def place_info(info, seg_ref, prefix_ref, m):
    glen = info.shape[1]
    prompt = glen // 3
    seg = jnp.broadcast_to(seg_ref[m], (8, glen))
    limit = jnp.where(seg == 0, prompt, 0)
    for c in range(prefix_ref.shape[1]):
        limit = jnp.where(seg == c + 1, prefix_ref[m, c], limit)
    place = lax.broadcasted_iota(jnp.int32, (8, glen), 1)
    after = (seg == pltpu.roll(seg, glen - 1, 1)) & (place < glen - 1)
    before = (seg == pltpu.roll(seg, 1, 1)) & (place > 0)
    sub = lax.broadcasted_iota(jnp.int32, (8, glen), 0)
    mixed = jnp.where(sub == 0, limit, seg)
    mixed = jnp.where(sub == 2, after.astype(jnp.int32), mixed)
    mixed = jnp.where(sub == 3, before.astype(jnp.int32), mixed)
    info[...] = mixed.astype(F32)


SMEM = pl.BlockSpec(memory_space=pltpu.SMEM)


def norm_forward(residual, gain, shift):
    average = jnp.mean(residual, axis=-1, keepdims=True)
    centred = residual - average
    variance = jnp.mean(centred * centred, axis=-1, keepdims=True)
    rstd = lax.rsqrt(variance + EPSILON)
    hat = centred * rstd
    return hat * gain + shift, hat, rstd


def norm_backward(upstream, hat, rstd, gain):
    d_hat = upstream * gain
    mean_d = jnp.mean(d_hat, axis=-1, keepdims=True)
    mean_dh = jnp.mean(d_hat * hat, axis=-1, keepdims=True)
    d_gain = jnp.sum(upstream * hat, axis=0, keepdims=True)
    d_shift = jnp.sum(upstream, axis=0, keepdims=True)
    return rstd * (d_hat - mean_d - hat * mean_dh), d_gain, d_shift


def gelu_parts(value):
    square = value * value
    t = jnp.tanh(GELU_C * value * (1.0 + 0.044715 * square))
    half = 0.5 * (1.0 + t)
    slope = half + 0.5 * value * (1.0 - t * t) * (GELU_C * (1.0 + 3.0 * 0.044715 * square))
    return value * half, slope


def head_sums(product_rows):
    rows, cols = 16, product_rows.shape[1]
    head = lax.broadcasted_iota(jnp.int32, (rows, cols), 0)
    lane = lax.broadcasted_iota(jnp.int32, (rows, cols), 1)
    pick = ((lane // HD) == head).astype(F32)
    return lax.dot_general(
        pick, product_rows, (((1,), (1,)), ((), ())),
        preferred_element_type=F32, precision=lax.Precision.HIGHEST,
    )[0:HEADS, :]


def middle_kernel(
    rows, enc,
    mix_ref, x_ref, edge_ref, e_ref, cot_ref, prev_ref, seg_ref, prefix_ref,
    w_ref, bup_ref, vec_ref,
    slot_out, dmix_out, dr1_out, genc_out, g_ref, gbup, gvec,
    lowx, lown, cqs, cks, cvs, lse_sc, lse_row, cmix, h1s, hats, rstds, slope,
    act, dpre, dffn, dcross, dcqs, dattn, dcks, dcvs, ckt, h3s, h2low, info, shs,
):
    ext = rows + HALO
    table, _ = rest_rows(w_ref.shape[0])
    gbup[...] = jnp.zeros_like(gbup)
    gvec[...] = jnp.zeros_like(gvec)

    def vec(i):
        return vec_ref[i : i + 1, :]

    def one_micro(m, _):
        own = pl.ds(0, rows)
        attn = nn(mix_ref[m], square(w_ref, table, "wout"))
        x_rows = jnp.concatenate([x_ref[m], edge_ref[m]], axis=0).astype(F32)
        h1, hat, rstd = norm_forward(x_rows + attn, vec(1), vec(2))
        h1s[...] = h1
        dr1_out[m] = hat[0:rows]
        rstds[:, 0:1] = rstd[0:rows]
        h1_low = h1.astype(BF)
        lown[0, m] = h1_low[0:rows]
        cqs[...] = (nn(h1_low, square(w_ref, table, "cq")).astype(BF) * SCALE).astype(BF)
        cks[...] = nn(e_ref[m], square(w_ref, table, "ck")).astype(BF)
        cvs[...] = nn(e_ref[m], square(w_ref, table, "cv")).astype(BF)

        def cross_pair(pair, _):
            at = lanes_of(pair)
            mix = attend_pair(cqs[:, at], cks[:, at], cvs[:, at], None, pair, lse_sc)
            cmix[:, at] = mix.astype(BF)
            return 0

        lax.fori_loop(0, HEADS // 2, cross_pair, 0)
        lse_row[0:HEADS, :] = lse_sc[0:rows, :].T[0:HEADS, :]
        lowx[m] = cmix[0:rows, :]
        h2, hat, rstd = norm_forward(
            h1s[...] + nn(cmix[...], square(w_ref, table, "cout")), vec(3), vec(4)
        )
        h1s[...] = h2
        hats[...] = hat[0:rows]
        rstds[:, 1:2] = rstd[0:rows]
        h2low[...] = h2.astype(BF)
        lown[1, m] = h2low[0:rows, :]
        h3s[...] = jnp.zeros_like(h3s)

        for c in range(FF // D):
            at = slice(c * D, (c + 1) * D)
            pre = nn(h2low[...], up_part(w_ref, table, c)) + bup_ref[0:1, at]
            value, grad = gelu_parts(pre)
            value = value.astype(BF)
            act[m, :, at] = value[0:rows]
            slope[:, at] = grad[0:rows]
            down = row_part(w_ref, table, "down", c)
            h3s[...] += nn(value, down)
        h3, hat, rstd = norm_forward(h1s[...] + h3s[...] + vec(0), vec(5), vec(6))
        h3_low = h3.astype(BF)
        h3s[...] = h3_low.astype(F32)
        lown[2, m] = h3_low[0:rows]
        top = row_part(w_ref, table, "slot", 0)
        bottom = row_part(w_ref, table, "slot", 1)
        place_info(info, seg_ref, prefix_ref, m)
        flags = info[:, pl.ds(pl.multiple_of(lax.axis_index("seq") * rows, 128), rows)].T
        follow = (h3s[pl.ds(1, rows), :] * flags[:, 2:3]).astype(BF)
        slot_out[m] = (nn(h3_low[0:rows], top) + nn(follow, bottom)).astype(BF)
        h3s[0:8, :] = prev_ref[m].astype(F32)[HALO - 8 : HALO]
        h3s[8 : rows + 8, :] = cot_ref[m].astype(F32)
        shifted = h3s[pl.ds(7, rows), :]
        shs[m] = (shifted * flags[:, 3:4]).astype(BF)
        d_follow = nt(shifted.astype(BF), bottom).astype(BF).astype(F32) * flags[:, 3:4]
        d_three = nt(cot_ref[m], top) + d_follow
        d_r3, d_gain, d_shift = norm_backward(d_three, hat[0:rows], rstd[0:rows], vec(5))
        gvec[5:6, :] += d_gain
        gvec[6:7, :] += d_shift
        d_ffn = d_r3.astype(BF)
        dffn[m] = d_ffn
        gvec[0:1, :] += jnp.sum(d_ffn.astype(F32), axis=0, keepdims=True)
        d_two = d_r3
        for c in range(FF // D):
            at = slice(c * D, (c + 1) * D)
            down = row_part(w_ref, table, "down", c)
            grad = (nt(d_ffn, down) * slope[:, at]).astype(BF)
            dpre[m, :, at] = grad
            gbup[0:1, at] += jnp.sum(grad.astype(F32), axis=0, keepdims=True)
            d_two = d_two + nt(grad, up_part(w_ref, table, c))
        d_r2, d_gain, d_shift = norm_backward(d_two, hats[...], rstds[:, 1:2], vec(3))
        gvec[3:4, :] += d_gain
        gvec[4:5, :] += d_shift
        d_cross = d_r2.astype(BF)
        dcross[m] = d_cross
        d_cmix = nt(d_cross, square(w_ref, table, "cout")).astype(BF)
        dmix_out[m] = d_cmix
        delta = head_sums(d_cmix.astype(F32) * cmix[0:rows, :].astype(F32))
        lse_row[HEADS : 2 * HEADS, :] = delta
        ckt[...] = cks[...].T

        def cross_back(pair, _):
            at = lanes_of(pair)
            kp, vp = cks[:, at], cvs[:, at]
            qp, dp = cqs[0:rows, at], dmix_out[m, :, at]
            kt = ckt[at, :]
            d_k = d_v = None
            d_qt = []
            for head in range(2):
                qm, dm = head_masked(qp, head), head_masked(dp, head)
                row = pair * 2 + head
                prob = jnp.exp(nt(kp, qm) - lse_row[pl.ds(row, 1), :])
                d_score = (prob * (nt(vp, dm) - lse_row[pl.ds(HEADS + row, 1), :])).astype(BF)
                dk, dv = nn(d_score, qm), nn(prob.astype(BF), dm)
                d_k = dk if d_k is None else d_k + dk
                d_v = dv if d_v is None else d_v + dv
                d_qt.append(nn(kt, d_score))
            sub = lax.broadcasted_iota(jnp.int32, d_qt[0].shape, 0)
            d_q = jnp.where(sub < 64, d_qt[0], d_qt[1]) * SCALE
            dcqs[m, :, at] = d_q.T.astype(BF)
            dcks[m, :, at] = d_k.astype(BF)
            dcvs[m, :, at] = d_v.astype(BF)
            return 0

        lax.fori_loop(0, HEADS // 2, cross_back, 0)
        genc_out[m] = (
            nt(dcks[m], square(w_ref, table, "ck")) + nt(dcvs[m], square(w_ref, table, "cv"))
        ).astype(BF)
        d_one = d_r2 + nt(dcqs[m], square(w_ref, table, "cq"))
        d_r1, d_gain, d_shift = norm_backward(d_one, dr1_out[m], rstds[:, 0:1], vec(1))
        gvec[1:2, :] += d_gain
        gvec[2:3, :] += d_shift
        dr1_out[m] = d_r1
        d_attn = d_r1.astype(BF)
        dattn[m] = d_attn
        dmix_out[m] = nt(d_attn, square(w_ref, table, "wout")).astype(BF)
        return 0

    lax.fori_loop(0, MICRO, one_micro, 0)

    total = MICRO * rows

    def flat(ref, *lead):
        return ref[lead].reshape(total, D) if lead else ref[...].reshape(total, D)

    def grad_of(left, right):
        return tn(left, right).astype(BF)

    cot = cot_ref[...].reshape(total, D)
    flagged = shs[...].reshape(total, D)
    h3_all = lown[2].reshape(total, D)
    store_part(g_ref, table, "slot", 0, grad_of(h3_all, cot))
    store_part(g_ref, table, "slot", 1, grad_of(h3_all, flagged))
    dffn_all = dffn[...].reshape(total, D)
    h2_all = lown[1].reshape(total, D)
    for c in range(FF // D):
        at = slice(c * D, (c + 1) * D)
        store_part(g_ref, table, "down", c, grad_of(act[:, :, at].reshape(total, D), dffn_all))
        store_up(g_ref, table, c, grad_of(h2_all, dpre[:, :, at].reshape(total, D)))
    store_square(g_ref, table, "cout", grad_of(lowx[...].reshape(total, D), dcross[...].reshape(total, D)))
    store_square(g_ref, table, "cq", grad_of(lown[0].reshape(total, D), dcqs[...].reshape(total, D)))
    e_all = e_ref[...].reshape(MICRO * enc, D)
    store_square(g_ref, table, "ck", grad_of(e_all, dcks[...].reshape(MICRO * enc, D)))
    store_square(g_ref, table, "cv", grad_of(e_all, dcvs[...].reshape(MICRO * enc, D)))
    mix_all = jnp.concatenate([mix_ref[m, 0:rows, :] for m in range(MICRO)], axis=0)
    store_square(g_ref, table, "wout", grad_of(mix_all, dattn[...].reshape(total, D)))


def middle(mix, tokens, edges, e_all, cot, prev, seg, prefix, w, bup, vecs, rows):
    glen = seg.shape[2]
    enc = e_all.shape[1]
    ext = rows + HALO
    out_shape = [
        jax.ShapeDtypeStruct((MICRO, rows, D), BF),
        jax.ShapeDtypeStruct((MICRO, rows, D), BF),
        jax.ShapeDtypeStruct((MICRO, rows, D), F32),
        jax.ShapeDtypeStruct((MICRO, enc, D), BF),
        jax.ShapeDtypeStruct(w.shape, BF),
        jax.ShapeDtypeStruct((8, FF), F32),
        jax.ShapeDtypeStruct((8, D), F32),
    ]
    V = pltpu.VMEM
    scratch = [
        V((MICRO, rows, D), BF),
        V((3, MICRO, rows, D), BF),
        V((ext, D), BF), V((enc, D), BF), V((enc, D), BF),
        V((ext, 128), F32), V((2 * HEADS, rows), F32),
        V((ext, D), BF),
        V((ext, D), F32),
        V((rows, D), F32), V((rows, 128), F32),
        V((rows, FF), F32),
        V((MICRO, rows, FF), BF), V((MICRO, rows, FF), BF),
        V((MICRO, rows, D), BF), V((MICRO, rows, D), BF), V((MICRO, rows, D), BF),
        V((MICRO, rows, D), BF),
        V((MICRO, enc, D), BF), V((MICRO, enc, D), BF),
        V((D, enc), BF),
        V((ext, D), F32), V((ext, D), BF),
        V((8, glen), F32), V((MICRO, rows, D), BF),
    ]
    return pl.pallas_call(
        functools.partial(middle_kernel, rows, enc),
        in_specs=[VM] * 7 + [SMEM] + [VM] * 3,
        out_specs=[VM] * len(out_shape),
        out_shape=out_shape,
        scratch_shapes=scratch,
        compiler_params=pltpu.CompilerParams(vmem_limit_bytes=60 * MIB),
        name="middle",
    )(mix, tokens, edges, e_all, cot, prev, seg, prefix, w, bup, vecs)


def weight_units(n):
    piece = D // n
    units = []
    for array, start, count in (
        (0, 0, 3 * piece), (1, 0, 5 * piece), (1, 5 * piece, 4 * piece),
        (1, 9 * piece, 4 * piece), (1, 13 * piece, 2 * piece),
    ):
        for half in range(2):
            units.append((array, start, count, half * 256, 256, half))
    return units


def greet(peers):
    barrier = pltpu.get_barrier_semaphore()
    for axis, target, when in peers:
        if when is None:
            pl.semaphore_signal(barrier, inc=1, device_id={axis: target}, device_id_type=MESH_ID)
        else:

            @pl.when(when)
            def _():
                pl.semaphore_signal(barrier, inc=1, device_id={axis: target}, device_id_type=MESH_ID)

    always = sum(1 for peer in peers if peer[2] is None)
    amount = jnp.int32(always)
    for axis, target, when in peers:
        if when is not None:
            amount = amount + when.astype(jnp.int32)
    pl.semaphore_wait(barrier, amount if always < len(peers) else always)


STRIP = 128


def key_span(rank, rows, glen):
    prompt = glen // 3
    least = (glen - prompt) // 8
    most = (glen - prompt) - 3 * least
    first, stop = rank * rows, (rank + 1) * rows + 1
    low = jnp.maximum(first - most, jnp.where(first >= prompt + most, prompt + least, prompt))
    high = jnp.minimum(stop + most, jnp.where(stop <= glen - most, glen - least, glen))
    return low, jnp.where(stop > prompt, high, 0)


class Chain:
    def __init__(self, ref, rows, strips, sems, lane, rank, count, needed):
        self.ref, self.rows, self.lane, self.needed = ref, rows, lane, needed
        self.strips, self.height = strips, rows // strips
        self.send, self.recv = sems
        self.rank, self.count = rank, count

    def copy(self, side, step, j, block, target):
        at = pl.ds(pl.multiple_of(block * self.rows + j * self.height, 16), self.height)
        part = self.ref.at[:, at] if len(self.ref.shape) == 3 else self.ref.at[at]
        return pltpu.make_async_remote_copy(
            src_ref=part, dst_ref=part,
            send_sem=self.send.at[self.lane, side, step, j],
            recv_sem=self.recv.at[self.lane, side, step, j],
            device_id={"seq": target}, device_id_type=MESH_ID,
        )

    def goes(self, side, sender, block, j):
        last = self.count - 1
        if side == 0:
            there = (sender >= 0) & (sender < last) & (block >= 0)
            taker = sender + 1
        else:
            there = (sender <= last) & (sender > 0) & (block <= last)
            taker = sender - 1
        if self.needed is None:
            return there
        return there & self.needed(side, taker, block * self.rows + j * self.height, self.height)

    def outgoing(self, step, j, act):
        r = self.rank
        for side, block, target in ((0, r - step, r + 1), (1, r + step, r - 1)):

            @pl.when(self.goes(side, r, block, j))
            def _():
                act(self.copy(side, step, j, block, target))

    def start(self, step):
        for j in range(self.strips):
            self.outgoing(step, j, lambda c: c.start())

    def arrived(self, step, onward):
        r = self.rank
        for j in range(self.strips):
            for side, block, source in ((0, r - 1 - step, r - 1), (1, r + 1 + step, r + 1)):

                @pl.when(self.goes(side, source, block, j))
                def _():
                    self.copy(side, step, j, block, source).wait_recv()

            if onward:
                self.outgoing(step + 1, j, lambda c: c.start())

    def sent(self, step):
        for j in range(self.strips):
            self.outgoing(step, j, lambda c: c.wait_send())


def front_kernel(n, count, rows, erows, *refs):
    shards = refs[0:11]
    small, tok, enc, cot, seg_ref, prefix_ref = refs[11:17]
    wa, wb, small_all, x_all, e_all, prev, halo_out, q_ref, k_ref, v_ref, mix_ref, lse_out = refs[17:29]
    stage, bias, lse_sc, info, local, fsend, frecv, zsend, zrecv, csend, crecv = refs[29:]
    me, bits = my_place(n)
    rank = lax.axis_index("seq")
    last = count - 1
    glen = count * rows
    prompt = glen // 3
    piece = D // n
    d = bit_count(n)

    here = at_bits(bits, ())
    table_a, _ = qkv_rows(n)
    table_b, _ = rest_rows(n)
    copies = []

    def keep(src, dst):
        copy = pltpu.make_async_copy(src, dst, local.at[len(copies)])
        copy.start()
        copies.append(copy)

    keep(tok, x_all.at[:, pl.ds(pl.multiple_of(rank * rows, 16), rows)])
    keep(enc, e_all.at[:, pl.ds(pl.multiple_of(rank * erows, 16), erows)])
    names = ("wq", "wk", "wv", "wout", "cq", "ck", "cv", "cout", "up", "down", "slot")
    for name, shard in zip(names, shards):
        start, size = (table_a if name in table_a else table_b)[name]
        target = wa.at[here] if name in table_a else stage
        if name == "up":
            for c in range(4):
                keep(shard.at[:, pl.ds(c * D, D)], target.at[pl.ds(start + c * piece, piece)])
        else:
            keep(shard, target.at[pl.ds(start, size)])
    keep(small, small_all.at[here])

    peers = [("fsdp", partner_of(me, bits, b), None) for b in range(d)]
    peers += [("seq", rank - 1, rank > 0), ("seq", rank + 1, rank < last)]
    greet(peers)

    arrays = (wa, wb, small_all)
    units = weight_units(n) + [(2, 0, 8, 0, 128, 0)]
    order_list = orders(n)

    def hop(u, phase, theirs=False):
        array, r0, nr, c0, nc, which = units[u]
        order = order_list[which]
        b = order[phase]
        cut = (pl.ds(r0, nr), pl.ds(c0, nc))
        fixed = {b: 1 - bits[b]} if theirs else {}
        part = arrays[array].at[at_bits(bits, order[:phase], fixed) + cut]
        src = stage.at[cut] if array == 1 and phase == 0 and not theirs else part
        return pltpu.make_async_remote_copy(
            src_ref=src, dst_ref=part, send_sem=fsend.at[u, phase], recv_sem=frecv.at[u, phase],
            device_id={"fsdp": partner_of(me, bits, b)}, device_id_type=MESH_ID,
        )

    def landed(u, phase):
        hop(u, phase, True).wait_recv()

    def onward(some, phase):
        for u in some:
            landed(u, phase - 1)
            hop(u, phase).start()

    def needed(side, taker, start, height):
        low, high = key_span(taker, rows, glen)
        if side == 0:
            return (start < prompt) | (start + height > low)
        return (start < prompt) | (start < high)

    copies[0].wait()
    copies[1].wait()
    sems = (zsend, zrecv)
    strips = rows // STRIP
    toks = [Chain(x_all.at[m], rows, strips, sems, m, rank, count, needed) for m in range(MICRO)]
    encs = Chain(e_all, erows, 1, sems, MICRO, rank, count, None)
    toks[0].start(0)
    encs.start(0)
    halo = pltpu.make_async_remote_copy(
        src_ref=cot.at[:, pl.ds(rows - HALO, HALO)], dst_ref=prev, send_sem=csend, recv_sem=crecv,
        device_id={"seq": rank + 1}, device_id_type=MESH_ID,
    )

    @pl.when(rank < last)
    def _():
        halo.start()

    for strip in range(glen // STRIP):
        start, block = strip * STRIP, strip * STRIP // rows
        side0, side1 = needed(0, rank, start, STRIP), needed(1, rank, start, STRIP)
        unseen = ((block < rank) & jnp.logical_not(side0)) | ((block > rank) & jnp.logical_not(side1))

        @pl.when(unseen)
        def _():
            x_all[:, start : start + STRIP, :] = jnp.zeros((MICRO, STRIP, D), BF)

    for copy in copies[2:]:
        copy.wait()
    everything = list(range(len(units)))
    for u in everything:
        hop(u, 0).start()
    settle = pltpu.make_async_copy(stage, wb.at[here], local.at[len(copies)])
    settle.start()
    first = pltpu.make_async_copy(cot.at[:, pl.ds(rows - HALO, HALO)], prev, local.at[len(copies) + 1])

    @pl.when(rank == 0)
    def _():
        first.start()

    settle.wait()
    onward(everything[:6], 1)
    for s in range(1, count):
        toks[0].arrived(s - 1, s < count - 1)
        if s == 1:
            onward(everything[6:], 1)
            toks[1].start(0) if count == 2 else None
        if s == count - 2:
            toks[1].start(0)
        encs.arrived(s - 1, s < count - 1)
    if d > 2:
        for phase in range(2, d):
            onward(everything[:2], phase)
    landed(0, d - 1)
    landed(1, d - 1)

    off = pl.multiple_of(rank * rows, 128)
    edge = pl.multiple_of(jnp.minimum(rank * rows + rows, glen - 128), 128)
    n_lead = (n, 3 * piece, D)

    def weight(name):
        start, size = table_a[name]
        return wa[(slice(None),) * d + (slice(start, start + size),)].reshape(D, D)

    def project(m):
        def one_tile(tile, _):
            at = pl.ds(pl.multiple_of(tile * 256, 256), 256)
            part = x_all[m, at, :]
            k_ref[m, at, :] = nn(part, weight("wk")).astype(BF)
            v_ref[m, at, :] = nn(part, weight("wv")).astype(BF)
            return 0

        lax.fori_loop(0, glen // 256, one_tile, 0)
        edge_rows = x_all[m, pl.ds(edge, HALO), :]
        halo_out[m] = edge_rows
        q_ref[m, 0:rows, :] = (nn(x_all[m, pl.ds(off, rows), :], weight("wq")).astype(BF) * SCALE).astype(BF)
        q_ref[m, rows : rows + HALO, :] = (nn(edge_rows, weight("wq")).astype(BF) * SCALE).astype(BF)
        place_info(info, seg_ref, prefix_ref, m)
        seg_row = info[1:2, :]
        place = lax.broadcasted_iota(jnp.int32, (1, glen), 1)
        for start, size, span in ((0, rows, pl.ds(off, rows)), (rows, HALO, pl.ds(edge, 128))):
            column = info[:, span].T[0:size]
            limit, seg = column[:, 0:1], column[:, 1:2]
            seen = jnp.where(
                place < prompt, (place.astype(F32) < limit).astype(jnp.int32), (seg_row == seg).astype(jnp.int32)
            )
            bias[start : start + size, :] = jnp.where(seen == 1, 0.0, NEG)

    def pairs(m, low, high):
        def one_pair(pair, _):
            at = lanes_of(pair)
            mix = attend_pair(
                q_ref[m, :, at], k_ref[m, :, at], v_ref[m, :, at], bias[...], pair, lse_sc
            )
            mix_ref[m, :, at] = mix.astype(BF)
            return 0

        lax.fori_loop(low, high, one_pair, 0)
        if high == HEADS // 2:
            lse_out[m] = lse_sc[0:rows, :].T[0:HEADS, :]

    rest = everything[2:]
    project(0)
    pairs(0, 0, 2)
    toks[1].arrived(0, count > 2)
    for phase in range(2, d):
        onward(rest[: len(rest) // 2], phase)
    pairs(0, 2, 4)
    for s in range(2, count):
        toks[1].arrived(s - 1, s < count - 1)
    for phase in range(2, d):
        onward(rest[len(rest) // 2 :], phase)
    project(1)
    pairs(1, 0, 4)

    for u in rest:
        landed(u, d - 1)

    @pl.when(rank > 0)
    def _():
        halo.wait_recv()

    @pl.when(rank == 0)
    def _():
        first.wait()

    @pl.when(rank < last)
    def _():
        halo.wait_send()

    for u in everything:
        for phase in range(d):
            hop(u, phase).wait_send()
    for chain in toks + [encs]:
        for s in range(count - 1):
            chain.sent(s)


def front(n, count, shards, small, tok, enc, cot, seg, prefix):
    rows, erows = tok.shape[1], enc.shape[1]
    glen = count * rows
    ext = rows + HALO
    lead = (2,) * bit_count(n)
    _, ra = qkv_rows(n)
    _, rb = rest_rows(n)
    units = len(weight_units(n)) + 1
    d = bit_count(n)
    hbm = pl.BlockSpec(memory_space=pl.ANY)
    dma = pltpu.SemaphoreType.DMA
    strips = rows // STRIP
    return pl.pallas_call(
        functools.partial(front_kernel, n, count, rows, erows),
        in_specs=[hbm] * 15 + [VM, SMEM],
        out_specs=[VM, hbm] + [VM] * 10,
        out_shape=[
            jax.ShapeDtypeStruct(lead + (ra, D), BF),
            jax.ShapeDtypeStruct(lead + (rb, D), BF),
            jax.ShapeDtypeStruct(lead + (8, 128), F32),
            jax.ShapeDtypeStruct((MICRO, glen, D), BF),
            jax.ShapeDtypeStruct((MICRO, count * erows, D), BF),
            jax.ShapeDtypeStruct((MICRO, HALO, D), BF),
            jax.ShapeDtypeStruct((MICRO, HALO, D), BF),
            jax.ShapeDtypeStruct((MICRO, ext, D), BF),
            jax.ShapeDtypeStruct((MICRO, glen, D), BF),
            jax.ShapeDtypeStruct((MICRO, glen, D), BF),
            jax.ShapeDtypeStruct((MICRO, ext, D), BF),
            jax.ShapeDtypeStruct((MICRO, HEADS, rows), F32),
        ],
        scratch_shapes=[
            pltpu.VMEM((rb, D), BF), pltpu.VMEM((ext, glen), F32), pltpu.VMEM((ext, 128), F32),
            pltpu.VMEM((8, glen), F32),
            dma((20,)), dma((units, d)), dma((units, d)),
            dma((MICRO + 1, 2, count, strips)), dma((MICRO + 1, 2, count, strips)), dma(()), dma(()),
        ],
        compiler_params=pltpu.CompilerParams(
            collective_id=0, has_side_effects=True, vmem_limit_bytes=60 * MIB
        ),
        name="front",
    )(*shards, small, tok, enc, cot, seg, prefix)


TILE = 256
GROUPS = 12


def seen_from(side, taker, start, height, rows, glen):
    low, high = key_span(taker, rows, glen)
    if side == 0:
        return (start < glen // 3) | (start + height > low)
    return (start < glen // 3) | (start < high)


def static_wants(side, taker, start, rows, glen):
    prompt = glen // 3
    least = (glen - prompt) // 8
    most = (glen - prompt) - 3 * least
    first, stop = taker * rows, (taker + 1) * rows + 1
    low = max(first - most, prompt + least if first >= prompt + most else prompt)
    high = min(stop + most, glen - least if stop <= glen - most else glen) if stop > prompt else 0
    return start < prompt or (start + STRIP > low if side == 0 else start < high)


def back_kernel(n, count, rows, erows, *refs):
    q_ref, mix_ref, dmix_ref, lse_ref, tok_ref, wa, genc, gs, seg_ref, prefix_ref = refs[0:10]
    x_hbm, k_hbm, v_hbm, dr1_hbm, gb = refs[10:15]
    outs = refs[15:18]
    tok_out, enc_out = refs[18:20]
    rest = list(refs[20:])
    d = bit_count(n)
    glen = count * rows
    prompt = glen // 3
    tiles = glen // TILE

    def take(k):
        got = rest[:k]
        del rest[:k]
        return got

    accs, zls, zrs, zss, fins = take(3), take(3), take(3), take(3), take(3)
    recvs = [take(d) for _ in range(3)]
    ebuf, ga, part, inc, wkv, qst, dst, stats, info, bias, dqt, dkv, gkv, dqs = take(14)
    kbuf, vbuf, xbuf = take(3)
    fsend, frecv, zsend, zrecv, tsend, trecv, esend, erecv, lsem, tsem, dsem = rest
    grads = (ga, gb, gs)
    me, bits = my_place(n)
    rank = lax.axis_index("seq")
    last = count - 1
    off = pl.multiple_of(rank * rows, 128)
    table, _ = qkv_rows(n)

    def weight(name):
        start, size = table[name]
        return wa[:, start : start + size, :].reshape(D, D)

    def tile_copies(i, slot):
        m, at = i // tiles, pl.ds(pl.multiple_of((i % tiles) * TILE, TILE), TILE)
        return [
            pltpu.make_async_copy(hbm.at[m, at], buf.at[slot], tsem.at[slot, j])
            for j, (hbm, buf) in enumerate(((k_hbm, kbuf), (v_hbm, vbuf), (x_hbm, xbuf)))
        ]

    for copy in tile_copies(0, 0):
        copy.start()
    start_out = pltpu.make_async_copy(dr1_hbm, tok_out, dsem)
    start_out.start()

    units = weight_units(n)
    units = units[2:] + [(2, 0, 8, 0, 128, 0)] + units[:2]
    early, late = list(range(len(units) - 2)), [len(units) - 2, len(units) - 1]
    order_list = [o[::-1] for o in orders(n)]

    def own_half(u):
        array, r0, nr, c0, nc, which = units[u]
        cut = (pl.ds(r0, nr), pl.ds(c0, nc))
        index = at_bits(bits, range(1, d))
        return pltpu.make_async_copy(
            gb.at[index + cut], accs[1].at[(slice(None),) * (d - 1) + cut], lsem.at[u]
        )

    big = [u for u in early if units[u][0] == 1]
    for u in big:
        own_half(u).start()

    peers = [("fsdp", partner_of(me, bits, b), None) for b in range(d)]
    peers += [("seq", lax.rem(rank + k, count), None) for k in range(1, count)]
    greet(peers)

    def hop(u, phase):
        array, r0, nr, c0, nc, which = units[u]
        order = order_list[which]
        b = order[phase]
        free = [x for x in range(d) if x not in order[: phase + 1]]
        cut = (pl.ds(r0, nr), pl.ds(c0, nc))
        index = at_bits(bits, free, {b: 1 - bits[b]})
        src = grads[array].at[index + cut] if phase == 0 else accs[array].at[index[:-1] + cut]
        to = recvs[array][phase].at[(slice(None),) * len(free) + cut]
        return pltpu.make_async_remote_copy(
            src_ref=src, dst_ref=to, send_sem=fsend.at[u, phase], recv_sem=frecv.at[u, phase],
            device_id={"fsdp": partner_of(me, bits, b)}, device_id_type=MESH_ID,
        )

    def add(u, phase):
        array, r0, nr, c0, nc, which = units[u]
        order = order_list[which]
        free = [x for x in range(d) if x not in order[: phase + 1]]
        cut = (slice(r0, r0 + nr), slice(c0, c0 + nc))
        index = at_bits(bits, free)
        hop(u, phase).wait_recv()
        if phase == 0 and array == 1:
            own_half(u).wait()
        base = grads[array][index + cut] if phase == 0 and array != 1 else accs[array][index[:-1] + cut]
        more = recvs[array][phase][(slice(None),) * len(free) + cut]
        accs[array][index[:-1] + cut] = (base.astype(F32) + more.astype(F32)).astype(base.dtype)
        if phase + 1 < d:
            hop(u, phase + 1).start()

    here = at_bits(bits, ())[:-1]

    def root_of(which):
        return (count - 1) // 2 if which == 0 else count // 2

    def z_copy(u, kind, src, to, target):
        return pltpu.make_async_remote_copy(
            src_ref=src, dst_ref=to, send_sem=zsend.at[u, kind], recv_sem=zrecv.at[u, kind],
            device_id={"seq": target}, device_id_type=MESH_ID,
        )

    def z_refs(u):
        array, r0, nr, c0, nc, which = units[u]
        cut = (pl.ds(r0, nr), pl.ds(c0, nc))
        return [x[array].at[cut] for x in (zss, zls, zrs, fins)], root_of(which)

    def z_in(u, step):
        array, r0, nr, c0, nc, which = units[u]
        cut = (slice(r0, r0 + nr), slice(c0, c0 + nc))
        (zs, zl, zr, fin), root = z_refs(u)
        turn = max(root, last - root)

        def own():
            return accs[array][here + cut].astype(F32)

        if step < turn:

            @pl.when((rank < root) & (rank == step))
            def _():
                if step == 0:
                    zss[array][cut] = accs[array][here + cut]
                else:
                    z_copy(u, 0, zs, zl, rank - 1).wait_recv()
                    zss[array][cut] = (own() + zls[array][cut].astype(F32)).astype(zss[array].dtype)
                z_copy(u, 0, zs, zl, rank + 1).start()

            @pl.when((rank > root) & (last - rank == step))
            def _():
                if step == 0:
                    zss[array][cut] = accs[array][here + cut]
                else:
                    z_copy(u, 1, zs, zr, rank + 1).wait_recv()
                    zss[array][cut] = (own() + zrs[array][cut].astype(F32)).astype(zss[array].dtype)
                z_copy(u, 1, zs, zr, rank - 1).start()

        if step == turn:

            @pl.when(rank == root)
            def _():
                total = own()
                if root > 0:
                    z_copy(u, 0, zs, zl, rank - 1).wait_recv()
                    total = total + zls[array][cut].astype(F32)
                if root < last:
                    z_copy(u, 1, zs, zr, rank + 1).wait_recv()
                    total = total + zrs[array][cut].astype(F32)
                fins[array][cut] = total.astype(fins[array].dtype)
                if root > 0:
                    z_copy(u, 2, fin, fin, rank - 1).start()
                if root < last:
                    z_copy(u, 3, fin, fin, rank + 1).start()
                outs[array][cut] = fins[array][cut].astype(F32)

    def z_out(u, step):
        array, r0, nr, c0, nc, which = units[u]
        cut = (slice(r0, r0 + nr), slice(c0, c0 + nc))
        (zs, zl, zr, fin), root = z_refs(u)
        far = step + 1

        if root - far >= 0:

            @pl.when(rank == root - far)
            def _():
                z_copy(u, 2, fin, fin, rank + 1).wait_recv()
                if root - far > 0:
                    z_copy(u, 2, fin, fin, rank - 1).start()
                outs[array][cut] = fins[array][cut].astype(F32)

        if root + far <= last:

            @pl.when(rank == root + far)
            def _():
                z_copy(u, 3, fin, fin, rank - 1).wait_recv()
                if root + far < last:
                    z_copy(u, 3, fin, fin, rank + 1).start()
                outs[array][cut] = fins[array][cut].astype(F32)

    def z_sent(u):
        (zs, zl, zr, fin), root = z_refs(u)

        @pl.when(rank < root)
        def _():
            z_copy(u, 0, zs, zl, rank + 1).wait_send()

        @pl.when(rank > root)
        def _():
            z_copy(u, 1, zs, zr, rank - 1).wait_send()

        @pl.when((rank <= root) & (rank > 0))
        def _():
            z_copy(u, 2, fin, fin, rank - 1).wait_send()

        @pl.when((rank >= root) & (rank < last))
        def _():
            z_copy(u, 3, fin, fin, rank + 1).wait_send()

    for u in early:
        hop(u, 0).start()

    moves = []
    for k in range(1, count):
        to = lax.rem(rank + k, count)
        moves.append(
            pltpu.make_async_remote_copy(
                src_ref=genc.at[:, pl.ds(pl.multiple_of(to * erows, 16), erows)],
                dst_ref=ebuf.at[k - 1],
                send_sem=esend.at[k - 1], recv_sem=erecv.at[k - 1],
                device_id={"seq": to}, device_id_type=MESH_ID,
            )
        )
    for move in moves:
        move.start()

    def wants(side, taker, start):
        return seen_from(side, taker, start, STRIP, rows, glen)

    def strip_copy(m, strip, side, target):
        start = strip * STRIP
        if not isinstance(start, int):
            start = pl.multiple_of(start, STRIP)
        return pltpu.make_async_remote_copy(
            src_ref=part.at[m, pl.ds(start, STRIP)],
            dst_ref=inc.at[m, pl.ds(start + side * rows, STRIP)],
            send_sem=tsend.at[m, strip, side], recv_sem=trecv.at[m, strip, side],
            device_id={"seq": target}, device_id_type=MESH_ID,
        )

    def coming(strip, side):
        start = strip * STRIP
        owner = start // rows
        if side == 0:
            return (owner <= rank) & (rank < last) & wants(0, rank + 1, start)
        return (owner >= rank) & (rank > 0) & wants(1, rank - 1, start)

    def going(strip, side):
        start = strip * STRIP
        owner = start // rows
        if side == 0:
            return (owner < rank) & wants(0, rank, start)
        return (owner > rank) & wants(1, rank, start)

    def static_going(strip, side, who):
        start = strip * STRIP
        owner = start // rows
        if side == 0:
            return owner < who <= last and bool(static_wants(0, who, start, rows, glen))
        return owner > who >= 0 and bool(static_wants(1, who, start, rows, glen))

    def pass_on(m, strip, side, who):
        start = strip * STRIP
        at = slice(start, start + STRIP)
        source = who + 1 if side == 0 else who - 1

        @pl.when(rank == who)
        def _():
            if static_going(strip, side, source):
                strip_copy(m, strip, side, source).wait_recv()
                there = slice(start + side * rows, start + side * rows + STRIP)
                part[m, at, :] = (part[m, at, :].astype(F32) + inc[m, there, :].astype(F32)).astype(BF)
            strip_copy(m, strip, side, who - 1 if side == 0 else who + 1).start()

    def finish_rows(m):
        for j in range(rows // STRIP):
            strip = rank * (rows // STRIP) + j
            at = pl.ds(pl.multiple_of(strip * STRIP, STRIP), STRIP)
            mine = slice(j * STRIP, (j + 1) * STRIP)
            tok_out[m, mine, :] += part[m, at, :].astype(F32)
            for side in range(2):

                @pl.when(coming(strip, side))
                def _():
                    strip_copy(m, strip, side, rank).wait_recv()
                    there = pl.ds(pl.multiple_of(strip * STRIP + side * rows, STRIP), STRIP)
                    tok_out[m, mine, :] += inc[m, there, :].astype(F32)

    wkv[:, 0:D] = weight("wk")
    wkv[:, D : 2 * D] = weight("wv")
    gkv[...] = jnp.zeros_like(gkv)

    def begin(m):
        place_info(info, seg_ref, prefix_ref, m)
        dqt[...] = jnp.zeros_like(dqt)
        delta = head_sums(dmix_ref[m].astype(F32) * mix_ref[m, 0:rows, :].astype(F32))
        for pair in range(HEADS // 2):
            at = slice(pair * 128, (pair + 1) * 128)
            for h in range(2):
                row = 2 * pair + h
                span = slice(h * rows, (h + 1) * rows)
                qst[pair, span, :] = head_masked(q_ref[m, 0:rows, at], h)
                dst[pair, span, :] = head_masked(dmix_ref[m, :, at], h)
                stats[pair : pair + 1, span] = lse_ref[m, row : row + 1, :]
                stats[4 + pair : 5 + pair, span] = delta[row : row + 1, :]

    def one_tile(m):
        def body(t, _):
            i = m * tiles + t
            slot = i % 2

            for copy in tile_copies(i, slot):
                copy.wait()

            @pl.when(i + 1 < MICRO * tiles)
            def _():
                for copy in tile_copies(i + 1, 1 - slot):
                    copy.start()

            at_keys = pl.ds(pl.multiple_of(t * TILE, TILE), TILE)
            place = lax.broadcasted_iota(jnp.int32, (TILE, 1), 0) + t * TILE
            key_seg = info[:, at_keys].T[:, 1:2]
            limit = info[0:1, pl.ds(off, rows)]
            seg = info[1:2, pl.ds(off, rows)]
            seen = jnp.where(
                place < prompt, (place.astype(F32) < limit).astype(jnp.int32), (key_seg == seg).astype(jnp.int32)
            )
            mask = jnp.where(seen == 1, 0.0, NEG)
            bias[:, 0:rows] = mask
            bias[:, rows : 2 * rows] = mask

            def one_pair(pair, _):
                at = lanes_of(pair)
                kp, vp = kbuf[slot, :, at], vbuf[slot, :, at]
                prob = jnp.exp(nt(kp, qst[pair]) + bias[...] - stats[pl.ds(pair, 1), :])
                d_score = (prob * (nt(vp, dst[pair]) - stats[pl.ds(4 + pair, 1), :])).astype(BF)
                dkv[:, at] = nn(d_score, qst[pair]).astype(BF)
                dkv[:, pl.ds(pl.multiple_of(D + pair * 128, 128), 128)] = nn(
                    prob.astype(BF), dst[pair]
                ).astype(BF)
                d_q = nn(kp.T, d_score)
                sub = lax.broadcasted_iota(jnp.int32, (128, rows), 0)
                dqt[at, :] += jnp.where(sub < 64, d_q[:, 0:rows], d_q[:, rows : 2 * rows])
                return 0

            lax.fori_loop(0, HEADS // 2, one_pair, 0)
            part[m, at_keys, :] = nt(dkv[...], wkv[...]).astype(BF)
            gkv[...] += tn(xbuf[slot], dkv[...])
            return 0

        return body

    def end(m):
        for pair in range(HEADS // 2):
            at = slice(pair * 128, (pair + 1) * 128)
            dqs[m, :, at] = (dqt[at, :] * SCALE).T.astype(BF)
        if m == 0:
            start_out.wait()
        tok_out[m] += nt(dqs[m], weight("wq"))

    todo = {}

    def later(when, job, *what):
        todo.setdefault(when, []).append(functools.partial(job, *what))

    def plan(some, when, gap):
        for u in some:
            at = when
            for phase in range(d):
                later(at, add, u, phase)
                at += gap[phase]
            root = root_of(units[u][5])
            turn = max(root, last - root)
            for step in range(turn + 1):
                later(at + step, z_in, u, step)
            for step in range(last):
                later(at + turn + 1 + step, z_out, u, step)

    half = (len(big) + 1) // 2
    plan(early[:half], 0, [3] + [2] * (d - 2) + [0])
    plan(early[half:], 1, [4] + [2] * (d - 2) + [0])
    per = MICRO * tiles // GROUPS
    strips = TILE // STRIP
    passes = []
    for i in range(GROUPS):
        m, t0 = i * per // tiles, (i * per) % tiles
        for strip in range(t0 * strips, (t0 + per) * strips):
            for dist in range(count):
                for side in range(2):
                    who = last - dist if side == 0 else dist
                    if static_going(strip, side, who):
                        passes.append((m, strip, side, who))
                        later(i + 2 * (dist if side == 0 else max(dist - 1, 0)), pass_on, m, strip, side, who)
    later(GROUPS - 2, finish_rows, 0)

    for i in range(GROUPS):
        m, t0 = i * per // tiles, (i * per) % tiles
        if t0 == 0:
            begin(m)
        lax.fori_loop(t0, t0 + per, one_tile(m), 0)
        if t0 + per == tiles:
            end(m)
        for job in todo.pop(i, []):
            job()

    def put(name, value):
        start, size = table[name]
        where = (slice(None),) * d + (slice(start, start + size),)
        ga[where] = value.astype(BF).reshape((2,) * d + (size, D))

    put("wk", gkv[:, 0:D])
    put("wv", gkv[:, D : 2 * D])
    put("wq", tn(tok_ref[...].reshape(MICRO * rows, D), dqs[...].reshape(MICRO * rows, D)))
    for u in late:
        hop(u, 0).start()
    plan(late, GROUPS, [1] * (d - 1) + [0])
    for i in sorted(todo):
        for job in todo[i]:
            job()
    finish_rows(1)
    for move in moves:
        move.wait_recv()
    emine = pl.ds(pl.multiple_of(rank * erows, 16), erows)
    for m in range(MICRO):
        states = genc[m, emine, :].astype(F32)
        for k in range(1, count):
            states = states + ebuf[k - 1, m].astype(F32)
        enc_out[m] = states
    for move in moves:
        move.wait_send()
    for m, strip, side, who in passes:

        @pl.when(rank == who)
        def _():
            strip_copy(m, strip, side, who - 1 if side == 0 else who + 1).wait_send()

    for u in range(len(units)):
        for phase in range(d):
            hop(u, phase).wait_send()
        z_sent(u)


def back(n, count, q, mix, dmix, lse, tok, wa, genc, gs, seg, prefix, x_all, k, v, dr1, gb):
    rows = tok.shape[1]
    erows = genc.shape[1] // count
    glen = count * rows
    d = bit_count(n)
    units = len(weight_units(n)) + 1
    dma = pltpu.SemaphoreType.DMA
    V = pltpu.VMEM
    hbm = pl.BlockSpec(memory_space=pl.ANY)
    flat = [(wa.shape[-2], D), (gb.shape[-2], D), (8, 128)]
    types = [BF, BF, F32]
    scratch = [V((2,) * (d - 1) + f, t) for f, t in zip(flat, types)]
    for _ in range(4):
        scratch += [V(f, t) for f, t in zip(flat, types)]
    for f, t in zip(flat, types):
        scratch += [V((2,) * (d - 1 - p) + f, t) for p in range(d)]
    scratch += [
        V((count - 1, MICRO, erows, D), BF),
        V((2,) * d + flat[0], BF),
        V((MICRO, glen, D), BF), V((MICRO, glen + rows, D), BF),
        V((D, 2 * D), BF),
        V((HEADS // 2, 2 * rows, 128), BF), V((HEADS // 2, 2 * rows, 128), BF),
        V((8, 2 * rows), F32), V((8, glen), F32), V((TILE, 2 * rows), F32),
        V((D, rows), F32), V((TILE, 2 * D), BF), V((D, 2 * D), F32),
        V((MICRO, rows, D), BF),
        V((2, TILE, D), BF), V((2, TILE, D), BF), V((2, TILE, D), BF),
    ]
    strips = glen // STRIP
    scratch += [
        dma((units, d)), dma((units, d)), dma((units, 4)), dma((units, 4)),
        dma((MICRO, strips, 2)), dma((MICRO, strips, 2)), dma((count - 1,)), dma((count - 1,)),
        dma((units,)), dma((2, 3)), dma(()),
    ]
    return pl.pallas_call(
        functools.partial(back_kernel, n, count, rows, erows),
        in_specs=[VM] * 9 + [SMEM] + [hbm] * 5,
        out_specs=[VM] * 5,
        out_shape=[jax.ShapeDtypeStruct(f, F32) for f in flat]
        + [jax.ShapeDtypeStruct((MICRO, rows, D), F32), jax.ShapeDtypeStruct((MICRO, erows, D), F32)],
        scratch_shapes=scratch,
        compiler_params=pltpu.CompilerParams(
            collective_id=1, has_side_effects=True, vmem_limit_bytes=60 * MIB
        ),
        name="back",
    )(q, mix, dmix, lse, tok, wa, genc, gs, seg, prefix, x_all, k, v, dr1, gb)


def on_device(
    tokens, encoded, segment_ids, prefix_len, cotangent,
    w_query, w_key, w_value, w_out, c_query, c_key, c_value, c_out,
    w_up, b_up, w_down, b_down,
    gain_one, shift_one, gain_two, shift_two, gain_three, shift_three, w_slot,
):
    n = lax.axis_size("fsdp")
    count = lax.axis_size("seq")
    tokens = tokens[:, 0]
    rows = tokens.shape[1]
    prefix = prefix_len[:, 0]
    cot = cotangent[:, 0]

    shards = (w_query, w_key, w_value, w_out, c_query, c_key, c_value, c_out, w_up, w_down, w_slot)
    edge, side = FF // n, D // n
    small = jnp.concatenate(
        [b_up, b_down, gain_one, shift_one, gain_two, shift_two, gain_three, shift_three]
    ).astype(F32)
    small = jnp.pad(small, (0, 1024 - small.shape[0])).reshape(8, 128)
    (
        wa, wb, small_all, x_all, e_all, previous, edges, q, k, v, mix, lse
    ) = front(n, count, shards, small, tokens, encoded[:, 0], cot, segment_ids, prefix)
    wa = wa.reshape((n,) + wa.shape[-2:])
    wb = wb.reshape((n,) + wb.shape[-2:])
    small_all = small_all.reshape(n, 1024)
    bup = small_all[:, :edge].reshape(1, FF)
    vecs = small_all[:, edge : edge + 7 * side].reshape(n, 7, side).transpose(1, 0, 2).reshape(7, D)
    vecs = jnp.concatenate([vecs, jnp.zeros((1, D), F32)], axis=0)

    slot_out, dmix, dr1, genc, gb, g_bup, g_vec = middle(
        mix, tokens, edges, e_all, cot, previous, segment_ids, prefix, wb, bup, vecs, rows
    )
    gs = jnp.concatenate(
        [
            g_bup[0:1].reshape(n, edge),
            g_vec[:7].reshape(7, n, side).transpose(1, 0, 2).reshape(n, 7 * side),
            jnp.zeros((n, 1024 - edge - 7 * side), F32),
        ],
        axis=1,
    )
    lead = (2,) * bit_count(n)
    gb = gb.reshape(lead + gb.shape[1:])
    gs = gs.reshape(lead + (8, 128))
    oa, ob, os, grad_tokens, grad_encoded = back(
        n, count, q, mix, dmix, lse, tokens, wa, genc, gs, segment_ids, prefix, x_all, k, v, dr1, gb
    )
    table_a, _ = qkv_rows(n)
    table_b, _ = rest_rows(n)
    g = {name: oa[start : start + size] for name, (start, size) in table_a.items()}
    g.update({name: ob[start : start + size] for name, (start, size) in table_b.items()})
    g["up"] = g["up"].reshape(4, side, D).transpose(1, 0, 2).reshape(side, FF)
    line = os.reshape(1024)
    b_up_g = line[:edge]
    b_down_g, g1, s1, g2, s2, g3, s3 = [
        line[edge + i * side : edge + (i + 1) * side] for i in range(7)
    ]
    return (
        slot_out[:, None], grad_tokens[:, None], grad_encoded[:, None],
        g["wq"], g["wk"], g["wv"], g["wout"], g["cq"], g["ck"], g["cv"], g["cout"],
        g["up"], b_up_g, g["down"], b_down_g, g1, s1, g2, s2, g3, s3, g["slot"],
    )


def solution(mesh):
    act = P(None, "fsdp", "seq", None)
    ids = P(None, "fsdp", None)
    mat, one = P("fsdp", None), P("fsdp")
    in_specs = (
        (act, act, ids, ids, act) + (mat,) * 9 + (one, mat) + (one,) * 7 + (mat,)
    )
    out_specs = (act, act, act) + (mat,) * 9 + (one, mat) + (one,) * 7 + (mat,)
    return jax.shard_map(
        on_device, mesh=mesh, in_specs=in_specs, out_specs=out_specs, check_vma=False
    )
```

```python
import functools
import math

import jax
import jax.numpy as jnp
from jax import lax
from jax.experimental import pallas as pl
from jax.experimental.pallas import tpu as pltpu
from jax.sharding import PartitionSpec as P

D = 512
HD = 64
HEADS = 8
FF = 2048
MICRO = 2
HALO = 16
EPSILON = 1e-05
BF = jnp.bfloat16
F32 = jnp.float32
SCALE = 1.0 / math.sqrt(HD)
NEG = -1e30
MIB = 1024 * 1024
GELU_C = math.sqrt(2.0 / math.pi)

VM = pl.BlockSpec(memory_space=pltpu.VMEM)


def nn(a, b):
    return lax.dot_general(a, b, (((1,), (0,)), ((), ())), preferred_element_type=F32)


def nt(a, b):
    return lax.dot_general(a, b, (((1,), (1,)), ((), ())), preferred_element_type=F32)


def tn(a, b):
    return lax.dot_general(a, b, (((0,), (0,)), ((), ())), preferred_element_type=F32)


def lanes_of(pair):
    return pl.ds(pl.multiple_of(pair * 128, 128), 128)


def head_masked(value, head):
    lane = lax.broadcasted_iota(jnp.int32, value.shape, 1)
    return jnp.where((lane >= 64) == (head == 1), value, jnp.zeros_like(value))


def softmax_parts(scores):
    top = jnp.max(scores, axis=-1, keepdims=True)
    raw = jnp.exp(scores - top)
    total = jnp.sum(raw, axis=-1, keepdims=True)
    return raw, top, total


def attend_pair(query_pair, key_pair, value_pair, bias, pair, lse_ref):
    mixed = []
    for head in range(2):
        scores = nt(head_masked(query_pair, head), key_pair)
        if bias is not None:
            scores = scores + bias
        raw, top, total = softmax_parts(scores)
        mixed.append(nn(raw.astype(BF), value_pair) / total)
        lane = lax.broadcasted_iota(jnp.int32, lse_ref.shape, 1)
        lse_ref[...] = jnp.where(lane == pair * 2 + head, top + jnp.log(total), lse_ref[...])
    lane = lax.broadcasted_iota(jnp.int32, mixed[0].shape, 1)
    return jnp.where(lane < 64, mixed[0], mixed[1])


def bit_count(n):
    return n.bit_length() - 1


def qkv_rows(n):
    piece = D // n
    return {"wq": (0, piece), "wk": (piece, piece), "wv": (2 * piece, piece)}, 3 * piece


def rest_rows(n):
    piece = D // n
    table, start = {}, 0
    for name, times in (
        ("wout", 1), ("cq", 1), ("ck", 1), ("cv", 1), ("cout", 1), ("up", 4), ("down", 4), ("slot", 2)
    ):
        table[name] = (start, times * piece)
        start += times * piece
    return table, start


def square(ref, table, name):
    start, count = table[name]
    return ref[:, start : start + count, :].reshape(D, D)


def up_part(ref, table, c):
    start, count = table["up"]
    piece = count // 4
    return ref[:, start + c * piece : start + (c + 1) * piece, :].reshape(D, D)


def row_part(ref, table, name, c):
    start, count = table[name]
    many = D // count
    return ref[c * many : (c + 1) * many, start : start + count, :].reshape(D, D)


def store_square(ref, table, name, value):
    start, count = table[name]
    ref[:, start : start + count, :] = value.reshape(ref.shape[0], count, D)


def store_up(ref, table, c, value):
    start, count = table["up"]
    piece = count // 4
    ref[:, start + c * piece : start + (c + 1) * piece, :] = value.reshape(ref.shape[0], piece, D)


def store_part(ref, table, name, c, value):
    start, count = table[name]
    many = D // count
    ref[c * many : (c + 1) * many, start : start + count, :] = value.reshape(many, count, D)


def my_place(n):
    me = lax.axis_index("fsdp")
    bits = [(me // (1 << b)) % 2 for b in range(bit_count(n))]
    return me, bits


def partner_of(me, bits, b):
    return me + (1 - 2 * bits[b]) * (1 << b)


def orders(n):
    d = bit_count(n)
    far = list(range(1, d))
    return [far + [0], far[::-1] + [0]]


def at_bits(bits, free, fixed=None):
    fixed = fixed or {}
    return tuple(
        slice(None) if b in free else fixed.get(b, bits[b]) for b in range(len(bits) - 1, -1, -1)
    )


MESH_ID = pl.DeviceIdType.MESH

def place_info(info, seg_ref, prefix_ref, m):
    glen = info.shape[1]
    prompt = glen // 3
    seg = jnp.broadcast_to(seg_ref[m], (8, glen))
    limit = jnp.where(seg == 0, prompt, 0)
    for c in range(prefix_ref.shape[1]):
        limit = jnp.where(seg == c + 1, prefix_ref[m, c], limit)
    place = lax.broadcasted_iota(jnp.int32, (8, glen), 1)
    after = (seg == pltpu.roll(seg, glen - 1, 1)) & (place < glen - 1)
    before = (seg == pltpu.roll(seg, 1, 1)) & (place > 0)
    sub = lax.broadcasted_iota(jnp.int32, (8, glen), 0)
    mixed = jnp.where(sub == 0, limit, seg)
    mixed = jnp.where(sub == 2, after.astype(jnp.int32), mixed)
    mixed = jnp.where(sub == 3, before.astype(jnp.int32), mixed)
    info[...] = mixed.astype(F32)


SMEM = pl.BlockSpec(memory_space=pltpu.SMEM)


def spread_rows(tiles, first, count, width, out):
    group = max(1, 128 // width)
    lane = lax.broadcasted_iota(jnp.int32, (count, 128), 1)
    for p in range(tiles.shape[0] // group):
        block = tiles[p * group, first : first + count, :]
        for j in range(1, group):
            piece = pltpu.roll(tiles[p * group + j, first : first + count, :], j * width, 1)
            block = jnp.where(lane >= j * width, piece, block)
        out[0:count, p * 128 : (p + 1) * 128] = block


def gather_rows(values, count, width, tiles, first):
    group = max(1, 128 // width)
    for i in range(tiles.shape[0]):
        p, j = i // group, i % group
        block = values[0:8, p * 128 : (p + 1) * 128]
        if j:
            block = pltpu.roll(block, 128 - j * width, 1)
        tiles[i, first : first + count, :] = block[0:count]


def norm_forward(residual, gain, shift):
    average = jnp.mean(residual, axis=-1, keepdims=True)
    centred = residual - average
    variance = jnp.mean(centred * centred, axis=-1, keepdims=True)
    rstd = lax.rsqrt(variance + EPSILON)
    hat = centred * rstd
    return hat * gain + shift, hat, rstd


def norm_backward(upstream, hat, rstd, gain):
    d_hat = upstream * gain
    mean_d = jnp.mean(d_hat, axis=-1, keepdims=True)
    mean_dh = jnp.mean(d_hat * hat, axis=-1, keepdims=True)
    d_gain = jnp.sum(upstream * hat, axis=0, keepdims=True)
    d_shift = jnp.sum(upstream, axis=0, keepdims=True)
    return rstd * (d_hat - mean_d - hat * mean_dh), d_gain, d_shift


def gelu_parts(value):
    square = value * value
    t = jnp.tanh(GELU_C * value * (1.0 + 0.044715 * square))
    half = 0.5 * (1.0 + t)
    slope = half + 0.5 * value * (1.0 - t * t) * (GELU_C * (1.0 + 3.0 * 0.044715 * square))
    return value * half, slope


def head_sums(product_rows):
    rows, cols = 16, product_rows.shape[1]
    head = lax.broadcasted_iota(jnp.int32, (rows, cols), 0)
    lane = lax.broadcasted_iota(jnp.int32, (rows, cols), 1)
    pick = ((lane // HD) == head).astype(F32)
    return lax.dot_general(
        pick, product_rows, (((1,), (1,)), ((), ())),
        preferred_element_type=F32, precision=lax.Precision.HIGHEST,
    )[0:HEADS, :]


def middle_kernel(
    rows, enc,
    mix_ref, x_ref, edge_ref, e_ref, cot_ref, prev_ref, seg_ref, prefix_ref,
    w_hbm, small_ref,
    slot_out, dmix_out, dr1_out, genc_out, g_out, gs_out,
    w_ref, g_ref, bup_ref, vec_ref, gbup, gvec, wsem, gsem,
    lowx, lown, cqs, cks, cvs, lse_sc, lse_row, cmix, h1s, hats, rstds, slope,
    act, dpre, dffn, dcross, dcqs, dattn, dcks, dcvs, ckt, h3s, h2low, info, shs,
):
    ext = rows + HALO
    n = w_ref.shape[0]
    table, _ = rest_rows(n)
    piece = D // n
    spans = ((0, 5 * piece), (5 * piece, 4 * piece), (9 * piece, 4 * piece), (13 * piece, 2 * piece))

    def part_copy(k, out=False):
        cut = pl.ds(*spans[k])
        if out:
            return pltpu.make_async_copy(g_ref.at[:, cut], g_out.at[:, cut], gsem.at[k])
        return pltpu.make_async_copy(w_hbm.at[:, cut], w_ref.at[:, cut], wsem.at[k])

    for k in range(4):
        part_copy(k).start()
    spread_rows(small_ref, 0, 8, D // n, vec_ref)
    edge = FF // n
    if edge >= 128:
        for i in range(n):
            for r in range(edge // 128):
                lane = i * edge + r * 128
                bup_ref[0:1, lane : lane + 128] = small_ref[i, 8 + r : 9 + r, :]
    else:
        spread_rows(small_ref, 8, 1, edge, bup_ref)
    part_copy(0).wait()
    gbup[...] = jnp.zeros_like(gbup)
    gvec[...] = jnp.zeros_like(gvec)

    def vec(i):
        return vec_ref[i : i + 1, :]

    def one_micro(m, _):
        own = pl.ds(0, rows)
        attn = nn(mix_ref[m], square(w_ref, table, "wout"))
        x_rows = jnp.concatenate([x_ref[m], edge_ref[m]], axis=0).astype(F32)
        h1, hat, rstd = norm_forward(x_rows + attn, vec(1), vec(2))
        h1s[...] = h1
        dr1_out[m] = hat[0:rows]
        rstds[:, 0:1] = rstd[0:rows]
        h1_low = h1.astype(BF)
        lown[0, m] = h1_low[0:rows]
        cqs[...] = (nn(h1_low, square(w_ref, table, "cq")).astype(BF) * SCALE).astype(BF)
        cks[...] = nn(e_ref[m], square(w_ref, table, "ck")).astype(BF)
        cvs[...] = nn(e_ref[m], square(w_ref, table, "cv")).astype(BF)

        def cross_pair(pair, _):
            at = lanes_of(pair)
            mix = attend_pair(cqs[:, at], cks[:, at], cvs[:, at], None, pair, lse_sc)
            cmix[:, at] = mix.astype(BF)
            return 0

        lax.fori_loop(0, HEADS // 2, cross_pair, 0)
        lse_row[0:HEADS, :] = lse_sc[0:rows, :].T[0:HEADS, :]
        lowx[m] = cmix[0:rows, :]
        h2, hat, rstd = norm_forward(
            h1s[...] + nn(cmix[...], square(w_ref, table, "cout")), vec(3), vec(4)
        )
        h1s[...] = h2
        hats[...] = hat[0:rows]
        rstds[:, 1:2] = rstd[0:rows]
        h2low[...] = h2.astype(BF)
        lown[1, m] = h2low[0:rows, :]
        @pl.when(m == 0)
        def _():
            for k in range(1, 4):
                part_copy(k).wait()

        h3s[...] = jnp.zeros_like(h3s)

        for c in range(FF // D):
            at = slice(c * D, (c + 1) * D)
            pre = nn(h2low[...], up_part(w_ref, table, c)) + bup_ref[0:1, at]
            value, grad = gelu_parts(pre)
            value = value.astype(BF)
            act[m, :, at] = value[0:rows]
            slope[:, at] = grad[0:rows]
            down = row_part(w_ref, table, "down", c)
            h3s[...] += nn(value, down)
        h3, hat, rstd = norm_forward(h1s[...] + h3s[...] + vec(0), vec(5), vec(6))
        h3_low = h3.astype(BF)
        h3s[...] = h3_low.astype(F32)
        lown[2, m] = h3_low[0:rows]
        top = row_part(w_ref, table, "slot", 0)
        bottom = row_part(w_ref, table, "slot", 1)
        place_info(info, seg_ref, prefix_ref, m)
        flags = info[:, pl.ds(pl.multiple_of(lax.axis_index("seq") * rows, 128), rows)].T
        follow = (h3s[pl.ds(1, rows), :] * flags[:, 2:3]).astype(BF)
        slot_out[m] = (nn(h3_low[0:rows], top) + nn(follow, bottom)).astype(BF)
        h3s[0:8, :] = prev_ref[m].astype(F32)[HALO - 8 : HALO]
        h3s[8 : rows + 8, :] = cot_ref[m].astype(F32)
        shifted = h3s[pl.ds(7, rows), :]
        shs[m] = (shifted * flags[:, 3:4]).astype(BF)
        d_follow = nt(shifted.astype(BF), bottom).astype(BF).astype(F32) * flags[:, 3:4]
        d_three = nt(cot_ref[m], top) + d_follow
        d_r3, d_gain, d_shift = norm_backward(d_three, hat[0:rows], rstd[0:rows], vec(5))
        gvec[5:6, :] += d_gain
        gvec[6:7, :] += d_shift
        d_ffn = d_r3.astype(BF)
        dffn[m] = d_ffn
        gvec[0:1, :] += jnp.sum(d_ffn.astype(F32), axis=0, keepdims=True)
        d_two = d_r3
        for c in range(FF // D):
            at = slice(c * D, (c + 1) * D)
            down = row_part(w_ref, table, "down", c)
            grad = (nt(d_ffn, down) * slope[:, at]).astype(BF)
            dpre[m, :, at] = grad
            gbup[0:1, at] += jnp.sum(grad.astype(F32), axis=0, keepdims=True)
            d_two = d_two + nt(grad, up_part(w_ref, table, c))
        d_r2, d_gain, d_shift = norm_backward(d_two, hats[...], rstds[:, 1:2], vec(3))
        gvec[3:4, :] += d_gain
        gvec[4:5, :] += d_shift
        d_cross = d_r2.astype(BF)
        dcross[m] = d_cross
        d_cmix = nt(d_cross, square(w_ref, table, "cout")).astype(BF)
        dmix_out[m] = d_cmix
        delta = head_sums(d_cmix.astype(F32) * cmix[0:rows, :].astype(F32))
        lse_row[HEADS : 2 * HEADS, :] = delta
        ckt[...] = cks[...].T

        def cross_back(pair, _):
            at = lanes_of(pair)
            kp, vp = cks[:, at], cvs[:, at]
            qp, dp = cqs[0:rows, at], dmix_out[m, :, at]
            kt = ckt[at, :]
            d_k = d_v = None
            d_qt = []
            for head in range(2):
                qm, dm = head_masked(qp, head), head_masked(dp, head)
                row = pair * 2 + head
                prob = jnp.exp(nt(kp, qm) - lse_row[pl.ds(row, 1), :])
                d_score = (prob * (nt(vp, dm) - lse_row[pl.ds(HEADS + row, 1), :])).astype(BF)
                dk, dv = nn(d_score, qm), nn(prob.astype(BF), dm)
                d_k = dk if d_k is None else d_k + dk
                d_v = dv if d_v is None else d_v + dv
                d_qt.append(nn(kt, d_score))
            sub = lax.broadcasted_iota(jnp.int32, d_qt[0].shape, 0)
            d_q = jnp.where(sub < 64, d_qt[0], d_qt[1]) * SCALE
            dcqs[m, :, at] = d_q.T.astype(BF)
            dcks[m, :, at] = d_k.astype(BF)
            dcvs[m, :, at] = d_v.astype(BF)
            return 0

        lax.fori_loop(0, HEADS // 2, cross_back, 0)
        genc_out[m] = (
            nt(dcks[m], square(w_ref, table, "ck")) + nt(dcvs[m], square(w_ref, table, "cv"))
        ).astype(BF)
        d_one = d_r2 + nt(dcqs[m], square(w_ref, table, "cq"))
        d_r1, d_gain, d_shift = norm_backward(d_one, dr1_out[m], rstds[:, 0:1], vec(1))
        gvec[1:2, :] += d_gain
        gvec[2:3, :] += d_shift
        dr1_out[m] = d_r1
        d_attn = d_r1.astype(BF)
        dattn[m] = d_attn
        dmix_out[m] = nt(d_attn, square(w_ref, table, "wout")).astype(BF)
        return 0

    lax.fori_loop(0, MICRO, one_micro, 0)

    total = MICRO * rows

    def flat(ref, *lead):
        return ref[lead].reshape(total, D) if lead else ref[...].reshape(total, D)

    def grad_of(left, right):
        return tn(left, right).astype(BF)

    cot = cot_ref[...].reshape(total, D)
    flagged = shs[...].reshape(total, D)
    h3_all = lown[2].reshape(total, D)
    store_part(g_ref, table, "slot", 0, grad_of(h3_all, cot))
    store_part(g_ref, table, "slot", 1, grad_of(h3_all, flagged))
    part_copy(3, True).start()
    dffn_all = dffn[...].reshape(total, D)
    h2_all = lown[1].reshape(total, D)
    for c in range(FF // D):
        at = slice(c * D, (c + 1) * D)
        store_part(g_ref, table, "down", c, grad_of(act[:, :, at].reshape(total, D), dffn_all))
        store_up(g_ref, table, c, grad_of(h2_all, dpre[:, :, at].reshape(total, D)))
    part_copy(2, True).start()
    part_copy(1, True).start()
    store_square(g_ref, table, "cout", grad_of(lowx[...].reshape(total, D), dcross[...].reshape(total, D)))
    store_square(g_ref, table, "cq", grad_of(lown[0].reshape(total, D), dcqs[...].reshape(total, D)))
    e_all = e_ref[...].reshape(MICRO * enc, D)
    store_square(g_ref, table, "ck", grad_of(e_all, dcks[...].reshape(MICRO * enc, D)))
    store_square(g_ref, table, "cv", grad_of(e_all, dcvs[...].reshape(MICRO * enc, D)))
    mix_all = jnp.concatenate([mix_ref[m, 0:rows, :] for m in range(MICRO)], axis=0)
    store_square(g_ref, table, "wout", grad_of(mix_all, dattn[...].reshape(total, D)))
    part_copy(0, True).start()
    gs_out[...] = jnp.zeros_like(gs_out)
    gather_rows(gvec, 8, D // n, gs_out, 0)
    if edge >= 128:
        for i in range(n):
            for r in range(edge // 128):
                lane = i * edge + r * 128
                gs_out[i, 8 + r : 9 + r, :] = gbup[0:1, lane : lane + 128]
    else:
        gather_rows(gbup, 1, edge, gs_out, 8)
    for k in range(4):
        part_copy(k, True).wait()


def middle(mix, tokens, edges, e_all, cot, prev, seg, prefix, w, small, rows):
    glen = seg.shape[2]
    enc = e_all.shape[1]
    ext = rows + HALO
    out_shape = [
        jax.ShapeDtypeStruct((MICRO, rows, D), BF),
        jax.ShapeDtypeStruct((MICRO, rows, D), BF),
        jax.ShapeDtypeStruct((MICRO, rows, D), F32),
        jax.ShapeDtypeStruct((MICRO, enc, D), BF),
        jax.ShapeDtypeStruct(w.shape, BF),
        jax.ShapeDtypeStruct(small.shape, F32),
    ]
    V = pltpu.VMEM
    hbm = pl.BlockSpec(memory_space=pl.ANY)
    scratch = [
        V(w.shape, BF), V(w.shape, BF), V((8, FF), F32), V((8, D), F32),
        V((8, FF), F32), V((8, D), F32),
        pltpu.SemaphoreType.DMA((4,)), pltpu.SemaphoreType.DMA((4,)),
        V((MICRO, rows, D), BF),
        V((3, MICRO, rows, D), BF),
        V((ext, D), BF), V((enc, D), BF), V((enc, D), BF),
        V((ext, 128), F32), V((2 * HEADS, rows), F32),
        V((ext, D), BF),
        V((ext, D), F32),
        V((rows, D), F32), V((rows, 128), F32),
        V((rows, FF), F32),
        V((MICRO, rows, FF), BF), V((MICRO, rows, FF), BF),
        V((MICRO, rows, D), BF), V((MICRO, rows, D), BF), V((MICRO, rows, D), BF),
        V((MICRO, rows, D), BF),
        V((MICRO, enc, D), BF), V((MICRO, enc, D), BF),
        V((D, enc), BF),
        V((ext, D), F32), V((ext, D), BF),
        V((8, glen), F32), V((MICRO, rows, D), BF),
    ]
    return pl.pallas_call(
        functools.partial(middle_kernel, rows, enc),
        in_specs=[VM] * 7 + [SMEM, hbm, VM],
        out_specs=[VM] * 4 + [hbm, VM],
        out_shape=out_shape,
        scratch_shapes=scratch,
        compiler_params=pltpu.CompilerParams(vmem_limit_bytes=61 * MIB),
        name="middle",
    )(mix, tokens, edges, e_all, cot, prev, seg, prefix, w, small)


def weight_units(n):
    piece = D // n
    units = []
    for array, start, count in (
        (0, 0, 3 * piece), (1, 0, 5 * piece), (1, 5 * piece, 4 * piece),
        (1, 9 * piece, 4 * piece), (1, 13 * piece, 2 * piece),
    ):
        for half in range(2):
            units.append((array, start, count, half * 256, 256, half))
    return units


def greet(peers):
    barrier = pltpu.get_barrier_semaphore()
    for axis, target, when in peers:
        if when is None:
            pl.semaphore_signal(barrier, inc=1, device_id={axis: target}, device_id_type=MESH_ID)
        else:

            @pl.when(when)
            def _():
                pl.semaphore_signal(barrier, inc=1, device_id={axis: target}, device_id_type=MESH_ID)

    always = sum(1 for peer in peers if peer[2] is None)
    amount = jnp.int32(always)
    for axis, target, when in peers:
        if when is not None:
            amount = amount + when.astype(jnp.int32)
    pl.semaphore_wait(barrier, amount if always < len(peers) else always)


STRIP = 128


def key_span(rank, rows, glen):
    prompt = glen // 3
    least = (glen - prompt) // 8
    most = (glen - prompt) - 3 * least
    first, stop = rank * rows, (rank + 1) * rows + 1
    low = jnp.maximum(first - most, jnp.where(first >= prompt + most, prompt + least, prompt))
    high = jnp.minimum(stop + most, jnp.where(stop <= glen - most, glen - least, glen))
    return low, jnp.where(stop > prompt, high, 0)


class Chain:
    def __init__(self, ref, rows, strips, sems, lane, rank, count, needed):
        self.ref, self.rows, self.lane, self.needed = ref, rows, lane, needed
        self.strips, self.height = strips, rows // strips
        self.send, self.recv = sems
        self.rank, self.count = rank, count

    def copy(self, side, step, j, block, target):
        at = pl.ds(pl.multiple_of(block * self.rows + j * self.height, 16), self.height)
        part = self.ref.at[:, at] if len(self.ref.shape) == 3 else self.ref.at[at]
        return pltpu.make_async_remote_copy(
            src_ref=part, dst_ref=part,
            send_sem=self.send.at[self.lane, side, step, j],
            recv_sem=self.recv.at[self.lane, side, step, j],
            device_id={"seq": target}, device_id_type=MESH_ID,
        )

    def goes(self, side, sender, block, j):
        last = self.count - 1
        if side == 0:
            there = (sender >= 0) & (sender < last) & (block >= 0)
            taker = sender + 1
        else:
            there = (sender <= last) & (sender > 0) & (block <= last)
            taker = sender - 1
        if self.needed is None:
            return there
        return there & self.needed(side, taker, block * self.rows + j * self.height, self.height)

    def outgoing(self, step, j, act):
        r = self.rank
        for side, block, target in ((0, r - step, r + 1), (1, r + step, r - 1)):

            @pl.when(self.goes(side, r, block, j))
            def _():
                act(self.copy(side, step, j, block, target))

    def start(self, step):
        for j in range(self.strips):
            self.outgoing(step, j, lambda c: c.start())

    def arrived(self, step, onward):
        r = self.rank
        for j in range(self.strips):
            for side, block, source in ((0, r - 1 - step, r - 1), (1, r + 1 + step, r + 1)):

                @pl.when(self.goes(side, source, block, j))
                def _():
                    self.copy(side, step, j, block, source).wait_recv()

            if onward:
                self.outgoing(step + 1, j, lambda c: c.start())

    def sent(self, step):
        for j in range(self.strips):
            self.outgoing(step, j, lambda c: c.wait_send())


def front_kernel(n, count, rows, erows, *refs):
    shards = refs[0:11]
    tok, enc, cot, seg_ref, prefix_ref = refs[11:16]
    vectors = refs[16:24]
    (
        wa_out, wb, small_all, x_out, e_all, prev, halo_out, q_out, k_out, v_out, mix_ref, lse_out
    ) = refs[24:36]
    wa, x_all, q_ref, k_ref, v_ref = refs[36:41]
    stage, bias, lse_sc, info, local, fsend, frecv, zsend, zrecv, csend, crecv, osem = refs[41:]
    me, bits = my_place(n)
    rank = lax.axis_index("seq")
    last = count - 1
    glen = count * rows
    prompt = glen // 3
    piece = D // n
    d = bit_count(n)

    here = at_bits(bits, ())
    table_a, _ = qkv_rows(n)
    table_b, _ = rest_rows(n)
    copies = []

    def keep(src, dst):
        copy = pltpu.make_async_copy(src, dst, local.at[len(copies)])
        copy.start()
        copies.append(copy)

    keep(tok, x_all.at[:, pl.ds(pl.multiple_of(rank * rows, 16), rows)])
    keep(enc, e_all.at[:, pl.ds(pl.multiple_of(rank * erows, 16), erows)])
    names = ("wq", "wk", "wv", "wout", "cq", "ck", "cv", "cout", "up", "down", "slot")
    for name, shard in zip(names, shards):
        start, size = (table_a if name in table_a else table_b)[name]
        target = wa.at[here] if name in table_a else stage
        if name == "up":
            for c in range(4):
                keep(shard.at[:, pl.ds(c * D, D)], target.at[pl.ds(start + c * piece, piece)])
        else:
            keep(shard, target.at[pl.ds(start, size)])
    small_all[here] = jnp.zeros((16, 128), F32)
    for r, vector in enumerate(vectors[0:7]):
        small_all[here + (slice(r, r + 1), slice(0, D // n))] = vector[...].astype(F32).reshape(1, D // n)
    edge_rows, edge_width = max(1, FF // n // 128), min(128, FF // n)
    small_all[here + (slice(8, 8 + edge_rows), slice(0, edge_width))] = (
        vectors[7][...].astype(F32).reshape(edge_rows, edge_width)
    )

    peers = [("fsdp", partner_of(me, bits, b), None) for b in range(d)]
    peers += [("seq", rank - 1, rank > 0), ("seq", rank + 1, rank < last)]
    greet(peers)

    arrays = (wa, wb, small_all)
    units = weight_units(n) + [(2, 0, 16, 0, 128, 0)]
    order_list = orders(n)

    def hop(u, phase, theirs=False):
        array, r0, nr, c0, nc, which = units[u]
        order = order_list[which]
        b = order[phase]
        cut = (pl.ds(r0, nr), pl.ds(c0, nc))
        fixed = {b: 1 - bits[b]} if theirs else {}
        part = arrays[array].at[at_bits(bits, order[:phase], fixed) + cut]
        src = stage.at[cut] if array == 1 and phase == 0 and not theirs else part
        return pltpu.make_async_remote_copy(
            src_ref=src, dst_ref=part, send_sem=fsend.at[u, phase], recv_sem=frecv.at[u, phase],
            device_id={"fsdp": partner_of(me, bits, b)}, device_id_type=MESH_ID,
        )

    def landed(u, phase):
        hop(u, phase, True).wait_recv()

    def onward(some, phase):
        for u in some:
            landed(u, phase - 1)
            hop(u, phase).start()

    def needed(side, taker, start, height):
        low, high = key_span(taker, rows, glen)
        if side == 0:
            return (start < prompt) | (start + height > low)
        return (start < prompt) | (start < high)

    copies[0].wait()
    copies[1].wait()
    sems = (zsend, zrecv)
    strips = rows // STRIP
    toks = [Chain(x_all.at[m], rows, strips, sems, m, rank, count, needed) for m in range(MICRO)]
    encs = Chain(e_all, erows, 1, sems, MICRO, rank, count, None)
    toks[0].start(0)
    halo = pltpu.make_async_remote_copy(
        src_ref=cot.at[:, pl.ds(rows - HALO, HALO)], dst_ref=prev, send_sem=csend, recv_sem=crecv,
        device_id={"seq": rank + 1}, device_id_type=MESH_ID,
    )

    @pl.when(rank < last)
    def _():
        halo.start()

    for strip in range(glen // STRIP):
        start, block = strip * STRIP, strip * STRIP // rows
        side0, side1 = needed(0, rank, start, STRIP), needed(1, rank, start, STRIP)
        unseen = ((block < rank) & jnp.logical_not(side0)) | ((block > rank) & jnp.logical_not(side1))

        @pl.when(unseen)
        def _():
            x_all[:, start : start + STRIP, :] = jnp.zeros((MICRO, STRIP, D), BF)

    for copy in copies[2:]:
        copy.wait()
    everything = list(range(len(units)))
    for u in everything:
        hop(u, 0).start()
    settle = pltpu.make_async_copy(stage, wb.at[here], local.at[len(copies)])
    settle.start()
    first = pltpu.make_async_copy(cot.at[:, pl.ds(rows - HALO, HALO)], prev, local.at[len(copies) + 1])

    @pl.when(rank == 0)
    def _():
        first.start()

    settle.wait()
    onward(everything[:6], 1)
    for s in range(1, count):
        toks[0].arrived(s - 1, s < count - 1)
        if s == 1:
            onward(everything[6:], 1)
        if s == count - 2:
            toks[1].start(0)
    if d > 2:
        for phase in range(2, d):
            onward(everything[:2], phase)
    landed(0, d - 1)
    landed(1, d - 1)

    off = pl.multiple_of(rank * rows, 128)
    edge = pl.multiple_of(jnp.minimum(rank * rows + rows, glen - 128), 128)
    n_lead = (n, 3 * piece, D)

    def weight(name):
        start, size = table_a[name]
        return wa[(slice(None),) * d + (slice(start, start + size),)].reshape(D, D)

    def project(m, low, high):
        def one_tile(tile, _):
            at = pl.ds(pl.multiple_of(tile * 256, 256), 256)
            part = x_all[m, at, :]
            k_ref[m, at, :] = nn(part, weight("wk")).astype(BF)
            v_ref[m, at, :] = nn(part, weight("wv")).astype(BF)
            return 0

        lax.fori_loop(low, high, one_tile, 0)

    def query(m):
        edge_rows = x_all[m, pl.ds(edge, HALO), :]
        halo_out[m] = edge_rows
        q_ref[m, 0:rows, :] = (nn(x_all[m, pl.ds(off, rows), :], weight("wq")).astype(BF) * SCALE).astype(BF)
        q_ref[m, rows : rows + HALO, :] = (nn(edge_rows, weight("wq")).astype(BF) * SCALE).astype(BF)
        place_info(info, seg_ref, prefix_ref, m)
        seg_row = info[1:2, :]
        place = lax.broadcasted_iota(jnp.int32, (1, glen), 1)
        for start, size, span in ((0, rows, pl.ds(off, rows)), (rows, HALO, pl.ds(edge, 128))):
            column = info[:, span].T[0:size]
            limit, seg = column[:, 0:1], column[:, 1:2]
            seen = jnp.where(
                place < prompt, (place.astype(F32) < limit).astype(jnp.int32), (seg_row == seg).astype(jnp.int32)
            )
            bias[start : start + size, :] = jnp.where(seen == 1, 0.0, NEG)

    def pairs(m, low, high):
        def one_pair(pair, _):
            at = lanes_of(pair)
            mix = attend_pair(
                q_ref[m, :, at], k_ref[m, :, at], v_ref[m, :, at], bias[...], pair, lse_sc
            )
            mix_ref[m, :, at] = mix.astype(BF)
            return 0

        lax.fori_loop(low, high, one_pair, 0)
        if high == HEADS // 2:
            lse_out[m] = lse_sc[0:rows, :].T[0:HEADS, :]

    stores = []

    def store(src, to):
        copy = pltpu.make_async_copy(src, to, osem.at[len(stores)])
        copy.start()
        stores.append(copy)

    def store_micro(m):
        for src, to in ((x_all, x_out), (k_ref, k_out), (v_ref, v_out), (q_ref, q_out)):
            store(src.at[m], to.at[m])

    rest = everything[2:]
    near = -(-rows // 256)
    project(0, 0, glen // 256)
    query(0)
    store(wa, wa_out)
    store_micro(0)
    pairs(0, 0, 2)
    toks[1].arrived(0, count > 2)
    encs.start(0)
    for phase in range(2, d):
        onward(rest[: len(rest) // 2], phase)
    pairs(0, 2, 4)
    for s in range(1, count - 2):
        toks[1].arrived(s, True)
    encs.arrived(0, count > 2)
    for phase in range(2, d):
        onward(rest[len(rest) // 2 :], phase)
    project(1, near, glen // 256)
    query(1)
    toks[1].arrived(count - 2, False)
    project(1, 0, near)
    store_micro(1)
    pairs(1, 0, 2)
    for s in range(1, count - 1):
        encs.arrived(s, s < count - 2)
    pairs(1, 2, 4)

    for u in rest:
        landed(u, d - 1)

    @pl.when(rank > 0)
    def _():
        halo.wait_recv()

    @pl.when(rank == 0)
    def _():
        first.wait()

    @pl.when(rank < last)
    def _():
        halo.wait_send()

    for u in everything:
        for phase in range(d):
            hop(u, phase).wait_send()
    for chain in toks + [encs]:
        for s in range(count - 1):
            chain.sent(s)
    for copy in stores:
        copy.wait()


def front(n, count, shards, vectors, tok, enc, cot, seg, prefix):
    rows, erows = tok.shape[1], enc.shape[1]
    glen = count * rows
    ext = rows + HALO
    lead = (2,) * bit_count(n)
    _, ra = qkv_rows(n)
    _, rb = rest_rows(n)
    units = len(weight_units(n)) + 1
    d = bit_count(n)
    hbm = pl.BlockSpec(memory_space=pl.ANY)
    dma = pltpu.SemaphoreType.DMA
    strips = rows // STRIP
    return pl.pallas_call(
        functools.partial(front_kernel, n, count, rows, erows),
        in_specs=[hbm] * 14 + [VM, SMEM] + [VM] * 8,
        out_specs=[hbm, hbm, VM, hbm, VM, VM, VM, hbm, hbm, hbm, VM, VM],
        out_shape=[
            jax.ShapeDtypeStruct(lead + (ra, D), BF),
            jax.ShapeDtypeStruct(lead + (rb, D), BF),
            jax.ShapeDtypeStruct(lead + (16, 128), F32),
            jax.ShapeDtypeStruct((MICRO, glen, D), BF),
            jax.ShapeDtypeStruct((MICRO, count * erows, D), BF),
            jax.ShapeDtypeStruct((MICRO, HALO, D), BF),
            jax.ShapeDtypeStruct((MICRO, HALO, D), BF),
            jax.ShapeDtypeStruct((MICRO, ext, D), BF),
            jax.ShapeDtypeStruct((MICRO, glen, D), BF),
            jax.ShapeDtypeStruct((MICRO, glen, D), BF),
            jax.ShapeDtypeStruct((MICRO, ext, D), BF),
            jax.ShapeDtypeStruct((MICRO, HEADS, rows), F32),
        ],
        scratch_shapes=[
            pltpu.VMEM(lead + (ra, D), BF), pltpu.VMEM((MICRO, glen, D), BF),
            pltpu.VMEM((MICRO, ext, D), BF), pltpu.VMEM((MICRO, glen, D), BF),
            pltpu.VMEM((MICRO, glen, D), BF),
            pltpu.VMEM((rb, D), BF), pltpu.VMEM((ext, glen), F32), pltpu.VMEM((ext, 128), F32),
            pltpu.VMEM((8, glen), F32),
            dma((20,)), dma((units, d)), dma((units, d)),
            dma((MICRO + 1, 2, count, strips)), dma((MICRO + 1, 2, count, strips)), dma(()), dma(()), dma((10,)),
        ],
        compiler_params=pltpu.CompilerParams(
            collective_id=0, has_side_effects=True, vmem_limit_bytes=60 * MIB
        ),
        name="front",
    )(*shards, tok, enc, cot, seg, prefix, *vectors)


TILE = 256
GROUPS = 12
SLOTS = ((-2, -1, 1, 4), (-2, 0, 3, 6), (-2, 1, 5, 7), (-2, 3, 6, 8), (-2, 3, 6, 8))


def seen_from(side, taker, start, height, rows, glen):
    low, high = key_span(taker, rows, glen)
    if side == 0:
        return (start < glen // 3) | (start + height > low)
    return (start < glen // 3) | (start < high)


def static_wants(side, taker, start, rows, glen):
    prompt = glen // 3
    least = (glen - prompt) // 8
    most = (glen - prompt) - 3 * least
    first, stop = taker * rows, (taker + 1) * rows + 1
    low = max(first - most, prompt + least if first >= prompt + most else prompt)
    high = min(stop + most, glen - least if stop <= glen - most else glen) if stop > prompt else 0
    return start < prompt or (start + STRIP > low if side == 0 else start < high)


def back_kernel(n, count, rows, erows, *refs):
    q_ref, mix_ref, dmix_ref, lse_ref, tok_ref, wa, genc, gs, seg_ref, prefix_ref = refs[0:10]
    x_hbm, k_hbm, v_hbm, dr1_hbm, gb = refs[10:15]
    outs = refs[15:18]
    tok_out, enc_out = refs[18:20]
    rest = list(refs[20:])
    d = bit_count(n)
    glen = count * rows
    prompt = glen // 3
    tiles = glen // TILE

    def take(k):
        got = rest[:k]
        del rest[:k]
        return got

    accs, zls, zrs, zss, fins = take(3), take(3), take(3), take(3), take(3)
    recvs = [take(d) for _ in range(3)]
    ebuf, ga, part, inc, wkv, qst, dst, stats, info, bias, dqt, dkv, gkv, dqs = take(14)
    kbuf, vbuf, xbuf = take(3)
    fsend, frecv, zsend, zrecv, tsend, trecv, esend, erecv, lsem, tsem, dsem = rest
    grads = (ga, gb, gs)
    me, bits = my_place(n)
    rank = lax.axis_index("seq")
    last = count - 1
    off = pl.multiple_of(rank * rows, 128)
    table, _ = qkv_rows(n)

    def weight(name):
        start, size = table[name]
        return wa[:, start : start + size, :].reshape(D, D)

    def tile_copies(i, slot):
        m, at = i // tiles, pl.ds(pl.multiple_of((i % tiles) * TILE, TILE), TILE)
        return [
            pltpu.make_async_copy(hbm.at[m, at], buf.at[slot], tsem.at[slot, j])
            for j, (hbm, buf) in enumerate(((k_hbm, kbuf), (v_hbm, vbuf), (x_hbm, xbuf)))
        ]

    for copy in tile_copies(0, 0):
        copy.start()
    start_out = pltpu.make_async_copy(dr1_hbm, tok_out, dsem)
    start_out.start()

    piece = D // n
    early_units = weight_units(n)[2:] + [(2, 0, 16, 0, 128, 0)]
    late_units = [(0, c * piece, piece, half * 256, 256, half) for c in (1, 2, 0) for half in range(2)]
    units = early_units + late_units
    early, late = list(range(len(early_units))), list(range(len(early_units), len(units)))
    order_list = [o[::-1] for o in orders(n)]

    def own_half(u):
        array, r0, nr, c0, nc, which = units[u]
        cut = (pl.ds(r0, nr), pl.ds(c0, nc))
        index = at_bits(bits, range(1, d))
        return pltpu.make_async_copy(
            gb.at[index + cut], accs[1].at[(slice(None),) * (d - 1) + cut], lsem.at[u]
        )

    big = [u for u in early if units[u][0] == 1]
    for u in big:
        own_half(u).start()

    peers = [("fsdp", partner_of(me, bits, b), None) for b in range(d)]
    peers += [("seq", lax.rem(rank + k, count), None) for k in range(1, count)]
    greet(peers)

    def hop(u, phase):
        array, r0, nr, c0, nc, which = units[u]
        order = order_list[which]
        b = order[phase]
        free = [x for x in range(d) if x not in order[: phase + 1]]
        cut = (pl.ds(r0, nr), pl.ds(c0, nc))
        index = at_bits(bits, free, {b: 1 - bits[b]})
        src = grads[array].at[index + cut] if phase == 0 else accs[array].at[index[:-1] + cut]
        to = recvs[array][phase].at[(slice(None),) * len(free) + cut]
        return pltpu.make_async_remote_copy(
            src_ref=src, dst_ref=to, send_sem=fsend.at[u, phase], recv_sem=frecv.at[u, phase],
            device_id={"fsdp": partner_of(me, bits, b)}, device_id_type=MESH_ID,
        )

    def add(u, phase):
        array, r0, nr, c0, nc, which = units[u]
        order = order_list[which]
        free = [x for x in range(d) if x not in order[: phase + 1]]
        cut = (slice(r0, r0 + nr), slice(c0, c0 + nc))
        index = at_bits(bits, free)
        hop(u, phase).wait_recv()
        if phase == 0 and array == 1:
            own_half(u).wait()
        base = grads[array][index + cut] if phase == 0 and array != 1 else accs[array][index[:-1] + cut]
        more = recvs[array][phase][(slice(None),) * len(free) + cut]
        accs[array][index[:-1] + cut] = (base.astype(F32) + more.astype(F32)).astype(base.dtype)
        if phase + 1 < d:
            hop(u, phase + 1).start()

    here = at_bits(bits, ())[:-1]

    def root_of(which):
        return (count - 1) // 2 if which == 0 else count // 2

    def z_copy(u, kind, src, to, target):
        return pltpu.make_async_remote_copy(
            src_ref=src, dst_ref=to, send_sem=zsend.at[u, kind], recv_sem=zrecv.at[u, kind],
            device_id={"seq": target}, device_id_type=MESH_ID,
        )

    def z_refs(u):
        array, r0, nr, c0, nc, which = units[u]
        cut = (pl.ds(r0, nr), pl.ds(c0, nc))
        return [x[array].at[cut] for x in (zss, zls, zrs, fins)], root_of(which)

    def z_in(u, step):
        array, r0, nr, c0, nc, which = units[u]
        cut = (slice(r0, r0 + nr), slice(c0, c0 + nc))
        (zs, zl, zr, fin), root = z_refs(u)
        turn = max(root, last - root)

        def own():
            return accs[array][here + cut].astype(F32)

        if step < turn:

            @pl.when((rank < root) & (rank == step))
            def _():
                if step == 0:
                    zss[array][cut] = accs[array][here + cut]
                else:
                    z_copy(u, 0, zs, zl, rank - 1).wait_recv()
                    zss[array][cut] = (own() + zls[array][cut].astype(F32)).astype(zss[array].dtype)
                z_copy(u, 0, zs, zl, rank + 1).start()

            @pl.when((rank > root) & (last - rank == step))
            def _():
                if step == 0:
                    zss[array][cut] = accs[array][here + cut]
                else:
                    z_copy(u, 1, zs, zr, rank + 1).wait_recv()
                    zss[array][cut] = (own() + zrs[array][cut].astype(F32)).astype(zss[array].dtype)
                z_copy(u, 1, zs, zr, rank - 1).start()

        if step == turn:

            @pl.when(rank == root)
            def _():
                total = own()
                if root > 0:
                    z_copy(u, 0, zs, zl, rank - 1).wait_recv()
                    total = total + zls[array][cut].astype(F32)
                if root < last:
                    z_copy(u, 1, zs, zr, rank + 1).wait_recv()
                    total = total + zrs[array][cut].astype(F32)
                fins[array][cut] = total.astype(fins[array].dtype)
                if root > 0:
                    z_copy(u, 2, fin, fin, rank - 1).start()
                if root < last:
                    z_copy(u, 3, fin, fin, rank + 1).start()
                outs[array][cut] = fins[array][cut]

    def z_out(u, step):
        array, r0, nr, c0, nc, which = units[u]
        cut = (slice(r0, r0 + nr), slice(c0, c0 + nc))
        (zs, zl, zr, fin), root = z_refs(u)
        far = step + 1

        if root - far >= 0:

            @pl.when(rank == root - far)
            def _():
                z_copy(u, 2, fin, fin, rank + 1).wait_recv()
                if root - far > 0:
                    z_copy(u, 2, fin, fin, rank - 1).start()
                outs[array][cut] = fins[array][cut]

        if root + far <= last:

            @pl.when(rank == root + far)
            def _():
                z_copy(u, 3, fin, fin, rank - 1).wait_recv()
                if root + far < last:
                    z_copy(u, 3, fin, fin, rank + 1).start()
                outs[array][cut] = fins[array][cut]

    def z_sent(u):
        (zs, zl, zr, fin), root = z_refs(u)

        @pl.when(rank < root)
        def _():
            z_copy(u, 0, zs, zl, rank + 1).wait_send()

        @pl.when(rank > root)
        def _():
            z_copy(u, 1, zs, zr, rank - 1).wait_send()

        @pl.when((rank <= root) & (rank > 0))
        def _():
            z_copy(u, 2, fin, fin, rank - 1).wait_send()

        @pl.when((rank >= root) & (rank < last))
        def _():
            z_copy(u, 3, fin, fin, rank + 1).wait_send()

    moves = []
    for k in range(1, count):
        to = lax.rem(rank + k, count)
        moves.append(
            pltpu.make_async_remote_copy(
                src_ref=genc.at[:, pl.ds(pl.multiple_of(to * erows, 16), erows)],
                dst_ref=ebuf.at[k - 1],
                send_sem=esend.at[k - 1], recv_sem=erecv.at[k - 1],
                device_id={"seq": to}, device_id_type=MESH_ID,
            )
        )
    for move in moves:
        move.start()

    def wants(side, taker, start):
        return seen_from(side, taker, start, STRIP, rows, glen)

    def strip_copy(m, strip, side, target):
        start = strip * STRIP
        if not isinstance(start, int):
            start = pl.multiple_of(start, STRIP)
        return pltpu.make_async_remote_copy(
            src_ref=part.at[m, pl.ds(start, STRIP)],
            dst_ref=inc.at[m, pl.ds(start + side * rows, STRIP)],
            send_sem=tsend.at[m, strip, side], recv_sem=trecv.at[m, strip, side],
            device_id={"seq": target}, device_id_type=MESH_ID,
        )

    def coming(strip, side):
        start = strip * STRIP
        owner = start // rows
        if side == 0:
            return (owner <= rank) & (rank < last) & wants(0, rank + 1, start)
        return (owner >= rank) & (rank > 0) & wants(1, rank - 1, start)

    def going(strip, side):
        start = strip * STRIP
        owner = start // rows
        if side == 0:
            return (owner < rank) & wants(0, rank, start)
        return (owner > rank) & wants(1, rank, start)

    def static_going(strip, side, who):
        start = strip * STRIP
        owner = start // rows
        if side == 0:
            return owner < who <= last and bool(static_wants(0, who, start, rows, glen))
        return owner > who >= 0 and bool(static_wants(1, who, start, rows, glen))

    def pass_on(m, strip, side, who):
        start = strip * STRIP
        at = slice(start, start + STRIP)
        source = who + 1 if side == 0 else who - 1

        @pl.when(rank == who)
        def _():
            if static_going(strip, side, source):
                strip_copy(m, strip, side, source).wait_recv()
                there = slice(start + side * rows, start + side * rows + STRIP)
                part[m, at, :] = (part[m, at, :].astype(F32) + inc[m, there, :].astype(F32)).astype(BF)
            strip_copy(m, strip, side, who - 1 if side == 0 else who + 1).start()

    def finish_rows(m):
        for j in range(rows // STRIP):
            strip = rank * (rows // STRIP) + j
            at = pl.ds(pl.multiple_of(strip * STRIP, STRIP), STRIP)
            mine = slice(j * STRIP, (j + 1) * STRIP)
            tok_out[m, mine, :] += part[m, at, :].astype(F32)
            for side in range(2):

                @pl.when(coming(strip, side))
                def _():
                    strip_copy(m, strip, side, rank).wait_recv()
                    there = pl.ds(pl.multiple_of(strip * STRIP + side * rows, STRIP), STRIP)
                    tok_out[m, mine, :] += inc[m, there, :].astype(F32)

    wkv[:, 0:D] = weight("wk")
    wkv[:, D : 2 * D] = weight("wv")
    gkv[...] = jnp.zeros_like(gkv)

    def begin(m):
        place_info(info, seg_ref, prefix_ref, m)
        dqt[...] = jnp.zeros_like(dqt)
        delta = head_sums(dmix_ref[m].astype(F32) * mix_ref[m, 0:rows, :].astype(F32))
        for pair in range(HEADS // 2):
            at = slice(pair * 128, (pair + 1) * 128)
            for h in range(2):
                row = 2 * pair + h
                span = slice(h * rows, (h + 1) * rows)
                qst[pair, span, :] = head_masked(q_ref[m, 0:rows, at], h)
                dst[pair, span, :] = head_masked(dmix_ref[m, :, at], h)
                stats[pair : pair + 1, span] = lse_ref[m, row : row + 1, :]
                stats[4 + pair : 5 + pair, span] = delta[row : row + 1, :]

    def one_tile(m):
        def body(t, _):
            i = m * tiles + t
            slot = i % 2

            for copy in tile_copies(i, slot):
                copy.wait()

            @pl.when(i + 1 < MICRO * tiles)
            def _():
                for copy in tile_copies(i + 1, 1 - slot):
                    copy.start()

            at_keys = pl.ds(pl.multiple_of(t * TILE, TILE), TILE)
            place = lax.broadcasted_iota(jnp.int32, (TILE, 1), 0) + t * TILE
            key_seg = info[:, at_keys].T[:, 1:2]
            limit = info[0:1, pl.ds(off, rows)]
            seg = info[1:2, pl.ds(off, rows)]
            seen = jnp.where(
                place < prompt, (place.astype(F32) < limit).astype(jnp.int32), (key_seg == seg).astype(jnp.int32)
            )
            mask = jnp.where(seen == 1, 0.0, NEG)
            bias[:, 0:rows] = mask
            bias[:, rows : 2 * rows] = mask

            def one_pair(pair, _):
                at = lanes_of(pair)
                kp, vp = kbuf[slot, :, at], vbuf[slot, :, at]
                prob = jnp.exp(nt(kp, qst[pair]) + bias[...] - stats[pl.ds(pair, 1), :])
                d_score = (prob * (nt(vp, dst[pair]) - stats[pl.ds(4 + pair, 1), :])).astype(BF)
                dkv[:, at] = nn(d_score, qst[pair]).astype(BF)
                dkv[:, pl.ds(pl.multiple_of(D + pair * 128, 128), 128)] = nn(
                    prob.astype(BF), dst[pair]
                ).astype(BF)
                d_q = nn(kp.T, d_score)
                sub = lax.broadcasted_iota(jnp.int32, (128, rows), 0)
                dqt[at, :] += jnp.where(sub < 64, d_q[:, 0:rows], d_q[:, rows : 2 * rows])
                return 0

            lax.fori_loop(0, HEADS // 2, one_pair, 0)
            part[m, at_keys, :] = nt(dkv[...], wkv[...]).astype(BF)
            gkv[...] += tn(xbuf[slot], dkv[...])
            return 0

        return body

    def end(m):
        for pair in range(HEADS // 2):
            at = slice(pair * 128, (pair + 1) * 128)
            dqs[m, :, at] = (dqt[at, :] * SCALE).T.astype(BF)
        if m == 0:
            start_out.wait()
        tok_out[m] += nt(dqs[m], weight("wq"))

    todo = {}

    def later(when, job, *what):
        todo.setdefault(when, []).append(functools.partial(job, *what))

    def plan(some, times):
        for u in some:
            for phase in range(d):
                later(times[min(phase, 2)] + max(phase - 2, 0), add, u, phase)
            at = times[2] + max(d - 3, 0)
            root = root_of(units[u][5])
            turn = max(root, last - root)
            for step in range(turn + 1):
                later(at + step, z_in, u, step)
            for step in range(last):
                later(at + turn + 1 + step, z_out, u, step)

    def begin_sum(some):
        for u in some:
            hop(u, 0).start()

    for c, times in enumerate(SLOTS):
        plan(early[2 * c : 2 * c + 2], times[1:])
        later(times[0], begin_sum, early[2 * c : 2 * c + 2])
    per = MICRO * tiles // GROUPS
    strips = TILE // STRIP
    passes = []
    for i in range(GROUPS):
        m, t0 = i * per // tiles, (i * per) % tiles
        for strip in range(t0 * strips, (t0 + per) * strips):
            for dist in range(count):
                for side in range(2):
                    who = last - dist if side == 0 else dist
                    if static_going(strip, side, who):
                        passes.append((m, strip, side, who))
                        later(i + 2 * (dist if side == 0 else max(dist - 1, 0)), pass_on, m, strip, side, who)
    later(GROUPS - 2, finish_rows, 0)

    for job in todo.pop(-2, []):
        job()
    for i in range(GROUPS):
        m, t0 = i * per // tiles, (i * per) % tiles
        if t0 == 0:
            begin(m)
        if i == 0:
            for job in todo.pop(-1, []):
                job()
        lax.fori_loop(t0, t0 + per, one_tile(m), 0)
        if t0 + per == tiles:
            end(m)
        for job in todo.pop(i, []):
            job()

    def put(name, value):
        start, size = table[name]
        where = (slice(None),) * d + (slice(start, start + size),)
        ga[where] = value.astype(BF).reshape((2,) * d + (size, D))

    put("wk", gkv[:, 0:D])
    begin_sum(late[0:2])
    put("wv", gkv[:, D : 2 * D])
    begin_sum(late[2:4])
    put("wq", tn(tok_ref[...].reshape(MICRO * rows, D), dqs[...].reshape(MICRO * rows, D)))
    begin_sum(late[4:6])
    for c in range(3):
        plan(late[2 * c : 2 * c + 2], (GROUPS + c, GROUPS + c + 1, GROUPS + c + 2))
    for i in sorted(todo):
        for job in todo[i]:
            job()
    finish_rows(1)
    for move in moves:
        move.wait_recv()
    emine = pl.ds(pl.multiple_of(rank * erows, 16), erows)
    for m in range(MICRO):
        states = genc[m, emine, :].astype(F32)
        for k in range(1, count):
            states = states + ebuf[k - 1, m].astype(F32)
        enc_out[m] = states
    for move in moves:
        move.wait_send()
    for m, strip, side, who in passes:

        @pl.when(rank == who)
        def _():
            strip_copy(m, strip, side, who - 1 if side == 0 else who + 1).wait_send()

    for u in range(len(units)):
        for phase in range(d):
            hop(u, phase).wait_send()
        z_sent(u)


def back(n, count, q, mix, dmix, lse, tok, wa, genc, gs, seg, prefix, x_all, k, v, dr1, gb):
    rows = tok.shape[1]
    erows = genc.shape[1] // count
    glen = count * rows
    d = bit_count(n)
    units = len(weight_units(n)) + 5
    dma = pltpu.SemaphoreType.DMA
    V = pltpu.VMEM
    hbm = pl.BlockSpec(memory_space=pl.ANY)
    flat = [(wa.shape[-2], D), (gb.shape[-2], D), (16, 128)]
    types = [BF, BF, F32]
    scratch = [V((2,) * (d - 1) + f, t) for f, t in zip(flat, types)]
    for _ in range(4):
        scratch += [V(f, t) for f, t in zip(flat, types)]
    for f, t in zip(flat, types):
        scratch += [V((2,) * (d - 1 - p) + f, t) for p in range(d)]
    scratch += [
        V((count - 1, MICRO, erows, D), BF),
        V((2,) * d + flat[0], BF),
        V((MICRO, glen, D), BF), V((MICRO, glen + rows, D), BF),
        V((D, 2 * D), BF),
        V((HEADS // 2, 2 * rows, 128), BF), V((HEADS // 2, 2 * rows, 128), BF),
        V((8, 2 * rows), F32), V((8, glen), F32), V((TILE, 2 * rows), F32),
        V((D, rows), F32), V((TILE, 2 * D), BF), V((D, 2 * D), F32),
        V((MICRO, rows, D), BF),
        V((2, TILE, D), BF), V((2, TILE, D), BF), V((2, TILE, D), BF),
    ]
    strips = glen // STRIP
    scratch += [
        dma((units, d)), dma((units, d)), dma((units, 4)), dma((units, 4)),
        dma((MICRO, strips, 2)), dma((MICRO, strips, 2)), dma((count - 1,)), dma((count - 1,)),
        dma((units,)), dma((2, 3)), dma(()),
    ]
    return pl.pallas_call(
        functools.partial(back_kernel, n, count, rows, erows),
        in_specs=[VM] * 9 + [SMEM] + [hbm] * 5,
        out_specs=[VM] * 5,
        out_shape=[jax.ShapeDtypeStruct(f, t) for f, t in zip(flat, types)]
        + [jax.ShapeDtypeStruct((MICRO, rows, D), F32), jax.ShapeDtypeStruct((MICRO, erows, D), F32)],
        scratch_shapes=scratch,
        compiler_params=pltpu.CompilerParams(
            collective_id=1, has_side_effects=True, vmem_limit_bytes=60 * MIB
        ),
        name="back",
    )(q, mix, dmix, lse, tok, wa, genc, gs, seg, prefix, x_all, k, v, dr1, gb)


FIRST = ("wq", "wk", "wv", "wout", "cq", "ck", "cv", "cout", "up")


def finish_kernel(n, *refs):
    oa, ob, os, tok, states = refs[0:5]
    outs = list(refs[5:])
    table_a, _ = qkv_rows(n)
    table_b, _ = rest_rows(n)
    outs[0][...] = tok[...]
    outs[1][...] = states[...]

    def matrix(name, out):
        table, src = (table_a, oa) if name in table_a else (table_b, ob)
        start, size = table[name]
        if name == "up":
            piece = size // 4
            for c in range(4):
                out[:, c * D : (c + 1) * D] = src[start + c * piece : start + (c + 1) * piece, :].astype(F32)
        else:
            out[...] = src[start : start + size, :].astype(F32)

    for name, out in zip(FIRST, outs[2:11]):
        matrix(name, out)
    edge, side = FF // n, D // n
    wide = outs[11]
    wide[...] = os[8 : 8 + max(1, edge // 128), 0 : min(edge, 128)].reshape(edge)
    matrix("down", outs[12])
    for k in range(7):
        outs[13 + k][...] = os[k : k + 1, 0:side].reshape(side)
    matrix("slot", outs[20])


def finish(n, oa, ob, os, tok, states):
    side, edge = D // n, FF // n
    square = (side, D)
    shapes = [tok.shape, states.shape] + [square] * 8 + [(side, FF), (edge,), (edge, D)]
    shapes += [(side,)] * 7 + [(2 * side, D)]
    return pl.pallas_call(
        functools.partial(finish_kernel, n),
        in_specs=[VM] * 5,
        out_specs=[VM] * len(shapes),
        out_shape=[jax.ShapeDtypeStruct(shape, F32) for shape in shapes],
        compiler_params=pltpu.CompilerParams(vmem_limit_bytes=60 * MIB),
        name="finish",
    )(oa, ob, os, tok, states)


def on_device(
    tokens, encoded, segment_ids, prefix_len, cotangent,
    w_query, w_key, w_value, w_out, c_query, c_key, c_value, c_out,
    w_up, b_up, w_down, b_down,
    gain_one, shift_one, gain_two, shift_two, gain_three, shift_three, w_slot,
):
    n = lax.axis_size("fsdp")
    count = lax.axis_size("seq")
    tokens = tokens[:, 0]
    rows = tokens.shape[1]
    prefix = prefix_len[:, 0]
    cot = cotangent[:, 0]

    shards = (w_query, w_key, w_value, w_out, c_query, c_key, c_value, c_out, w_up, w_down, w_slot)
    vectors = (b_down, gain_one, shift_one, gain_two, shift_two, gain_three, shift_three, b_up)
    (
        wa, wb, small_all, x_all, e_all, previous, edges, q, k, v, mix, lse
    ) = front(n, count, shards, vectors, tokens, encoded[:, 0], cot, segment_ids, prefix)
    wa = wa.reshape((n,) + wa.shape[-2:])
    wb = wb.reshape((n,) + wb.shape[-2:])
    small_all = small_all.reshape(n, 16, 128)
    slot_out, dmix, dr1, genc, gb, gs = middle(
        mix, tokens, edges, e_all, cot, previous, segment_ids, prefix, wb, small_all, rows
    )
    lead = (2,) * bit_count(n)
    gb = gb.reshape(lead + gb.shape[1:])
    gs = gs.reshape(lead + (16, 128))
    oa, ob, os, grad_tokens, grad_encoded = back(
        n, count, q, mix, dmix, lse, tokens, wa, genc, gs, segment_ids, prefix, x_all, k, v, dr1, gb
    )
    grad_tokens, grad_encoded, *others = finish(n, oa, ob, os, grad_tokens, grad_encoded)
    return (slot_out[:, None], grad_tokens[:, None], grad_encoded[:, None], *others)


def solution(mesh):
    act = P(None, "fsdp", "seq", None)
    ids = P(None, "fsdp", None)
    mat, one = P("fsdp", None), P("fsdp")
    in_specs = (
        (act, act, ids, ids, act) + (mat,) * 9 + (one, mat) + (one,) * 7 + (mat,)
    )
    out_specs = (act, act, act) + (mat,) * 9 + (one, mat) + (one,) * 7 + (mat,)
    return jax.shard_map(
        on_device, mesh=mesh, in_specs=in_specs, out_specs=out_specs, check_vma=False
    )
```

```python
import functools
import math

import jax
import jax.numpy as jnp
from jax import lax
from jax.experimental import pallas as pl
from jax.experimental.pallas import tpu as pltpu
from jax.sharding import PartitionSpec as P

D = 512
HD = 64
HEADS = 8
FF = 2048
MICRO = 2
HALO = 16
EPSILON = 1e-05
BF = jnp.bfloat16
F32 = jnp.float32
SCALE = 1.0 / math.sqrt(HD)
NEG = -1e30
MIB = 1024 * 1024
GELU_C = math.sqrt(2.0 / math.pi)

VM = pl.BlockSpec(memory_space=pltpu.VMEM)


def nn(a, b):
    return lax.dot_general(a, b, (((1,), (0,)), ((), ())), preferred_element_type=F32)


def nt(a, b):
    return lax.dot_general(a, b, (((1,), (1,)), ((), ())), preferred_element_type=F32)


def tn(a, b):
    return lax.dot_general(a, b, (((0,), (0,)), ((), ())), preferred_element_type=F32)


def lanes_of(pair):
    return pl.ds(pl.multiple_of(pair * 128, 128), 128)


def head_masked(value, head):
    lane = lax.broadcasted_iota(jnp.int32, value.shape, 1)
    return jnp.where((lane >= 64) == (head == 1), value, jnp.zeros_like(value))


def softmax_parts(scores):
    top = jnp.max(scores, axis=-1, keepdims=True)
    raw = jnp.exp(scores - top)
    total = jnp.sum(raw, axis=-1, keepdims=True)
    return raw, top, total


def attend_pair(query_pair, key_pair, value_pair, bias, pair, lse_ref):
    mixed = []
    for head in range(2):
        scores = nt(head_masked(query_pair, head), key_pair)
        if bias is not None:
            scores = scores + bias
        raw, top, total = softmax_parts(scores)
        mixed.append(nn(raw.astype(BF), value_pair) / total)
        lane = lax.broadcasted_iota(jnp.int32, lse_ref.shape, 1)
        lse_ref[...] = jnp.where(lane == pair * 2 + head, top + jnp.log(total), lse_ref[...])
    lane = lax.broadcasted_iota(jnp.int32, mixed[0].shape, 1)
    return jnp.where(lane < 64, mixed[0], mixed[1])


def attend_far(query_pair, key_pair, value_pair, bias, pair, mixed_ref, top_ref, total_ref):
    mixed = []
    lane = lax.broadcasted_iota(jnp.int32, top_ref.shape, 1)
    for head in range(2):
        raw, top, total = softmax_parts(nt(head_masked(query_pair, head), key_pair) + bias)
        mixed.append(nn(raw.astype(BF), value_pair))
        top_ref[...] = jnp.where(lane == pair * 2 + head, top, top_ref[...])
        total_ref[...] = jnp.where(lane == pair * 2 + head, total, total_ref[...])
    mixed_ref[:, lanes_of(pair)] = jnp.where(lane < 64, mixed[0], mixed[1])


def attend_near(
    query_pair, key_pair, value_pair, bias, pair, lse_ref, mixed_ref, top_ref, total_ref
):
    mixed = []
    lane = lax.broadcasted_iota(jnp.int32, lse_ref.shape, 1)
    far = mixed_ref[:, lanes_of(pair)]
    for head in range(2):
        mine = lane == pair * 2 + head
        far_top = jnp.sum(jnp.where(mine, top_ref[...], 0.0), axis=1, keepdims=True)
        far_total = jnp.sum(jnp.where(mine, total_ref[...], 0.0), axis=1, keepdims=True)
        scores = nt(head_masked(query_pair, head), key_pair) + bias
        top = jnp.maximum(jnp.max(scores, axis=-1, keepdims=True), far_top)
        raw = jnp.exp(scores - top)
        weight = jnp.exp(far_top - top)
        total = jnp.sum(raw, axis=-1, keepdims=True) + far_total * weight
        mixed.append((nn(raw.astype(BF), value_pair) + far * weight) / total)
        lse_ref[...] = jnp.where(mine, top + jnp.log(total), lse_ref[...])
    return jnp.where(lane < 64, mixed[0], mixed[1])


def bit_count(n):
    return n.bit_length() - 1


def qkv_rows(n):
    piece = D // n
    return {"wq": (0, piece), "wk": (piece, piece), "wv": (2 * piece, piece)}, 3 * piece


def rest_rows(n):
    piece = D // n
    table, start = {}, 0
    for name, times in (
        ("wout", 1), ("cq", 1), ("ck", 1), ("cv", 1), ("cout", 1), ("up", 4), ("down", 4), ("slot", 2)
    ):
        table[name] = (start, times * piece)
        start += times * piece
    return table, start


def square(ref, table, name):
    start, count = table[name]
    return ref[:, start : start + count, :].reshape(D, D)


def up_part(ref, table, c):
    start, count = table["up"]
    piece = count // 4
    return ref[:, start + c * piece : start + (c + 1) * piece, :].reshape(D, D)


def row_part(ref, table, name, c):
    start, count = table[name]
    many = D // count
    return ref[c * many : (c + 1) * many, start : start + count, :].reshape(D, D)


def store_square(ref, table, name, value):
    start, count = table[name]
    ref[:, start : start + count, :] = value.reshape(ref.shape[0], count, D)


def store_up(ref, table, c, value):
    start, count = table["up"]
    piece = count // 4
    ref[:, start + c * piece : start + (c + 1) * piece, :] = value.reshape(ref.shape[0], piece, D)


def store_part(ref, table, name, c, value):
    start, count = table[name]
    many = D // count
    ref[c * many : (c + 1) * many, start : start + count, :] = value.reshape(many, count, D)


def my_place(n):
    me = lax.axis_index("fsdp")
    bits = [(me // (1 << b)) % 2 for b in range(bit_count(n))]
    return me, bits


def partner_of(me, bits, b):
    return me + (1 - 2 * bits[b]) * (1 << b)


def orders(n):
    d = bit_count(n)
    far = list(range(1, d))
    return [far + [0], far[::-1] + [0]]


def at_bits(bits, free, fixed=None):
    fixed = fixed or {}
    return tuple(
        slice(None) if b in free else fixed.get(b, bits[b]) for b in range(len(bits) - 1, -1, -1)
    )


MESH_ID = pl.DeviceIdType.MESH

def place_info(info, seg_ref, prefix_ref, m):
    glen = info.shape[1]
    prompt = glen // 3
    seg = jnp.broadcast_to(seg_ref[m], (8, glen))
    limit = jnp.where(seg == 0, prompt, 0)
    for c in range(prefix_ref.shape[1]):
        limit = jnp.where(seg == c + 1, prefix_ref[m, c], limit)
    place = lax.broadcasted_iota(jnp.int32, (8, glen), 1)
    after = (seg == pltpu.roll(seg, glen - 1, 1)) & (place < glen - 1)
    before = (seg == pltpu.roll(seg, 1, 1)) & (place > 0)
    sub = lax.broadcasted_iota(jnp.int32, (8, glen), 0)
    mixed = jnp.where(sub == 0, limit, seg)
    mixed = jnp.where(sub == 2, after.astype(jnp.int32), mixed)
    mixed = jnp.where(sub == 3, before.astype(jnp.int32), mixed)
    info[...] = mixed.astype(F32)


SMEM = pl.BlockSpec(memory_space=pltpu.SMEM)


def spread_rows(tiles, first, count, width, out):
    group = max(1, 128 // width)
    lane = lax.broadcasted_iota(jnp.int32, (count, 128), 1)
    for p in range(tiles.shape[0] // group):
        block = tiles[p * group, first : first + count, :]
        for j in range(1, group):
            piece = pltpu.roll(tiles[p * group + j, first : first + count, :], j * width, 1)
            block = jnp.where(lane >= j * width, piece, block)
        out[0:count, p * 128 : (p + 1) * 128] = block


def gather_rows(values, count, width, tiles, first):
    group = max(1, 128 // width)
    for i in range(tiles.shape[0]):
        p, j = i // group, i % group
        block = values[0:8, p * 128 : (p + 1) * 128]
        if j:
            block = pltpu.roll(block, 128 - j * width, 1)
        tiles[i, first : first + count, :] = block[0:count]


def norm_forward(residual, gain, shift):
    average = jnp.mean(residual, axis=-1, keepdims=True)
    centred = residual - average
    variance = jnp.mean(centred * centred, axis=-1, keepdims=True)
    rstd = lax.rsqrt(variance + EPSILON)
    hat = centred * rstd
    return hat * gain + shift, hat, rstd


def norm_backward(upstream, hat, rstd, gain):
    d_hat = upstream * gain
    mean_d = jnp.mean(d_hat, axis=-1, keepdims=True)
    mean_dh = jnp.mean(d_hat * hat, axis=-1, keepdims=True)
    d_gain = jnp.sum(upstream * hat, axis=0, keepdims=True)
    d_shift = jnp.sum(upstream, axis=0, keepdims=True)
    return rstd * (d_hat - mean_d - hat * mean_dh), d_gain, d_shift


def gelu_parts(value):
    square = value * value
    t = jnp.tanh(GELU_C * value * (1.0 + 0.044715 * square))
    half = 0.5 * (1.0 + t)
    slope = half + 0.5 * value * (1.0 - t * t) * (GELU_C * (1.0 + 3.0 * 0.044715 * square))
    return value * half, slope


def head_sums(product_rows):
    rows, cols = 16, product_rows.shape[1]
    head = lax.broadcasted_iota(jnp.int32, (rows, cols), 0)
    lane = lax.broadcasted_iota(jnp.int32, (rows, cols), 1)
    pick = ((lane // HD) == head).astype(F32)
    return lax.dot_general(
        pick, product_rows, (((1,), (1,)), ((), ())),
        preferred_element_type=F32, precision=lax.Precision.HIGHEST,
    )[0:HEADS, :]


def middle_kernel(
    rows, enc,
    mix_ref, x_ref, edge_ref, e_ref, cot_ref, prev_ref, seg_ref, prefix_ref,
    w_hbm, small_ref,
    slot_out, dmix_out, dr1_out, genc_out, g_out, gs_out,
    w_ref, g_ref, bup_ref, vec_ref, gbup, gvec, wsem, gsem,
    lowx, lown, cqs, cks, cvs, lse_sc, lse_row, cmix, h1s, hats, rstds, slope,
    act, dpre, dffn, dcross, dcqs, dattn, dcks, dcvs, ckt, h3s, h2low, info, shs,
):
    ext = rows + HALO
    n = w_ref.shape[0]
    table, _ = rest_rows(n)
    piece = D // n
    spans = ((0, 5 * piece), (5 * piece, 4 * piece), (9 * piece, 4 * piece), (13 * piece, 2 * piece))

    def part_copy(k, out=False):
        cut = pl.ds(*spans[k])
        if out:
            return pltpu.make_async_copy(g_ref.at[:, cut], g_out.at[:, cut], gsem.at[k])
        return pltpu.make_async_copy(w_hbm.at[:, cut], w_ref.at[:, cut], wsem.at[k])

    for k in range(4):
        part_copy(k).start()
    spread_rows(small_ref, 0, 8, D // n, vec_ref)
    edge = FF // n
    if edge >= 128:
        for i in range(n):
            for r in range(edge // 128):
                lane = i * edge + r * 128
                bup_ref[0:1, lane : lane + 128] = small_ref[i, 8 + r : 9 + r, :]
    else:
        spread_rows(small_ref, 8, 1, edge, bup_ref)
    part_copy(0).wait()
    gbup[...] = jnp.zeros_like(gbup)
    gvec[...] = jnp.zeros_like(gvec)

    def vec(i):
        return vec_ref[i : i + 1, :]

    def one_micro(m, _):
        own = pl.ds(0, rows)
        attn = nn(mix_ref[m], square(w_ref, table, "wout"))
        x_rows = jnp.concatenate([x_ref[m], edge_ref[m]], axis=0).astype(F32)
        h1, hat, rstd = norm_forward(x_rows + attn, vec(1), vec(2))
        h1s[...] = h1
        dr1_out[m] = hat[0:rows]
        rstds[:, 0:1] = rstd[0:rows]
        h1_low = h1.astype(BF)
        lown[0, m] = h1_low[0:rows]
        cqs[...] = (nn(h1_low, square(w_ref, table, "cq")).astype(BF) * SCALE).astype(BF)
        cks[...] = nn(e_ref[m], square(w_ref, table, "ck")).astype(BF)
        cvs[...] = nn(e_ref[m], square(w_ref, table, "cv")).astype(BF)

        def cross_pair(pair, _):
            at = lanes_of(pair)
            mix = attend_pair(cqs[:, at], cks[:, at], cvs[:, at], None, pair, lse_sc)
            cmix[:, at] = mix.astype(BF)
            return 0

        lax.fori_loop(0, HEADS // 2, cross_pair, 0)
        lse_row[0:HEADS, :] = lse_sc[0:rows, :].T[0:HEADS, :]
        lowx[m] = cmix[0:rows, :]
        h2, hat, rstd = norm_forward(
            h1s[...] + nn(cmix[...], square(w_ref, table, "cout")), vec(3), vec(4)
        )
        h1s[...] = h2
        hats[...] = hat[0:rows]
        rstds[:, 1:2] = rstd[0:rows]
        h2low[...] = h2.astype(BF)
        lown[1, m] = h2low[0:rows, :]
        @pl.when(m == 0)
        def _():
            for k in range(1, 4):
                part_copy(k).wait()

        h3s[...] = jnp.zeros_like(h3s)

        for c in range(FF // D):
            at = slice(c * D, (c + 1) * D)
            pre = nn(h2low[...], up_part(w_ref, table, c)) + bup_ref[0:1, at]
            value, grad = gelu_parts(pre)
            value = value.astype(BF)
            act[m, :, at] = value[0:rows]
            slope[:, at] = grad[0:rows]
            down = row_part(w_ref, table, "down", c)
            h3s[...] += nn(value, down)
        h3, hat, rstd = norm_forward(h1s[...] + h3s[...] + vec(0), vec(5), vec(6))
        h3_low = h3.astype(BF)
        h3s[...] = h3_low.astype(F32)
        lown[2, m] = h3_low[0:rows]
        top = row_part(w_ref, table, "slot", 0)
        bottom = row_part(w_ref, table, "slot", 1)
        place_info(info, seg_ref, prefix_ref, m)
        flags = info[:, pl.ds(pl.multiple_of(lax.axis_index("seq") * rows, 128), rows)].T
        follow = (h3s[pl.ds(1, rows), :] * flags[:, 2:3]).astype(BF)
        slot_out[m] = (nn(h3_low[0:rows], top) + nn(follow, bottom)).astype(BF)
        h3s[0:8, :] = prev_ref[m].astype(F32)[HALO - 8 : HALO]
        h3s[8 : rows + 8, :] = cot_ref[m].astype(F32)
        shifted = h3s[pl.ds(7, rows), :]
        shs[m] = (shifted * flags[:, 3:4]).astype(BF)
        d_follow = nt(shifted.astype(BF), bottom).astype(BF).astype(F32) * flags[:, 3:4]
        d_three = nt(cot_ref[m], top) + d_follow
        d_r3, d_gain, d_shift = norm_backward(d_three, hat[0:rows], rstd[0:rows], vec(5))
        gvec[5:6, :] += d_gain
        gvec[6:7, :] += d_shift
        d_ffn = d_r3.astype(BF)
        dffn[m] = d_ffn
        gvec[0:1, :] += jnp.sum(d_ffn.astype(F32), axis=0, keepdims=True)
        d_two = d_r3
        for c in range(FF // D):
            at = slice(c * D, (c + 1) * D)
            down = row_part(w_ref, table, "down", c)
            grad = (nt(d_ffn, down) * slope[:, at]).astype(BF)
            dpre[m, :, at] = grad
            gbup[0:1, at] += jnp.sum(grad.astype(F32), axis=0, keepdims=True)
            d_two = d_two + nt(grad, up_part(w_ref, table, c))
        d_r2, d_gain, d_shift = norm_backward(d_two, hats[...], rstds[:, 1:2], vec(3))
        gvec[3:4, :] += d_gain
        gvec[4:5, :] += d_shift
        d_cross = d_r2.astype(BF)
        dcross[m] = d_cross
        d_cmix = nt(d_cross, square(w_ref, table, "cout")).astype(BF)
        dmix_out[m] = d_cmix
        delta = head_sums(d_cmix.astype(F32) * cmix[0:rows, :].astype(F32))
        lse_row[HEADS : 2 * HEADS, :] = delta
        ckt[...] = cks[...].T

        def cross_back(pair, _):
            at = lanes_of(pair)
            kp, vp = cks[:, at], cvs[:, at]
            qp, dp = cqs[0:rows, at], dmix_out[m, :, at]
            kt = ckt[at, :]
            d_k = d_v = None
            d_qt = []
            for head in range(2):
                qm, dm = head_masked(qp, head), head_masked(dp, head)
                row = pair * 2 + head
                prob = jnp.exp(nt(kp, qm) - lse_row[pl.ds(row, 1), :])
                d_score = (prob * (nt(vp, dm) - lse_row[pl.ds(HEADS + row, 1), :])).astype(BF)
                dk, dv = nn(d_score, qm), nn(prob.astype(BF), dm)
                d_k = dk if d_k is None else d_k + dk
                d_v = dv if d_v is None else d_v + dv
                d_qt.append(nn(kt, d_score))
            sub = lax.broadcasted_iota(jnp.int32, d_qt[0].shape, 0)
            d_q = jnp.where(sub < 64, d_qt[0], d_qt[1]) * SCALE
            dcqs[m, :, at] = d_q.T.astype(BF)
            dcks[m, :, at] = d_k.astype(BF)
            dcvs[m, :, at] = d_v.astype(BF)
            return 0

        lax.fori_loop(0, HEADS // 2, cross_back, 0)
        genc_out[m] = (
            nt(dcks[m], square(w_ref, table, "ck")) + nt(dcvs[m], square(w_ref, table, "cv"))
        ).astype(BF)
        d_one = d_r2 + nt(dcqs[m], square(w_ref, table, "cq"))
        d_r1, d_gain, d_shift = norm_backward(d_one, dr1_out[m], rstds[:, 0:1], vec(1))
        gvec[1:2, :] += d_gain
        gvec[2:3, :] += d_shift
        dr1_out[m] = d_r1
        d_attn = d_r1.astype(BF)
        dattn[m] = d_attn
        dmix_out[m] = nt(d_attn, square(w_ref, table, "wout")).astype(BF)
        return 0

    lax.fori_loop(0, MICRO, one_micro, 0)

    total = MICRO * rows

    def flat(ref, *lead):
        return ref[lead].reshape(total, D) if lead else ref[...].reshape(total, D)

    def grad_of(left, right):
        return tn(left, right).astype(BF)

    cot = cot_ref[...].reshape(total, D)
    flagged = shs[...].reshape(total, D)
    h3_all = lown[2].reshape(total, D)
    store_part(g_ref, table, "slot", 0, grad_of(h3_all, cot))
    store_part(g_ref, table, "slot", 1, grad_of(h3_all, flagged))
    part_copy(3, True).start()
    dffn_all = dffn[...].reshape(total, D)
    h2_all = lown[1].reshape(total, D)
    for c in range(FF // D):
        at = slice(c * D, (c + 1) * D)
        store_part(g_ref, table, "down", c, grad_of(act[:, :, at].reshape(total, D), dffn_all))
        store_up(g_ref, table, c, grad_of(h2_all, dpre[:, :, at].reshape(total, D)))
    part_copy(2, True).start()
    part_copy(1, True).start()
    store_square(g_ref, table, "cout", grad_of(lowx[...].reshape(total, D), dcross[...].reshape(total, D)))
    store_square(g_ref, table, "cq", grad_of(lown[0].reshape(total, D), dcqs[...].reshape(total, D)))
    e_all = e_ref[...].reshape(MICRO * enc, D)
    store_square(g_ref, table, "ck", grad_of(e_all, dcks[...].reshape(MICRO * enc, D)))
    store_square(g_ref, table, "cv", grad_of(e_all, dcvs[...].reshape(MICRO * enc, D)))
    mix_all = jnp.concatenate([mix_ref[m, 0:rows, :] for m in range(MICRO)], axis=0)
    store_square(g_ref, table, "wout", grad_of(mix_all, dattn[...].reshape(total, D)))
    part_copy(0, True).start()
    gs_out[...] = jnp.zeros_like(gs_out)
    gather_rows(gvec, 8, D // n, gs_out, 0)
    if edge >= 128:
        for i in range(n):
            for r in range(edge // 128):
                lane = i * edge + r * 128
                gs_out[i, 8 + r : 9 + r, :] = gbup[0:1, lane : lane + 128]
    else:
        gather_rows(gbup, 1, edge, gs_out, 8)
    for k in range(4):
        part_copy(k, True).wait()


def middle(mix, tokens, edges, e_all, cot, prev, seg, prefix, w, small, rows):
    glen = seg.shape[2]
    enc = e_all.shape[1]
    ext = rows + HALO
    out_shape = [
        jax.ShapeDtypeStruct((MICRO, rows, D), BF),
        jax.ShapeDtypeStruct((MICRO, rows, D), BF),
        jax.ShapeDtypeStruct((MICRO, rows, D), F32),
        jax.ShapeDtypeStruct((MICRO, enc, D), BF),
        jax.ShapeDtypeStruct(w.shape, BF),
        jax.ShapeDtypeStruct(small.shape, F32),
    ]
    V = pltpu.VMEM
    hbm = pl.BlockSpec(memory_space=pl.ANY)
    scratch = [
        V(w.shape, BF), V(w.shape, BF), V((8, FF), F32), V((8, D), F32),
        V((8, FF), F32), V((8, D), F32),
        pltpu.SemaphoreType.DMA((4,)), pltpu.SemaphoreType.DMA((4,)),
        V((MICRO, rows, D), BF),
        V((3, MICRO, rows, D), BF),
        V((ext, D), BF), V((enc, D), BF), V((enc, D), BF),
        V((ext, 128), F32), V((2 * HEADS, rows), F32),
        V((ext, D), BF),
        V((ext, D), F32),
        V((rows, D), F32), V((rows, 128), F32),
        V((rows, FF), F32),
        V((MICRO, rows, FF), BF), V((MICRO, rows, FF), BF),
        V((MICRO, rows, D), BF), V((MICRO, rows, D), BF), V((MICRO, rows, D), BF),
        V((MICRO, rows, D), BF),
        V((MICRO, enc, D), BF), V((MICRO, enc, D), BF),
        V((D, enc), BF),
        V((ext, D), F32), V((ext, D), BF),
        V((8, glen), F32), V((MICRO, rows, D), BF),
    ]
    return pl.pallas_call(
        functools.partial(middle_kernel, rows, enc),
        in_specs=[VM] * 7 + [SMEM, hbm, VM],
        out_specs=[VM] * 4 + [hbm, VM],
        out_shape=out_shape,
        scratch_shapes=scratch,
        compiler_params=pltpu.CompilerParams(vmem_limit_bytes=61 * MIB),
        name="middle",
    )(mix, tokens, edges, e_all, cot, prev, seg, prefix, w, small)


def weight_units(n):
    piece = D // n
    units = []
    for array, start, count in (
        (0, 0, 3 * piece), (1, 0, 5 * piece), (1, 5 * piece, 4 * piece),
        (1, 9 * piece, 4 * piece), (1, 13 * piece, 2 * piece),
    ):
        for half in range(2):
            units.append((array, start, count, half * 256, 256, half))
    return units


def greet(peers):
    barrier = pltpu.get_barrier_semaphore()
    for axis, target, when in peers:
        if when is None:
            pl.semaphore_signal(barrier, inc=1, device_id={axis: target}, device_id_type=MESH_ID)
        else:

            @pl.when(when)
            def _():
                pl.semaphore_signal(barrier, inc=1, device_id={axis: target}, device_id_type=MESH_ID)

    always = sum(1 for peer in peers if peer[2] is None)
    amount = jnp.int32(always)
    for axis, target, when in peers:
        if when is not None:
            amount = amount + when.astype(jnp.int32)
    pl.semaphore_wait(barrier, amount if always < len(peers) else always)


STRIP = 128


def key_span(rank, rows, glen):
    prompt = glen // 3
    least = (glen - prompt) // 8
    most = (glen - prompt) - 3 * least
    first, stop = rank * rows, (rank + 1) * rows + 1
    low = jnp.maximum(first - most, jnp.where(first >= prompt + most, prompt + least, prompt))
    high = jnp.minimum(stop + most, jnp.where(stop <= glen - most, glen - least, glen))
    return low, jnp.where(stop > prompt, high, 0)


class Chain:
    def __init__(self, ref, rows, strips, sems, lane, rank, count, needed):
        self.ref, self.rows, self.lane, self.needed = ref, rows, lane, needed
        self.strips, self.height = strips, rows // strips
        self.send, self.recv = sems
        self.rank, self.count = rank, count

    def copy(self, side, step, j, block, target):
        at = pl.ds(pl.multiple_of(block * self.rows + j * self.height, 16), self.height)
        part = self.ref.at[:, at] if len(self.ref.shape) == 3 else self.ref.at[at]
        return pltpu.make_async_remote_copy(
            src_ref=part, dst_ref=part,
            send_sem=self.send.at[self.lane, side, step, j],
            recv_sem=self.recv.at[self.lane, side, step, j],
            device_id={"seq": target}, device_id_type=MESH_ID,
        )

    def goes(self, side, sender, block, j):
        last = self.count - 1
        if side == 0:
            there = (sender >= 0) & (sender < last) & (block >= 0)
            taker = sender + 1
        else:
            there = (sender <= last) & (sender > 0) & (block <= last)
            taker = sender - 1
        if self.needed is None:
            return there
        return there & self.needed(side, taker, block * self.rows + j * self.height, self.height)

    def outgoing(self, step, j, act):
        r = self.rank
        for side, block, target in ((0, r - step, r + 1), (1, r + step, r - 1)):

            @pl.when(self.goes(side, r, block, j))
            def _():
                act(self.copy(side, step, j, block, target))

    def start(self, step):
        for j in range(self.strips):
            self.outgoing(step, j, lambda c: c.start())

    def arrived(self, step, onward):
        r = self.rank
        for j in range(self.strips):
            for side, block, source in ((0, r - 1 - step, r - 1), (1, r + 1 + step, r + 1)):

                @pl.when(self.goes(side, source, block, j))
                def _():
                    self.copy(side, step, j, block, source).wait_recv()

            if onward:
                self.outgoing(step + 1, j, lambda c: c.start())

    def sent(self, step):
        for j in range(self.strips):
            self.outgoing(step, j, lambda c: c.wait_send())


def front_kernel(n, count, rows, erows, *refs):
    shards = refs[0:11]
    tok, enc, cot, seg_ref, prefix_ref = refs[11:16]
    vectors = refs[16:24]
    (
        wa_out, wb, small_all, x_out, e_all, prev, halo_out, q_out, k_out, v_out, mix_ref, lse_out
    ) = refs[24:36]
    wa, x_all, q_ref, k_ref, v_ref = refs[36:41]
    far_mix, far_top, far_total = refs[41:44]
    stage, bias, lse_sc, info, local, fsend, frecv, zsend, zrecv, csend, crecv, osem = refs[44:]
    me, bits = my_place(n)
    rank = lax.axis_index("seq")
    last = count - 1
    glen = count * rows
    prompt = glen // 3
    piece = D // n
    d = bit_count(n)

    here = at_bits(bits, ())
    table_a, _ = qkv_rows(n)
    table_b, _ = rest_rows(n)
    copies = []

    def keep(src, dst):
        copy = pltpu.make_async_copy(src, dst, local.at[len(copies)])
        copy.start()
        copies.append(copy)

    keep(tok, x_all.at[:, pl.ds(pl.multiple_of(rank * rows, 16), rows)])
    keep(enc, e_all.at[:, pl.ds(pl.multiple_of(rank * erows, 16), erows)])
    names = ("wq", "wk", "wv", "wout", "cq", "ck", "cv", "cout", "up", "down", "slot")
    for name, shard in zip(names, shards):
        start, size = (table_a if name in table_a else table_b)[name]
        target = wa.at[here] if name in table_a else stage
        if name == "up":
            for c in range(4):
                keep(shard.at[:, pl.ds(c * D, D)], target.at[pl.ds(start + c * piece, piece)])
        else:
            keep(shard, target.at[pl.ds(start, size)])
    small_all[here] = jnp.zeros((16, 128), F32)
    for r, vector in enumerate(vectors[0:7]):
        small_all[here + (slice(r, r + 1), slice(0, D // n))] = vector[...].astype(F32).reshape(1, D // n)
    edge_rows, edge_width = max(1, FF // n // 128), min(128, FF // n)
    small_all[here + (slice(8, 8 + edge_rows), slice(0, edge_width))] = (
        vectors[7][...].astype(F32).reshape(edge_rows, edge_width)
    )

    peers = [("fsdp", partner_of(me, bits, b), None) for b in range(d)]
    peers += [("seq", rank - 1, rank > 0), ("seq", rank + 1, rank < last)]
    greet(peers)

    arrays = (wa, wb, small_all)
    units = weight_units(n) + [(2, 0, 16, 0, 128, 0)]
    order_list = orders(n)

    def hop(u, phase, theirs=False):
        array, r0, nr, c0, nc, which = units[u]
        order = order_list[which]
        b = order[phase]
        cut = (pl.ds(r0, nr), pl.ds(c0, nc))
        fixed = {b: 1 - bits[b]} if theirs else {}
        part = arrays[array].at[at_bits(bits, order[:phase], fixed) + cut]
        src = stage.at[cut] if array == 1 and phase == 0 and not theirs else part
        return pltpu.make_async_remote_copy(
            src_ref=src, dst_ref=part, send_sem=fsend.at[u, phase], recv_sem=frecv.at[u, phase],
            device_id={"fsdp": partner_of(me, bits, b)}, device_id_type=MESH_ID,
        )

    def landed(u, phase):
        hop(u, phase, True).wait_recv()

    def onward(some, phase):
        for u in some:
            landed(u, phase - 1)
            hop(u, phase).start()

    def needed(side, taker, start, height):
        low, high = key_span(taker, rows, glen)
        if side == 0:
            return (start < prompt) | (start + height > low)
        return (start < prompt) | (start < high)

    copies[0].wait()
    copies[1].wait()
    sems = (zsend, zrecv)
    strips = rows // STRIP
    toks = [Chain(x_all.at[m], rows, strips, sems, m, rank, count, needed) for m in range(MICRO)]
    encs = Chain(e_all, erows, 1, sems, MICRO, rank, count, None)
    toks[0].start(0)
    halo = pltpu.make_async_remote_copy(
        src_ref=cot.at[:, pl.ds(rows - HALO, HALO)], dst_ref=prev, send_sem=csend, recv_sem=crecv,
        device_id={"seq": rank + 1}, device_id_type=MESH_ID,
    )

    @pl.when(rank < last)
    def _():
        halo.start()

    for strip in range(glen // STRIP):
        start, block = strip * STRIP, strip * STRIP // rows
        side0, side1 = needed(0, rank, start, STRIP), needed(1, rank, start, STRIP)
        unseen = ((block < rank) & jnp.logical_not(side0)) | ((block > rank) & jnp.logical_not(side1))

        @pl.when(unseen)
        def _():
            x_all[:, start : start + STRIP, :] = jnp.zeros((MICRO, STRIP, D), BF)

    for copy in copies[2:]:
        copy.wait()
    everything = list(range(len(units)))
    for u in everything:
        hop(u, 0).start()
    settle = pltpu.make_async_copy(stage, wb.at[here], local.at[len(copies)])
    settle.start()
    first = pltpu.make_async_copy(cot.at[:, pl.ds(rows - HALO, HALO)], prev, local.at[len(copies) + 1])

    @pl.when(rank == 0)
    def _():
        first.start()

    settle.wait()
    onward(everything[:6], 1)
    for s in range(1, count):
        toks[0].arrived(s - 1, s < count - 1)
        if s == 1:
            onward(everything[6:], 1)
        if s == count - 2:
            toks[1].start(0)
    if d > 2:
        for phase in range(2, d):
            onward(everything[:2], phase)
    landed(0, d - 1)
    landed(1, d - 1)

    off = pl.multiple_of(rank * rows, 128)
    edge = pl.multiple_of(jnp.minimum(rank * rows + rows, glen - 128), 128)
    n_lead = (n, 3 * piece, D)

    def weight(name):
        start, size = table_a[name]
        return wa[(slice(None),) * d + (slice(start, start + size),)].reshape(D, D)

    def project(m, low, high):
        def one_tile(tile, _):
            at = pl.ds(pl.multiple_of(tile * 256, 256), 256)
            part = x_all[m, at, :]
            k_ref[m, at, :] = nn(part, weight("wk")).astype(BF)
            v_ref[m, at, :] = nn(part, weight("wv")).astype(BF)
            return 0

        lax.fori_loop(low, high, one_tile, 0)

    def query(m):
        edge_rows = x_all[m, pl.ds(edge, HALO), :]
        halo_out[m] = edge_rows
        q_ref[m, 0:rows, :] = (nn(x_all[m, pl.ds(off, rows), :], weight("wq")).astype(BF) * SCALE).astype(BF)
        q_ref[m, rows : rows + HALO, :] = (nn(edge_rows, weight("wq")).astype(BF) * SCALE).astype(BF)
        place_info(info, seg_ref, prefix_ref, m)
        seg_row = info[1:2, :]
        place = lax.broadcasted_iota(jnp.int32, (1, glen), 1)
        for start, size, span in ((0, rows, pl.ds(off, rows)), (rows, HALO, pl.ds(edge, 128))):
            column = info[:, span].T[0:size]
            limit, seg = column[:, 0:1], column[:, 1:2]
            seen = jnp.where(
                place < prompt, (place.astype(F32) < limit).astype(jnp.int32), (seg_row == seg).astype(jnp.int32)
            )
            bias[start : start + size, :] = jnp.where(seen == 1, 0.0, NEG)

    def pairs(m, low, high):
        def one_pair(pair, _):
            at = lanes_of(pair)
            mix = attend_pair(
                q_ref[m, :, at], k_ref[m, :, at], v_ref[m, :, at], bias[...], pair, lse_sc
            )
            mix_ref[m, :, at] = mix.astype(BF)
            return 0

        lax.fori_loop(low, high, one_pair, 0)
        if high == HEADS // 2:
            lse_out[m] = lse_sc[0:rows, :].T[0:HEADS, :]

    stores = []

    def store(src, to):
        copy = pltpu.make_async_copy(src, to, osem.at[len(stores)])
        copy.start()
        stores.append(copy)

    def store_micro(m):
        for src, to in ((x_all, x_out), (k_ref, k_out), (v_ref, v_out), (q_ref, q_out)):
            store(src.at[m], to.at[m])

    def far_pairs(m, split):
        def one_pair(pair, _):
            at = lanes_of(pair)
            attend_far(
                q_ref[m, :, at], k_ref[m, split:glen, at], v_ref[m, split:glen, at],
                bias[:, split:glen], pair, far_mix, far_top, far_total,
            )
            return 0

        lax.fori_loop(0, HEADS // 2, one_pair, 0)

    def near_pairs(m, split, low, high):
        def one_pair(pair, _):
            at = lanes_of(pair)
            mix = attend_near(
                q_ref[m, :, at], k_ref[m, 0:split, at], v_ref[m, 0:split, at],
                bias[:, 0:split], pair, lse_sc, far_mix, far_top, far_total,
            )
            mix_ref[m, :, at] = mix.astype(BF)
            return 0

        lax.fori_loop(low, high, one_pair, 0)
        if high == HEADS // 2:
            lse_out[m] = lse_sc[0:rows, :].T[0:HEADS, :]

    rest = everything[2:]
    near = -(-rows // 256)
    project(0, 0, glen // 256)
    query(0)
    store(wa, wa_out)
    store_micro(0)
    pairs(0, 0, 2)
    toks[1].arrived(0, count > 2)
    encs.start(0)
    for phase in range(2, d):
        onward(rest[: len(rest) // 2], phase)
    pairs(0, 2, 4)
    for s in range(1, count - 2):
        toks[1].arrived(s, True)
    encs.arrived(0, count > 2)
    for phase in range(2, d):
        onward(rest[len(rest) // 2 :], phase)
    project(1, near, glen // 256)
    query(1)
    far_pairs(1, near * 256)
    toks[1].arrived(count - 2, False)
    project(1, 0, near)
    store_micro(1)
    near_pairs(1, near * 256, 0, 2)
    for s in range(1, count - 1):
        encs.arrived(s, s < count - 2)
    near_pairs(1, near * 256, 2, 4)

    for u in rest:
        landed(u, d - 1)

    @pl.when(rank > 0)
    def _():
        halo.wait_recv()

    @pl.when(rank == 0)
    def _():
        first.wait()

    @pl.when(rank < last)
    def _():
        halo.wait_send()

    for u in everything:
        for phase in range(d):
            hop(u, phase).wait_send()
    for chain in toks + [encs]:
        for s in range(count - 1):
            chain.sent(s)
    for copy in stores:
        copy.wait()


def front(n, count, shards, vectors, tok, enc, cot, seg, prefix):
    rows, erows = tok.shape[1], enc.shape[1]
    glen = count * rows
    ext = rows + HALO
    lead = (2,) * bit_count(n)
    _, ra = qkv_rows(n)
    _, rb = rest_rows(n)
    units = len(weight_units(n)) + 1
    d = bit_count(n)
    hbm = pl.BlockSpec(memory_space=pl.ANY)
    dma = pltpu.SemaphoreType.DMA
    strips = rows // STRIP
    return pl.pallas_call(
        functools.partial(front_kernel, n, count, rows, erows),
        in_specs=[hbm] * 14 + [VM, SMEM] + [VM] * 8,
        out_specs=[hbm, hbm, VM, hbm, VM, VM, VM, hbm, hbm, hbm, VM, VM],
        out_shape=[
            jax.ShapeDtypeStruct(lead + (ra, D), BF),
            jax.ShapeDtypeStruct(lead + (rb, D), BF),
            jax.ShapeDtypeStruct(lead + (16, 128), F32),
            jax.ShapeDtypeStruct((MICRO, glen, D), BF),
            jax.ShapeDtypeStruct((MICRO, count * erows, D), BF),
            jax.ShapeDtypeStruct((MICRO, HALO, D), BF),
            jax.ShapeDtypeStruct((MICRO, HALO, D), BF),
            jax.ShapeDtypeStruct((MICRO, ext, D), BF),
            jax.ShapeDtypeStruct((MICRO, glen, D), BF),
            jax.ShapeDtypeStruct((MICRO, glen, D), BF),
            jax.ShapeDtypeStruct((MICRO, ext, D), BF),
            jax.ShapeDtypeStruct((MICRO, HEADS, rows), F32),
        ],
        scratch_shapes=[
            pltpu.VMEM(lead + (ra, D), BF), pltpu.VMEM((MICRO, glen, D), BF),
            pltpu.VMEM((MICRO, ext, D), BF), pltpu.VMEM((MICRO, glen, D), BF),
            pltpu.VMEM((MICRO, glen, D), BF),
            pltpu.VMEM((ext, D), F32), pltpu.VMEM((ext, 128), F32), pltpu.VMEM((ext, 128), F32),
            pltpu.VMEM((rb, D), BF), pltpu.VMEM((ext, glen), F32), pltpu.VMEM((ext, 128), F32),
            pltpu.VMEM((8, glen), F32),
            dma((20,)), dma((units, d)), dma((units, d)),
            dma((MICRO + 1, 2, count, strips)), dma((MICRO + 1, 2, count, strips)), dma(()), dma(()), dma((10,)),
        ],
        compiler_params=pltpu.CompilerParams(
            collective_id=0, has_side_effects=True, vmem_limit_bytes=60 * MIB
        ),
        name="front",
    )(*shards, tok, enc, cot, seg, prefix, *vectors)


TILE = 256
GROUPS = 12
SLOTS = ((-2, -1, 1, 4), (-2, 0, 3, 6), (-2, 1, 5, 7), (-2, 3, 6, 8), (-2, 3, 6, 8))


def seen_from(side, taker, start, height, rows, glen):
    low, high = key_span(taker, rows, glen)
    if side == 0:
        return (start < glen // 3) | (start + height > low)
    return (start < glen // 3) | (start < high)


def static_wants(side, taker, start, rows, glen):
    prompt = glen // 3
    least = (glen - prompt) // 8
    most = (glen - prompt) - 3 * least
    first, stop = taker * rows, (taker + 1) * rows + 1
    low = max(first - most, prompt + least if first >= prompt + most else prompt)
    high = min(stop + most, glen - least if stop <= glen - most else glen) if stop > prompt else 0
    return start < prompt or (start + STRIP > low if side == 0 else start < high)


def back_kernel(n, count, rows, erows, *refs):
    q_ref, mix_ref, dmix_ref, lse_ref, tok_ref, wa, genc, gs, seg_ref, prefix_ref = refs[0:10]
    x_hbm, k_hbm, v_hbm, dr1_hbm, gb = refs[10:15]
    outs = refs[15:18]
    tok_out, enc_out = refs[18:20]
    rest = list(refs[20:])
    d = bit_count(n)
    glen = count * rows
    prompt = glen // 3
    tiles = glen // TILE

    def take(k):
        got = rest[:k]
        del rest[:k]
        return got

    accs, zls, zrs, zss, fins = take(3), take(3), take(3), take(3), take(3)
    recvs = [take(d) for _ in range(3)]
    ebuf, ga, part, inc, wkv, qst, dst, stats, info, bias, dqt, dkv, gkv, dqs = take(14)
    kbuf, vbuf, xbuf = take(3)
    fsend, frecv, zsend, zrecv, tsend, trecv, esend, erecv, lsem, tsem, dsem = rest
    grads = (ga, gb, gs)
    me, bits = my_place(n)
    rank = lax.axis_index("seq")
    last = count - 1
    off = pl.multiple_of(rank * rows, 128)
    table, _ = qkv_rows(n)

    def weight(name):
        start, size = table[name]
        return wa[:, start : start + size, :].reshape(D, D)

    def tile_copies(i, slot):
        m, at = i // tiles, pl.ds(pl.multiple_of((i % tiles) * TILE, TILE), TILE)
        return [
            pltpu.make_async_copy(hbm.at[m, at], buf.at[slot], tsem.at[slot, j])
            for j, (hbm, buf) in enumerate(((k_hbm, kbuf), (v_hbm, vbuf), (x_hbm, xbuf)))
        ]

    for copy in tile_copies(0, 0):
        copy.start()
    start_out = pltpu.make_async_copy(dr1_hbm, tok_out, dsem)
    start_out.start()

    piece = D // n
    early_units = weight_units(n)[2:] + [(2, 0, 16, 0, 128, 0)]
    late_units = [
        (0, c * piece, w * piece, half * 256, 256, half) for c, w in ((1, 2), (0, 1)) for half in range(2)
    ]
    units = early_units + late_units
    early, late = list(range(len(early_units))), list(range(len(early_units), len(units)))
    order_list = [o[::-1] for o in orders(n)]

    def own_half(u):
        array, r0, nr, c0, nc, which = units[u]
        cut = (pl.ds(r0, nr), pl.ds(c0, nc))
        index = at_bits(bits, range(1, d))
        return pltpu.make_async_copy(
            gb.at[index + cut], accs[1].at[(slice(None),) * (d - 1) + cut], lsem.at[u]
        )

    big = [u for u in early if units[u][0] == 1]
    for u in big:
        own_half(u).start()

    peers = [("fsdp", partner_of(me, bits, b), None) for b in range(d)]
    peers += [("seq", lax.rem(rank + k, count), None) for k in range(1, count)]
    greet(peers)

    def hop(u, phase):
        array, r0, nr, c0, nc, which = units[u]
        order = order_list[which]
        b = order[phase]
        free = [x for x in range(d) if x not in order[: phase + 1]]
        cut = (pl.ds(r0, nr), pl.ds(c0, nc))
        index = at_bits(bits, free, {b: 1 - bits[b]})
        src = grads[array].at[index + cut] if phase == 0 else accs[array].at[index[:-1] + cut]
        to = recvs[array][phase].at[(slice(None),) * len(free) + cut]
        return pltpu.make_async_remote_copy(
            src_ref=src, dst_ref=to, send_sem=fsend.at[u, phase], recv_sem=frecv.at[u, phase],
            device_id={"fsdp": partner_of(me, bits, b)}, device_id_type=MESH_ID,
        )

    def add(u, phase):
        array, r0, nr, c0, nc, which = units[u]
        order = order_list[which]
        free = [x for x in range(d) if x not in order[: phase + 1]]
        cut = (slice(r0, r0 + nr), slice(c0, c0 + nc))
        index = at_bits(bits, free)
        hop(u, phase).wait_recv()
        if phase == 0 and array == 1:
            own_half(u).wait()
        base = grads[array][index + cut] if phase == 0 and array != 1 else accs[array][index[:-1] + cut]
        more = recvs[array][phase][(slice(None),) * len(free) + cut]
        accs[array][index[:-1] + cut] = (base.astype(F32) + more.astype(F32)).astype(base.dtype)
        if phase + 1 < d:
            hop(u, phase + 1).start()

    here = at_bits(bits, ())[:-1]

    def root_of(which):
        return (count - 1) // 2 if which == 0 else count // 2

    def z_copy(u, kind, src, to, target):
        return pltpu.make_async_remote_copy(
            src_ref=src, dst_ref=to, send_sem=zsend.at[u, kind], recv_sem=zrecv.at[u, kind],
            device_id={"seq": target}, device_id_type=MESH_ID,
        )

    def z_refs(u):
        array, r0, nr, c0, nc, which = units[u]
        cut = (pl.ds(r0, nr), pl.ds(c0, nc))
        return [x[array].at[cut] for x in (zss, zls, zrs, fins)], root_of(which)

    def z_in(u, step):
        array, r0, nr, c0, nc, which = units[u]
        cut = (slice(r0, r0 + nr), slice(c0, c0 + nc))
        (zs, zl, zr, fin), root = z_refs(u)
        turn = max(root, last - root)

        def own():
            return accs[array][here + cut].astype(F32)

        if step < turn:

            @pl.when((rank < root) & (rank == step))
            def _():
                if step == 0:
                    zss[array][cut] = accs[array][here + cut]
                else:
                    z_copy(u, 0, zs, zl, rank - 1).wait_recv()
                    zss[array][cut] = (own() + zls[array][cut].astype(F32)).astype(zss[array].dtype)
                z_copy(u, 0, zs, zl, rank + 1).start()

            @pl.when((rank > root) & (last - rank == step))
            def _():
                if step == 0:
                    zss[array][cut] = accs[array][here + cut]
                else:
                    z_copy(u, 1, zs, zr, rank + 1).wait_recv()
                    zss[array][cut] = (own() + zrs[array][cut].astype(F32)).astype(zss[array].dtype)
                z_copy(u, 1, zs, zr, rank - 1).start()

        if step == turn:

            @pl.when(rank == root)
            def _():
                total = own()
                if root > 0:
                    z_copy(u, 0, zs, zl, rank - 1).wait_recv()
                    total = total + zls[array][cut].astype(F32)
                if root < last:
                    z_copy(u, 1, zs, zr, rank + 1).wait_recv()
                    total = total + zrs[array][cut].astype(F32)
                fins[array][cut] = total.astype(fins[array].dtype)
                if root > 0:
                    z_copy(u, 2, fin, fin, rank - 1).start()
                if root < last:
                    z_copy(u, 3, fin, fin, rank + 1).start()
                outs[array][cut] = fins[array][cut]

    def z_out(u, step):
        array, r0, nr, c0, nc, which = units[u]
        cut = (slice(r0, r0 + nr), slice(c0, c0 + nc))
        (zs, zl, zr, fin), root = z_refs(u)
        far = step + 1

        if root - far >= 0:

            @pl.when(rank == root - far)
            def _():
                z_copy(u, 2, fin, fin, rank + 1).wait_recv()
                if root - far > 0:
                    z_copy(u, 2, fin, fin, rank - 1).start()
                outs[array][cut] = fins[array][cut]

        if root + far <= last:

            @pl.when(rank == root + far)
            def _():
                z_copy(u, 3, fin, fin, rank - 1).wait_recv()
                if root + far < last:
                    z_copy(u, 3, fin, fin, rank + 1).start()
                outs[array][cut] = fins[array][cut]

    def z_sent(u):
        (zs, zl, zr, fin), root = z_refs(u)

        @pl.when(rank < root)
        def _():
            z_copy(u, 0, zs, zl, rank + 1).wait_send()

        @pl.when(rank > root)
        def _():
            z_copy(u, 1, zs, zr, rank - 1).wait_send()

        @pl.when((rank <= root) & (rank > 0))
        def _():
            z_copy(u, 2, fin, fin, rank - 1).wait_send()

        @pl.when((rank >= root) & (rank < last))
        def _():
            z_copy(u, 3, fin, fin, rank + 1).wait_send()

    moves = []
    for k in range(1, count):
        to = lax.rem(rank + k, count)
        moves.append(
            pltpu.make_async_remote_copy(
                src_ref=genc.at[:, pl.ds(pl.multiple_of(to * erows, 16), erows)],
                dst_ref=ebuf.at[k - 1],
                send_sem=esend.at[k - 1], recv_sem=erecv.at[k - 1],
                device_id={"seq": to}, device_id_type=MESH_ID,
            )
        )
    for move in moves:
        move.start()

    def wants(side, taker, start):
        return seen_from(side, taker, start, STRIP, rows, glen)

    def strip_copy(m, strip, side, target):
        start = strip * STRIP
        if not isinstance(start, int):
            start = pl.multiple_of(start, STRIP)
        return pltpu.make_async_remote_copy(
            src_ref=part.at[m, pl.ds(start, STRIP)],
            dst_ref=inc.at[m, pl.ds(start + side * rows, STRIP)],
            send_sem=tsend.at[m, strip, side], recv_sem=trecv.at[m, strip, side],
            device_id={"seq": target}, device_id_type=MESH_ID,
        )

    def coming(strip, side):
        start = strip * STRIP
        owner = start // rows
        if side == 0:
            return (owner <= rank) & (rank < last) & wants(0, rank + 1, start)
        return (owner >= rank) & (rank > 0) & wants(1, rank - 1, start)

    def going(strip, side):
        start = strip * STRIP
        owner = start // rows
        if side == 0:
            return (owner < rank) & wants(0, rank, start)
        return (owner > rank) & wants(1, rank, start)

    def static_going(strip, side, who):
        start = strip * STRIP
        owner = start // rows
        if side == 0:
            return owner < who <= last and bool(static_wants(0, who, start, rows, glen))
        return owner > who >= 0 and bool(static_wants(1, who, start, rows, glen))

    def pass_on(m, strip, side, who):
        start = strip * STRIP
        at = slice(start, start + STRIP)
        source = who + 1 if side == 0 else who - 1

        @pl.when(rank == who)
        def _():
            if static_going(strip, side, source):
                strip_copy(m, strip, side, source).wait_recv()
                there = slice(start + side * rows, start + side * rows + STRIP)
                part[m, at, :] = (part[m, at, :].astype(F32) + inc[m, there, :].astype(F32)).astype(BF)
            strip_copy(m, strip, side, who - 1 if side == 0 else who + 1).start()

    def finish_rows(m):
        for j in range(rows // STRIP):
            strip = rank * (rows // STRIP) + j
            at = pl.ds(pl.multiple_of(strip * STRIP, STRIP), STRIP)
            mine = slice(j * STRIP, (j + 1) * STRIP)
            tok_out[m, mine, :] += part[m, at, :].astype(F32)
            for side in range(2):

                @pl.when(coming(strip, side))
                def _():
                    strip_copy(m, strip, side, rank).wait_recv()
                    there = pl.ds(pl.multiple_of(strip * STRIP + side * rows, STRIP), STRIP)
                    tok_out[m, mine, :] += inc[m, there, :].astype(F32)

    wkv[:, 0:D] = weight("wk")
    wkv[:, D : 2 * D] = weight("wv")
    gkv[...] = jnp.zeros_like(gkv)

    def begin(m):
        place_info(info, seg_ref, prefix_ref, m)
        dqt[...] = jnp.zeros_like(dqt)
        delta = head_sums(dmix_ref[m].astype(F32) * mix_ref[m, 0:rows, :].astype(F32))
        for pair in range(HEADS // 2):
            at = slice(pair * 128, (pair + 1) * 128)
            for h in range(2):
                row = 2 * pair + h
                span = slice(h * rows, (h + 1) * rows)
                qst[pair, span, :] = head_masked(q_ref[m, 0:rows, at], h)
                dst[pair, span, :] = head_masked(dmix_ref[m, :, at], h)
                stats[pair : pair + 1, span] = lse_ref[m, row : row + 1, :]
                stats[4 + pair : 5 + pair, span] = delta[row : row + 1, :]

    def one_tile(m):
        def body(t, _):
            i = m * tiles + t
            slot = i % 2

            for copy in tile_copies(i, slot):
                copy.wait()

            @pl.when(i + 1 < MICRO * tiles)
            def _():
                for copy in tile_copies(i + 1, 1 - slot):
                    copy.start()

            at_keys = pl.ds(pl.multiple_of(t * TILE, TILE), TILE)
            place = lax.broadcasted_iota(jnp.int32, (TILE, 1), 0) + t * TILE
            key_seg = info[:, at_keys].T[:, 1:2]
            limit = info[0:1, pl.ds(off, rows)]
            seg = info[1:2, pl.ds(off, rows)]
            seen = jnp.where(
                place < prompt, (place.astype(F32) < limit).astype(jnp.int32), (key_seg == seg).astype(jnp.int32)
            )
            mask = jnp.where(seen == 1, 0.0, NEG)
            bias[:, 0:rows] = mask
            bias[:, rows : 2 * rows] = mask

            def one_pair(pair, _):
                at = lanes_of(pair)
                kp, vp = kbuf[slot, :, at], vbuf[slot, :, at]
                prob = jnp.exp(nt(kp, qst[pair]) + bias[...] - stats[pl.ds(pair, 1), :])
                d_score = (prob * (nt(vp, dst[pair]) - stats[pl.ds(4 + pair, 1), :])).astype(BF)
                dkv[:, at] = nn(d_score, qst[pair]).astype(BF)
                dkv[:, pl.ds(pl.multiple_of(D + pair * 128, 128), 128)] = nn(
                    prob.astype(BF), dst[pair]
                ).astype(BF)
                d_q = nn(kp.T, d_score)
                sub = lax.broadcasted_iota(jnp.int32, (128, rows), 0)
                dqt[at, :] += jnp.where(sub < 64, d_q[:, 0:rows], d_q[:, rows : 2 * rows])
                return 0

            lax.fori_loop(0, HEADS // 2, one_pair, 0)
            part[m, at_keys, :] = nt(dkv[...], wkv[...]).astype(BF)
            gkv[...] += tn(xbuf[slot], dkv[...])
            return 0

        return body

    def end(m):
        for pair in range(HEADS // 2):
            at = slice(pair * 128, (pair + 1) * 128)
            dqs[m, :, at] = (dqt[at, :] * SCALE).T.astype(BF)
        if m == 0:
            start_out.wait()
        tok_out[m] += nt(dqs[m], weight("wq"))

    todo = {}

    def later(when, job, *what):
        todo.setdefault(when, []).append(functools.partial(job, *what))

    def plan(some, times):
        for u in some:
            for phase in range(d):
                later(times[min(phase, 2)] + max(phase - 2, 0), add, u, phase)
            at = times[2] + max(d - 3, 0)
            root = root_of(units[u][5])
            turn = max(root, last - root)
            for step in range(turn + 1):
                later(at + step, z_in, u, step)
            for step in range(last):
                later(at + turn + 1 + step, z_out, u, step)

    def begin_sum(some):
        for u in some:
            hop(u, 0).start()

    for c, times in enumerate(SLOTS):
        plan(early[2 * c : 2 * c + 2], times[1:])
        later(times[0], begin_sum, early[2 * c : 2 * c + 2])
    per = MICRO * tiles // GROUPS
    strips = TILE // STRIP
    passes = []
    for i in range(GROUPS):
        m, t0 = i * per // tiles, (i * per) % tiles
        for strip in range(t0 * strips, (t0 + per) * strips):
            for dist in range(count):
                for side in range(2):
                    who = last - dist if side == 0 else dist
                    if static_going(strip, side, who):
                        passes.append((m, strip, side, who))
                        later(i + 2 * (dist if side == 0 else max(dist - 1, 0)), pass_on, m, strip, side, who)
    later(GROUPS - 2, finish_rows, 0)

    for job in todo.pop(-2, []):
        job()
    for i in range(GROUPS):
        m, t0 = i * per // tiles, (i * per) % tiles
        if t0 == 0:
            begin(m)
        if i == 0:
            for job in todo.pop(-1, []):
                job()
        lax.fori_loop(t0, t0 + per, one_tile(m), 0)
        if t0 + per == tiles:
            end(m)
        for job in todo.pop(i, []):
            job()

    def put(name, value):
        start, size = table[name]
        where = (slice(None),) * d + (slice(start, start + size),)
        ga[where] = value.astype(BF).reshape((2,) * d + (size, D))

    put("wk", gkv[:, 0:D])
    put("wv", gkv[:, D : 2 * D])
    begin_sum(late[0:2])
    put("wq", tn(tok_ref[...].reshape(MICRO * rows, D), dqs[...].reshape(MICRO * rows, D)))
    begin_sum(late[2:4])
    for c in range(2):
        plan(late[2 * c : 2 * c + 2], (GROUPS + c, GROUPS + c + 1, GROUPS + c + 2))
    for i in sorted(todo):
        for job in todo[i]:
            job()
    finish_rows(1)
    for move in moves:
        move.wait_recv()
    emine = pl.ds(pl.multiple_of(rank * erows, 16), erows)
    for m in range(MICRO):
        states = genc[m, emine, :].astype(F32)
        for k in range(1, count):
            states = states + ebuf[k - 1, m].astype(F32)
        enc_out[m] = states
    for move in moves:
        move.wait_send()
    for m, strip, side, who in passes:

        @pl.when(rank == who)
        def _():
            strip_copy(m, strip, side, who - 1 if side == 0 else who + 1).wait_send()

    for u in range(len(units)):
        for phase in range(d):
            hop(u, phase).wait_send()
        z_sent(u)


def back(n, count, q, mix, dmix, lse, tok, wa, genc, gs, seg, prefix, x_all, k, v, dr1, gb):
    rows = tok.shape[1]
    erows = genc.shape[1] // count
    glen = count * rows
    d = bit_count(n)
    units = len(weight_units(n)) + 3
    dma = pltpu.SemaphoreType.DMA
    V = pltpu.VMEM
    hbm = pl.BlockSpec(memory_space=pl.ANY)
    flat = [(wa.shape[-2], D), (gb.shape[-2], D), (16, 128)]
    types = [BF, BF, F32]
    scratch = [V((2,) * (d - 1) + f, t) for f, t in zip(flat, types)]
    for _ in range(4):
        scratch += [V(f, t) for f, t in zip(flat, types)]
    for f, t in zip(flat, types):
        scratch += [V((2,) * (d - 1 - p) + f, t) for p in range(d)]
    scratch += [
        V((count - 1, MICRO, erows, D), BF),
        V((2,) * d + flat[0], BF),
        V((MICRO, glen, D), BF), V((MICRO, glen + rows, D), BF),
        V((D, 2 * D), BF),
        V((HEADS // 2, 2 * rows, 128), BF), V((HEADS // 2, 2 * rows, 128), BF),
        V((8, 2 * rows), F32), V((8, glen), F32), V((TILE, 2 * rows), F32),
        V((D, rows), F32), V((TILE, 2 * D), BF), V((D, 2 * D), F32),
        V((MICRO, rows, D), BF),
        V((2, TILE, D), BF), V((2, TILE, D), BF), V((2, TILE, D), BF),
    ]
    strips = glen // STRIP
    scratch += [
        dma((units, d)), dma((units, d)), dma((units, 4)), dma((units, 4)),
        dma((MICRO, strips, 2)), dma((MICRO, strips, 2)), dma((count - 1,)), dma((count - 1,)),
        dma((units,)), dma((2, 3)), dma(()),
    ]
    return pl.pallas_call(
        functools.partial(back_kernel, n, count, rows, erows),
        in_specs=[VM] * 9 + [SMEM] + [hbm] * 5,
        out_specs=[VM] * 5,
        out_shape=[jax.ShapeDtypeStruct(f, t) for f, t in zip(flat, types)]
        + [jax.ShapeDtypeStruct((MICRO, rows, D), F32), jax.ShapeDtypeStruct((MICRO, erows, D), F32)],
        scratch_shapes=scratch,
        compiler_params=pltpu.CompilerParams(
            collective_id=1, has_side_effects=True, vmem_limit_bytes=60 * MIB
        ),
        name="back",
    )(q, mix, dmix, lse, tok, wa, genc, gs, seg, prefix, x_all, k, v, dr1, gb)


FIRST = ("wq", "wk", "wv", "wout", "cq", "ck", "cv", "cout", "up")


def finish_kernel(n, *refs):
    oa, ob, os, tok, states = refs[0:5]
    outs = list(refs[5:])
    table_a, _ = qkv_rows(n)
    table_b, _ = rest_rows(n)
    outs[0][...] = tok[...]
    outs[1][...] = states[...]

    def matrix(name, out):
        table, src = (table_a, oa) if name in table_a else (table_b, ob)
        start, size = table[name]
        if name == "up":
            piece = size // 4
            for c in range(4):
                out[:, c * D : (c + 1) * D] = src[start + c * piece : start + (c + 1) * piece, :].astype(F32)
        else:
            out[...] = src[start : start + size, :].astype(F32)

    for name, out in zip(FIRST, outs[2:11]):
        matrix(name, out)
    edge, side = FF // n, D // n
    wide = outs[11]
    wide[...] = os[8 : 8 + max(1, edge // 128), 0 : min(edge, 128)].reshape(edge)
    matrix("down", outs[12])
    for k in range(7):
        outs[13 + k][...] = os[k : k + 1, 0:side].reshape(side)
    matrix("slot", outs[20])


def finish(n, oa, ob, os, tok, states):
    side, edge = D // n, FF // n
    square = (side, D)
    shapes = [tok.shape, states.shape] + [square] * 8 + [(side, FF), (edge,), (edge, D)]
    shapes += [(side,)] * 7 + [(2 * side, D)]
    return pl.pallas_call(
        functools.partial(finish_kernel, n),
        in_specs=[VM] * 5,
        out_specs=[VM] * len(shapes),
        out_shape=[jax.ShapeDtypeStruct(shape, F32) for shape in shapes],
        compiler_params=pltpu.CompilerParams(vmem_limit_bytes=60 * MIB),
        name="finish",
    )(oa, ob, os, tok, states)


def on_device(
    tokens, encoded, segment_ids, prefix_len, cotangent,
    w_query, w_key, w_value, w_out, c_query, c_key, c_value, c_out,
    w_up, b_up, w_down, b_down,
    gain_one, shift_one, gain_two, shift_two, gain_three, shift_three, w_slot,
):
    n = lax.axis_size("fsdp")
    count = lax.axis_size("seq")
    tokens = tokens[:, 0]
    rows = tokens.shape[1]
    prefix = prefix_len[:, 0]
    cot = cotangent[:, 0]

    shards = (w_query, w_key, w_value, w_out, c_query, c_key, c_value, c_out, w_up, w_down, w_slot)
    vectors = (b_down, gain_one, shift_one, gain_two, shift_two, gain_three, shift_three, b_up)
    (
        wa, wb, small_all, x_all, e_all, previous, edges, q, k, v, mix, lse
    ) = front(n, count, shards, vectors, tokens, encoded[:, 0], cot, segment_ids, prefix)
    wa = wa.reshape((n,) + wa.shape[-2:])
    wb = wb.reshape((n,) + wb.shape[-2:])
    small_all = small_all.reshape(n, 16, 128)
    slot_out, dmix, dr1, genc, gb, gs = middle(
        mix, tokens, edges, e_all, cot, previous, segment_ids, prefix, wb, small_all, rows
    )
    lead = (2,) * bit_count(n)
    gb = gb.reshape(lead + gb.shape[1:])
    gs = gs.reshape(lead + (16, 128))
    oa, ob, os, grad_tokens, grad_encoded = back(
        n, count, q, mix, dmix, lse, tokens, wa, genc, gs, segment_ids, prefix, x_all, k, v, dr1, gb
    )
    grad_tokens, grad_encoded, *others = finish(n, oa, ob, os, grad_tokens, grad_encoded)
    return (slot_out[:, None], grad_tokens[:, None], grad_encoded[:, None], *others)


def solution(mesh):
    act = P(None, "fsdp", "seq", None)
    ids = P(None, "fsdp", None)
    mat, one = P("fsdp", None), P("fsdp")
    in_specs = (
        (act, act, ids, ids, act) + (mat,) * 9 + (one, mat) + (one,) * 7 + (mat,)
    )
    out_specs = (act, act, act) + (mat,) * 9 + (one, mat) + (one,) * 7 + (mat,)
    return jax.shard_map(
        on_device, mesh=mesh, in_specs=in_specs, out_specs=out_specs, check_vma=False
    )
```

```python
import functools
import math

import jax
import jax.numpy as jnp
from jax import lax
from jax.experimental import pallas as pl
from jax.experimental.pallas import tpu as pltpu
from jax.sharding import PartitionSpec as P

D = 512
HD = 64
HEADS = 8
FF = 2048
MICRO = 2
HALO = 16
EPSILON = 1e-05
BF = jnp.bfloat16
F32 = jnp.float32
SCALE = 1.0 / math.sqrt(HD)
NEG = -1e30
MIB = 1024 * 1024
GELU_C = math.sqrt(2.0 / math.pi)

VM = pl.BlockSpec(memory_space=pltpu.VMEM)


def nn(a, b):
    return lax.dot_general(a, b, (((1,), (0,)), ((), ())), preferred_element_type=F32)


def nt(a, b):
    return lax.dot_general(a, b, (((1,), (1,)), ((), ())), preferred_element_type=F32)


def tn(a, b):
    return lax.dot_general(a, b, (((0,), (0,)), ((), ())), preferred_element_type=F32)


def lanes_of(pair):
    return pl.ds(pl.multiple_of(pair * 128, 128), 128)


def head_masked(value, head):
    lane = lax.broadcasted_iota(jnp.int32, value.shape, 1)
    return jnp.where((lane >= 64) == (head == 1), value, jnp.zeros_like(value))


def softmax_parts(scores):
    top = jnp.max(scores, axis=-1, keepdims=True)
    raw = jnp.exp(scores - top)
    total = jnp.sum(raw, axis=-1, keepdims=True)
    return raw, top, total


def attend_pair(query_pair, key_pair, value_pair, bias, pair, lse_ref):
    mixed = []
    for head in range(2):
        scores = nt(head_masked(query_pair, head), key_pair)
        if bias is not None:
            scores = scores + bias
        raw, top, total = softmax_parts(scores)
        mixed.append(nn(raw.astype(BF), value_pair) / total)
        lane = lax.broadcasted_iota(jnp.int32, lse_ref.shape, 1)
        lse_ref[...] = jnp.where(lane == pair * 2 + head, top + jnp.log(total), lse_ref[...])
    lane = lax.broadcasted_iota(jnp.int32, mixed[0].shape, 1)
    return jnp.where(lane < 64, mixed[0], mixed[1])


def attend_far(query_pair, key_pair, value_pair, bias, pair, mixed_ref, top_ref, total_ref):
    mixed = []
    lane = lax.broadcasted_iota(jnp.int32, top_ref.shape, 1)
    for head in range(2):
        raw, top, total = softmax_parts(nt(head_masked(query_pair, head), key_pair) + bias)
        mixed.append(nn(raw.astype(BF), value_pair))
        top_ref[...] = jnp.where(lane == pair * 2 + head, top, top_ref[...])
        total_ref[...] = jnp.where(lane == pair * 2 + head, total, total_ref[...])
    mixed_ref[:, lanes_of(pair)] = jnp.where(lane < 64, mixed[0], mixed[1])


def attend_near(
    query_pair, key_pair, value_pair, bias, pair, lse_ref, mixed_ref, top_ref, total_ref
):
    mixed = []
    lane = lax.broadcasted_iota(jnp.int32, lse_ref.shape, 1)
    far = mixed_ref[:, lanes_of(pair)]
    for head in range(2):
        mine = lane == pair * 2 + head
        far_top = jnp.sum(jnp.where(mine, top_ref[...], 0.0), axis=1, keepdims=True)
        far_total = jnp.sum(jnp.where(mine, total_ref[...], 0.0), axis=1, keepdims=True)
        scores = nt(head_masked(query_pair, head), key_pair) + bias
        top = jnp.maximum(jnp.max(scores, axis=-1, keepdims=True), far_top)
        raw = jnp.exp(scores - top)
        weight = jnp.exp(far_top - top)
        total = jnp.sum(raw, axis=-1, keepdims=True) + far_total * weight
        mixed.append((nn(raw.astype(BF), value_pair) + far * weight) / total)
        lse_ref[...] = jnp.where(mine, top + jnp.log(total), lse_ref[...])
    return jnp.where(lane < 64, mixed[0], mixed[1])


def bit_count(n):
    return n.bit_length() - 1


def qkv_rows(n):
    piece = D // n
    return {"wq": (0, piece), "wk": (piece, piece), "wv": (2 * piece, piece)}, 3 * piece


def rest_rows(n):
    piece = D // n
    table, start = {}, 0
    for name, times in (
        ("wout", 1), ("cq", 1), ("ck", 1), ("cv", 1), ("cout", 1), ("up", 4), ("down", 4), ("slot", 2)
    ):
        table[name] = (start, times * piece)
        start += times * piece
    return table, start


def square(ref, table, name):
    start, count = table[name]
    return ref[:, start : start + count, :].reshape(D, D)


def up_part(ref, table, c):
    start, count = table["up"]
    piece = count // 4
    return ref[:, start + c * piece : start + (c + 1) * piece, :].reshape(D, D)


def row_part(ref, table, name, c):
    start, count = table[name]
    many = D // count
    return ref[c * many : (c + 1) * many, start : start + count, :].reshape(D, D)


def store_square(ref, table, name, value):
    start, count = table[name]
    ref[:, start : start + count, :] = value.reshape(ref.shape[0], count, D)


def store_up(ref, table, c, value):
    start, count = table["up"]
    piece = count // 4
    ref[:, start + c * piece : start + (c + 1) * piece, :] = value.reshape(ref.shape[0], piece, D)


def store_part(ref, table, name, c, value):
    start, count = table[name]
    many = D // count
    ref[c * many : (c + 1) * many, start : start + count, :] = value.reshape(many, count, D)


def my_place(n):
    me = lax.axis_index("fsdp")
    bits = [(me // (1 << b)) % 2 for b in range(bit_count(n))]
    return me, bits


def partner_of(me, bits, b):
    return me + (1 - 2 * bits[b]) * (1 << b)


def orders(n):
    d = bit_count(n)
    far = list(range(1, d))
    return [far + [0], far[::-1] + [0]]


def at_bits(bits, free, fixed=None):
    fixed = fixed or {}
    return tuple(
        slice(None) if b in free else fixed.get(b, bits[b]) for b in range(len(bits) - 1, -1, -1)
    )


MESH_ID = pl.DeviceIdType.MESH

def place_info(info, seg_ref, prefix_ref, m):
    glen = info.shape[1]
    prompt = glen // 3
    seg = jnp.broadcast_to(seg_ref[m], (8, glen))
    limit = jnp.where(seg == 0, prompt, 0)
    for c in range(prefix_ref.shape[1]):
        limit = jnp.where(seg == c + 1, prefix_ref[m, c], limit)
    place = lax.broadcasted_iota(jnp.int32, (8, glen), 1)
    after = (seg == pltpu.roll(seg, glen - 1, 1)) & (place < glen - 1)
    before = (seg == pltpu.roll(seg, 1, 1)) & (place > 0)
    sub = lax.broadcasted_iota(jnp.int32, (8, glen), 0)
    mixed = jnp.where(sub == 0, limit, seg)
    mixed = jnp.where(sub == 2, after.astype(jnp.int32), mixed)
    mixed = jnp.where(sub == 3, before.astype(jnp.int32), mixed)
    info[...] = mixed.astype(F32)


SMEM = pl.BlockSpec(memory_space=pltpu.SMEM)


def spread_rows(tiles, first, count, width, out):
    group = max(1, 128 // width)
    lane = lax.broadcasted_iota(jnp.int32, (count, 128), 1)
    for p in range(tiles.shape[0] // group):
        block = tiles[p * group, first : first + count, :]
        for j in range(1, group):
            piece = pltpu.roll(tiles[p * group + j, first : first + count, :], j * width, 1)
            block = jnp.where(lane >= j * width, piece, block)
        out[0:count, p * 128 : (p + 1) * 128] = block


def gather_rows(values, count, width, tiles, first):
    group = max(1, 128 // width)
    for i in range(tiles.shape[0]):
        p, j = i // group, i % group
        block = values[0:8, p * 128 : (p + 1) * 128]
        if j:
            block = pltpu.roll(block, 128 - j * width, 1)
        tiles[i, first : first + count, :] = block[0:count]


def norm_forward(residual, gain, shift):
    average = jnp.mean(residual, axis=-1, keepdims=True)
    centred = residual - average
    variance = jnp.mean(centred * centred, axis=-1, keepdims=True)
    rstd = lax.rsqrt(variance + EPSILON)
    hat = centred * rstd
    return hat * gain + shift, hat, rstd


def norm_backward(upstream, hat, rstd, gain):
    d_hat = upstream * gain
    mean_d = jnp.mean(d_hat, axis=-1, keepdims=True)
    mean_dh = jnp.mean(d_hat * hat, axis=-1, keepdims=True)
    d_gain = jnp.sum(upstream * hat, axis=0, keepdims=True)
    d_shift = jnp.sum(upstream, axis=0, keepdims=True)
    return rstd * (d_hat - mean_d - hat * mean_dh), d_gain, d_shift


def gelu_parts(value):
    square = value * value
    t = jnp.tanh(GELU_C * value * (1.0 + 0.044715 * square))
    half = 0.5 * (1.0 + t)
    slope = half + 0.5 * value * (1.0 - t * t) * (GELU_C * (1.0 + 3.0 * 0.044715 * square))
    return value * half, slope


def head_sums(product_rows):
    rows, cols = 16, product_rows.shape[1]
    head = lax.broadcasted_iota(jnp.int32, (rows, cols), 0)
    lane = lax.broadcasted_iota(jnp.int32, (rows, cols), 1)
    pick = ((lane // HD) == head).astype(F32)
    return lax.dot_general(
        pick, product_rows, (((1,), (1,)), ((), ())),
        preferred_element_type=F32, precision=lax.Precision.HIGHEST,
    )[0:HEADS, :]


def middle_kernel(
    rows, enc,
    mix_ref, x_ref, edge_ref, e_ref, cot_ref, prev_ref, seg_ref, prefix_ref,
    w_hbm, small_ref,
    slot_out, dmix_out, dr1_out, genc_out, g_out, gs_out,
    w_ref, g_ref, bup_ref, vec_ref, gbup, gvec, wsem, gsem,
    lowx, lown, cqs, cks, cvs, lse_sc, lse_row, cmix, h1s, hats, rstds, slope,
    act, dpre, dffn, dcross, dcqs, dattn, dcks, dcvs, ckt, h3s, h2low, info, shs,
):
    ext = rows + HALO
    n = w_ref.shape[0]
    table, _ = rest_rows(n)
    piece = D // n
    spans = ((0, 5 * piece), (5 * piece, 4 * piece), (9 * piece, 4 * piece), (13 * piece, 2 * piece))

    def part_copy(k, out=False):
        cut = pl.ds(*spans[k])
        if out:
            return pltpu.make_async_copy(g_ref.at[:, cut], g_out.at[:, cut], gsem.at[k])
        return pltpu.make_async_copy(w_hbm.at[:, cut], w_ref.at[:, cut], wsem.at[k])

    for k in range(4):
        part_copy(k).start()
    spread_rows(small_ref, 0, 8, D // n, vec_ref)
    edge = FF // n
    if edge >= 128:
        for i in range(n):
            for r in range(edge // 128):
                lane = i * edge + r * 128
                bup_ref[0:1, lane : lane + 128] = small_ref[i, 8 + r : 9 + r, :]
    else:
        spread_rows(small_ref, 8, 1, edge, bup_ref)
    part_copy(0).wait()
    gbup[...] = jnp.zeros_like(gbup)
    gvec[...] = jnp.zeros_like(gvec)

    def vec(i):
        return vec_ref[i : i + 1, :]

    def one_micro(m, _):
        own = pl.ds(0, rows)
        attn = nn(mix_ref[m], square(w_ref, table, "wout"))
        x_rows = jnp.concatenate([x_ref[m], edge_ref[m]], axis=0).astype(F32)
        h1, hat, rstd = norm_forward(x_rows + attn, vec(1), vec(2))
        h1s[...] = h1
        dr1_out[m] = hat[0:rows]
        rstds[:, 0:1] = rstd[0:rows]
        h1_low = h1.astype(BF)
        lown[0, m] = h1_low[0:rows]
        cqs[...] = (nn(h1_low, square(w_ref, table, "cq")).astype(BF) * SCALE).astype(BF)
        cks[...] = nn(e_ref[m], square(w_ref, table, "ck")).astype(BF)
        cvs[...] = nn(e_ref[m], square(w_ref, table, "cv")).astype(BF)

        def cross_pair(pair, _):
            at = lanes_of(pair)
            mix = attend_pair(cqs[:, at], cks[:, at], cvs[:, at], None, pair, lse_sc)
            cmix[:, at] = mix.astype(BF)
            return 0

        lax.fori_loop(0, HEADS // 2, cross_pair, 0)
        lse_row[0:HEADS, :] = lse_sc[0:rows, :].T[0:HEADS, :]
        lowx[m] = cmix[0:rows, :]
        h2, hat, rstd = norm_forward(
            h1s[...] + nn(cmix[...], square(w_ref, table, "cout")), vec(3), vec(4)
        )
        h1s[...] = h2
        hats[...] = hat[0:rows]
        rstds[:, 1:2] = rstd[0:rows]
        h2low[...] = h2.astype(BF)
        lown[1, m] = h2low[0:rows, :]
        @pl.when(m == 0)
        def _():
            for k in range(1, 4):
                part_copy(k).wait()

        h3s[...] = jnp.zeros_like(h3s)

        for c in range(FF // D):
            at = slice(c * D, (c + 1) * D)
            pre = nn(h2low[...], up_part(w_ref, table, c)) + bup_ref[0:1, at]
            value, grad = gelu_parts(pre)
            value = value.astype(BF)
            act[m, :, at] = value[0:rows]
            slope[:, at] = grad[0:rows]
            down = row_part(w_ref, table, "down", c)
            h3s[...] += nn(value, down)
        h3, hat, rstd = norm_forward(h1s[...] + h3s[...] + vec(0), vec(5), vec(6))
        h3_low = h3.astype(BF)
        h3s[...] = h3_low.astype(F32)
        lown[2, m] = h3_low[0:rows]
        top = row_part(w_ref, table, "slot", 0)
        bottom = row_part(w_ref, table, "slot", 1)
        place_info(info, seg_ref, prefix_ref, m)
        flags = info[:, pl.ds(pl.multiple_of(lax.axis_index("seq") * rows, 128), rows)].T
        follow = (h3s[pl.ds(1, rows), :] * flags[:, 2:3]).astype(BF)
        slot_out[m] = (nn(h3_low[0:rows], top) + nn(follow, bottom)).astype(BF)
        h3s[0:8, :] = prev_ref[m].astype(F32)[HALO - 8 : HALO]
        h3s[8 : rows + 8, :] = cot_ref[m].astype(F32)
        shifted = h3s[pl.ds(7, rows), :]
        shs[m] = (shifted * flags[:, 3:4]).astype(BF)
        d_follow = nt(shifted.astype(BF), bottom).astype(BF).astype(F32) * flags[:, 3:4]
        d_three = nt(cot_ref[m], top) + d_follow
        d_r3, d_gain, d_shift = norm_backward(d_three, hat[0:rows], rstd[0:rows], vec(5))
        gvec[5:6, :] += d_gain
        gvec[6:7, :] += d_shift
        d_ffn = d_r3.astype(BF)
        dffn[m] = d_ffn
        gvec[0:1, :] += jnp.sum(d_ffn.astype(F32), axis=0, keepdims=True)
        d_two = d_r3
        for c in range(FF // D):
            at = slice(c * D, (c + 1) * D)
            down = row_part(w_ref, table, "down", c)
            grad = (nt(d_ffn, down) * slope[:, at]).astype(BF)
            dpre[m, :, at] = grad
            gbup[0:1, at] += jnp.sum(grad.astype(F32), axis=0, keepdims=True)
            d_two = d_two + nt(grad, up_part(w_ref, table, c))
        d_r2, d_gain, d_shift = norm_backward(d_two, hats[...], rstds[:, 1:2], vec(3))
        gvec[3:4, :] += d_gain
        gvec[4:5, :] += d_shift
        d_cross = d_r2.astype(BF)
        dcross[m] = d_cross
        d_cmix = nt(d_cross, square(w_ref, table, "cout")).astype(BF)
        dmix_out[m] = d_cmix
        delta = head_sums(d_cmix.astype(F32) * cmix[0:rows, :].astype(F32))
        lse_row[HEADS : 2 * HEADS, :] = delta
        ckt[...] = cks[...].T

        def cross_back(pair, _):
            at = lanes_of(pair)
            kp, vp = cks[:, at], cvs[:, at]
            qp, dp = cqs[0:rows, at], dmix_out[m, :, at]
            kt = ckt[at, :]
            d_k = d_v = None
            d_qt = []
            for head in range(2):
                qm, dm = head_masked(qp, head), head_masked(dp, head)
                row = pair * 2 + head
                prob = jnp.exp(nt(kp, qm) - lse_row[pl.ds(row, 1), :])
                d_score = (prob * (nt(vp, dm) - lse_row[pl.ds(HEADS + row, 1), :])).astype(BF)
                dk, dv = nn(d_score, qm), nn(prob.astype(BF), dm)
                d_k = dk if d_k is None else d_k + dk
                d_v = dv if d_v is None else d_v + dv
                d_qt.append(nn(kt, d_score))
            sub = lax.broadcasted_iota(jnp.int32, d_qt[0].shape, 0)
            d_q = jnp.where(sub < 64, d_qt[0], d_qt[1]) * SCALE
            dcqs[m, :, at] = d_q.T.astype(BF)
            dcks[m, :, at] = d_k.astype(BF)
            dcvs[m, :, at] = d_v.astype(BF)
            return 0

        lax.fori_loop(0, HEADS // 2, cross_back, 0)
        genc_out[m] = (
            nt(dcks[m], square(w_ref, table, "ck")) + nt(dcvs[m], square(w_ref, table, "cv"))
        ).astype(BF)
        d_one = d_r2 + nt(dcqs[m], square(w_ref, table, "cq"))
        d_r1, d_gain, d_shift = norm_backward(d_one, dr1_out[m], rstds[:, 0:1], vec(1))
        gvec[1:2, :] += d_gain
        gvec[2:3, :] += d_shift
        dr1_out[m] = d_r1
        d_attn = d_r1.astype(BF)
        dattn[m] = d_attn
        dmix_out[m] = nt(d_attn, square(w_ref, table, "wout")).astype(BF)
        return 0

    lax.fori_loop(0, MICRO, one_micro, 0)

    total = MICRO * rows

    def flat(ref, *lead):
        return ref[lead].reshape(total, D) if lead else ref[...].reshape(total, D)

    def grad_of(left, right):
        return tn(left, right).astype(BF)

    cot = cot_ref[...].reshape(total, D)
    flagged = shs[...].reshape(total, D)
    h3_all = lown[2].reshape(total, D)
    store_part(g_ref, table, "slot", 0, grad_of(h3_all, cot))
    store_part(g_ref, table, "slot", 1, grad_of(h3_all, flagged))
    part_copy(3, True).start()
    dffn_all = dffn[...].reshape(total, D)
    h2_all = lown[1].reshape(total, D)
    for c in range(FF // D):
        at = slice(c * D, (c + 1) * D)
        store_part(g_ref, table, "down", c, grad_of(act[:, :, at].reshape(total, D), dffn_all))
        store_up(g_ref, table, c, grad_of(h2_all, dpre[:, :, at].reshape(total, D)))
    part_copy(2, True).start()
    part_copy(1, True).start()
    store_square(g_ref, table, "cout", grad_of(lowx[...].reshape(total, D), dcross[...].reshape(total, D)))
    store_square(g_ref, table, "cq", grad_of(lown[0].reshape(total, D), dcqs[...].reshape(total, D)))
    e_all = e_ref[...].reshape(MICRO * enc, D)
    store_square(g_ref, table, "ck", grad_of(e_all, dcks[...].reshape(MICRO * enc, D)))
    store_square(g_ref, table, "cv", grad_of(e_all, dcvs[...].reshape(MICRO * enc, D)))
    mix_all = jnp.concatenate([mix_ref[m, 0:rows, :] for m in range(MICRO)], axis=0)
    store_square(g_ref, table, "wout", grad_of(mix_all, dattn[...].reshape(total, D)))
    part_copy(0, True).start()
    gs_out[...] = jnp.zeros_like(gs_out)
    gather_rows(gvec, 8, D // n, gs_out, 0)
    if edge >= 128:
        for i in range(n):
            for r in range(edge // 128):
                lane = i * edge + r * 128
                gs_out[i, 8 + r : 9 + r, :] = gbup[0:1, lane : lane + 128]
    else:
        gather_rows(gbup, 1, edge, gs_out, 8)
    for k in range(4):
        part_copy(k, True).wait()


def middle(mix, tokens, edges, e_all, cot, prev, seg, prefix, w, small, rows):
    glen = seg.shape[2]
    enc = e_all.shape[1]
    ext = rows + HALO
    out_shape = [
        jax.ShapeDtypeStruct((MICRO, rows, D), BF),
        jax.ShapeDtypeStruct((MICRO, rows, D), BF),
        jax.ShapeDtypeStruct((MICRO, rows, D), F32),
        jax.ShapeDtypeStruct((MICRO, enc, D), BF),
        jax.ShapeDtypeStruct(w.shape, BF),
        jax.ShapeDtypeStruct(small.shape, F32),
    ]
    V = pltpu.VMEM
    hbm = pl.BlockSpec(memory_space=pl.ANY)
    scratch = [
        V(w.shape, BF), V(w.shape, BF), V((8, FF), F32), V((8, D), F32),
        V((8, FF), F32), V((8, D), F32),
        pltpu.SemaphoreType.DMA((4,)), pltpu.SemaphoreType.DMA((4,)),
        V((MICRO, rows, D), BF),
        V((3, MICRO, rows, D), BF),
        V((ext, D), BF), V((enc, D), BF), V((enc, D), BF),
        V((ext, 128), F32), V((2 * HEADS, rows), F32),
        V((ext, D), BF),
        V((ext, D), F32),
        V((rows, D), F32), V((rows, 128), F32),
        V((rows, FF), F32),
        V((MICRO, rows, FF), BF), V((MICRO, rows, FF), BF),
        V((MICRO, rows, D), BF), V((MICRO, rows, D), BF), V((MICRO, rows, D), BF),
        V((MICRO, rows, D), BF),
        V((MICRO, enc, D), BF), V((MICRO, enc, D), BF),
        V((D, enc), BF),
        V((ext, D), F32), V((ext, D), BF),
        V((8, glen), F32), V((MICRO, rows, D), BF),
    ]
    return pl.pallas_call(
        functools.partial(middle_kernel, rows, enc),
        in_specs=[VM] * 7 + [SMEM, hbm, VM],
        out_specs=[VM] * 4 + [hbm, VM],
        out_shape=out_shape,
        scratch_shapes=scratch,
        compiler_params=pltpu.CompilerParams(vmem_limit_bytes=61 * MIB),
        name="middle",
    )(mix, tokens, edges, e_all, cot, prev, seg, prefix, w, small)


def weight_units(n):
    piece = D // n
    units = []
    for array, start, count in (
        (0, 0, 3 * piece), (1, 0, 5 * piece), (1, 5 * piece, 4 * piece),
        (1, 9 * piece, 4 * piece), (1, 13 * piece, 2 * piece),
    ):
        for half in range(2):
            units.append((array, start, count, half * 256, 256, half))
    return units


def greet(peers):
    barrier = pltpu.get_barrier_semaphore()
    for axis, target, when in peers:
        if when is None:
            pl.semaphore_signal(barrier, inc=1, device_id={axis: target}, device_id_type=MESH_ID)
        else:

            @pl.when(when)
            def _():
                pl.semaphore_signal(barrier, inc=1, device_id={axis: target}, device_id_type=MESH_ID)

    always = sum(1 for peer in peers if peer[2] is None)
    amount = jnp.int32(always)
    for axis, target, when in peers:
        if when is not None:
            amount = amount + when.astype(jnp.int32)
    pl.semaphore_wait(barrier, amount if always < len(peers) else always)


STRIP = 128


def key_span(rank, rows, glen):
    prompt = glen // 3
    least = (glen - prompt) // 8
    most = (glen - prompt) - 3 * least
    first, stop = rank * rows, (rank + 1) * rows + 1
    low = jnp.maximum(first - most, jnp.where(first >= prompt + most, prompt + least, prompt))
    high = jnp.minimum(stop + most, jnp.where(stop <= glen - most, glen - least, glen))
    return low, jnp.where(stop > prompt, high, 0)


class Chain:
    def __init__(self, ref, rows, strips, sems, lane, rank, count, needed):
        self.ref, self.rows, self.lane, self.needed = ref, rows, lane, needed
        self.strips, self.height = strips, rows // strips
        self.send, self.recv = sems
        self.rank, self.count = rank, count

    def copy(self, side, step, j, block, target):
        at = pl.ds(pl.multiple_of(block * self.rows + j * self.height, 16), self.height)
        part = self.ref.at[:, at] if len(self.ref.shape) == 3 else self.ref.at[at]
        return pltpu.make_async_remote_copy(
            src_ref=part, dst_ref=part,
            send_sem=self.send.at[self.lane, side, step, j],
            recv_sem=self.recv.at[self.lane, side, step, j],
            device_id={"seq": target}, device_id_type=MESH_ID,
        )

    def goes(self, side, sender, block, j):
        last = self.count - 1
        if side == 0:
            there = (sender >= 0) & (sender < last) & (block >= 0)
            taker = sender + 1
        else:
            there = (sender <= last) & (sender > 0) & (block <= last)
            taker = sender - 1
        if self.needed is None:
            return there
        return there & self.needed(side, taker, block * self.rows + j * self.height, self.height)

    def outgoing(self, step, j, act):
        r = self.rank
        for side, block, target in ((0, r - step, r + 1), (1, r + step, r - 1)):

            @pl.when(self.goes(side, r, block, j))
            def _():
                act(self.copy(side, step, j, block, target))

    def start(self, step):
        for j in range(self.strips):
            self.outgoing(step, j, lambda c: c.start())

    def arrived(self, step, onward):
        r = self.rank
        for j in range(self.strips):
            for side, block, source in ((0, r - 1 - step, r - 1), (1, r + 1 + step, r + 1)):

                @pl.when(self.goes(side, source, block, j))
                def _():
                    self.copy(side, step, j, block, source).wait_recv()

            if onward:
                self.outgoing(step + 1, j, lambda c: c.start())

    def sent(self, step):
        for j in range(self.strips):
            self.outgoing(step, j, lambda c: c.wait_send())


def front_kernel(n, count, rows, erows, *refs):
    shards = refs[0:11]
    tok, enc, cot, seg_ref, prefix_ref = refs[11:16]
    vectors = refs[16:24]
    (
        wa_out, wb, small_all, x_out, e_all, prev, halo_out, q_out, k_out, v_out, mix_ref, lse_out
    ) = refs[24:36]
    wa, x_all, q_ref, k_ref, v_ref = refs[36:41]
    far_mix, far_top, far_total = refs[41:44]
    stage, bias, lse_sc, info, local, fsend, frecv, zsend, zrecv, csend, crecv, osem = refs[44:]
    me, bits = my_place(n)
    rank = lax.axis_index("seq")
    last = count - 1
    glen = count * rows
    prompt = glen // 3
    piece = D // n
    d = bit_count(n)

    here = at_bits(bits, ())
    table_a, _ = qkv_rows(n)
    table_b, _ = rest_rows(n)
    copies = []

    def keep(src, dst):
        copy = pltpu.make_async_copy(src, dst, local.at[len(copies)])
        copy.start()
        copies.append(copy)

    keep(tok, x_all.at[:, pl.ds(pl.multiple_of(rank * rows, 16), rows)])
    keep(enc, e_all.at[:, pl.ds(pl.multiple_of(rank * erows, 16), erows)])
    names = ("wq", "wk", "wv", "wout", "cq", "ck", "cv", "cout", "up", "down", "slot")
    for name, shard in zip(names, shards):
        start, size = (table_a if name in table_a else table_b)[name]
        target = wa.at[here] if name in table_a else stage
        if name == "up":
            for c in range(4):
                keep(shard.at[:, pl.ds(c * D, D)], target.at[pl.ds(start + c * piece, piece)])
        else:
            keep(shard, target.at[pl.ds(start, size)])
    small_all[here] = jnp.zeros((16, 128), F32)
    for r, vector in enumerate(vectors[0:7]):
        small_all[here + (slice(r, r + 1), slice(0, D // n))] = vector[...].astype(F32).reshape(1, D // n)
    edge_rows, edge_width = max(1, FF // n // 128), min(128, FF // n)
    small_all[here + (slice(8, 8 + edge_rows), slice(0, edge_width))] = (
        vectors[7][...].astype(F32).reshape(edge_rows, edge_width)
    )

    peers = [("fsdp", partner_of(me, bits, b), None) for b in range(d)]
    peers += [("seq", rank - 1, rank > 0), ("seq", rank + 1, rank < last)]
    greet(peers)

    arrays = (wa, wb, small_all)
    units = weight_units(n) + [(2, 0, 16, 0, 128, 0)]
    order_list = orders(n)

    def hop(u, phase, theirs=False):
        array, r0, nr, c0, nc, which = units[u]
        order = order_list[which]
        b = order[phase]
        cut = (pl.ds(r0, nr), pl.ds(c0, nc))
        fixed = {b: 1 - bits[b]} if theirs else {}
        part = arrays[array].at[at_bits(bits, order[:phase], fixed) + cut]
        src = stage.at[cut] if array == 1 and phase == 0 and not theirs else part
        return pltpu.make_async_remote_copy(
            src_ref=src, dst_ref=part, send_sem=fsend.at[u, phase], recv_sem=frecv.at[u, phase],
            device_id={"fsdp": partner_of(me, bits, b)}, device_id_type=MESH_ID,
        )

    def landed(u, phase):
        hop(u, phase, True).wait_recv()

    def onward(some, phase):
        for u in some:
            landed(u, phase - 1)
            hop(u, phase).start()

    def needed(side, taker, start, height):
        low, high = key_span(taker, rows, glen)
        if side == 0:
            return (start < prompt) | (start + height > low)
        return (start < prompt) | (start < high)

    copies[0].wait()
    copies[1].wait()
    sems = (zsend, zrecv)
    strips = rows // STRIP
    toks = [Chain(x_all.at[m], rows, strips, sems, m, rank, count, needed) for m in range(MICRO)]
    encs = Chain(e_all, erows, 1, sems, MICRO, rank, count, None)
    toks[0].start(0)
    halo = pltpu.make_async_remote_copy(
        src_ref=cot.at[:, pl.ds(rows - HALO, HALO)], dst_ref=prev, send_sem=csend, recv_sem=crecv,
        device_id={"seq": rank + 1}, device_id_type=MESH_ID,
    )

    @pl.when(rank < last)
    def _():
        halo.start()

    for strip in range(glen // STRIP):
        start, block = strip * STRIP, strip * STRIP // rows
        side0, side1 = needed(0, rank, start, STRIP), needed(1, rank, start, STRIP)
        unseen = ((block < rank) & jnp.logical_not(side0)) | ((block > rank) & jnp.logical_not(side1))

        @pl.when(unseen)
        def _():
            x_all[:, start : start + STRIP, :] = jnp.zeros((MICRO, STRIP, D), BF)

    for copy in copies[2:]:
        copy.wait()
    everything = list(range(len(units)))
    for u in everything:
        hop(u, 0).start()
    settle = pltpu.make_async_copy(stage, wb.at[here], local.at[len(copies)])
    settle.start()
    first = pltpu.make_async_copy(cot.at[:, pl.ds(rows - HALO, HALO)], prev, local.at[len(copies) + 1])

    @pl.when(rank == 0)
    def _():
        first.start()

    settle.wait()
    onward(everything[:6], 1)
    for s in range(1, count):
        toks[0].arrived(s - 1, s < count - 1)
        if s == 1:
            onward(everything[6:], 1)
        if s == count - 2:
            toks[1].start(0)
    if d > 2:
        for phase in range(2, d):
            onward(everything[:2], phase)
    landed(0, d - 1)
    landed(1, d - 1)

    off = pl.multiple_of(rank * rows, 128)
    edge = pl.multiple_of(jnp.minimum(rank * rows + rows, glen - 128), 128)
    n_lead = (n, 3 * piece, D)

    def weight(name):
        start, size = table_a[name]
        return wa[(slice(None),) * d + (slice(start, start + size),)].reshape(D, D)

    def project(m, low, high):
        def one_tile(tile, _):
            at = pl.ds(pl.multiple_of(tile * 256, 256), 256)
            part = x_all[m, at, :]
            k_ref[m, at, :] = nn(part, weight("wk")).astype(BF)
            v_ref[m, at, :] = nn(part, weight("wv")).astype(BF)
            return 0

        lax.fori_loop(low, high, one_tile, 0)

    def query(m):
        edge_rows = x_all[m, pl.ds(edge, HALO), :]
        halo_out[m] = edge_rows
        q_ref[m, 0:rows, :] = (nn(x_all[m, pl.ds(off, rows), :], weight("wq")).astype(BF) * SCALE).astype(BF)
        q_ref[m, rows : rows + HALO, :] = (nn(edge_rows, weight("wq")).astype(BF) * SCALE).astype(BF)
        place_info(info, seg_ref, prefix_ref, m)
        seg_row = info[1:2, :]
        place = lax.broadcasted_iota(jnp.int32, (1, glen), 1)
        for start, size, span in ((0, rows, pl.ds(off, rows)), (rows, HALO, pl.ds(edge, 128))):
            column = info[:, span].T[0:size]
            limit, seg = column[:, 0:1], column[:, 1:2]
            seen = jnp.where(
                place < prompt, (place.astype(F32) < limit).astype(jnp.int32), (seg_row == seg).astype(jnp.int32)
            )
            bias[start : start + size, :] = jnp.where(seen == 1, 0.0, NEG)

    def pairs(m, low, high):
        def one_pair(pair, _):
            at = lanes_of(pair)
            mix = attend_pair(
                q_ref[m, :, at], k_ref[m, :, at], v_ref[m, :, at], bias[...], pair, lse_sc
            )
            mix_ref[m, :, at] = mix.astype(BF)
            return 0

        lax.fori_loop(low, high, one_pair, 0)
        if high == HEADS // 2:
            lse_out[m] = lse_sc[0:rows, :].T[0:HEADS, :]

    stores = []

    def store(src, to):
        copy = pltpu.make_async_copy(src, to, osem.at[len(stores)])
        copy.start()
        stores.append(copy)

    def store_micro(m):
        for src, to in ((x_all, x_out), (k_ref, k_out), (v_ref, v_out), (q_ref, q_out)):
            store(src.at[m], to.at[m])

    def far_pairs(m, split):
        def one_pair(pair, _):
            at = lanes_of(pair)
            attend_far(
                q_ref[m, :, at], k_ref[m, split:glen, at], v_ref[m, split:glen, at],
                bias[:, split:glen], pair, far_mix, far_top, far_total,
            )
            return 0

        lax.fori_loop(0, HEADS // 2, one_pair, 0)

    def near_pairs(m, split, low, high):
        def one_pair(pair, _):
            at = lanes_of(pair)
            mix = attend_near(
                q_ref[m, :, at], k_ref[m, 0:split, at], v_ref[m, 0:split, at],
                bias[:, 0:split], pair, lse_sc, far_mix, far_top, far_total,
            )
            mix_ref[m, :, at] = mix.astype(BF)
            return 0

        lax.fori_loop(low, high, one_pair, 0)
        if high == HEADS // 2:
            lse_out[m] = lse_sc[0:rows, :].T[0:HEADS, :]

    rest = everything[2:]
    near = -(-rows // 256)
    project(0, 0, glen // 256)
    query(0)
    store(wa, wa_out)
    store_micro(0)
    pairs(0, 0, 2)
    toks[1].arrived(0, count > 2)
    encs.start(0)
    for phase in range(2, d):
        onward(rest[: len(rest) // 2], phase)
    pairs(0, 2, 4)
    for s in range(1, count - 2):
        toks[1].arrived(s, True)
    encs.arrived(0, count > 2)
    for phase in range(2, d):
        onward(rest[len(rest) // 2 :], phase)
    project(1, near, glen // 256)
    query(1)
    far_pairs(1, near * 256)
    toks[1].arrived(count - 2, False)
    project(1, 0, near)
    store_micro(1)
    near_pairs(1, near * 256, 0, 2)
    for s in range(1, count - 1):
        encs.arrived(s, s < count - 2)
    near_pairs(1, near * 256, 2, 4)

    for u in rest:
        landed(u, d - 1)

    @pl.when(rank > 0)
    def _():
        halo.wait_recv()

    @pl.when(rank == 0)
    def _():
        first.wait()

    @pl.when(rank < last)
    def _():
        halo.wait_send()

    for u in everything:
        for phase in range(d):
            hop(u, phase).wait_send()
    for chain in toks + [encs]:
        for s in range(count - 1):
            chain.sent(s)
    for copy in stores:
        copy.wait()


def front(n, count, shards, vectors, tok, enc, cot, seg, prefix):
    rows, erows = tok.shape[1], enc.shape[1]
    glen = count * rows
    ext = rows + HALO
    lead = (2,) * bit_count(n)
    _, ra = qkv_rows(n)
    _, rb = rest_rows(n)
    units = len(weight_units(n)) + 1
    d = bit_count(n)
    hbm = pl.BlockSpec(memory_space=pl.ANY)
    dma = pltpu.SemaphoreType.DMA
    strips = rows // STRIP
    return pl.pallas_call(
        functools.partial(front_kernel, n, count, rows, erows),
        in_specs=[hbm] * 14 + [VM, SMEM] + [VM] * 8,
        out_specs=[hbm, hbm, VM, hbm, VM, VM, VM, hbm, hbm, hbm, VM, VM],
        out_shape=[
            jax.ShapeDtypeStruct(lead + (ra, D), BF),
            jax.ShapeDtypeStruct(lead + (rb, D), BF),
            jax.ShapeDtypeStruct(lead + (16, 128), F32),
            jax.ShapeDtypeStruct((MICRO, glen, D), BF),
            jax.ShapeDtypeStruct((MICRO, count * erows, D), BF),
            jax.ShapeDtypeStruct((MICRO, HALO, D), BF),
            jax.ShapeDtypeStruct((MICRO, HALO, D), BF),
            jax.ShapeDtypeStruct((MICRO, ext, D), BF),
            jax.ShapeDtypeStruct((MICRO, glen, D), BF),
            jax.ShapeDtypeStruct((MICRO, glen, D), BF),
            jax.ShapeDtypeStruct((MICRO, ext, D), BF),
            jax.ShapeDtypeStruct((MICRO, HEADS, rows), F32),
        ],
        scratch_shapes=[
            pltpu.VMEM(lead + (ra, D), BF), pltpu.VMEM((MICRO, glen, D), BF),
            pltpu.VMEM((MICRO, ext, D), BF), pltpu.VMEM((MICRO, glen, D), BF),
            pltpu.VMEM((MICRO, glen, D), BF),
            pltpu.VMEM((ext, D), F32), pltpu.VMEM((ext, 128), F32), pltpu.VMEM((ext, 128), F32),
            pltpu.VMEM((rb, D), BF), pltpu.VMEM((ext, glen), F32), pltpu.VMEM((ext, 128), F32),
            pltpu.VMEM((8, glen), F32),
            dma((20,)), dma((units, d)), dma((units, d)),
            dma((MICRO + 1, 2, count, strips)), dma((MICRO + 1, 2, count, strips)), dma(()), dma(()), dma((10,)),
        ],
        compiler_params=pltpu.CompilerParams(
            collective_id=0, has_side_effects=True, vmem_limit_bytes=60 * MIB
        ),
        name="front",
    )(*shards, tok, enc, cot, seg, prefix, *vectors)


TILE = 256
GROUPS = 12
SLOTS = ((-2, -1, 1, 4), (-2, 0, 3, 6), (-2, 1, 5, 7), (-2, 3, 6, 8), (-2, 3, 6, 8))


def seen_from(side, taker, start, height, rows, glen):
    low, high = key_span(taker, rows, glen)
    if side == 0:
        return (start < glen // 3) | (start + height > low)
    return (start < glen // 3) | (start < high)


def static_wants(side, taker, start, rows, glen):
    prompt = glen // 3
    least = (glen - prompt) // 8
    most = (glen - prompt) - 3 * least
    first, stop = taker * rows, (taker + 1) * rows + 1
    low = max(first - most, prompt + least if first >= prompt + most else prompt)
    high = min(stop + most, glen - least if stop <= glen - most else glen) if stop > prompt else 0
    return start < prompt or (start + STRIP > low if side == 0 else start < high)


def back_kernel(n, count, rows, erows, *refs):
    q_ref, mix_ref, dmix_ref, lse_ref, tok_ref, wa, genc, gs, seg_ref, prefix_ref = refs[0:10]
    x_hbm, k_hbm, v_hbm, dr1_hbm, gb = refs[10:15]
    outs = refs[15:18]
    tok_out, enc_out = refs[18:20]
    rest = list(refs[20:])
    d = bit_count(n)
    glen = count * rows
    prompt = glen // 3
    tiles = glen // TILE

    def take(k):
        got = rest[:k]
        del rest[:k]
        return got

    accs, zls, zrs, zss, fins = take(3), take(3), take(3), take(3), take(3)
    recvs = [take(d) for _ in range(3)]
    ebuf, ga, part, inc, wkv, qst, dst, stats, info, bias, dqt, dkv, gkv, dqs = take(14)
    kbuf, vbuf, xbuf = take(3)
    fsend, frecv, zsend, zrecv, tsend, trecv, esend, erecv, lsem, tsem, dsem = rest
    grads = (ga, gb, gs)
    me, bits = my_place(n)
    rank = lax.axis_index("seq")
    last = count - 1
    off = pl.multiple_of(rank * rows, 128)
    table, _ = qkv_rows(n)

    def weight(name):
        start, size = table[name]
        return wa[:, start : start + size, :].reshape(D, D)

    def tile_copies(i, slot):
        m, at = i // tiles, pl.ds(pl.multiple_of((i % tiles) * TILE, TILE), TILE)
        return [
            pltpu.make_async_copy(hbm.at[m, at], buf.at[slot], tsem.at[slot, j])
            for j, (hbm, buf) in enumerate(((k_hbm, kbuf), (v_hbm, vbuf), (x_hbm, xbuf)))
        ]

    for copy in tile_copies(0, 0):
        copy.start()
    start_out = pltpu.make_async_copy(dr1_hbm, tok_out, dsem)
    start_out.start()

    piece = D // n
    early_units = weight_units(n)[2:] + [(2, 0, 16, 0, 128, 0)]
    late_units = [
        (0, c * piece, w * piece, half * 256, 256, half) for c, w in ((1, 2), (0, 1)) for half in range(2)
    ]
    units = early_units + late_units
    early, late = list(range(len(early_units))), list(range(len(early_units), len(units)))
    order_list = [o[::-1] for o in orders(n)]

    def own_half(u):
        array, r0, nr, c0, nc, which = units[u]
        cut = (pl.ds(r0, nr), pl.ds(c0, nc))
        index = at_bits(bits, range(1, d))
        return pltpu.make_async_copy(
            gb.at[index + cut], accs[1].at[(slice(None),) * (d - 1) + cut], lsem.at[u]
        )

    big = [u for u in early if units[u][0] == 1]
    for u in big:
        own_half(u).start()

    peers = [("fsdp", partner_of(me, bits, b), None) for b in range(d)]
    peers += [("seq", lax.rem(rank + k, count), None) for k in range(1, count)]
    greet(peers)

    def hop(u, phase):
        array, r0, nr, c0, nc, which = units[u]
        order = order_list[which]
        b = order[phase]
        free = [x for x in range(d) if x not in order[: phase + 1]]
        cut = (pl.ds(r0, nr), pl.ds(c0, nc))
        index = at_bits(bits, free, {b: 1 - bits[b]})
        src = grads[array].at[index + cut] if phase == 0 else accs[array].at[index[:-1] + cut]
        to = recvs[array][phase].at[(slice(None),) * len(free) + cut]
        return pltpu.make_async_remote_copy(
            src_ref=src, dst_ref=to, send_sem=fsend.at[u, phase], recv_sem=frecv.at[u, phase],
            device_id={"fsdp": partner_of(me, bits, b)}, device_id_type=MESH_ID,
        )

    def add(u, phase):
        array, r0, nr, c0, nc, which = units[u]
        order = order_list[which]
        free = [x for x in range(d) if x not in order[: phase + 1]]
        cut = (slice(r0, r0 + nr), slice(c0, c0 + nc))
        index = at_bits(bits, free)
        hop(u, phase).wait_recv()
        if phase == 0 and array == 1:
            own_half(u).wait()
        base = grads[array][index + cut] if phase == 0 and array != 1 else accs[array][index[:-1] + cut]
        more = recvs[array][phase][(slice(None),) * len(free) + cut]
        accs[array][index[:-1] + cut] = (base.astype(F32) + more.astype(F32)).astype(base.dtype)
        if phase + 1 < d:
            hop(u, phase + 1).start()

    here = at_bits(bits, ())[:-1]

    def root_of(which):
        return (count - 1) // 2 if which == 0 else count // 2

    def z_copy(u, kind, src, to, target):
        return pltpu.make_async_remote_copy(
            src_ref=src, dst_ref=to, send_sem=zsend.at[u, kind], recv_sem=zrecv.at[u, kind],
            device_id={"seq": target}, device_id_type=MESH_ID,
        )

    def z_refs(u):
        array, r0, nr, c0, nc, which = units[u]
        cut = (pl.ds(r0, nr), pl.ds(c0, nc))
        return [x[array].at[cut] for x in (zss, zls, zrs, fins)], root_of(which)

    def z_in(u, step):
        array, r0, nr, c0, nc, which = units[u]
        cut = (slice(r0, r0 + nr), slice(c0, c0 + nc))
        (zs, zl, zr, fin), root = z_refs(u)
        turn = max(root, last - root)

        def own():
            return accs[array][here + cut].astype(F32)

        if step < turn:

            @pl.when((rank < root) & (rank == step))
            def _():
                if step == 0:
                    zss[array][cut] = accs[array][here + cut]
                else:
                    z_copy(u, 0, zs, zl, rank - 1).wait_recv()
                    zss[array][cut] = (own() + zls[array][cut].astype(F32)).astype(zss[array].dtype)
                z_copy(u, 0, zs, zl, rank + 1).start()

            @pl.when((rank > root) & (last - rank == step))
            def _():
                if step == 0:
                    zss[array][cut] = accs[array][here + cut]
                else:
                    z_copy(u, 1, zs, zr, rank + 1).wait_recv()
                    zss[array][cut] = (own() + zrs[array][cut].astype(F32)).astype(zss[array].dtype)
                z_copy(u, 1, zs, zr, rank - 1).start()

        if step == turn:

            @pl.when(rank == root)
            def _():
                total = own()
                if root > 0:
                    z_copy(u, 0, zs, zl, rank - 1).wait_recv()
                    total = total + zls[array][cut].astype(F32)
                if root < last:
                    z_copy(u, 1, zs, zr, rank + 1).wait_recv()
                    total = total + zrs[array][cut].astype(F32)
                fins[array][cut] = total.astype(fins[array].dtype)
                if root > 0:
                    z_copy(u, 2, fin, fin, rank - 1).start()
                if root < last:
                    z_copy(u, 3, fin, fin, rank + 1).start()
                outs[array][cut] = fins[array][cut]

    def z_out(u, step):
        array, r0, nr, c0, nc, which = units[u]
        cut = (slice(r0, r0 + nr), slice(c0, c0 + nc))
        (zs, zl, zr, fin), root = z_refs(u)
        far = step + 1

        if root - far >= 0:

            @pl.when(rank == root - far)
            def _():
                z_copy(u, 2, fin, fin, rank + 1).wait_recv()
                if root - far > 0:
                    z_copy(u, 2, fin, fin, rank - 1).start()
                outs[array][cut] = fins[array][cut]

        if root + far <= last:

            @pl.when(rank == root + far)
            def _():
                z_copy(u, 3, fin, fin, rank - 1).wait_recv()
                if root + far < last:
                    z_copy(u, 3, fin, fin, rank + 1).start()
                outs[array][cut] = fins[array][cut]

    def z_sent(u):
        (zs, zl, zr, fin), root = z_refs(u)

        @pl.when(rank < root)
        def _():
            z_copy(u, 0, zs, zl, rank + 1).wait_send()

        @pl.when(rank > root)
        def _():
            z_copy(u, 1, zs, zr, rank - 1).wait_send()

        @pl.when((rank <= root) & (rank > 0))
        def _():
            z_copy(u, 2, fin, fin, rank - 1).wait_send()

        @pl.when((rank >= root) & (rank < last))
        def _():
            z_copy(u, 3, fin, fin, rank + 1).wait_send()

    moves = []
    for k in range(1, count):
        to = lax.rem(rank + k, count)
        moves.append(
            pltpu.make_async_remote_copy(
                src_ref=genc.at[:, pl.ds(pl.multiple_of(to * erows, 16), erows)],
                dst_ref=ebuf.at[k - 1],
                send_sem=esend.at[k - 1], recv_sem=erecv.at[k - 1],
                device_id={"seq": to}, device_id_type=MESH_ID,
            )
        )
    for move in moves:
        move.start()

    def wants(side, taker, start):
        return seen_from(side, taker, start, STRIP, rows, glen)

    def strip_copy(m, strip, side, target):
        start = strip * STRIP
        if not isinstance(start, int):
            start = pl.multiple_of(start, STRIP)
        return pltpu.make_async_remote_copy(
            src_ref=part.at[m, pl.ds(start, STRIP)],
            dst_ref=inc.at[m, pl.ds(start + side * rows, STRIP)],
            send_sem=tsend.at[m, strip, side], recv_sem=trecv.at[m, strip, side],
            device_id={"seq": target}, device_id_type=MESH_ID,
        )

    def coming(strip, side):
        start = strip * STRIP
        owner = start // rows
        if side == 0:
            return (owner <= rank) & (rank < last) & wants(0, rank + 1, start)
        return (owner >= rank) & (rank > 0) & wants(1, rank - 1, start)

    def going(strip, side):
        start = strip * STRIP
        owner = start // rows
        if side == 0:
            return (owner < rank) & wants(0, rank, start)
        return (owner > rank) & wants(1, rank, start)

    def static_going(strip, side, who):
        start = strip * STRIP
        owner = start // rows
        if side == 0:
            return owner < who <= last and bool(static_wants(0, who, start, rows, glen))
        return owner > who >= 0 and bool(static_wants(1, who, start, rows, glen))

    def pass_on(m, strip, side, who):
        start = strip * STRIP
        at = slice(start, start + STRIP)
        source = who + 1 if side == 0 else who - 1

        @pl.when(rank == who)
        def _():
            if static_going(strip, side, source):
                strip_copy(m, strip, side, source).wait_recv()
                there = slice(start + side * rows, start + side * rows + STRIP)
                part[m, at, :] = (part[m, at, :].astype(F32) + inc[m, there, :].astype(F32)).astype(BF)
            strip_copy(m, strip, side, who - 1 if side == 0 else who + 1).start()

    def finish_rows(m):
        for j in range(rows // STRIP):
            strip = rank * (rows // STRIP) + j
            at = pl.ds(pl.multiple_of(strip * STRIP, STRIP), STRIP)
            mine = slice(j * STRIP, (j + 1) * STRIP)
            tok_out[m, mine, :] += part[m, at, :].astype(F32)
            for side in range(2):

                @pl.when(coming(strip, side))
                def _():
                    strip_copy(m, strip, side, rank).wait_recv()
                    there = pl.ds(pl.multiple_of(strip * STRIP + side * rows, STRIP), STRIP)
                    tok_out[m, mine, :] += inc[m, there, :].astype(F32)

    wkv[:, 0:D] = weight("wk")
    wkv[:, D : 2 * D] = weight("wv")
    gkv[...] = jnp.zeros_like(gkv)

    def begin(m):
        place_info(info, seg_ref, prefix_ref, m)
        dqt[...] = jnp.zeros_like(dqt)
        delta = head_sums(dmix_ref[m].astype(F32) * mix_ref[m, 0:rows, :].astype(F32))
        for pair in range(HEADS // 2):
            at = slice(pair * 128, (pair + 1) * 128)
            for h in range(2):
                row = 2 * pair + h
                span = slice(h * rows, (h + 1) * rows)
                qst[pair, span, :] = head_masked(q_ref[m, 0:rows, at], h)
                dst[pair, span, :] = head_masked(dmix_ref[m, :, at], h)
                stats[pair : pair + 1, span] = lse_ref[m, row : row + 1, :]
                stats[4 + pair : 5 + pair, span] = delta[row : row + 1, :]

    def one_tile(m):
        def body(t, _):
            i = m * tiles + t
            slot = i % 2

            for copy in tile_copies(i, slot):
                copy.wait()

            @pl.when(i + 1 < MICRO * tiles)
            def _():
                for copy in tile_copies(i + 1, 1 - slot):
                    copy.start()

            at_keys = pl.ds(pl.multiple_of(t * TILE, TILE), TILE)
            place = lax.broadcasted_iota(jnp.int32, (TILE, 1), 0) + t * TILE
            key_seg = info[:, at_keys].T[:, 1:2]
            limit = info[0:1, pl.ds(off, rows)]
            seg = info[1:2, pl.ds(off, rows)]
            seen = jnp.where(
                place < prompt, (place.astype(F32) < limit).astype(jnp.int32), (key_seg == seg).astype(jnp.int32)
            )
            mask = jnp.where(seen == 1, 0.0, NEG)
            bias[:, 0:rows] = mask
            bias[:, rows : 2 * rows] = mask

            def one_pair(pair, _):
                at = lanes_of(pair)
                kp, vp = kbuf[slot, :, at], vbuf[slot, :, at]
                prob = jnp.exp(nt(kp, qst[pair]) + bias[...] - stats[pl.ds(pair, 1), :])
                d_score = (prob * (nt(vp, dst[pair]) - stats[pl.ds(4 + pair, 1), :])).astype(BF)
                dkv[:, at] = nn(d_score, qst[pair]).astype(BF)
                dkv[:, pl.ds(pl.multiple_of(D + pair * 128, 128), 128)] = nn(
                    prob.astype(BF), dst[pair]
                ).astype(BF)
                d_q = nn(kp.T, d_score)
                sub = lax.broadcasted_iota(jnp.int32, (128, rows), 0)
                dqt[at, :] += jnp.where(sub < 64, d_q[:, 0:rows], d_q[:, rows : 2 * rows])
                return 0

            lax.fori_loop(0, HEADS // 2, one_pair, 0)
            part[m, at_keys, :] = nt(dkv[...], wkv[...]).astype(BF)
            gkv[...] += tn(xbuf[slot], dkv[...])
            return 0

        return body

    def end(m):
        for pair in range(HEADS // 2):
            at = slice(pair * 128, (pair + 1) * 128)
            dqs[m, :, at] = (dqt[at, :] * SCALE).T.astype(BF)
        if m == 0:
            start_out.wait()
        tok_out[m] += nt(dqs[m], weight("wq"))

    todo = {}

    def later(when, job, *what):
        todo.setdefault(when, []).append(functools.partial(job, *what))

    def plan(some, times):
        for u in some:
            for phase in range(d):
                later(times[min(phase, 2)] + max(phase - 2, 0), add, u, phase)
            at = times[2] + max(d - 3, 0)
            root = root_of(units[u][5])
            turn = max(root, last - root)
            for step in range(turn + 1):
                later(at + step, z_in, u, step)
            for step in range(last):
                later(at + turn + 1 + step, z_out, u, step)

    def begin_sum(some):
        for u in some:
            hop(u, 0).start()

    for c, times in enumerate(SLOTS):
        plan(early[2 * c : 2 * c + 2], times[1:])
        later(times[0], begin_sum, early[2 * c : 2 * c + 2])
    per = MICRO * tiles // GROUPS
    strips = TILE // STRIP
    passes = []
    for i in range(GROUPS):
        m, t0 = i * per // tiles, (i * per) % tiles
        for strip in range(t0 * strips, (t0 + per) * strips):
            for dist in range(count):
                for side in range(2):
                    who = last - dist if side == 0 else dist
                    if static_going(strip, side, who):
                        passes.append((m, strip, side, who))
                        later(i + 2 * (dist if side == 0 else max(dist - 1, 0)), pass_on, m, strip, side, who)
    later(GROUPS - 2, finish_rows, 0)

    def put(name, value):
        start, size = table[name]
        where = (slice(None),) * d + (slice(start, start + size),)
        ga[where] = value.astype(BF).reshape((2,) * d + (size, D))

    for job in todo.pop(-2, []):
        job()
    for i in range(GROUPS):
        m, t0 = i * per // tiles, (i * per) % tiles
        if t0 == 0:
            begin(m)
        if i == 0:
            for job in todo.pop(-1, []):
                job()
        lax.fori_loop(t0, t0 + per, one_tile(m), 0)
        if i == GROUPS - 1:
            put("wk", gkv[:, 0:D])
            put("wv", gkv[:, D : 2 * D])
            begin_sum(late[0:2])
        if t0 + per == tiles:
            end(m)
        for job in todo.pop(i, []):
            job()

    put("wq", tn(tok_ref[...].reshape(MICRO * rows, D), dqs[...].reshape(MICRO * rows, D)))
    begin_sum(late[2:4])
    waiting = dict(todo)
    todo.clear()
    for c in range(2):
        plan(late[2 * c : 2 * c + 2], (GROUPS + c, GROUPS + c + 1, GROUPS + c + 2))
    for when in waiting:
        todo.setdefault(when, []).extend(waiting[when])
    for i in sorted(todo):
        for job in todo[i]:
            job()
    finish_rows(1)
    for move in moves:
        move.wait_recv()
    emine = pl.ds(pl.multiple_of(rank * erows, 16), erows)
    for m in range(MICRO):
        states = genc[m, emine, :].astype(F32)
        for k in range(1, count):
            states = states + ebuf[k - 1, m].astype(F32)
        enc_out[m] = states
    for move in moves:
        move.wait_send()
    for m, strip, side, who in passes:

        @pl.when(rank == who)
        def _():
            strip_copy(m, strip, side, who - 1 if side == 0 else who + 1).wait_send()

    for u in range(len(units)):
        for phase in range(d):
            hop(u, phase).wait_send()
        z_sent(u)


def back(n, count, q, mix, dmix, lse, tok, wa, genc, gs, seg, prefix, x_all, k, v, dr1, gb):
    rows = tok.shape[1]
    erows = genc.shape[1] // count
    glen = count * rows
    d = bit_count(n)
    units = len(weight_units(n)) + 3
    dma = pltpu.SemaphoreType.DMA
    V = pltpu.VMEM
    hbm = pl.BlockSpec(memory_space=pl.ANY)
    flat = [(wa.shape[-2], D), (gb.shape[-2], D), (16, 128)]
    types = [BF, BF, F32]
    scratch = [V((2,) * (d - 1) + f, t) for f, t in zip(flat, types)]
    for _ in range(4):
        scratch += [V(f, t) for f, t in zip(flat, types)]
    for f, t in zip(flat, types):
        scratch += [V((2,) * (d - 1 - p) + f, t) for p in range(d)]
    scratch += [
        V((count - 1, MICRO, erows, D), BF),
        V((2,) * d + flat[0], BF),
        V((MICRO, glen, D), BF), V((MICRO, glen + rows, D), BF),
        V((D, 2 * D), BF),
        V((HEADS // 2, 2 * rows, 128), BF), V((HEADS // 2, 2 * rows, 128), BF),
        V((8, 2 * rows), F32), V((8, glen), F32), V((TILE, 2 * rows), F32),
        V((D, rows), F32), V((TILE, 2 * D), BF), V((D, 2 * D), F32),
        V((MICRO, rows, D), BF),
        V((2, TILE, D), BF), V((2, TILE, D), BF), V((2, TILE, D), BF),
    ]
    strips = glen // STRIP
    scratch += [
        dma((units, d)), dma((units, d)), dma((units, 4)), dma((units, 4)),
        dma((MICRO, strips, 2)), dma((MICRO, strips, 2)), dma((count - 1,)), dma((count - 1,)),
        dma((units,)), dma((2, 3)), dma(()),
    ]
    return pl.pallas_call(
        functools.partial(back_kernel, n, count, rows, erows),
        in_specs=[VM] * 9 + [SMEM] + [hbm] * 5,
        out_specs=[VM] * 5,
        out_shape=[jax.ShapeDtypeStruct(f, t) for f, t in zip(flat, types)]
        + [jax.ShapeDtypeStruct((MICRO, rows, D), F32), jax.ShapeDtypeStruct((MICRO, erows, D), F32)],
        scratch_shapes=scratch,
        compiler_params=pltpu.CompilerParams(
            collective_id=1, has_side_effects=True, vmem_limit_bytes=60 * MIB
        ),
        name="back",
    )(q, mix, dmix, lse, tok, wa, genc, gs, seg, prefix, x_all, k, v, dr1, gb)


FIRST = ("wq", "wk", "wv", "wout", "cq", "ck", "cv", "cout", "up")


def finish_kernel(n, *refs):
    oa, ob, os, tok, states = refs[0:5]
    outs = list(refs[5:])
    table_a, _ = qkv_rows(n)
    table_b, _ = rest_rows(n)
    outs[0][...] = tok[...]
    outs[1][...] = states[...]

    def matrix(name, out):
        table, src = (table_a, oa) if name in table_a else (table_b, ob)
        start, size = table[name]
        if name == "up":
            piece = size // 4
            for c in range(4):
                out[:, c * D : (c + 1) * D] = src[start + c * piece : start + (c + 1) * piece, :].astype(F32)
        else:
            out[...] = src[start : start + size, :].astype(F32)

    for name, out in zip(FIRST, outs[2:11]):
        matrix(name, out)
    edge, side = FF // n, D // n
    wide = outs[11]
    wide[...] = os[8 : 8 + max(1, edge // 128), 0 : min(edge, 128)].reshape(edge)
    matrix("down", outs[12])
    for k in range(7):
        outs[13 + k][...] = os[k : k + 1, 0:side].reshape(side)
    matrix("slot", outs[20])


def finish(n, oa, ob, os, tok, states):
    side, edge = D // n, FF // n
    square = (side, D)
    shapes = [tok.shape, states.shape] + [square] * 8 + [(side, FF), (edge,), (edge, D)]
    shapes += [(side,)] * 7 + [(2 * side, D)]
    return pl.pallas_call(
        functools.partial(finish_kernel, n),
        in_specs=[VM] * 5,
        out_specs=[VM] * len(shapes),
        out_shape=[jax.ShapeDtypeStruct(shape, F32) for shape in shapes],
        compiler_params=pltpu.CompilerParams(vmem_limit_bytes=60 * MIB),
        name="finish",
    )(oa, ob, os, tok, states)


def on_device(
    tokens, encoded, segment_ids, prefix_len, cotangent,
    w_query, w_key, w_value, w_out, c_query, c_key, c_value, c_out,
    w_up, b_up, w_down, b_down,
    gain_one, shift_one, gain_two, shift_two, gain_three, shift_three, w_slot,
):
    n = lax.axis_size("fsdp")
    count = lax.axis_size("seq")
    tokens = tokens[:, 0]
    rows = tokens.shape[1]
    prefix = prefix_len[:, 0]
    cot = cotangent[:, 0]

    shards = (w_query, w_key, w_value, w_out, c_query, c_key, c_value, c_out, w_up, w_down, w_slot)
    vectors = (b_down, gain_one, shift_one, gain_two, shift_two, gain_three, shift_three, b_up)
    (
        wa, wb, small_all, x_all, e_all, previous, edges, q, k, v, mix, lse
    ) = front(n, count, shards, vectors, tokens, encoded[:, 0], cot, segment_ids, prefix)
    wa = wa.reshape((n,) + wa.shape[-2:])
    wb = wb.reshape((n,) + wb.shape[-2:])
    small_all = small_all.reshape(n, 16, 128)
    slot_out, dmix, dr1, genc, gb, gs = middle(
        mix, tokens, edges, e_all, cot, previous, segment_ids, prefix, wb, small_all, rows
    )
    lead = (2,) * bit_count(n)
    gb = gb.reshape(lead + gb.shape[1:])
    gs = gs.reshape(lead + (16, 128))
    oa, ob, os, grad_tokens, grad_encoded = back(
        n, count, q, mix, dmix, lse, tokens, wa, genc, gs, segment_ids, prefix, x_all, k, v, dr1, gb
    )
    grad_tokens, grad_encoded, *others = finish(n, oa, ob, os, grad_tokens, grad_encoded)
    return (slot_out[:, None], grad_tokens[:, None], grad_encoded[:, None], *others)


def solution(mesh):
    act = P(None, "fsdp", "seq", None)
    ids = P(None, "fsdp", None)
    mat, one = P("fsdp", None), P("fsdp")
    in_specs = (
        (act, act, ids, ids, act) + (mat,) * 9 + (one, mat) + (one,) * 7 + (mat,)
    )
    out_specs = (act, act, act) + (mat,) * 9 + (one, mat) + (one,) * 7 + (mat,)
    return jax.shard_map(
        on_device, mesh=mesh, in_specs=in_specs, out_specs=out_specs, check_vma=False
    )
```

```python
import functools
import math

import jax
import jax.numpy as jnp
from jax import lax
from jax.experimental import pallas as pl
from jax.experimental.pallas import tpu as pltpu
from jax.sharding import PartitionSpec as P

D = 512
HD = 64
HEADS = 8
FF = 2048
MICRO = 2
HALO = 16
EPSILON = 1e-05
BF = jnp.bfloat16
F32 = jnp.float32
SCALE = 1.0 / math.sqrt(HD)
NEG = -1e30
MIB = 1024 * 1024
GELU_C = math.sqrt(2.0 / math.pi)

VM = pl.BlockSpec(memory_space=pltpu.VMEM)


def nn(a, b):
    return lax.dot_general(a, b, (((1,), (0,)), ((), ())), preferred_element_type=F32)


def nt(a, b):
    return lax.dot_general(a, b, (((1,), (1,)), ((), ())), preferred_element_type=F32)


def tn(a, b):
    return lax.dot_general(a, b, (((0,), (0,)), ((), ())), preferred_element_type=F32)


def lanes_of(pair):
    return pl.ds(pl.multiple_of(pair * 128, 128), 128)


def head_masked(value, head):
    lane = lax.broadcasted_iota(jnp.int32, value.shape, 1)
    return jnp.where((lane >= 64) == (head == 1), value, jnp.zeros_like(value))


def softmax_parts(scores):
    top = jnp.max(scores, axis=-1, keepdims=True)
    raw = jnp.exp(scores - top)
    total = jnp.sum(raw, axis=-1, keepdims=True)
    return raw, top, total


def attend_pair(query_pair, key_pair, value_pair, bias, pair, lse_ref):
    mixed = []
    for head in range(2):
        scores = nt(head_masked(query_pair, head), key_pair)
        if bias is not None:
            scores = scores + bias
        raw, top, total = softmax_parts(scores)
        mixed.append(nn(raw.astype(BF), value_pair) / total)
        lane = lax.broadcasted_iota(jnp.int32, lse_ref.shape, 1)
        lse_ref[...] = jnp.where(lane == pair * 2 + head, top + jnp.log(total), lse_ref[...])
    lane = lax.broadcasted_iota(jnp.int32, mixed[0].shape, 1)
    return jnp.where(lane < 64, mixed[0], mixed[1])


def attend_far(query_pair, key_pair, value_pair, bias, pair, mixed_ref, top_ref, total_ref):
    mixed = []
    lane = lax.broadcasted_iota(jnp.int32, top_ref.shape, 1)
    for head in range(2):
        raw, top, total = softmax_parts(nt(head_masked(query_pair, head), key_pair) + bias)
        mixed.append(nn(raw.astype(BF), value_pair))
        top_ref[...] = jnp.where(lane == pair * 2 + head, top, top_ref[...])
        total_ref[...] = jnp.where(lane == pair * 2 + head, total, total_ref[...])
    mixed_ref[:, lanes_of(pair)] = jnp.where(lane < 64, mixed[0], mixed[1])


def attend_near(
    query_pair, key_pair, value_pair, bias, pair, lse_ref, mixed_ref, top_ref, total_ref
):
    mixed = []
    lane = lax.broadcasted_iota(jnp.int32, lse_ref.shape, 1)
    far = mixed_ref[:, lanes_of(pair)]
    for head in range(2):
        mine = lane == pair * 2 + head
        far_top = jnp.sum(jnp.where(mine, top_ref[...], 0.0), axis=1, keepdims=True)
        far_total = jnp.sum(jnp.where(mine, total_ref[...], 0.0), axis=1, keepdims=True)
        scores = nt(head_masked(query_pair, head), key_pair) + bias
        top = jnp.maximum(jnp.max(scores, axis=-1, keepdims=True), far_top)
        raw = jnp.exp(scores - top)
        weight = jnp.exp(far_top - top)
        total = jnp.sum(raw, axis=-1, keepdims=True) + far_total * weight
        mixed.append((nn(raw.astype(BF), value_pair) + far * weight) / total)
        lse_ref[...] = jnp.where(mine, top + jnp.log(total), lse_ref[...])
    return jnp.where(lane < 64, mixed[0], mixed[1])


def bit_count(n):
    return n.bit_length() - 1


def qkv_rows(n):
    piece = D // n
    return {"wq": (0, piece), "wk": (piece, piece), "wv": (2 * piece, piece)}, 3 * piece


def rest_rows(n):
    piece = D // n
    table, start = {}, 0
    for name, times in (
        ("wout", 1), ("cq", 1), ("ck", 1), ("cv", 1), ("cout", 1), ("up", 4), ("down", 4), ("slot", 2)
    ):
        table[name] = (start, times * piece)
        start += times * piece
    return table, start


def square(ref, table, name):
    start, count = table[name]
    return ref[:, start : start + count, :].reshape(D, D)


def up_part(ref, table, c):
    start, count = table["up"]
    piece = count // 4
    return ref[:, start + c * piece : start + (c + 1) * piece, :].reshape(D, D)


def row_part(ref, table, name, c):
    start, count = table[name]
    many = D // count
    return ref[c * many : (c + 1) * many, start : start + count, :].reshape(D, D)


def store_square(ref, table, name, value):
    start, count = table[name]
    ref[:, start : start + count, :] = value.reshape(ref.shape[0], count, D)


def store_up(ref, table, c, value):
    start, count = table["up"]
    piece = count // 4
    ref[:, start + c * piece : start + (c + 1) * piece, :] = value.reshape(ref.shape[0], piece, D)


def store_part(ref, table, name, c, value):
    start, count = table[name]
    many = D // count
    ref[c * many : (c + 1) * many, start : start + count, :] = value.reshape(many, count, D)


def my_place(n):
    me = lax.axis_index("fsdp")
    bits = [(me // (1 << b)) % 2 for b in range(bit_count(n))]
    return me, bits


def partner_of(me, bits, b):
    return me + (1 - 2 * bits[b]) * (1 << b)


def orders(n):
    d = bit_count(n)
    far = list(range(1, d))
    return [far + [0], far[::-1] + [0]]


def at_bits(bits, free, fixed=None):
    fixed = fixed or {}
    return tuple(
        slice(None) if b in free else fixed.get(b, bits[b]) for b in range(len(bits) - 1, -1, -1)
    )


MESH_ID = pl.DeviceIdType.MESH

def place_info(info, seg_ref, prefix_ref, m):
    glen = info.shape[1]
    prompt = glen // 3
    seg = jnp.broadcast_to(seg_ref[m], (8, glen))
    limit = jnp.where(seg == 0, prompt, 0)
    for c in range(prefix_ref.shape[1]):
        limit = jnp.where(seg == c + 1, prefix_ref[m, c], limit)
    place = lax.broadcasted_iota(jnp.int32, (8, glen), 1)
    after = (seg == pltpu.roll(seg, glen - 1, 1)) & (place < glen - 1)
    before = (seg == pltpu.roll(seg, 1, 1)) & (place > 0)
    sub = lax.broadcasted_iota(jnp.int32, (8, glen), 0)
    mixed = jnp.where(sub == 0, limit, seg)
    mixed = jnp.where(sub == 2, after.astype(jnp.int32), mixed)
    mixed = jnp.where(sub == 3, before.astype(jnp.int32), mixed)
    info[...] = mixed.astype(F32)


SMEM = pl.BlockSpec(memory_space=pltpu.SMEM)


def spread_rows(tiles, first, count, width, out):
    group = max(1, 128 // width)
    lane = lax.broadcasted_iota(jnp.int32, (count, 128), 1)
    for p in range(tiles.shape[0] // group):
        block = tiles[p * group, first : first + count, :]
        for j in range(1, group):
            piece = pltpu.roll(tiles[p * group + j, first : first + count, :], j * width, 1)
            block = jnp.where(lane >= j * width, piece, block)
        out[0:count, p * 128 : (p + 1) * 128] = block


def gather_rows(values, count, width, tiles, first):
    group = max(1, 128 // width)
    for i in range(tiles.shape[0]):
        p, j = i // group, i % group
        block = values[0:8, p * 128 : (p + 1) * 128]
        if j:
            block = pltpu.roll(block, 128 - j * width, 1)
        tiles[i, first : first + count, :] = block[0:count]


def norm_forward(residual, gain, shift):
    average = jnp.mean(residual, axis=-1, keepdims=True)
    centred = residual - average
    variance = jnp.mean(centred * centred, axis=-1, keepdims=True)
    rstd = lax.rsqrt(variance + EPSILON)
    hat = centred * rstd
    return hat * gain + shift, hat, rstd


def norm_backward(upstream, hat, rstd, gain):
    d_hat = upstream * gain
    mean_d = jnp.mean(d_hat, axis=-1, keepdims=True)
    mean_dh = jnp.mean(d_hat * hat, axis=-1, keepdims=True)
    d_gain = jnp.sum(upstream * hat, axis=0, keepdims=True)
    d_shift = jnp.sum(upstream, axis=0, keepdims=True)
    return rstd * (d_hat - mean_d - hat * mean_dh), d_gain, d_shift


def gelu_parts(value):
    square = value * value
    t = jnp.tanh(GELU_C * value * (1.0 + 0.044715 * square))
    half = 0.5 * (1.0 + t)
    slope = half + 0.5 * value * (1.0 - t * t) * (GELU_C * (1.0 + 3.0 * 0.044715 * square))
    return value * half, slope


def head_sums(product_rows):
    rows, cols = 16, product_rows.shape[1]
    head = lax.broadcasted_iota(jnp.int32, (rows, cols), 0)
    lane = lax.broadcasted_iota(jnp.int32, (rows, cols), 1)
    pick = ((lane // HD) == head).astype(F32)
    return lax.dot_general(
        pick, product_rows, (((1,), (1,)), ((), ())),
        preferred_element_type=F32, precision=lax.Precision.HIGHEST,
    )[0:HEADS, :]


def middle_kernel(
    rows, enc,
    mix_ref, x_ref, edge_ref, e_ref, cot_ref, prev_ref, seg_ref, prefix_ref,
    w_hbm, small_ref,
    slot_out, dmix_out, dr1_out, genc_out, g_out, gs_out,
    w_ref, g_ref, bup_ref, vec_ref, gbup, gvec, wsem, gsem,
    lowx, lown, cqs, cks, cvs, lse_sc, lse_row, cmix, h1s, hats, rstds, slope,
    act, dpre, dffn, dcross, dcqs, dattn, dcks, dcvs, ckt, h3s, h2low, info, shs,
):
    ext = rows + HALO
    n = w_ref.shape[0]
    table, _ = rest_rows(n)
    piece = D // n
    spans = ((0, 5 * piece), (5 * piece, 4 * piece), (9 * piece, 4 * piece), (13 * piece, 2 * piece))

    def part_copy(k, out=False):
        cut = pl.ds(*spans[k])
        if out:
            return pltpu.make_async_copy(g_ref.at[:, cut], g_out.at[:, cut], gsem.at[k])
        return pltpu.make_async_copy(w_hbm.at[:, cut], w_ref.at[:, cut], wsem.at[k])

    for k in range(4):
        part_copy(k).start()
    spread_rows(small_ref, 0, 8, D // n, vec_ref)
    edge = FF // n
    if edge >= 128:
        for i in range(n):
            for r in range(edge // 128):
                lane = i * edge + r * 128
                bup_ref[0:1, lane : lane + 128] = small_ref[i, 8 + r : 9 + r, :]
    else:
        spread_rows(small_ref, 8, 1, edge, bup_ref)
    part_copy(0).wait()
    gbup[...] = jnp.zeros_like(gbup)
    gvec[...] = jnp.zeros_like(gvec)

    def vec(i):
        return vec_ref[i : i + 1, :]

    def one_micro(m, _):
        own = pl.ds(0, rows)
        attn = nn(mix_ref[m], square(w_ref, table, "wout"))
        x_rows = jnp.concatenate([x_ref[m], edge_ref[m]], axis=0).astype(F32)
        h1, hat, rstd = norm_forward(x_rows + attn, vec(1), vec(2))
        h1s[...] = h1
        dr1_out[m] = hat[0:rows]
        rstds[:, 0:1] = rstd[0:rows]
        h1_low = h1.astype(BF)
        lown[0, m] = h1_low[0:rows]
        cqs[...] = (nn(h1_low, square(w_ref, table, "cq")).astype(BF) * SCALE).astype(BF)
        cks[...] = nn(e_ref[m], square(w_ref, table, "ck")).astype(BF)
        cvs[...] = nn(e_ref[m], square(w_ref, table, "cv")).astype(BF)

        def cross_pair(pair, _):
            at = lanes_of(pair)
            mix = attend_pair(cqs[:, at], cks[:, at], cvs[:, at], None, pair, lse_sc)
            cmix[:, at] = mix.astype(BF)
            return 0

        lax.fori_loop(0, HEADS // 2, cross_pair, 0)
        lse_row[0:HEADS, :] = lse_sc[0:rows, :].T[0:HEADS, :]
        lowx[m] = cmix[0:rows, :]
        h2, hat, rstd = norm_forward(
            h1s[...] + nn(cmix[...], square(w_ref, table, "cout")), vec(3), vec(4)
        )
        h1s[...] = h2
        hats[...] = hat[0:rows]
        rstds[:, 1:2] = rstd[0:rows]
        h2low[...] = h2.astype(BF)
        lown[1, m] = h2low[0:rows, :]
        @pl.when(m == 0)
        def _():
            for k in range(1, 4):
                part_copy(k).wait()

        h3s[...] = jnp.zeros_like(h3s)

        for c in range(FF // D):
            at = slice(c * D, (c + 1) * D)
            pre = nn(h2low[...], up_part(w_ref, table, c)) + bup_ref[0:1, at]
            value, grad = gelu_parts(pre)
            value = value.astype(BF)
            act[m, :, at] = value[0:rows]
            slope[:, at] = grad[0:rows]
            down = row_part(w_ref, table, "down", c)
            h3s[...] += nn(value, down)
        h3, hat, rstd = norm_forward(h1s[...] + h3s[...] + vec(0), vec(5), vec(6))
        h3_low = h3.astype(BF)
        h3s[...] = h3_low.astype(F32)
        lown[2, m] = h3_low[0:rows]
        top = row_part(w_ref, table, "slot", 0)
        bottom = row_part(w_ref, table, "slot", 1)
        place_info(info, seg_ref, prefix_ref, m)
        flags = info[:, pl.ds(pl.multiple_of(lax.axis_index("seq") * rows, 128), rows)].T
        follow = (h3s[pl.ds(1, rows), :] * flags[:, 2:3]).astype(BF)
        slot_out[m] = (nn(h3_low[0:rows], top) + nn(follow, bottom)).astype(BF)
        h3s[0:8, :] = prev_ref[m].astype(F32)[HALO - 8 : HALO]
        h3s[8 : rows + 8, :] = cot_ref[m].astype(F32)
        shifted = h3s[pl.ds(7, rows), :]
        shs[m] = (shifted * flags[:, 3:4]).astype(BF)
        d_follow = nt(shifted.astype(BF), bottom).astype(BF).astype(F32) * flags[:, 3:4]
        d_three = nt(cot_ref[m], top) + d_follow
        d_r3, d_gain, d_shift = norm_backward(d_three, hat[0:rows], rstd[0:rows], vec(5))
        gvec[5:6, :] += d_gain
        gvec[6:7, :] += d_shift
        d_ffn = d_r3.astype(BF)
        dffn[m] = d_ffn
        gvec[0:1, :] += jnp.sum(d_ffn.astype(F32), axis=0, keepdims=True)
        d_two = d_r3
        for c in range(FF // D):
            at = slice(c * D, (c + 1) * D)
            down = row_part(w_ref, table, "down", c)
            grad = (nt(d_ffn, down) * slope[:, at]).astype(BF)
            dpre[m, :, at] = grad
            gbup[0:1, at] += jnp.sum(grad.astype(F32), axis=0, keepdims=True)
            d_two = d_two + nt(grad, up_part(w_ref, table, c))
        d_r2, d_gain, d_shift = norm_backward(d_two, hats[...], rstds[:, 1:2], vec(3))
        gvec[3:4, :] += d_gain
        gvec[4:5, :] += d_shift
        d_cross = d_r2.astype(BF)
        dcross[m] = d_cross
        d_cmix = nt(d_cross, square(w_ref, table, "cout")).astype(BF)
        dmix_out[m] = d_cmix
        delta = head_sums(d_cmix.astype(F32) * cmix[0:rows, :].astype(F32))
        lse_row[HEADS : 2 * HEADS, :] = delta
        ckt[...] = cks[...].T

        def cross_back(pair, _):
            at = lanes_of(pair)
            kp, vp = cks[:, at], cvs[:, at]
            qp, dp = cqs[0:rows, at], dmix_out[m, :, at]
            kt = ckt[at, :]
            d_k = d_v = None
            d_qt = []
            for head in range(2):
                qm, dm = head_masked(qp, head), head_masked(dp, head)
                row = pair * 2 + head
                prob = jnp.exp(nt(kp, qm) - lse_row[pl.ds(row, 1), :])
                d_score = (prob * (nt(vp, dm) - lse_row[pl.ds(HEADS + row, 1), :])).astype(BF)
                dk, dv = nn(d_score, qm), nn(prob.astype(BF), dm)
                d_k = dk if d_k is None else d_k + dk
                d_v = dv if d_v is None else d_v + dv
                d_qt.append(nn(kt, d_score))
            sub = lax.broadcasted_iota(jnp.int32, d_qt[0].shape, 0)
            d_q = jnp.where(sub < 64, d_qt[0], d_qt[1]) * SCALE
            dcqs[m, :, at] = d_q.T.astype(BF)
            dcks[m, :, at] = d_k.astype(BF)
            dcvs[m, :, at] = d_v.astype(BF)
            return 0

        lax.fori_loop(0, HEADS // 2, cross_back, 0)
        genc_out[m] = (
            nt(dcks[m], square(w_ref, table, "ck")) + nt(dcvs[m], square(w_ref, table, "cv"))
        ).astype(BF)
        d_one = d_r2 + nt(dcqs[m], square(w_ref, table, "cq"))
        d_r1, d_gain, d_shift = norm_backward(d_one, dr1_out[m], rstds[:, 0:1], vec(1))
        gvec[1:2, :] += d_gain
        gvec[2:3, :] += d_shift
        dr1_out[m] = d_r1
        d_attn = d_r1.astype(BF)
        dattn[m] = d_attn
        dmix_out[m] = nt(d_attn, square(w_ref, table, "wout")).astype(BF)
        return 0

    lax.fori_loop(0, MICRO, one_micro, 0)

    total = MICRO * rows

    def flat(ref, *lead):
        return ref[lead].reshape(total, D) if lead else ref[...].reshape(total, D)

    def grad_of(left, right):
        return tn(left, right).astype(BF)

    cot = cot_ref[...].reshape(total, D)
    flagged = shs[...].reshape(total, D)
    h3_all = lown[2].reshape(total, D)
    store_part(g_ref, table, "slot", 0, grad_of(h3_all, cot))
    store_part(g_ref, table, "slot", 1, grad_of(h3_all, flagged))
    part_copy(3, True).start()
    dffn_all = dffn[...].reshape(total, D)
    h2_all = lown[1].reshape(total, D)
    for c in range(FF // D):
        at = slice(c * D, (c + 1) * D)
        store_part(g_ref, table, "down", c, grad_of(act[:, :, at].reshape(total, D), dffn_all))
        store_up(g_ref, table, c, grad_of(h2_all, dpre[:, :, at].reshape(total, D)))
    part_copy(2, True).start()
    part_copy(1, True).start()
    store_square(g_ref, table, "cout", grad_of(lowx[...].reshape(total, D), dcross[...].reshape(total, D)))
    store_square(g_ref, table, "cq", grad_of(lown[0].reshape(total, D), dcqs[...].reshape(total, D)))
    e_all = e_ref[...].reshape(MICRO * enc, D)
    store_square(g_ref, table, "ck", grad_of(e_all, dcks[...].reshape(MICRO * enc, D)))
    store_square(g_ref, table, "cv", grad_of(e_all, dcvs[...].reshape(MICRO * enc, D)))
    mix_all = jnp.concatenate([mix_ref[m, 0:rows, :] for m in range(MICRO)], axis=0)
    store_square(g_ref, table, "wout", grad_of(mix_all, dattn[...].reshape(total, D)))
    part_copy(0, True).start()
    gs_out[...] = jnp.zeros_like(gs_out)
    gather_rows(gvec, 8, D // n, gs_out, 0)
    if edge >= 128:
        for i in range(n):
            for r in range(edge // 128):
                lane = i * edge + r * 128
                gs_out[i, 8 + r : 9 + r, :] = gbup[0:1, lane : lane + 128]
    else:
        gather_rows(gbup, 1, edge, gs_out, 8)
    for k in range(4):
        part_copy(k, True).wait()


def middle(mix, tokens, edges, e_all, cot, prev, seg, prefix, w, small, rows):
    glen = seg.shape[2]
    enc = e_all.shape[1]
    ext = rows + HALO
    out_shape = [
        jax.ShapeDtypeStruct((MICRO, rows, D), BF),
        jax.ShapeDtypeStruct((MICRO, rows, D), BF),
        jax.ShapeDtypeStruct((MICRO, rows, D), F32),
        jax.ShapeDtypeStruct((MICRO, enc, D), BF),
        jax.ShapeDtypeStruct(w.shape, BF),
        jax.ShapeDtypeStruct(small.shape, F32),
    ]
    V = pltpu.VMEM
    hbm = pl.BlockSpec(memory_space=pl.ANY)
    scratch = [
        V(w.shape, BF), V(w.shape, BF), V((8, FF), F32), V((8, D), F32),
        V((8, FF), F32), V((8, D), F32),
        pltpu.SemaphoreType.DMA((4,)), pltpu.SemaphoreType.DMA((4,)),
        V((MICRO, rows, D), BF),
        V((3, MICRO, rows, D), BF),
        V((ext, D), BF), V((enc, D), BF), V((enc, D), BF),
        V((ext, 128), F32), V((2 * HEADS, rows), F32),
        V((ext, D), BF),
        V((ext, D), F32),
        V((rows, D), F32), V((rows, 128), F32),
        V((rows, FF), F32),
        V((MICRO, rows, FF), BF), V((MICRO, rows, FF), BF),
        V((MICRO, rows, D), BF), V((MICRO, rows, D), BF), V((MICRO, rows, D), BF),
        V((MICRO, rows, D), BF),
        V((MICRO, enc, D), BF), V((MICRO, enc, D), BF),
        V((D, enc), BF),
        V((ext, D), F32), V((ext, D), BF),
        V((8, glen), F32), V((MICRO, rows, D), BF),
    ]
    return pl.pallas_call(
        functools.partial(middle_kernel, rows, enc),
        in_specs=[VM] * 7 + [SMEM, hbm, VM],
        out_specs=[VM] * 4 + [hbm, VM],
        out_shape=out_shape,
        scratch_shapes=scratch,
        compiler_params=pltpu.CompilerParams(vmem_limit_bytes=61 * MIB),
        name="middle",
    )(mix, tokens, edges, e_all, cot, prev, seg, prefix, w, small)


def weight_units(n):
    piece = D // n
    units = []
    for array, start, count in (
        (0, 0, 3 * piece), (1, 0, 5 * piece), (1, 5 * piece, 4 * piece),
        (1, 9 * piece, 4 * piece), (1, 13 * piece, 2 * piece),
    ):
        for half in range(2):
            units.append((array, start, count, half * 256, 256, half))
    return units


def greet(peers):
    barrier = pltpu.get_barrier_semaphore()
    for axis, target, when in peers:
        if when is None:
            pl.semaphore_signal(barrier, inc=1, device_id={axis: target}, device_id_type=MESH_ID)
        else:

            @pl.when(when)
            def _():
                pl.semaphore_signal(barrier, inc=1, device_id={axis: target}, device_id_type=MESH_ID)

    always = sum(1 for peer in peers if peer[2] is None)
    amount = jnp.int32(always)
    for axis, target, when in peers:
        if when is not None:
            amount = amount + when.astype(jnp.int32)
    pl.semaphore_wait(barrier, amount if always < len(peers) else always)


STRIP = 128


def key_span(rank, rows, glen):
    prompt = glen // 3
    least = (glen - prompt) // 8
    most = (glen - prompt) - 3 * least
    first, stop = rank * rows, (rank + 1) * rows + 1
    low = jnp.maximum(first - most, jnp.where(first >= prompt + most, prompt + least, prompt))
    high = jnp.minimum(stop + most, jnp.where(stop <= glen - most, glen - least, glen))
    return low, jnp.where(stop > prompt, high, 0)


class Chain:
    def __init__(self, ref, rows, strips, sems, lane, rank, count, needed):
        self.ref, self.rows, self.lane, self.needed = ref, rows, lane, needed
        self.strips, self.height = strips, rows // strips
        self.send, self.recv = sems
        self.rank, self.count = rank, count

    def copy(self, side, step, j, block, target):
        at = pl.ds(pl.multiple_of(block * self.rows + j * self.height, 16), self.height)
        part = self.ref.at[:, at] if len(self.ref.shape) == 3 else self.ref.at[at]
        return pltpu.make_async_remote_copy(
            src_ref=part, dst_ref=part,
            send_sem=self.send.at[self.lane, side, step, j],
            recv_sem=self.recv.at[self.lane, side, step, j],
            device_id={"seq": target}, device_id_type=MESH_ID,
        )

    def goes(self, side, sender, block, j):
        last = self.count - 1
        if side == 0:
            there = (sender >= 0) & (sender < last) & (block >= 0)
            taker = sender + 1
        else:
            there = (sender <= last) & (sender > 0) & (block <= last)
            taker = sender - 1
        if self.needed is None:
            return there
        return there & self.needed(side, taker, block * self.rows + j * self.height, self.height)

    def outgoing(self, step, j, act):
        r = self.rank
        for side, block, target in ((0, r - step, r + 1), (1, r + step, r - 1)):

            @pl.when(self.goes(side, r, block, j))
            def _():
                act(self.copy(side, step, j, block, target))

    def start(self, step):
        for j in range(self.strips):
            self.outgoing(step, j, lambda c: c.start())

    def arrived(self, step, onward):
        r = self.rank
        for j in range(self.strips):
            for side, block, source in ((0, r - 1 - step, r - 1), (1, r + 1 + step, r + 1)):

                @pl.when(self.goes(side, source, block, j))
                def _():
                    self.copy(side, step, j, block, source).wait_recv()

            if onward:
                self.outgoing(step + 1, j, lambda c: c.start())

    def sent(self, step):
        for j in range(self.strips):
            self.outgoing(step, j, lambda c: c.wait_send())


def front_kernel(n, count, rows, erows, *refs):
    shards = refs[0:11]
    tok, enc, cot, seg_ref, prefix_ref = refs[11:16]
    vectors = refs[16:24]
    (
        wa_out, wb, small_all, x_out, e_all, prev, halo_out, q_out, k_out, v_out, mix_ref, lse_out
    ) = refs[24:36]
    wa, x_all, q_ref, k_ref, v_ref = refs[36:41]
    far_mix, far_top, far_total = refs[41:44]
    stage, bias, lse_sc, info, local, fsend, frecv, zsend, zrecv, csend, crecv, osem = refs[44:]
    me, bits = my_place(n)
    rank = lax.axis_index("seq")
    last = count - 1
    glen = count * rows
    prompt = glen // 3
    piece = D // n
    d = bit_count(n)

    here = at_bits(bits, ())
    table_a, _ = qkv_rows(n)
    table_b, _ = rest_rows(n)
    copies = []

    def keep(src, dst):
        copy = pltpu.make_async_copy(src, dst, local.at[len(copies)])
        copy.start()
        copies.append(copy)

    keep(tok, x_all.at[:, pl.ds(pl.multiple_of(rank * rows, 16), rows)])
    keep(enc, e_all.at[:, pl.ds(pl.multiple_of(rank * erows, 16), erows)])
    names = ("wq", "wk", "wv", "wout", "cq", "ck", "cv", "cout", "up", "down", "slot")
    for name, shard in zip(names, shards):
        start, size = (table_a if name in table_a else table_b)[name]
        target = wa.at[here] if name in table_a else stage
        if name == "up":
            for c in range(4):
                keep(shard.at[:, pl.ds(c * D, D)], target.at[pl.ds(start + c * piece, piece)])
        else:
            keep(shard, target.at[pl.ds(start, size)])
    small_all[here] = jnp.zeros((16, 128), F32)
    for r, vector in enumerate(vectors[0:7]):
        small_all[here + (slice(r, r + 1), slice(0, D // n))] = vector[...].astype(F32).reshape(1, D // n)
    edge_rows, edge_width = max(1, FF // n // 128), min(128, FF // n)
    small_all[here + (slice(8, 8 + edge_rows), slice(0, edge_width))] = (
        vectors[7][...].astype(F32).reshape(edge_rows, edge_width)
    )

    peers = [("fsdp", partner_of(me, bits, b), None) for b in range(d)]
    peers += [("seq", rank - 1, rank > 0), ("seq", rank + 1, rank < last)]
    greet(peers)

    arrays = (wa, wb, small_all)
    units = weight_units(n) + [(2, 0, 16, 0, 128, 0)]
    order_list = orders(n)

    def hop(u, phase, theirs=False):
        array, r0, nr, c0, nc, which = units[u]
        order = order_list[which]
        b = order[phase]
        cut = (pl.ds(r0, nr), pl.ds(c0, nc))
        fixed = {b: 1 - bits[b]} if theirs else {}
        part = arrays[array].at[at_bits(bits, order[:phase], fixed) + cut]
        src = stage.at[cut] if array == 1 and phase == 0 and not theirs else part
        return pltpu.make_async_remote_copy(
            src_ref=src, dst_ref=part, send_sem=fsend.at[u, phase], recv_sem=frecv.at[u, phase],
            device_id={"fsdp": partner_of(me, bits, b)}, device_id_type=MESH_ID,
        )

    def landed(u, phase):
        hop(u, phase, True).wait_recv()

    def onward(some, phase):
        for u in some:
            landed(u, phase - 1)
            hop(u, phase).start()

    def needed(side, taker, start, height):
        low, high = key_span(taker, rows, glen)
        if side == 0:
            return (start < prompt) | (start + height > low)
        return (start < prompt) | (start < high)

    copies[0].wait()
    copies[1].wait()
    sems = (zsend, zrecv)
    strips = rows // STRIP
    toks = [Chain(x_all.at[m], rows, strips, sems, m, rank, count, needed) for m in range(MICRO)]
    encs = Chain(e_all, erows, 1, sems, MICRO, rank, count, None)
    toks[0].start(0)
    halo = pltpu.make_async_remote_copy(
        src_ref=cot.at[:, pl.ds(rows - HALO, HALO)], dst_ref=prev, send_sem=csend, recv_sem=crecv,
        device_id={"seq": rank + 1}, device_id_type=MESH_ID,
    )

    @pl.when(rank < last)
    def _():
        halo.start()

    for strip in range(glen // STRIP):
        start, block = strip * STRIP, strip * STRIP // rows
        side0, side1 = needed(0, rank, start, STRIP), needed(1, rank, start, STRIP)
        unseen = ((block < rank) & jnp.logical_not(side0)) | ((block > rank) & jnp.logical_not(side1))

        @pl.when(unseen)
        def _():
            x_all[:, start : start + STRIP, :] = jnp.zeros((MICRO, STRIP, D), BF)

    for copy in copies[2:]:
        copy.wait()
    everything = list(range(len(units)))
    for u in everything:
        hop(u, 0).start()
    settle = pltpu.make_async_copy(stage, wb.at[here], local.at[len(copies)])
    settle.start()
    first = pltpu.make_async_copy(cot.at[:, pl.ds(rows - HALO, HALO)], prev, local.at[len(copies) + 1])

    @pl.when(rank == 0)
    def _():
        first.start()

    settle.wait()
    onward(everything[:6], 1)
    for s in range(1, count):
        toks[0].arrived(s - 1, s < count - 1)
        if s == 1:
            onward(everything[6:], 1)
        if s == count - 2:
            toks[1].start(0)
    if d > 2:
        for phase in range(2, d):
            onward(everything[:2], phase)
    landed(0, d - 1)
    landed(1, d - 1)

    off = pl.multiple_of(rank * rows, 128)
    edge = pl.multiple_of(jnp.minimum(rank * rows + rows, glen - 128), 128)
    n_lead = (n, 3 * piece, D)

    def weight(name):
        start, size = table_a[name]
        return wa[(slice(None),) * d + (slice(start, start + size),)].reshape(D, D)

    def project(m, low, high):
        def one_tile(tile, _):
            at = pl.ds(pl.multiple_of(tile * 256, 256), 256)
            part = x_all[m, at, :]
            k_ref[m, at, :] = nn(part, weight("wk")).astype(BF)
            v_ref[m, at, :] = nn(part, weight("wv")).astype(BF)
            return 0

        lax.fori_loop(low, high, one_tile, 0)

    def query(m):
        edge_rows = x_all[m, pl.ds(edge, HALO), :]
        halo_out[m] = edge_rows
        q_ref[m, 0:rows, :] = (nn(x_all[m, pl.ds(off, rows), :], weight("wq")).astype(BF) * SCALE).astype(BF)
        q_ref[m, rows : rows + HALO, :] = (nn(edge_rows, weight("wq")).astype(BF) * SCALE).astype(BF)
        place_info(info, seg_ref, prefix_ref, m)
        seg_row = info[1:2, :]
        place = lax.broadcasted_iota(jnp.int32, (1, glen), 1)
        for start, size, span in ((0, rows, pl.ds(off, rows)), (rows, HALO, pl.ds(edge, 128))):
            column = info[:, span].T[0:size]
            limit, seg = column[:, 0:1], column[:, 1:2]
            seen = jnp.where(
                place < prompt, (place.astype(F32) < limit).astype(jnp.int32), (seg_row == seg).astype(jnp.int32)
            )
            bias[start : start + size, :] = jnp.where(seen == 1, 0.0, NEG)

    def pairs(m, low, high):
        def one_pair(pair, _):
            at = lanes_of(pair)
            mix = attend_pair(
                q_ref[m, :, at], k_ref[m, :, at], v_ref[m, :, at], bias[...], pair, lse_sc
            )
            mix_ref[m, :, at] = mix.astype(BF)
            return 0

        lax.fori_loop(low, high, one_pair, 0)
        if high == HEADS // 2:
            lse_out[m] = lse_sc[0:rows, :].T[0:HEADS, :]

    stores = []

    def store(src, to):
        copy = pltpu.make_async_copy(src, to, osem.at[len(stores)])
        copy.start()
        stores.append(copy)

    def store_micro(m):
        for src, to in ((x_all, x_out), (k_ref, k_out), (v_ref, v_out), (q_ref, q_out)):
            store(src.at[m], to.at[m])

    def far_pairs(m, split):
        def one_pair(pair, _):
            at = lanes_of(pair)
            attend_far(
                q_ref[m, :, at], k_ref[m, split:glen, at], v_ref[m, split:glen, at],
                bias[:, split:glen], pair, far_mix, far_top, far_total,
            )
            return 0

        lax.fori_loop(0, HEADS // 2, one_pair, 0)

    def near_pairs(m, split, low, high):
        def one_pair(pair, _):
            at = lanes_of(pair)
            mix = attend_near(
                q_ref[m, :, at], k_ref[m, 0:split, at], v_ref[m, 0:split, at],
                bias[:, 0:split], pair, lse_sc, far_mix, far_top, far_total,
            )
            mix_ref[m, :, at] = mix.astype(BF)
            return 0

        lax.fori_loop(low, high, one_pair, 0)
        if high == HEADS // 2:
            lse_out[m] = lse_sc[0:rows, :].T[0:HEADS, :]

    rest = everything[2:]
    near = -(-rows // 256)
    project(0, 0, glen // 256)
    query(0)
    store(wa, wa_out)
    store_micro(0)
    pairs(0, 0, 2)
    toks[1].arrived(0, count > 2)
    encs.start(0)
    for phase in range(2, d):
        onward(rest[: len(rest) // 2], phase)
    pairs(0, 2, 4)
    for s in range(1, count - 2):
        toks[1].arrived(s, True)
    encs.arrived(0, count > 2)
    for phase in range(2, d):
        onward(rest[len(rest) // 2 :], phase)
    project(1, near, glen // 256)
    query(1)
    far_pairs(1, near * 256)
    toks[1].arrived(count - 2, False)
    project(1, 0, near)
    store_micro(1)
    near_pairs(1, near * 256, 0, 2)
    for s in range(1, count - 1):
        encs.arrived(s, s < count - 2)
    near_pairs(1, near * 256, 2, 4)

    for u in rest:
        landed(u, d - 1)

    @pl.when(rank > 0)
    def _():
        halo.wait_recv()

    @pl.when(rank == 0)
    def _():
        first.wait()

    @pl.when(rank < last)
    def _():
        halo.wait_send()

    for u in everything:
        for phase in range(d):
            hop(u, phase).wait_send()
    for chain in toks + [encs]:
        for s in range(count - 1):
            chain.sent(s)
    for copy in stores:
        copy.wait()


def front(n, count, shards, vectors, tok, enc, cot, seg, prefix):
    rows, erows = tok.shape[1], enc.shape[1]
    glen = count * rows
    ext = rows + HALO
    lead = (2,) * bit_count(n)
    _, ra = qkv_rows(n)
    _, rb = rest_rows(n)
    units = len(weight_units(n)) + 1
    d = bit_count(n)
    hbm = pl.BlockSpec(memory_space=pl.ANY)
    dma = pltpu.SemaphoreType.DMA
    strips = rows // STRIP
    return pl.pallas_call(
        functools.partial(front_kernel, n, count, rows, erows),
        in_specs=[hbm] * 14 + [VM, SMEM] + [VM] * 8,
        out_specs=[hbm, hbm, VM, hbm, VM, VM, VM, hbm, hbm, hbm, VM, VM],
        out_shape=[
            jax.ShapeDtypeStruct(lead + (ra, D), BF),
            jax.ShapeDtypeStruct(lead + (rb, D), BF),
            jax.ShapeDtypeStruct(lead + (16, 128), F32),
            jax.ShapeDtypeStruct((MICRO, glen, D), BF),
            jax.ShapeDtypeStruct((MICRO, count * erows, D), BF),
            jax.ShapeDtypeStruct((MICRO, HALO, D), BF),
            jax.ShapeDtypeStruct((MICRO, HALO, D), BF),
            jax.ShapeDtypeStruct((MICRO, ext, D), BF),
            jax.ShapeDtypeStruct((MICRO, glen, D), BF),
            jax.ShapeDtypeStruct((MICRO, glen, D), BF),
            jax.ShapeDtypeStruct((MICRO, ext, D), BF),
            jax.ShapeDtypeStruct((MICRO, HEADS, rows), F32),
        ],
        scratch_shapes=[
            pltpu.VMEM(lead + (ra, D), BF), pltpu.VMEM((MICRO, glen, D), BF),
            pltpu.VMEM((MICRO, ext, D), BF), pltpu.VMEM((MICRO, glen, D), BF),
            pltpu.VMEM((MICRO, glen, D), BF),
            pltpu.VMEM((ext, D), F32), pltpu.VMEM((ext, 128), F32), pltpu.VMEM((ext, 128), F32),
            pltpu.VMEM((rb, D), BF), pltpu.VMEM((ext, glen), F32), pltpu.VMEM((ext, 128), F32),
            pltpu.VMEM((8, glen), F32),
            dma((20,)), dma((units, d)), dma((units, d)),
            dma((MICRO + 1, 2, count, strips)), dma((MICRO + 1, 2, count, strips)), dma(()), dma(()), dma((10,)),
        ],
        compiler_params=pltpu.CompilerParams(
            collective_id=0, has_side_effects=True, vmem_limit_bytes=60 * MIB
        ),
        name="front",
    )(*shards, tok, enc, cot, seg, prefix, *vectors)


TILE = 256
GROUPS = 12
SLOTS = ((-2, -1, 1, 4), (-2, 0, 3, 6), (-2, 1, 5, 7), (-2, 3, 6, 8), (-2, 3, 6, 8))


def seen_from(side, taker, start, height, rows, glen):
    low, high = key_span(taker, rows, glen)
    if side == 0:
        return (start < glen // 3) | (start + height > low)
    return (start < glen // 3) | (start < high)


def static_wants(side, taker, start, rows, glen):
    prompt = glen // 3
    least = (glen - prompt) // 8
    most = (glen - prompt) - 3 * least
    first, stop = taker * rows, (taker + 1) * rows + 1
    low = max(first - most, prompt + least if first >= prompt + most else prompt)
    high = min(stop + most, glen - least if stop <= glen - most else glen) if stop > prompt else 0
    return start < prompt or (start + STRIP > low if side == 0 else start < high)


def back_kernel(n, count, rows, erows, *refs):
    q_ref, mix_ref, dmix_ref, lse_ref, tok_ref, wa, genc, gs, seg_ref, prefix_ref = refs[0:10]
    x_hbm, k_hbm, v_hbm, dr1_hbm, gb = refs[10:15]
    outs = refs[15:18]
    tok_out, enc_out = refs[18:20]
    rest = list(refs[20:])
    d = bit_count(n)
    glen = count * rows
    prompt = glen // 3
    tiles = glen // TILE

    def take(k):
        got = rest[:k]
        del rest[:k]
        return got

    accs, zls, zrs, zss, fins = take(3), take(3), take(3), take(3), take(3)
    recvs = [take(d) for _ in range(3)]
    ebuf, ga, part, inc, wkv, qst, dst, stats, info, bias, dqt, dkv, gkv, dqs = take(14)
    kbuf, vbuf, xbuf = take(3)
    fsend, frecv, zsend, zrecv, tsend, trecv, esend, erecv, lsem, tsem, dsem = rest
    grads = (ga, gb, gs)
    me, bits = my_place(n)
    rank = lax.axis_index("seq")
    last = count - 1
    off = pl.multiple_of(rank * rows, 128)
    table, _ = qkv_rows(n)

    def weight(name):
        start, size = table[name]
        return wa[:, start : start + size, :].reshape(D, D)

    def tile_copies(i, slot):
        m, at = i // tiles, pl.ds(pl.multiple_of((i % tiles) * TILE, TILE), TILE)
        return [
            pltpu.make_async_copy(hbm.at[m, at], buf.at[slot], tsem.at[slot, j])
            for j, (hbm, buf) in enumerate(((k_hbm, kbuf), (v_hbm, vbuf), (x_hbm, xbuf)))
        ]

    for copy in tile_copies(0, 0):
        copy.start()
    start_out = pltpu.make_async_copy(dr1_hbm, tok_out, dsem)
    start_out.start()

    piece = D // n
    early_units = weight_units(n)[2:] + [(2, 0, 16, 0, 128, 0)]
    late_units = [
        (0, c * piece, w * piece, half * 256, 256, half) for c, w in ((1, 2), (0, 1)) for half in range(2)
    ]
    units = early_units + late_units
    early, late = list(range(len(early_units))), list(range(len(early_units), len(units)))
    order_list = [o[::-1] for o in orders(n)]

    def own_half(u):
        array, r0, nr, c0, nc, which = units[u]
        cut = (pl.ds(r0, nr), pl.ds(c0, nc))
        index = at_bits(bits, range(1, d))
        return pltpu.make_async_copy(
            gb.at[index + cut], accs[1].at[(slice(None),) * (d - 1) + cut], lsem.at[u]
        )

    big = [u for u in early if units[u][0] == 1]
    for u in big:
        own_half(u).start()

    peers = [("fsdp", partner_of(me, bits, b), None) for b in range(d)]
    peers += [("seq", lax.rem(rank + k, count), None) for k in range(1, count)]
    greet(peers)

    def hop(u, phase):
        array, r0, nr, c0, nc, which = units[u]
        order = order_list[which]
        b = order[phase]
        free = [x for x in range(d) if x not in order[: phase + 1]]
        cut = (pl.ds(r0, nr), pl.ds(c0, nc))
        index = at_bits(bits, free, {b: 1 - bits[b]})
        src = grads[array].at[index + cut] if phase == 0 else accs[array].at[index[:-1] + cut]
        to = recvs[array][phase].at[(slice(None),) * len(free) + cut]
        return pltpu.make_async_remote_copy(
            src_ref=src, dst_ref=to, send_sem=fsend.at[u, phase], recv_sem=frecv.at[u, phase],
            device_id={"fsdp": partner_of(me, bits, b)}, device_id_type=MESH_ID,
        )

    def add(u, phase):
        array, r0, nr, c0, nc, which = units[u]
        order = order_list[which]
        free = [x for x in range(d) if x not in order[: phase + 1]]
        cut = (slice(r0, r0 + nr), slice(c0, c0 + nc))
        index = at_bits(bits, free)
        hop(u, phase).wait_recv()
        if phase == 0 and array == 1:
            own_half(u).wait()
        base = grads[array][index + cut] if phase == 0 and array != 1 else accs[array][index[:-1] + cut]
        more = recvs[array][phase][(slice(None),) * len(free) + cut]
        accs[array][index[:-1] + cut] = (base.astype(F32) + more.astype(F32)).astype(base.dtype)
        if phase + 1 < d:
            hop(u, phase + 1).start()

    here = at_bits(bits, ())[:-1]

    def root_of(which):
        return (count - 1) // 2 if which == 0 else count // 2

    def z_copy(u, kind, src, to, target):
        return pltpu.make_async_remote_copy(
            src_ref=src, dst_ref=to, send_sem=zsend.at[u, kind], recv_sem=zrecv.at[u, kind],
            device_id={"seq": target}, device_id_type=MESH_ID,
        )

    def z_refs(u):
        array, r0, nr, c0, nc, which = units[u]
        cut = (pl.ds(r0, nr), pl.ds(c0, nc))
        return [x[array].at[cut] for x in (zss, zls, zrs, fins)], root_of(which)

    def z_in(u, step):
        array, r0, nr, c0, nc, which = units[u]
        cut = (slice(r0, r0 + nr), slice(c0, c0 + nc))
        (zs, zl, zr, fin), root = z_refs(u)
        turn = max(root, last - root)

        def own():
            return accs[array][here + cut].astype(F32)

        if step < turn:

            @pl.when((rank < root) & (rank == step))
            def _():
                if step == 0:
                    zss[array][cut] = accs[array][here + cut]
                else:
                    z_copy(u, 0, zs, zl, rank - 1).wait_recv()
                    zss[array][cut] = (own() + zls[array][cut].astype(F32)).astype(zss[array].dtype)
                z_copy(u, 0, zs, zl, rank + 1).start()

            @pl.when((rank > root) & (last - rank == step))
            def _():
                if step == 0:
                    zss[array][cut] = accs[array][here + cut]
                else:
                    z_copy(u, 1, zs, zr, rank + 1).wait_recv()
                    zss[array][cut] = (own() + zrs[array][cut].astype(F32)).astype(zss[array].dtype)
                z_copy(u, 1, zs, zr, rank - 1).start()

        if step == turn:

            @pl.when(rank == root)
            def _():
                total = own()
                if root > 0:
                    z_copy(u, 0, zs, zl, rank - 1).wait_recv()
                    total = total + zls[array][cut].astype(F32)
                if root < last:
                    z_copy(u, 1, zs, zr, rank + 1).wait_recv()
                    total = total + zrs[array][cut].astype(F32)
                fins[array][cut] = total.astype(fins[array].dtype)
                if root > 0:
                    z_copy(u, 2, fin, fin, rank - 1).start()
                if root < last:
                    z_copy(u, 3, fin, fin, rank + 1).start()
                outs[array][cut] = fins[array][cut]

    def z_out(u, step):
        array, r0, nr, c0, nc, which = units[u]
        cut = (slice(r0, r0 + nr), slice(c0, c0 + nc))
        (zs, zl, zr, fin), root = z_refs(u)
        far = step + 1

        if root - far >= 0:

            @pl.when(rank == root - far)
            def _():
                z_copy(u, 2, fin, fin, rank + 1).wait_recv()
                if root - far > 0:
                    z_copy(u, 2, fin, fin, rank - 1).start()
                outs[array][cut] = fins[array][cut]

        if root + far <= last:

            @pl.when(rank == root + far)
            def _():
                z_copy(u, 3, fin, fin, rank - 1).wait_recv()
                if root + far < last:
                    z_copy(u, 3, fin, fin, rank + 1).start()
                outs[array][cut] = fins[array][cut]

    def z_sent(u):
        (zs, zl, zr, fin), root = z_refs(u)

        @pl.when(rank < root)
        def _():
            z_copy(u, 0, zs, zl, rank + 1).wait_send()

        @pl.when(rank > root)
        def _():
            z_copy(u, 1, zs, zr, rank - 1).wait_send()

        @pl.when((rank <= root) & (rank > 0))
        def _():
            z_copy(u, 2, fin, fin, rank - 1).wait_send()

        @pl.when((rank >= root) & (rank < last))
        def _():
            z_copy(u, 3, fin, fin, rank + 1).wait_send()

    moves = []
    for k in range(1, count):
        to = lax.rem(rank + k, count)
        moves.append(
            pltpu.make_async_remote_copy(
                src_ref=genc.at[:, pl.ds(pl.multiple_of(to * erows, 16), erows)],
                dst_ref=ebuf.at[k - 1],
                send_sem=esend.at[k - 1], recv_sem=erecv.at[k - 1],
                device_id={"seq": to}, device_id_type=MESH_ID,
            )
        )
    for move in moves:
        move.start()

    def wants(side, taker, start):
        return seen_from(side, taker, start, STRIP, rows, glen)

    def strip_copy(m, strip, side, target):
        start = strip * STRIP
        if not isinstance(start, int):
            start = pl.multiple_of(start, STRIP)
        return pltpu.make_async_remote_copy(
            src_ref=part.at[m, pl.ds(start, STRIP)],
            dst_ref=inc.at[m, pl.ds(start + side * rows, STRIP)],
            send_sem=tsend.at[m, strip, side], recv_sem=trecv.at[m, strip, side],
            device_id={"seq": target}, device_id_type=MESH_ID,
        )

    def coming(strip, side):
        start = strip * STRIP
        owner = start // rows
        if side == 0:
            return (owner <= rank) & (rank < last) & wants(0, rank + 1, start)
        return (owner >= rank) & (rank > 0) & wants(1, rank - 1, start)

    def going(strip, side):
        start = strip * STRIP
        owner = start // rows
        if side == 0:
            return (owner < rank) & wants(0, rank, start)
        return (owner > rank) & wants(1, rank, start)

    def static_going(strip, side, who):
        start = strip * STRIP
        owner = start // rows
        if side == 0:
            return owner < who <= last and bool(static_wants(0, who, start, rows, glen))
        return owner > who >= 0 and bool(static_wants(1, who, start, rows, glen))

    def pass_on(m, strip, side, who):
        start = strip * STRIP
        at = slice(start, start + STRIP)
        source = who + 1 if side == 0 else who - 1

        @pl.when(rank == who)
        def _():
            if static_going(strip, side, source):
                strip_copy(m, strip, side, source).wait_recv()
                there = slice(start + side * rows, start + side * rows + STRIP)
                part[m, at, :] = (part[m, at, :].astype(F32) + inc[m, there, :].astype(F32)).astype(BF)
            strip_copy(m, strip, side, who - 1 if side == 0 else who + 1).start()

    def finish_rows(m):
        for j in range(rows // STRIP):
            strip = rank * (rows // STRIP) + j
            at = pl.ds(pl.multiple_of(strip * STRIP, STRIP), STRIP)
            mine = slice(j * STRIP, (j + 1) * STRIP)
            tok_out[m, mine, :] += part[m, at, :].astype(F32)
            for side in range(2):

                @pl.when(coming(strip, side))
                def _():
                    strip_copy(m, strip, side, rank).wait_recv()
                    there = pl.ds(pl.multiple_of(strip * STRIP + side * rows, STRIP), STRIP)
                    tok_out[m, mine, :] += inc[m, there, :].astype(F32)

    wkv[:, 0:D] = weight("wk")
    wkv[:, D : 2 * D] = weight("wv")
    gkv[...] = jnp.zeros_like(gkv)

    def begin(m):
        place_info(info, seg_ref, prefix_ref, m)
        dqt[...] = jnp.zeros_like(dqt)
        delta = head_sums(dmix_ref[m].astype(F32) * mix_ref[m, 0:rows, :].astype(F32))
        for pair in range(HEADS // 2):
            at = slice(pair * 128, (pair + 1) * 128)
            for h in range(2):
                row = 2 * pair + h
                span = slice(h * rows, (h + 1) * rows)
                qst[pair, span, :] = head_masked(q_ref[m, 0:rows, at], h)
                dst[pair, span, :] = head_masked(dmix_ref[m, :, at], h)
                stats[pair : pair + 1, span] = lse_ref[m, row : row + 1, :]
                stats[4 + pair : 5 + pair, span] = delta[row : row + 1, :]

    def one_tile(m):
        def body(t, _):
            i = m * tiles + t
            slot = i % 2

            for copy in tile_copies(i, slot):
                copy.wait()

            @pl.when(i + 1 < MICRO * tiles)
            def _():
                for copy in tile_copies(i + 1, 1 - slot):
                    copy.start()

            at_keys = pl.ds(pl.multiple_of(t * TILE, TILE), TILE)
            place = lax.broadcasted_iota(jnp.int32, (TILE, 1), 0) + t * TILE
            key_seg = info[:, at_keys].T[:, 1:2]
            limit = info[0:1, pl.ds(off, rows)]
            seg = info[1:2, pl.ds(off, rows)]
            seen = jnp.where(
                place < prompt, (place.astype(F32) < limit).astype(jnp.int32), (key_seg == seg).astype(jnp.int32)
            )
            mask = jnp.where(seen == 1, 0.0, NEG)
            bias[:, 0:rows] = mask
            bias[:, rows : 2 * rows] = mask

            def one_pair(pair, _):
                at = lanes_of(pair)
                kp, vp = kbuf[slot, :, at], vbuf[slot, :, at]
                prob = jnp.exp(nt(kp, qst[pair]) + bias[...] - stats[pl.ds(pair, 1), :])
                d_score = (prob * (nt(vp, dst[pair]) - stats[pl.ds(4 + pair, 1), :])).astype(BF)
                dkv[:, at] = nn(d_score, qst[pair]).astype(BF)
                dkv[:, pl.ds(pl.multiple_of(D + pair * 128, 128), 128)] = nn(
                    prob.astype(BF), dst[pair]
                ).astype(BF)
                d_q = nn(kp.T, d_score)
                sub = lax.broadcasted_iota(jnp.int32, (128, rows), 0)
                dqt[at, :] += jnp.where(sub < 64, d_q[:, 0:rows], d_q[:, rows : 2 * rows])
                return 0

            lax.fori_loop(0, HEADS // 2, one_pair, 0)
            part[m, at_keys, :] = nt(dkv[...], wkv[...]).astype(BF)
            gkv[...] += tn(xbuf[slot], dkv[...])
            return 0

        return body

    def end(m):
        for pair in range(HEADS // 2):
            at = slice(pair * 128, (pair + 1) * 128)
            dqs[m, :, at] = (dqt[at, :] * SCALE).T.astype(BF)
        if m == 0:
            start_out.wait()
        tok_out[m] += nt(dqs[m], weight("wq"))

    todo = {}

    def later(when, job, *what):
        todo.setdefault(when, []).append(functools.partial(job, *what))

    def plan(some, times, begun=0):
        for u in some:
            for phase in range(begun, d):
                later(times[min(phase, 2)] + max(phase - 2, 0), add, u, phase)
            at = times[2] + max(d - 3, 0)
            root = root_of(units[u][5])
            turn = max(root, last - root)
            for step in range(turn + 1):
                later(at + step, z_in, u, step)
            for step in range(last):
                later(at + turn + 1 + step, z_out, u, step)

    def begin_sum(some):
        for u in some:
            hop(u, 0).start()

    for c, times in enumerate(SLOTS):
        plan(early[2 * c : 2 * c + 2], times[1:])
        later(times[0], begin_sum, early[2 * c : 2 * c + 2])
    per = MICRO * tiles // GROUPS
    strips = TILE // STRIP
    passes = []
    for i in range(GROUPS):
        m, t0 = i * per // tiles, (i * per) % tiles
        for strip in range(t0 * strips, (t0 + per) * strips):
            for dist in range(count):
                for side in range(2):
                    who = last - dist if side == 0 else dist
                    if static_going(strip, side, who):
                        passes.append((m, strip, side, who))
                        later(i + 2 * (dist if side == 0 else max(dist - 1, 0)), pass_on, m, strip, side, who)
    later(GROUPS - 2, finish_rows, 0)

    def put(name, value):
        start, size = table[name]
        where = (slice(None),) * d + (slice(start, start + size),)
        ga[where] = value.astype(BF).reshape((2,) * d + (size, D))

    for job in todo.pop(-2, []):
        job()
    for i in range(GROUPS):
        m, t0 = i * per // tiles, (i * per) % tiles
        if t0 == 0:
            begin(m)
        if i == 0:
            for job in todo.pop(-1, []):
                job()
        lax.fori_loop(t0, t0 + per, one_tile(m), 0)
        if i == GROUPS - 1:
            put("wk", gkv[:, 0:D])
            put("wv", gkv[:, D : 2 * D])
            begin_sum(late[0:2])
        if t0 + per == tiles:
            end(m)
        if i == GROUPS - 1:
            for u in late[0:2]:
                add(u, 0)
        for job in todo.pop(i, []):
            job()

    put("wq", tn(tok_ref[...].reshape(MICRO * rows, D), dqs[...].reshape(MICRO * rows, D)))
    begin_sum(late[2:4])
    waiting = dict(todo)
    todo.clear()
    for c in range(2):
        plan(late[2 * c : 2 * c + 2], (GROUPS, GROUPS + c, GROUPS + c + 1), 1 - c)
    for when in waiting:
        todo.setdefault(when, []).extend(waiting[when])
    for i in sorted(todo):
        for job in todo[i]:
            job()
    finish_rows(1)
    for move in moves:
        move.wait_recv()
    emine = pl.ds(pl.multiple_of(rank * erows, 16), erows)
    for m in range(MICRO):
        states = genc[m, emine, :].astype(F32)
        for k in range(1, count):
            states = states + ebuf[k - 1, m].astype(F32)
        enc_out[m] = states
    for move in moves:
        move.wait_send()
    for m, strip, side, who in passes:

        @pl.when(rank == who)
        def _():
            strip_copy(m, strip, side, who - 1 if side == 0 else who + 1).wait_send()

    for u in range(len(units)):
        for phase in range(d):
            hop(u, phase).wait_send()
        z_sent(u)


def back(n, count, q, mix, dmix, lse, tok, wa, genc, gs, seg, prefix, x_all, k, v, dr1, gb):
    rows = tok.shape[1]
    erows = genc.shape[1] // count
    glen = count * rows
    d = bit_count(n)
    units = len(weight_units(n)) + 3
    dma = pltpu.SemaphoreType.DMA
    V = pltpu.VMEM
    hbm = pl.BlockSpec(memory_space=pl.ANY)
    flat = [(wa.shape[-2], D), (gb.shape[-2], D), (16, 128)]
    types = [BF, BF, F32]
    scratch = [V((2,) * (d - 1) + f, t) for f, t in zip(flat, types)]
    for _ in range(4):
        scratch += [V(f, t) for f, t in zip(flat, types)]
    for f, t in zip(flat, types):
        scratch += [V((2,) * (d - 1 - p) + f, t) for p in range(d)]
    scratch += [
        V((count - 1, MICRO, erows, D), BF),
        V((2,) * d + flat[0], BF),
        V((MICRO, glen, D), BF), V((MICRO, glen + rows, D), BF),
        V((D, 2 * D), BF),
        V((HEADS // 2, 2 * rows, 128), BF), V((HEADS // 2, 2 * rows, 128), BF),
        V((8, 2 * rows), F32), V((8, glen), F32), V((TILE, 2 * rows), F32),
        V((D, rows), F32), V((TILE, 2 * D), BF), V((D, 2 * D), F32),
        V((MICRO, rows, D), BF),
        V((2, TILE, D), BF), V((2, TILE, D), BF), V((2, TILE, D), BF),
    ]
    strips = glen // STRIP
    scratch += [
        dma((units, d)), dma((units, d)), dma((units, 4)), dma((units, 4)),
        dma((MICRO, strips, 2)), dma((MICRO, strips, 2)), dma((count - 1,)), dma((count - 1,)),
        dma((units,)), dma((2, 3)), dma(()),
    ]
    return pl.pallas_call(
        functools.partial(back_kernel, n, count, rows, erows),
        in_specs=[VM] * 9 + [SMEM] + [hbm] * 5,
        out_specs=[VM] * 5,
        out_shape=[jax.ShapeDtypeStruct(f, t) for f, t in zip(flat, types)]
        + [jax.ShapeDtypeStruct((MICRO, rows, D), F32), jax.ShapeDtypeStruct((MICRO, erows, D), F32)],
        scratch_shapes=scratch,
        compiler_params=pltpu.CompilerParams(
            collective_id=1, has_side_effects=True, vmem_limit_bytes=60 * MIB
        ),
        name="back",
    )(q, mix, dmix, lse, tok, wa, genc, gs, seg, prefix, x_all, k, v, dr1, gb)


FIRST = ("wq", "wk", "wv", "wout", "cq", "ck", "cv", "cout", "up")


def finish_kernel(n, *refs):
    oa, ob, os, tok, states = refs[0:5]
    outs = list(refs[5:])
    table_a, _ = qkv_rows(n)
    table_b, _ = rest_rows(n)
    outs[0][...] = tok[...]
    outs[1][...] = states[...]

    def matrix(name, out):
        table, src = (table_a, oa) if name in table_a else (table_b, ob)
        start, size = table[name]
        if name == "up":
            piece = size // 4
            for c in range(4):
                out[:, c * D : (c + 1) * D] = src[start + c * piece : start + (c + 1) * piece, :].astype(F32)
        else:
            out[...] = src[start : start + size, :].astype(F32)

    for name, out in zip(FIRST, outs[2:11]):
        matrix(name, out)
    edge, side = FF // n, D // n
    wide = outs[11]
    wide[...] = os[8 : 8 + max(1, edge // 128), 0 : min(edge, 128)].reshape(edge)
    matrix("down", outs[12])
    for k in range(7):
        outs[13 + k][...] = os[k : k + 1, 0:side].reshape(side)
    matrix("slot", outs[20])


def finish(n, oa, ob, os, tok, states):
    side, edge = D // n, FF // n
    square = (side, D)
    shapes = [tok.shape, states.shape] + [square] * 8 + [(side, FF), (edge,), (edge, D)]
    shapes += [(side,)] * 7 + [(2 * side, D)]
    return pl.pallas_call(
        functools.partial(finish_kernel, n),
        in_specs=[VM] * 5,
        out_specs=[VM] * len(shapes),
        out_shape=[jax.ShapeDtypeStruct(shape, F32) for shape in shapes],
        compiler_params=pltpu.CompilerParams(vmem_limit_bytes=60 * MIB),
        name="finish",
    )(oa, ob, os, tok, states)


def on_device(
    tokens, encoded, segment_ids, prefix_len, cotangent,
    w_query, w_key, w_value, w_out, c_query, c_key, c_value, c_out,
    w_up, b_up, w_down, b_down,
    gain_one, shift_one, gain_two, shift_two, gain_three, shift_three, w_slot,
):
    n = lax.axis_size("fsdp")
    count = lax.axis_size("seq")
    tokens = tokens[:, 0]
    rows = tokens.shape[1]
    prefix = prefix_len[:, 0]
    cot = cotangent[:, 0]

    shards = (w_query, w_key, w_value, w_out, c_query, c_key, c_value, c_out, w_up, w_down, w_slot)
    vectors = (b_down, gain_one, shift_one, gain_two, shift_two, gain_three, shift_three, b_up)
    (
        wa, wb, small_all, x_all, e_all, previous, edges, q, k, v, mix, lse
    ) = front(n, count, shards, vectors, tokens, encoded[:, 0], cot, segment_ids, prefix)
    wa = wa.reshape((n,) + wa.shape[-2:])
    wb = wb.reshape((n,) + wb.shape[-2:])
    small_all = small_all.reshape(n, 16, 128)
    slot_out, dmix, dr1, genc, gb, gs = middle(
        mix, tokens, edges, e_all, cot, previous, segment_ids, prefix, wb, small_all, rows
    )
    lead = (2,) * bit_count(n)
    gb = gb.reshape(lead + gb.shape[1:])
    gs = gs.reshape(lead + (16, 128))
    oa, ob, os, grad_tokens, grad_encoded = back(
        n, count, q, mix, dmix, lse, tokens, wa, genc, gs, segment_ids, prefix, x_all, k, v, dr1, gb
    )
    grad_tokens, grad_encoded, *others = finish(n, oa, ob, os, grad_tokens, grad_encoded)
    return (slot_out[:, None], grad_tokens[:, None], grad_encoded[:, None], *others)


def solution(mesh):
    act = P(None, "fsdp", "seq", None)
    ids = P(None, "fsdp", None)
    mat, one = P("fsdp", None), P("fsdp")
    in_specs = (
        (act, act, ids, ids, act) + (mat,) * 9 + (one, mat) + (one,) * 7 + (mat,)
    )
    out_specs = (act, act, act) + (mat,) * 9 + (one, mat) + (one,) * 7 + (mat,)
    return jax.shard_map(
        on_device, mesh=mesh, in_specs=in_specs, out_specs=out_specs, check_vma=False
    )
```
